32 devices in a mesh: res: 8 (over z, y), dp: 4 (over x, core).
Axes of the slice: x: 2, y: 2, z: 4, core: 2. Of those that a mesh axis runs over, the one named last changes fastest.
Arguments:
- aligned_chain_features: bfloat16 [512, 256, 256], P('dp', 'res'), parts along dimension 0, may hold values from -6 to 6
- pair_representation_state: bfloat16 [1024, 256, 128], P(('dp', 'res')), parts along dimension 0, may hold values from -6 to 6
- gap_block_flags: int32 [512, 2], P('dp'), parts along dimension 0, may hold values from 0 to 1, as said below
- pair_norm_gain: float32 [128], replicated, may hold values from 0.1 to 1.9
- pair_head_weight: bfloat16 [128, 8], replicated, may hold values from -0.5 to 0.5
- horizontal_scaling_factor: float32 [256], replicated, may hold values from 0.1 to 1.9
- row_input_weight: bfloat16 [256, 1024], replicated, may hold values from -2 to 2
- horizontal_final_matrix: bfloat16 [256, 256], replicated, may hold values from -0.375 to 0.375
- vertical_scaling_factor: float32 [256], replicated, may hold values from 0.1 to 1.9
- column_input_weight: bfloat16 [256, 1024], replicated, may hold values from -2 to 2
- vertical_final_matrix: bfloat16 [256, 256], replicated, may hold values from -0.375 to 0.375
- feedforward_scaling_factor: float32 [256], replicated, may hold values from 0.1 to 1.9
- feedforward_widen_matrix: bfloat16 [256, 1024], replicated, may hold values from -0.375 to 0.375
- feedforward_shrink_matrix: bfloat16 [1024, 256], replicated, may hold values from -0.1875 to 0.1875
Outputs:
- msa_out: bfloat16 [512, 256, 256], P('dp', 'res'), parts along dimension 0
The draws below stay inside these ranges and needn't reach their ends.
There are 4 independent parts, one for each index of `dp`. The reference program is written for one: setup_inputs(seed, part) draws one part's arguments, and reference() takes and returns one part's arrays. A program takes and returns all parts, laid end to end along the dimension named above; an argument that names none is the same for every part. Nothing has to cross between parts.
Inputs may be any that keep to these rules, and one draw needn't show every extreme that they name: `gap_block_flags`: row 0 holds no gap block, and every row has at least one block that is not a gap.
All inputs are finite; a program needn't handle non-finite values.
Results may differ from the reference program's by a relative error of at most 0.015.
The reference program's roundings to bfloat16 on the way count: a program that leaves them out, or rounds other values in their place, can miss the bound.
Values may be sent and summed in bfloat16 or wider, within the bound.
No kernel may reach another device: no remote copies, remote signals or barrier semaphores. Data moves between devices by JAX's collectives and lax.ppermute only.
A program may use at most 128 MiB of HBM per device.

```python
import jax
import jax.numpy as jnp
from jax import lax

FEATURE_DEPTH = 256
FOCUS_COUNT = 8
PER_HEADER_DEPTH = 32
CZ = 128
GROUPED_CHAINS = 128
WINDOW_SITES_N = 256
BLOCK = 128
WIDENED_UNITS = 1024


def draw_gap_block_flags(key, part):
    key = jax.random.fold_in(key, 11)
    key_level, key_rolls, key_keep = jax.random.split(key, 3)
    block_total = WINDOW_SITES_N // BLOCK
    gap_level = jax.random.randint(key_level, (GROUPED_CHAINS, 1), 0, 90)
    dice_rolls = jax.random.randint(key_rolls, (GROUPED_CHAINS, block_total), 0, 100)
    kept_block = jax.random.randint(key_keep, (GROUPED_CHAINS, 1), 0, block_total)
    block_ids = jnp.arange(block_total, dtype=jnp.int32)[None, :]
    seq_ids = jnp.arange(GROUPED_CHAINS, dtype=jnp.int32)[:, None]
    gap_flags = jnp.where(dice_rolls < gap_level, 1, 0)
    gap_flags = jnp.where(block_ids == kept_block, 0, gap_flags)
    gap_flags = jnp.where(seq_ids == 0, 0, gap_flags)
    return gap_flags.astype(jnp.int32)


def draw_row_input_weight(key, part):
    key = jax.random.fold_in(key, 23)
    random_seed_root = jax.random.fold_in(key, 0)
    random_seed_draw = jnp.clip(jax.random.normal(random_seed_root, (FEATURE_DEPTH, 4, FOCUS_COUNT, PER_HEADER_DEPTH), jnp.float32), -3.0, 3.0)
    return (random_seed_draw * FEATURE_DEPTH ** (-0.5)).reshape(FEATURE_DEPTH, 4 * FOCUS_COUNT * PER_HEADER_DEPTH).astype(jnp.bfloat16)


def draw_column_input_weight(key, part):
    key = jax.random.fold_in(key, 37)
    random_seed_root = jax.random.fold_in(key, 0)
    random_seed_draw = jnp.clip(jax.random.normal(random_seed_root, (FEATURE_DEPTH, 4, FOCUS_COUNT, PER_HEADER_DEPTH), jnp.float32), -3.0, 3.0)
    return (random_seed_draw * FEATURE_DEPTH ** (-0.5)).reshape(FEATURE_DEPTH, 4 * FOCUS_COUNT * PER_HEADER_DEPTH).astype(jnp.bfloat16)


def levels(stream_key, extent, shards, smallest, high):
    def one(axis_at, parts):
        heights = jax.random.uniform(jax.random.fold_in(jax.random.fold_in(stream_key, 6), axis_at), (parts,), jnp.float32, smallest / len(shards), high / len(shards))
        return jnp.repeat(jnp.exp(heights), extent[axis_at] // parts).reshape((-1,) + (1,) * (len(extent) - axis_at - 1))

    gain = one(*shards[0])
    for cut in shards[1:]:
        gain = gain * one(*cut)
    return gain


def gaussian(key, dims, scale, bound, cuts=(), kind=jnp.bfloat16):
    gain = levels(key, dims, cuts, -0.22, 0.18) if cuts else 1.0
    result = jax.random.normal(key, dims, jnp.float32) * scale * gain
    return jnp.minimum(jnp.maximum(result, -bound), bound).astype(kind)


def setup_inputs(seed: int = 0, part: int = 0) -> dict:
    arg_keys = jax.random.split(jax.random.key(seed), 15)
    own_keys = jax.random.split(jax.random.fold_in(arg_keys[14], part), 15)
    aligned_chain_features = gaussian(own_keys[0], (GROUPED_CHAINS, WINDOW_SITES_N, FEATURE_DEPTH), 1.0, 6.0, ((1, 8),))
    pair_representation_state = gaussian(own_keys[1], (WINDOW_SITES_N, WINDOW_SITES_N, CZ), 1.0, 6.0, ((0, 8),))
    gap_block_flags = draw_gap_block_flags(jax.random.fold_in(jax.random.fold_in(arg_keys[14], part), 71), part)
    pair_norm_gain = jnp.clip(1.0 + 0.18 * jax.random.normal(arg_keys[3], (CZ,), jnp.float32), 0.1, 1.9)
    pair_head_weight = gaussian(arg_keys[4], (CZ, FOCUS_COUNT), CZ ** -0.5, 0.5)
    horizontal_scaling_factor = jnp.clip(1.0 + 0.18 * jax.random.normal(arg_keys[5], (FEATURE_DEPTH,), jnp.float32), 0.1, 1.9)
    row_input_weight = draw_row_input_weight(jax.random.fold_in(arg_keys[14], 71), part)
    horizontal_final_matrix = gaussian(arg_keys[7], (FOCUS_COUNT * PER_HEADER_DEPTH, FEATURE_DEPTH), (FOCUS_COUNT * PER_HEADER_DEPTH) ** -0.5, 0.375)
    vertical_scaling_factor = jnp.clip(1.0 + 0.18 * jax.random.normal(arg_keys[8], (FEATURE_DEPTH,), jnp.float32), 0.1, 1.9)
    column_input_weight = draw_column_input_weight(jax.random.fold_in(arg_keys[14], 71), part)
    vertical_final_matrix = gaussian(arg_keys[10], (FOCUS_COUNT * PER_HEADER_DEPTH, FEATURE_DEPTH), (FOCUS_COUNT * PER_HEADER_DEPTH) ** -0.5, 0.375)
    feedforward_scaling_factor = jnp.clip(1.0 + 0.18 * jax.random.normal(arg_keys[11], (FEATURE_DEPTH,), jnp.float32), 0.1, 1.9)
    feedforward_widen_matrix = gaussian(arg_keys[12], (FEATURE_DEPTH, WIDENED_UNITS), FEATURE_DEPTH ** -0.5, 0.375)
    feedforward_shrink_matrix = gaussian(arg_keys[13], (WIDENED_UNITS, FEATURE_DEPTH), WIDENED_UNITS ** -0.5, 0.1875)
    return dict(aligned_chain_features=aligned_chain_features, pair_representation_state=pair_representation_state, gap_block_flags=gap_block_flags, pair_norm_gain=pair_norm_gain, pair_head_weight=pair_head_weight, horizontal_scaling_factor=horizontal_scaling_factor, row_input_weight=row_input_weight, horizontal_final_matrix=horizontal_final_matrix, vertical_scaling_factor=vertical_scaling_factor, column_input_weight=column_input_weight, vertical_final_matrix=vertical_final_matrix, feedforward_scaling_factor=feedforward_scaling_factor, feedforward_widen_matrix=feedforward_widen_matrix, feedforward_shrink_matrix=feedforward_shrink_matrix)


EPSILON = 1e-05
MASKED_SCORE = -1000000000.0

def layer_normalize(inputs, scale_gain):
    values_f = inputs.astype(jnp.float32)
    centred = values_f - lax.optimization_barrier(jnp.mean(values_f, axis=-1, keepdims=True))
    spread = lax.optimization_barrier(jnp.mean(centred * centred, axis=-1, keepdims=True))
    return centred * lax.rsqrt(spread + EPSILON) * scale_gain

def project(normed_bf, weights_in):
    projected = jnp.dot(normed_bf, weights_in, preferred_element_type=jnp.float32)
    projected = projected.reshape(projected.shape[0], 4, FOCUS_COUNT, PER_HEADER_DEPTH)
    queries = (projected[:, 0] * PER_HEADER_DEPTH ** (-0.5)).astype(jnp.bfloat16)
    keys_bf = projected[:, 1].astype(jnp.bfloat16)
    values_bf = projected[:, 2].astype(jnp.bfloat16)
    gates = jax.nn.sigmoid(projected[:, 3])
    return (queries, keys_bf, values_bf, gates)

def attend(queries, keys_bf, values_bf, extra, masked):
    scores = jnp.einsum('qhd,khd->hqk', queries.astype(jnp.float32), keys_bf.astype(jnp.float32))
    scores = scores + extra
    scores = jnp.where(masked[None, None, :], MASKED_SCORE, scores)
    weights_bf = jax.nn.softmax(scores, axis=-1).astype(jnp.bfloat16)
    return jnp.einsum('hqk,khd->qhd', weights_bf.astype(jnp.float32), values_bf.astype(jnp.float32))

def reference(aligned_chain_features, pair_representation_state, gap_block_flags, pair_norm_gain, pair_head_weight, horizontal_scaling_factor, row_input_weight, horizontal_final_matrix, vertical_scaling_factor, column_input_weight, vertical_final_matrix, feedforward_scaling_factor, feedforward_widen_matrix, feedforward_shrink_matrix):
    pair_normed = layer_normalize(pair_representation_state, pair_norm_gain).astype(jnp.bfloat16)
    pair_bias = jnp.einsum('ijc,ch->hij', pair_normed.astype(jnp.float32), pair_head_weight.astype(jnp.float32)).astype(jnp.bfloat16)
    bias_f = pair_bias.astype(jnp.float32)
    key_gap_mask = jnp.repeat(gap_block_flags, BLOCK, axis=1)

    def row_attention_update(sequence_entries):
        sequence_rows, gap_keys = sequence_entries
        normed = layer_normalize(sequence_rows, horizontal_scaling_factor).astype(jnp.bfloat16)
        queries, keys_bf, values_bf, gates = project(normed, row_input_weight)
        attended = attend(queries, keys_bf, values_bf, bias_f, gap_keys == 1)
        gated_out = (attended * gates).astype(jnp.bfloat16).reshape(sequence_rows.shape[0], FOCUS_COUNT * PER_HEADER_DEPTH)
        layer_update = jnp.dot(gated_out, horizontal_final_matrix, preferred_element_type=jnp.float32)
        return (sequence_rows.astype(jnp.float32) + layer_update).astype(jnp.bfloat16)
    alignment_first = lax.map(row_attention_update, (aligned_chain_features, key_gap_mask))

    def column_attention_update(res_items):
        res_rows, gap_keys = res_items
        normed = layer_normalize(res_rows, vertical_scaling_factor).astype(jnp.bfloat16)
        queries, keys_bf, values_bf, gates = project(normed, column_input_weight)
        attended = attend(queries, keys_bf, values_bf, jnp.float32(0.0), gap_keys == 1)
        gated_out = (attended * gates).astype(jnp.bfloat16).reshape(res_rows.shape[0], FOCUS_COUNT * PER_HEADER_DEPTH)
        layer_update = jnp.dot(gated_out, vertical_final_matrix, preferred_element_type=jnp.float32)
        return (res_rows.astype(jnp.float32) + layer_update).astype(jnp.bfloat16)
    residue_major = lax.map(column_attention_update, (jnp.transpose(alignment_first, (1, 0, 2)), jnp.transpose(key_gap_mask)))
    alignment_second = jnp.transpose(residue_major, (1, 0, 2))

    def transition_update(sequence_rows):
        normed = layer_normalize(sequence_rows, feedforward_scaling_factor).astype(jnp.bfloat16)
        hidden_bf = jax.nn.relu(jnp.dot(normed, feedforward_widen_matrix, preferred_element_type=jnp.float32)).astype(jnp.bfloat16)
        layer_update = jnp.dot(hidden_bf, feedforward_shrink_matrix, preferred_element_type=jnp.float32)
        return (sequence_rows.astype(jnp.float32) + layer_update).astype(jnp.bfloat16)
    return lax.map(transition_update, alignment_second)
```

```python
import functools

import jax
import jax.numpy as jnp
from jax import lax
from jax.experimental import pallas as pl
from jax.experimental.pallas import tpu as pltpu
from jax.sharding import PartitionSpec as P

BLOCK = 128
EPSILON = 1e-05
MASKED_SCORE = -1000000000.0
LANES = 128
SLAB = 16
F32 = jnp.float32
BF16 = jnp.bfloat16
VMEM_BYTES = 48 * 1024 * 1024


def layer_normalize(values_f, scale_gain):
    centred = values_f - jnp.mean(values_f, axis=-1, keepdims=True)
    spread = jnp.mean(centred * centred, axis=-1, keepdims=True)
    return centred * lax.rsqrt(spread + EPSILON) * scale_gain


def mm(lhs, rhs):
    return jnp.dot(lhs, rhs, preferred_element_type=F32)


def mm_nt(lhs, rhs):
    return lax.dot_general(lhs, rhs, (((1,), (1,)), ((), ())), preferred_element_type=F32)


def swap_matrix(outer, inner):
    size = outer * inner
    to = lax.broadcasted_iota(jnp.int32, (size, size), 0)
    come = lax.broadcasted_iota(jnp.int32, (size, size), 1)
    source = lax.rem(to, outer) * inner + lax.div(to, outer)
    return jnp.where(come == source, 1.0, 0.0).astype(BF16)


def head_lanes(rows, width, head_depth, head):
    lane = lax.broadcasted_iota(jnp.int32, (rows, width), 1)
    return (lane >= head * head_depth) & (lane < (head + 1) * head_depth)


def bias_kernel(pair_ref, gain_ref, weight_ref, out_ref, rows_scr):
    heads, local_res, residues = out_ref.shape
    channels = pair_ref.shape[2]
    step = min(4, local_res)

    def body(i, carry):
        block = pair_ref[pl.ds(i * step, step)].reshape(step * residues, channels)
        normed = layer_normalize(block.astype(F32), gain_ref[...]).astype(BF16)
        projected = mm_nt(weight_ref[...], normed)
        for j in range(step):
            rows_scr[i * step + j] = projected[:, j * residues : (j + 1) * residues]
        return carry

    lax.fori_loop(0, local_res // step, body, 0)
    rows = rows_scr[...].reshape(local_res * heads, residues).astype(BF16)
    turned = mm(swap_matrix(local_res, heads), rows)
    out_ref[...] = turned.reshape(heads, local_res, residues).astype(BF16)


def row_kernel(gap_ref, x_ref, bias_ref, gain_ref, win_ref, wout_ref, out_ref, bias_scr, p_scr, v_scr):
    groups, seqs, local_res, channels = x_ref.shape
    heads = bias_ref.shape[1]
    residues = groups * local_res
    depth = channels // heads
    per = LANES // depth
    scale = depth ** (-0.5)

    for h in range(heads):
        bias_scr[h] = bias_ref[:, h].reshape(residues, residues).astype(F32)

    def body(s, carry):
        x = x_ref[:, pl.ds(s, 1)].reshape(residues, channels)
        normed = layer_normalize(x.astype(F32), gain_ref[...]).astype(BF16)
        proj = mm(normed, win_ref[...])
        q = (proj[:, :channels] * scale).astype(BF16)
        k = proj[:, channels : 2 * channels].astype(BF16)
        v = proj[:, 2 * channels : 3 * channels].astype(BF16)
        gates = jax.nn.sigmoid(proj[:, 3 * channels :])
        key = lax.broadcasted_iota(jnp.int32, (1, residues), 1)
        gap = jnp.zeros((1, residues), jnp.int32)
        for b in range(residues // BLOCK):
            gap = jnp.where(key // BLOCK == b, gap_ref[s, b], gap)
        masked = gap == 1
        attended = []
        for g in range(heads // per):
            lanes = slice(g * LANES, (g + 1) * LANES)
            for j in range(per):
                h = g * per + j
                mine = head_lanes(residues, LANES, depth, j)
                qm = jnp.where(mine, q[:, lanes], jnp.zeros((), BF16))
                scores = mm_nt(qm, k[:, lanes]) + bias_scr[h]
                scores = jnp.where(masked, MASKED_SCORE, scores)
                e = jnp.exp(scores - jnp.max(scores, axis=-1, keepdims=True))
                w = e * (1.0 / jnp.sum(e, axis=-1, keepdims=True))
                p_scr[:, j * residues : (j + 1) * residues] = w.astype(BF16)
                v_scr[j * residues : (j + 1) * residues] = jnp.where(mine, v[:, lanes], jnp.zeros((), BF16))
            attended.append(mm(p_scr[...], v_scr[...]))
        gated = (jnp.concatenate(attended, axis=1) * gates).astype(BF16)
        result = x.astype(F32) + mm(gated, wout_ref[...])
        out_ref[:, pl.ds(s, 1)] = result.astype(BF16).reshape(groups, 1, local_res, channels)
        return carry

    lax.fori_loop(0, seqs, body, 0)


def column_kernel(
    heads, turn, gap_ref, x_ref, gain_ref, win_ref, wout_ref, gain2_ref, widen_ref, shrink_ref,
    out_ref, turned_scr, proj_scr, gated_scr, p_scr, done_scr,
):
    seqs, channels = x_ref.shape[-2 if not turn else 0], x_ref.shape[2]
    local_res = x_ref.shape[1 if turn else 0]
    depth = channels // heads
    per = LANES // depth
    halves = heads // per
    scale = depth ** (-0.5)
    batch = proj_scr.shape[0]
    slabs = local_res // SLAB if turn else 0
    swap = swap_matrix(SLAB, SLAB)
    if not turn:
        turned_scr[...] = x_ref[...]
    for c in range(slabs):
        for g in range(seqs // SLAB):
            block = x_ref[g * SLAB : (g + 1) * SLAB, c * SLAB : (c + 1) * SLAB]
            turned = mm(swap, block.reshape(SLAB * SLAB, channels))
            turned_scr[c * SLAB : (c + 1) * SLAB, g * SLAB : (g + 1) * SLAB] = turned.astype(
                BF16
            ).reshape(SLAB, SLAB, channels)

    masked = gap_ref[...] == 1

    def body(i, carry):
        x = turned_scr[pl.ds(i * batch, batch)].reshape(batch * seqs, channels)
        normed = layer_normalize(x.astype(F32), gain_ref[...]).astype(BF16)
        proj_scr[...] = mm(normed, win_ref[...]).reshape(batch, seqs, 4 * channels)
        for r in range(batch):
            q = (proj_scr[r, :, :channels] * scale).astype(BF16)
            k = proj_scr[r, :, channels : 2 * channels].astype(BF16)
            v = proj_scr[r, :, 2 * channels : 3 * channels].astype(BF16)
            gates = jax.nn.sigmoid(proj_scr[r, :, 3 * channels :])
            zero = jnp.zeros((), BF16)
            lane = lax.broadcasted_iota(jnp.int32, (seqs, channels), 1)
            lane_head = lane // depth
            k_block = jnp.concatenate(
                [jnp.where(lane_head // per == g, k, zero) for g in range(halves)], axis=0
            )
            acc = jnp.zeros((seqs, channels), F32)
            for j in range(per):
                qm = jnp.where(lane_head % per == j, q, zero)
                scores = mm_nt(qm, k_block)
                weights = []
                for g in range(halves):
                    sc = jnp.where(masked, MASKED_SCORE, scores[:, g * seqs : (g + 1) * seqs])
                    e = jnp.exp(sc - jnp.max(sc, axis=-1, keepdims=True))
                    weights.append((e * (1.0 / jnp.sum(e, axis=-1, keepdims=True))).astype(BF16))
                v_block = jnp.concatenate(
                    [jnp.where(lane_head == g * per + j, v, zero) for g in range(halves)], axis=0
                )
                acc = acc + mm(jnp.concatenate(weights, axis=1), v_block)
            gated_scr[r] = (acc * gates).astype(BF16)
        second = (
            x.astype(F32) + mm(gated_scr[...].reshape(batch * seqs, channels), wout_ref[...])
        ).astype(BF16)
        second_f = second.astype(F32)
        normed2 = layer_normalize(second_f, gain2_ref[...]).astype(BF16)
        hidden = jnp.maximum(mm(normed2, widen_ref[...]), 0.0).astype(BF16)
        result = (second_f + mm(hidden, shrink_ref[...])).astype(BF16)
        done_scr[pl.ds(i * batch, batch)] = result.reshape(batch, seqs, channels)
        return carry

    lax.fori_loop(0, local_res // batch, body, 0)
    if not turn:
        out_ref[...] = done_scr[...]
    for c in range(slabs):
        for g in range(seqs // SLAB):
            block = done_scr[c * SLAB : (c + 1) * SLAB, g * SLAB : (g + 1) * SLAB]
            turned = mm(swap, block.reshape(SLAB * SLAB, channels))
            out_ref[g * SLAB : (g + 1) * SLAB, c * SLAB : (c + 1) * SLAB] = turned.astype(
                BF16
            ).reshape(SLAB, SLAB, channels)


def whole(count):
    return [pl.BlockSpec(memory_space=pltpu.VMEM)] * count


def body(
    aligned_chain_features,
    pair_representation_state,
    gap_block_flags,
    pair_norm_gain,
    pair_head_weight,
    horizontal_scaling_factor,
    row_input_weight,
    horizontal_final_matrix,
    vertical_scaling_factor,
    column_input_weight,
    vertical_final_matrix,
    feedforward_scaling_factor,
    feedforward_widen_matrix,
    feedforward_shrink_matrix,
):
    groups = lax.axis_size("res")
    here = lax.axis_index("res")
    total_seqs, local_res, channels = aligned_chain_features.shape
    residues = pair_representation_state.shape[1]
    heads = pair_head_weight.shape[1]
    local_seqs = total_seqs // groups
    params = pltpu.CompilerParams(vmem_limit_bytes=VMEM_BYTES)

    arrived = lax.all_to_all(
        aligned_chain_features.reshape(groups, local_seqs, local_res, channels),
        "res", split_axis=0, concat_axis=0, tiled=True,
    )
    bias_local = pl.pallas_call(
        bias_kernel,
        out_shape=jax.ShapeDtypeStruct((heads, local_res, residues), BF16),
        in_specs=whole(3),
        out_specs=pl.BlockSpec(memory_space=pltpu.VMEM),
        scratch_shapes=[pltpu.VMEM((local_res, heads, residues), F32)],
        compiler_params=params,
        name="pair_bias",
    )(pair_representation_state, pair_norm_gain[None, :], pair_head_weight.T)
    bias_all = lax.all_gather(bias_local, "res", axis=0, tiled=False)
    gap_local = lax.dynamic_slice_in_dim(gap_block_flags, here * local_seqs, local_seqs, 0)

    first = pl.pallas_call(
        row_kernel,
        out_shape=jax.ShapeDtypeStruct((groups, local_seqs, local_res, channels), BF16),
        in_specs=[pl.BlockSpec(memory_space=pltpu.SMEM)] + whole(5),
        out_specs=pl.BlockSpec(memory_space=pltpu.VMEM),
        scratch_shapes=[
            pltpu.VMEM((heads, residues, residues), F32),
            pltpu.VMEM((residues, residues * LANES * heads // channels), BF16),
            pltpu.VMEM((residues * LANES * heads // channels, LANES), BF16),
        ],
        compiler_params=params,
        name="row_attention",
    )(
        gap_local, arrived, bias_all, horizontal_scaling_factor[None, :],
        row_input_weight, horizontal_final_matrix,
    )
    back = lax.all_to_all(first, "res", split_axis=0, concat_axis=0, tiled=True)
    back = back.reshape(total_seqs, local_res, channels)
    column_block = (here * local_res) // BLOCK
    col_gap = lax.dynamic_slice_in_dim(gap_block_flags, column_block, 1, 1).reshape(1, total_seqs)
    batch = min(4, local_res)
    turn = local_res % SLAB == 0
    if not turn:
        back = jnp.swapaxes(back, 0, 1)
    done = pl.pallas_call(
        functools.partial(column_kernel, heads, turn),
        out_shape=jax.ShapeDtypeStruct(back.shape, BF16),
        in_specs=whole(8),
        out_specs=pl.BlockSpec(memory_space=pltpu.VMEM),
        scratch_shapes=[
            pltpu.VMEM((local_res, total_seqs, channels), BF16),
            pltpu.VMEM((batch, total_seqs, 4 * channels), F32),
            pltpu.VMEM((batch, total_seqs, channels), BF16),
            pltpu.VMEM((total_seqs, 2 * total_seqs), BF16),
            pltpu.VMEM((local_res, total_seqs, channels), BF16),
        ],
        compiler_params=params,
        name="column_transition",
    )(
        col_gap, back, vertical_scaling_factor[None, :], column_input_weight,
        vertical_final_matrix, feedforward_scaling_factor[None, :],
        feedforward_widen_matrix, feedforward_shrink_matrix,
    )
    return done if turn else jnp.swapaxes(done, 0, 1)


def solution(mesh):
    placed = (
        P("dp", "res", None),
        P(("dp", "res"), None, None),
        P("dp", None),
    ) + (P(),) * 11
    return jax.shard_map(
        body, mesh=mesh, in_specs=placed, out_specs=P("dp", "res", None), check_vma=False
    )
```

```python
import functools

import jax
import jax.numpy as jnp
from jax import lax
from jax.experimental import pallas as pl
from jax.experimental.pallas import tpu as pltpu
from jax.sharding import PartitionSpec as P

BLOCK = 128
EPSILON = 1e-05
MASKED_SCORE = -1000000000.0
LANES = 128
SLAB = 16
F32 = jnp.float32
BF16 = jnp.bfloat16
VMEM_BYTES = 48 * 1024 * 1024


def layer_normalize(values_f, scale_gain):
    centred = values_f - jnp.mean(values_f, axis=-1, keepdims=True)
    spread = jnp.mean(centred * centred, axis=-1, keepdims=True)
    return centred * lax.rsqrt(spread + EPSILON) * scale_gain


def mm(lhs, rhs):
    return jnp.dot(lhs, rhs, preferred_element_type=F32)


def mm_nt(lhs, rhs):
    return lax.dot_general(lhs, rhs, (((1,), (1,)), ((), ())), preferred_element_type=F32)


def swap_matrix(outer, inner):
    size = outer * inner
    to = lax.broadcasted_iota(jnp.int32, (size, size), 0)
    come = lax.broadcasted_iota(jnp.int32, (size, size), 1)
    source = lax.rem(to, outer) * inner + lax.div(to, outer)
    return jnp.where(come == source, 1.0, 0.0).astype(BF16)


def head_lanes(rows, width, head_depth, head):
    lane = lax.broadcasted_iota(jnp.int32, (rows, width), 1)
    return (lane >= head * head_depth) & (lane < (head + 1) * head_depth)


def bias_kernel(pair_ref, gain_ref, weight_ref, out_ref, rows_scr):
    heads, local_res, residues = out_ref.shape
    channels = pair_ref.shape[2]
    step = min(4, local_res)

    def body(i, carry):
        block = pair_ref[pl.ds(i * step, step)].reshape(step * residues, channels)
        normed = layer_normalize(block.astype(F32), gain_ref[...]).astype(BF16)
        projected = mm_nt(weight_ref[...], normed)
        for j in range(step):
            rows_scr[i * step + j] = projected[:, j * residues : (j + 1) * residues]
        return carry

    lax.fori_loop(0, local_res // step, body, 0)
    rows = rows_scr[...].reshape(local_res * heads, residues).astype(BF16)
    turned = mm(swap_matrix(local_res, heads), rows)
    out_ref[...] = turned.reshape(heads, local_res, residues).astype(BF16)


def row_kernel(low, count, gap_ref, x_ref, bias_ref, gain_ref, win_ref, wout_ref, out_ref, bias_scr, p_scr, v_scr):
    groups, seqs, local_res, channels = x_ref.shape
    heads = bias_ref.shape[1]
    residues = groups * local_res
    depth = channels // heads
    per = LANES // depth
    scale = depth ** (-0.5)

    queries = groups * count
    for h in range(heads):
        bias_scr[h] = bias_ref[:, h, low : low + count].reshape(queries, residues).astype(F32)

    def body(s, carry):
        x = x_ref[:, pl.ds(s, 1)].reshape(residues, channels)
        normed = layer_normalize(x.astype(F32), gain_ref[...]).astype(BF16)
        if count == local_res:
            mine_x, mine_normed = x, normed
        else:
            mine_x = x_ref[:, pl.ds(s, 1), low : low + count].reshape(queries, channels)
            mine_normed = normed.reshape(groups, local_res, channels)[:, low : low + count]
            mine_normed = mine_normed.reshape(queries, channels)
        q = (mm(mine_normed, win_ref[:, :channels]) * scale).astype(BF16)
        k = mm(normed, win_ref[:, channels : 2 * channels]).astype(BF16)
        v = mm(normed, win_ref[:, 2 * channels : 3 * channels]).astype(BF16)
        gates = jax.nn.sigmoid(mm(mine_normed, win_ref[:, 3 * channels :]))
        key = lax.broadcasted_iota(jnp.int32, (1, residues), 1)
        gap = jnp.zeros((1, residues), jnp.int32)
        for b in range(residues // BLOCK):
            gap = jnp.where(key // BLOCK == b, gap_ref[s, b], gap)
        masked = gap == 1
        attended = []
        for g in range(heads // per):
            lanes = slice(g * LANES, (g + 1) * LANES)
            for j in range(per):
                h = g * per + j
                mine = head_lanes(residues, LANES, depth, j)
                qm = jnp.where(mine[:queries], q[:, lanes], jnp.zeros((), BF16))
                scores = mm_nt(qm, k[:, lanes]) + bias_scr[h]
                scores = jnp.where(masked, MASKED_SCORE, scores)
                e = jnp.exp(scores - jnp.max(scores, axis=-1, keepdims=True))
                w = e * (1.0 / jnp.sum(e, axis=-1, keepdims=True))
                p_scr[:, j * residues : (j + 1) * residues] = w.astype(BF16)
                v_scr[j * residues : (j + 1) * residues] = jnp.where(mine, v[:, lanes], jnp.zeros((), BF16))
            attended.append(mm(p_scr[...], v_scr[...]))
        gated = (jnp.concatenate(attended, axis=1) * gates).astype(BF16)
        result = mine_x.astype(F32) + mm(gated, wout_ref[...])
        out_ref[:, pl.ds(s, 1)] = result.astype(BF16).reshape(groups, 1, count, channels)
        return carry

    lax.fori_loop(0, seqs, body, 0)


def column_kernel(heads, turn, lows, done_parts, *refs):
    pieces, refs = refs[: len(lows)], refs[len(lows) :]
    done_refs, refs = refs[:done_parts], refs[done_parts:]
    (gap_ref, gain_ref, win_ref, wout_ref, gain2_ref, widen_ref, shrink_ref) = refs[:7]
    (out_ref, turned_scr, proj_scr, gated_scr, p_scr, done_scr) = refs[7:]
    local_res, seqs, channels = turned_scr.shape
    depth = channels // heads
    per = LANES // depth
    halves = heads // per
    scale = depth ** (-0.5)
    batch = proj_scr.shape[0]
    slabs = local_res // SLAB if turn else 0
    swap = swap_matrix(SLAB, SLAB)
    if not turn:
        turned_scr[...] = pieces[0][...]
    for c in range(slabs):
        g = 0
        for piece, low in zip(pieces, lows):
            for p in range(piece.shape[0] // SLAB):
                start = low + c * SLAB
                block = piece[p * SLAB : (p + 1) * SLAB, start : start + SLAB]
                turned = mm(swap, block.reshape(SLAB * SLAB, channels))
                turned_scr[c * SLAB : (c + 1) * SLAB, g * SLAB : (g + 1) * SLAB] = turned.astype(
                    BF16
                ).reshape(SLAB, SLAB, channels)
                g += 1

    masked = gap_ref[...] == 1

    def body(i, carry):
        x = turned_scr[pl.ds(i * batch, batch)].reshape(batch * seqs, channels)
        normed = layer_normalize(x.astype(F32), gain_ref[...]).astype(BF16)
        proj_scr[...] = mm(normed, win_ref[...]).reshape(batch, seqs, 4 * channels)
        for r in range(batch):
            q = (proj_scr[r, :, :channels] * scale).astype(BF16)
            k = proj_scr[r, :, channels : 2 * channels].astype(BF16)
            v = proj_scr[r, :, 2 * channels : 3 * channels].astype(BF16)
            gates = jax.nn.sigmoid(proj_scr[r, :, 3 * channels :])
            zero = jnp.zeros((), BF16)
            lane = lax.broadcasted_iota(jnp.int32, (seqs, channels), 1)
            lane_head = lane // depth
            k_block = jnp.concatenate(
                [jnp.where(lane_head // per == g, k, zero) for g in range(halves)], axis=0
            )
            acc = jnp.zeros((seqs, channels), F32)
            for j in range(per):
                qm = jnp.where(lane_head % per == j, q, zero)
                scores = mm_nt(qm, k_block)
                weights = []
                for g in range(halves):
                    sc = jnp.where(masked, MASKED_SCORE, scores[:, g * seqs : (g + 1) * seqs])
                    e = jnp.exp(sc - jnp.max(sc, axis=-1, keepdims=True))
                    weights.append((e * (1.0 / jnp.sum(e, axis=-1, keepdims=True))).astype(BF16))
                v_block = jnp.concatenate(
                    [jnp.where(lane_head == g * per + j, v, zero) for g in range(halves)], axis=0
                )
                acc = acc + mm(jnp.concatenate(weights, axis=1), v_block)
            gated_scr[r] = (acc * gates).astype(BF16)
        second = (
            x.astype(F32) + mm(gated_scr[...].reshape(batch * seqs, channels), wout_ref[...])
        ).astype(BF16)
        second_f = second.astype(F32)
        normed2 = layer_normalize(second_f, gain2_ref[...]).astype(BF16)
        hidden = jnp.maximum(mm(normed2, widen_ref[...]), 0.0).astype(BF16)
        result = (second_f + mm(hidden, shrink_ref[...])).astype(BF16)
        done_scr[pl.ds(i * batch, batch)] = result.reshape(batch, seqs, channels)
        return carry

    lax.fori_loop(0, local_res // batch, body, 0)
    if not turn:
        out_ref[...] = done_scr[...]
    base = 0
    for done_ref in done_refs:
        out_ref[:, base : base + done_ref.shape[1]] = done_ref[...]
        base += done_ref.shape[1]
    for c in range(slabs):
        for g in range(seqs // SLAB):
            block = done_scr[c * SLAB : (c + 1) * SLAB, g * SLAB : (g + 1) * SLAB]
            turned = mm(swap, block.reshape(SLAB * SLAB, channels))
            start = base + c * SLAB
            out_ref[g * SLAB : (g + 1) * SLAB, start : start + SLAB] = turned.astype(
                BF16
            ).reshape(SLAB, SLAB, channels)


def whole(count):
    return [pl.BlockSpec(memory_space=pltpu.VMEM)] * count


def body(
    aligned_chain_features,
    pair_representation_state,
    gap_block_flags,
    pair_norm_gain,
    pair_head_weight,
    horizontal_scaling_factor,
    row_input_weight,
    horizontal_final_matrix,
    vertical_scaling_factor,
    column_input_weight,
    vertical_final_matrix,
    feedforward_scaling_factor,
    feedforward_widen_matrix,
    feedforward_shrink_matrix,
):
    groups = lax.axis_size("res")
    total_seqs, local_res, channels = aligned_chain_features.shape
    residues = pair_representation_state.shape[1]
    heads = pair_head_weight.shape[1]
    local_seqs = total_seqs // groups
    turn = local_res % SLAB == 0
    seq_parts = 2 if turn and local_seqs % 2 == 0 else 1
    res_parts = local_res // SLAB if turn else 1
    part_seqs = local_seqs // seq_parts
    part_total = total_seqs // seq_parts
    part_res = local_res // res_parts
    here = lax.axis_index("res")

    def exchange(values):
        return lax.all_to_all(values, "res", split_axis=0, concat_axis=0, tiled=True)

    def kernel_call(kernel, name, micros, in_specs, out_shape, scratch):
        return pl.pallas_call(
            kernel,
            out_shape=jax.ShapeDtypeStruct(out_shape, BF16),
            in_specs=in_specs,
            out_specs=pl.BlockSpec(memory_space=pltpu.VMEM),
            scratch_shapes=scratch,
            compiler_params=pltpu.CompilerParams(vmem_limit_bytes=VMEM_BYTES),
            cost_estimate=pl.CostEstimate(
                flops=int(micros * 1e9), bytes_accessed=1 << 20, transcendentals=0
            ),
            name=name,
        )

    bias_local = kernel_call(
        bias_kernel, "pair_bias", 5, whole(3), (heads, local_res, residues),
        [pltpu.VMEM((local_res, heads, residues), F32)],
    )(pair_representation_state, pair_norm_gain[None, :], pair_head_weight.T)
    bias_all = lax.all_gather(bias_local, "res", axis=0, tiled=False)

    def row_attention(part, arrived, low, count):
        gap = lax.dynamic_slice_in_dim(
            gap_block_flags, part * part_total + here * part_seqs, part_seqs, 0
        )
        return kernel_call(
            functools.partial(row_kernel, low, count), "row_attention",
            2 * part_seqs * count / local_res,
            [pl.BlockSpec(memory_space=pltpu.SMEM)] + whole(5),
            (groups, part_seqs, count, channels),
            [
                pltpu.VMEM((heads, groups * count, residues), F32),
                pltpu.VMEM((groups * count, residues * LANES * heads // channels), BF16),
                pltpu.VMEM((residues * LANES * heads // channels, LANES), BF16),
            ],
        )(
            gap, arrived, bias_all, horizontal_scaling_factor[None, :],
            row_input_weight, horizontal_final_matrix,
        )

    arrived = [
        exchange(
            aligned_chain_features[p * part_total : (p + 1) * part_total].reshape(
                groups, part_seqs, local_res, channels
            )
        )
        for p in range(seq_parts)
    ]
    returned = []
    for p in range(seq_parts - 1):
        back = exchange(row_attention(p, arrived[p], 0, local_res))
        returned.append(back.reshape(part_total, local_res, channels))
    column_block = (here * local_res) // BLOCK
    col_gap = lax.dynamic_slice_in_dim(gap_block_flags, column_block, 1, 1).reshape(1, total_seqs)
    last = seq_parts - 1
    finals = [
        exchange(row_attention(last, arrived[last], c * part_res, part_res))
        for c in range(res_parts)
    ]
    done = []
    batch = min(4, part_res)
    for c in range(res_parts):
        pieces = returned + [finals[c].reshape(part_total, part_res, channels)]
        if not turn:
            pieces = [jnp.swapaxes(piece, 0, 1) for piece in pieces]
        lows = (c * part_res,) * len(returned) + (0,)
        before = done if c == res_parts - 1 else []
        if not turn:
            shape = (part_res, total_seqs, channels)
        else:
            shape = (total_seqs, part_res * (1 + len(before)), channels)
        done.append(
            kernel_call(
                functools.partial(column_kernel, heads, turn, lows, len(before)),
                "column_transition", part_res, whole(len(pieces) + len(before) + 7), shape,
                [
                    pltpu.VMEM((part_res, total_seqs, channels), BF16),
                    pltpu.VMEM((batch, total_seqs, 4 * channels), F32),
                    pltpu.VMEM((batch, total_seqs, channels), BF16),
                    pltpu.VMEM((total_seqs, 2 * total_seqs), BF16),
                    pltpu.VMEM((part_res, total_seqs, channels), BF16),
                ],
            )(
                *pieces, *before, col_gap, vertical_scaling_factor[None, :], column_input_weight,
                vertical_final_matrix, feedforward_scaling_factor[None, :],
                feedforward_widen_matrix, feedforward_shrink_matrix,
            )
        )
    return done[-1] if turn else jnp.swapaxes(done[-1], 0, 1)


def solution(mesh):
    placed = (
        P("dp", "res", None),
        P(("dp", "res"), None, None),
        P("dp", None),
    ) + (P(),) * 11
    return jax.shard_map(
        body, mesh=mesh, in_specs=placed, out_specs=P("dp", "res", None), check_vma=False
    )
```

```python
import functools

import jax
import jax.numpy as jnp
from jax import lax
from jax.experimental import pallas as pl
from jax.experimental.pallas import tpu as pltpu
from jax.sharding import PartitionSpec as P

BLOCK = 128
EPSILON = 1e-05
MASKED_SCORE = -1000000000.0
LANES = 128
SLAB = 16
F32 = jnp.float32
BF16 = jnp.bfloat16
VMEM_BYTES = 48 * 1024 * 1024


def layer_normalize(values_f, scale_gain):
    centred = values_f - jnp.mean(values_f, axis=-1, keepdims=True)
    spread = jnp.mean(centred * centred, axis=-1, keepdims=True)
    return centred * lax.rsqrt(spread + EPSILON) * scale_gain


def mm(lhs, rhs):
    return jnp.dot(lhs, rhs, preferred_element_type=F32)


def mm_nt(lhs, rhs):
    return lax.dot_general(lhs, rhs, (((1,), (1,)), ((), ())), preferred_element_type=F32)


def swap_matrix(outer, inner):
    size = outer * inner
    to = lax.broadcasted_iota(jnp.int32, (size, size), 0)
    come = lax.broadcasted_iota(jnp.int32, (size, size), 1)
    source = lax.rem(to, outer) * inner + lax.div(to, outer)
    return jnp.where(come == source, 1.0, 0.0).astype(BF16)


def bias_kernel(pair_ref, gain_ref, weight_ref, out_ref, rows_scr):
    heads, local_res, residues = out_ref.shape
    channels = pair_ref.shape[2]
    step = min(4, local_res)

    def body(i, carry):
        block = pair_ref[pl.ds(i * step, step)].reshape(step * residues, channels)
        normed = layer_normalize(block.astype(F32), gain_ref[...]).astype(BF16)
        projected = mm_nt(weight_ref[...], normed)
        for j in range(step):
            rows_scr[i * step + j] = projected[:, j * residues : (j + 1) * residues]
        return carry

    lax.fori_loop(0, local_res // step, body, 0)
    rows = rows_scr[...].reshape(local_res * heads, residues).astype(BF16)
    turned = mm(swap_matrix(local_res, heads), rows)
    out_ref[...] = turned.reshape(heads, local_res, residues).astype(BF16)


def softmax_keys(scores):
    e = jnp.exp(scores - jnp.max(scores, axis=0, keepdims=True))
    return (e * (1.0 / jnp.sum(e, axis=0, keepdims=True))).astype(BF16)


def gate_of(values):
    return 0.5 * jnp.tanh(0.5 * values) + 0.5


def stack(parts, axis):
    return parts[0] if len(parts) == 1 else jnp.concatenate(parts, axis=axis)


def row_kernel(
    low, count, gap_ref, x_ref, bias_ref, gain_ref, wqk_ref, wvg_ref, wout_ref, out_ref,
    bias_scr, q_scr, k_scr, v_scr, gate_scr, gated_scr,
):
    groups, seqs, local_res, channels = x_ref.shape
    heads = bias_ref.shape[1]
    residues = groups * local_res
    queries = groups * count
    depth = channels // heads
    per = LANES // depth
    scale = depth ** (-0.5)
    pair = 2 if seqs % 2 == 0 else 1
    zero = jnp.zeros((), BF16)

    row_at = lax.broadcasted_iota(jnp.int32, (residues, residues), 0)
    lane_at = lax.broadcasted_iota(jnp.int32, (residues, residues), 1)
    identity = jnp.where(row_at == lane_at, 1.0, 0.0).astype(BF16)
    for h in range(heads):
        bias_scr[h] = mm_nt(
            identity, bias_ref[:, h, low : low + count].reshape(queries, residues)
        )

    def dense(i, carry):
        normed, mine = [], []
        for j in range(pair):
            x = x_ref[:, pl.ds(i * pair + j, 1)].reshape(residues, channels)
            n = layer_normalize(x.astype(F32), gain_ref[...]).astype(BF16)
            normed.append(n)
            if count != local_res:
                n = n.reshape(groups, local_res, channels)[:, low : low + count]
                n = n.reshape(queries, channels)
            mine.append(n)
        normed, mine = stack(normed, 0), stack(mine, 0)
        q = (mm(mine, wqk_ref[:, :channels]) * scale).astype(BF16)
        k = mm(normed, wqk_ref[:, channels:]).astype(BF16)
        v = mm_nt(wvg_ref[:channels], normed).astype(BF16)
        gates = gate_of(mm_nt(wvg_ref[channels:], mine))
        for j in range(pair):
            s = i * pair + j
            q_scr[s] = q[j * queries : (j + 1) * queries]
            k_scr[s] = k[j * residues : (j + 1) * residues]
            v_scr[s] = v[:, j * residues : (j + 1) * residues]
            gate_scr[s] = gates[:, j * queries : (j + 1) * queries]
        return carry

    lax.fori_loop(0, seqs // pair, dense, 0)

    lane = lax.broadcasted_iota(jnp.int32, (residues, LANES), 1)
    ones = jnp.where(lane[:queries] == 0, 1.0, 0.0).astype(BF16)

    def attend(s, carry):
        gap_rows = [
            jnp.where((lane[:BLOCK] == 0) & (gap_ref[s, b] == 1), MASKED_SCORE, 0.0).astype(BF16)
            for b in range(residues // BLOCK)
        ]
        mask = stack(gap_rows, 0)
        attended = []
        for g in range(heads // per):
            lanes = slice(g * LANES, (g + 1) * LANES)
            q = jnp.concatenate([q_scr[s, :, lanes], ones], axis=1)
            for j in range(per):
                h = g * per + j
                k = jnp.where((lane >= j * depth) & (lane < (j + 1) * depth), k_scr[s, :, lanes], zero)
                scores = mm_nt(jnp.concatenate([k, mask], axis=1), q) + bias_scr[h]
                weights = softmax_keys(scores)
                attended.append(mm(v_scr[s, h * depth : (h + 1) * depth], weights))
        gated = (jnp.concatenate(attended, axis=0) * gate_scr[s]).astype(BF16)
        gated_scr[s] = gated.T
        return carry

    lax.fori_loop(0, seqs, attend, 0)

    def finish(i, carry):
        gated = gated_scr[pl.ds(i * pair, pair)].reshape(pair * queries, channels)
        update = mm(gated, wout_ref[...])
        for j in range(pair):
            s = i * pair + j
            x = x_ref[:, pl.ds(s, 1), low : low + count].reshape(queries, channels)
            result = x.astype(F32) + update[j * queries : (j + 1) * queries]
            out_ref[:, pl.ds(s, 1)] = result.astype(BF16).reshape(groups, 1, count, channels)
        return carry

    lax.fori_loop(0, seqs // pair, finish, 0)


def column_kernel(heads, turn, lows, done_parts, *refs):
    pieces, refs = refs[: len(lows)], refs[len(lows) :]
    done_refs, refs = refs[:done_parts], refs[done_parts:]
    (gap_ref, gain_ref, wqk_ref, wvg_ref, wout_ref, gain2_ref, widen_ref, shrink_ref) = refs[:8]
    (out_ref, turned_scr, q_scr, k_scr, v_scr, gate_scr, gated_scr, done_scr) = refs[8:]
    local_res, seqs, channels = turned_scr.shape
    depth = channels // heads
    per = LANES // depth
    halves = heads // per
    scale = depth ** (-0.5)
    batch = min(4, local_res)
    zero = jnp.zeros((), BF16)
    slabs = local_res // SLAB if turn else 0
    swap = swap_matrix(SLAB, SLAB)
    if not turn:
        turned_scr[...] = pieces[0][...]
    for c in range(slabs):
        g = 0
        for piece, low in zip(pieces, lows):
            for p in range(piece.shape[0] // SLAB):
                start = low + c * SLAB
                block = piece[p * SLAB : (p + 1) * SLAB, start : start + SLAB]
                turned = mm(swap, block.reshape(SLAB * SLAB, channels))
                turned_scr[c * SLAB : (c + 1) * SLAB, g * SLAB : (g + 1) * SLAB] = turned.astype(
                    BF16
                ).reshape(SLAB, SLAB, channels)
                g += 1

    def dense(i, carry):
        x = turned_scr[pl.ds(i * batch, batch)].reshape(batch * seqs, channels)
        normed = layer_normalize(x.astype(F32), gain_ref[...]).astype(BF16)
        q = (mm(normed, wqk_ref[:, :channels]) * scale).astype(BF16)
        q_scr[pl.ds(i * batch, batch)] = q.reshape(batch, seqs, channels)
        k = mm(normed, wqk_ref[:, channels:]).astype(BF16)
        k_scr[pl.ds(i * batch, batch)] = k.reshape(batch, seqs, channels)
        v = mm_nt(wvg_ref[:channels], normed).astype(BF16)
        gates = gate_of(mm_nt(wvg_ref[channels:], normed))
        for r in range(batch):
            v_scr[i * batch + r] = v[:, r * seqs : (r + 1) * seqs]
            gate_scr[i * batch + r] = gates[:, r * seqs : (r + 1) * seqs]
        return carry

    lax.fori_loop(0, local_res // batch, dense, 0)

    lane_head = lax.broadcasted_iota(jnp.int32, (seqs, channels), 1) // depth
    masked = jnp.broadcast_to(gap_ref[...] == 1, (seqs, halves * seqs))

    def attend(r, carry):
        q, k = q_scr[r], k_scr[r]
        q_block = jnp.concatenate(
            [jnp.where(lane_head // per == g, q, zero) for g in range(halves)], axis=0
        )
        weights = []
        for j in range(per):
            scores = mm_nt(jnp.where(lane_head % per == j, k, zero), q_block)
            weights.append(softmax_keys(jnp.where(masked, MASKED_SCORE, scores)))
        attended = [None] * heads
        blank = jnp.zeros((depth, seqs), BF16)
        for j in range(0, per, 2):
            left = []
            for jj in (j, j + 1):
                for g in range(halves):
                    h = g * per + jj
                    v = v_scr[r, h * depth : (h + 1) * depth]
                    left.append(jnp.concatenate([v, blank] if jj == j else [blank, v], axis=1))
            both = mm(
                jnp.concatenate(left, axis=0), jnp.concatenate(weights[j : j + 2], axis=0)
            )
            at = 0
            for jj in (j, j + 1):
                for g in range(halves):
                    attended[g * per + jj] = both[at : at + depth, g * seqs : (g + 1) * seqs]
                    at += depth
        gated = (jnp.concatenate(attended, axis=0) * gate_scr[r]).astype(BF16)
        gated_scr[r] = gated.T
        return carry

    lax.fori_loop(0, local_res, attend, 0)

    def finish(i, carry):
        x = turned_scr[pl.ds(i * batch, batch)].reshape(batch * seqs, channels)
        gated = gated_scr[pl.ds(i * batch, batch)].reshape(batch * seqs, channels)
        second = (x.astype(F32) + mm(gated, wout_ref[...])).astype(BF16)
        second_f = second.astype(F32)
        normed = layer_normalize(second_f, gain2_ref[...]).astype(BF16)
        hidden = jnp.maximum(mm(normed, widen_ref[...]), 0.0).astype(BF16)
        result = (second_f + mm(hidden, shrink_ref[...])).astype(BF16)
        done_scr[pl.ds(i * batch, batch)] = result.reshape(batch, seqs, channels)
        return carry

    lax.fori_loop(0, local_res // batch, finish, 0)
    if not turn:
        out_ref[...] = done_scr[...]
    base = 0
    for done_ref in done_refs:
        out_ref[:, base : base + done_ref.shape[1]] = done_ref[...]
        base += done_ref.shape[1]
    for c in range(slabs):
        for g in range(seqs // SLAB):
            block = done_scr[c * SLAB : (c + 1) * SLAB, g * SLAB : (g + 1) * SLAB]
            turned = mm(swap, block.reshape(SLAB * SLAB, channels))
            start = base + c * SLAB
            out_ref[g * SLAB : (g + 1) * SLAB, start : start + SLAB] = turned.astype(
                BF16
            ).reshape(SLAB, SLAB, channels)


def gather_bias(block, groups):
    if groups != 8:
        return lax.all_gather(block, "res", axis=0, tiled=False)
    side, lines = 2, groups // 2
    here = lax.axis_index("res")
    across = lax.ppermute(block, "res", [(i, i ^ 1) for i in range(groups)])
    odd = here % side == 1
    own = jnp.stack([jnp.where(odd, across, block), jnp.where(odd, block, across)])
    up, down = [own], [own]
    for _ in range(lines - 1):
        up.append(lax.ppermute(up[-1], "res", [(i, i + side) for i in range(groups - side)]))
        down.append(lax.ppermute(down[-1], "res", [(i, i - side) for i in range(side, groups)]))
    line = here // side
    pairs = []
    for at in range(lines):
        pairs.append(
            lax.select_n(line, *[up[z - at] if z >= at else down[at - z] for z in range(lines)])
        )
    return jnp.concatenate(pairs, axis=0)


def whole(count):
    return [pl.BlockSpec(memory_space=pltpu.VMEM)] * count


def body(
    aligned_chain_features,
    pair_representation_state,
    gap_block_flags,
    pair_norm_gain,
    pair_head_weight,
    horizontal_scaling_factor,
    row_input_weight,
    horizontal_final_matrix,
    vertical_scaling_factor,
    column_input_weight,
    vertical_final_matrix,
    feedforward_scaling_factor,
    feedforward_widen_matrix,
    feedforward_shrink_matrix,
):
    groups = lax.axis_size("res")
    total_seqs, local_res, channels = aligned_chain_features.shape
    residues = pair_representation_state.shape[1]
    heads = pair_head_weight.shape[1]
    local_seqs = total_seqs // groups
    turn = local_res % SLAB == 0
    seq_parts = 2 if turn and local_seqs % 2 == 0 else 1
    res_parts = local_res // SLAB if turn else 1
    part_seqs = local_seqs // seq_parts
    part_total = total_seqs // seq_parts
    part_res = local_res // res_parts
    here = lax.axis_index("res")

    def exchange(values):
        return lax.all_to_all(values, "res", split_axis=0, concat_axis=0, tiled=True)

    def kernel_call(kernel, name, micros, in_specs, out_shape, scratch):
        return pl.pallas_call(
            kernel,
            out_shape=jax.ShapeDtypeStruct(out_shape, BF16),
            in_specs=in_specs,
            out_specs=pl.BlockSpec(memory_space=pltpu.VMEM),
            scratch_shapes=scratch,
            compiler_params=pltpu.CompilerParams(vmem_limit_bytes=VMEM_BYTES),
            cost_estimate=pl.CostEstimate(
                flops=int(micros * 1e9), bytes_accessed=1 << 20, transcendentals=0
            ),
            name=name,
        )

    bias_local = kernel_call(
        bias_kernel, "pair_bias", 5, whole(3), (heads, local_res, residues),
        [pltpu.VMEM((local_res, heads, residues), F32)],
    )(pair_representation_state, pair_norm_gain[None, :], pair_head_weight.T)
    bias_all = gather_bias(bias_local, groups)
    row_qk, row_vg = row_input_weight[:, : 2 * channels], row_input_weight[:, 2 * channels :].T
    col_qk, col_vg = column_input_weight[:, : 2 * channels], column_input_weight[:, 2 * channels :].T

    def row_attention(part, arrived, low, count):
        gap = lax.dynamic_slice_in_dim(
            gap_block_flags, part * part_total + here * part_seqs, part_seqs, 0
        )
        return kernel_call(
            functools.partial(row_kernel, low, count), "row_attention",
            2 * part_seqs * count / local_res,
            [pl.BlockSpec(memory_space=pltpu.SMEM)] + whole(6),
            (groups, part_seqs, count, channels),
            [
                pltpu.VMEM((heads, residues, groups * count), F32),
                pltpu.VMEM((part_seqs, groups * count, channels), BF16),
                pltpu.VMEM((part_seqs, residues, channels), BF16),
                pltpu.VMEM((part_seqs, channels, residues), BF16),
                pltpu.VMEM((part_seqs, channels, groups * count), F32),
                pltpu.VMEM((part_seqs, groups * count, channels), BF16),
            ],
        )(
            gap, arrived, bias_all, horizontal_scaling_factor[None, :],
            row_qk, row_vg, horizontal_final_matrix,
        )

    arrived = [
        exchange(
            aligned_chain_features[p * part_total : (p + 1) * part_total].reshape(
                groups, part_seqs, local_res, channels
            )
        )
        for p in range(seq_parts)
    ]
    returned = []
    last = seq_parts - 1
    for p in range(last):
        first = row_attention(p, arrived[p], 0, local_res)
        first, arrived[p + 1] = lax.optimization_barrier((first, arrived[p + 1]))
        returned.append(exchange(first).reshape(part_total, local_res, channels))
    column_block = (here * local_res) // BLOCK
    col_gap = lax.dynamic_slice_in_dim(gap_block_flags, column_block, 1, 1)
    finals = []
    entries = arrived[last]
    for c in range(res_parts):
        first = row_attention(last, entries, c * part_res, part_res)
        first, entries = lax.optimization_barrier((first, entries))
        finals.append(exchange(first))
    done = []
    for c in range(res_parts):
        pieces = returned + [finals[c].reshape(part_total, part_res, channels)]
        if not turn:
            pieces = [jnp.swapaxes(piece, 0, 1) for piece in pieces]
        lows = (c * part_res,) * len(returned) + (0,)
        before = done if c == res_parts - 1 else []
        if not turn:
            shape = (part_res, total_seqs, channels)
        else:
            shape = (total_seqs, part_res * (1 + len(before)), channels)
        done.append(
            kernel_call(
                functools.partial(column_kernel, heads, turn, lows, len(before)),
                "column_transition", part_res, whole(len(pieces) + len(before) + 8), shape,
                [
                    pltpu.VMEM((part_res, total_seqs, channels), BF16),
                    pltpu.VMEM((part_res, total_seqs, channels), BF16),
                    pltpu.VMEM((part_res, total_seqs, channels), BF16),
                    pltpu.VMEM((part_res, channels, total_seqs), BF16),
                    pltpu.VMEM((part_res, channels, total_seqs), F32),
                    pltpu.VMEM((part_res, total_seqs, channels), BF16),
                    pltpu.VMEM((part_res, total_seqs, channels), BF16),
                ],
            )(
                *pieces, *before, col_gap, vertical_scaling_factor[None, :], col_qk, col_vg,
                vertical_final_matrix, feedforward_scaling_factor[None, :],
                feedforward_widen_matrix, feedforward_shrink_matrix,
            )
        )
    return done[-1] if turn else jnp.swapaxes(done[-1], 0, 1)


def solution(mesh):
    placed = (
        P("dp", "res", None),
        P(("dp", "res"), None, None),
        P("dp", None),
    ) + (P(),) * 11
    return jax.shard_map(
        body, mesh=mesh, in_specs=placed, out_specs=P("dp", "res", None), check_vma=False
    )
```

```python
import functools

import jax
import jax.numpy as jnp
from jax import lax
from jax.experimental import pallas as pl
from jax.experimental.pallas import tpu as pltpu
from jax.sharding import PartitionSpec as P

BLOCK = 128
EPSILON = 1e-05
MASKED_SCORE = -1000000000.0
LANES = 128
SLAB = 16
F32 = jnp.float32
BF16 = jnp.bfloat16
VMEM_BYTES = 48 * 1024 * 1024


def layer_normalize(values_f, scale_gain):
    centred = values_f - jnp.mean(values_f, axis=-1, keepdims=True)
    spread = jnp.mean(centred * centred, axis=-1, keepdims=True)
    return centred * lax.rsqrt(spread + EPSILON) * scale_gain


def mm(lhs, rhs):
    return jnp.dot(lhs, rhs, preferred_element_type=F32)


def mm_nt(lhs, rhs):
    return lax.dot_general(lhs, rhs, (((1,), (1,)), ((), ())), preferred_element_type=F32)


def swap_matrix(outer, inner):
    size = outer * inner
    to = lax.broadcasted_iota(jnp.int32, (size, size), 0)
    come = lax.broadcasted_iota(jnp.int32, (size, size), 1)
    source = lax.rem(to, outer) * inner + lax.div(to, outer)
    return jnp.where(come == source, 1.0, 0.0).astype(BF16)


def bias_kernel(pair_ref, gain_ref, weight_ref, out_ref, rows_scr):
    heads, local_res, residues = out_ref.shape
    channels = pair_ref.shape[2]
    step = min(4, local_res)

    def body(i, carry):
        block = pair_ref[pl.ds(i * step, step)].reshape(step * residues, channels)
        normed = layer_normalize(block.astype(F32), gain_ref[...]).astype(BF16)
        projected = mm_nt(weight_ref[...], normed)
        for j in range(step):
            rows_scr[i * step + j] = projected[:, j * residues : (j + 1) * residues]
        return carry

    lax.fori_loop(0, local_res // step, body, 0)
    rows = rows_scr[...].reshape(local_res * heads, residues).astype(BF16)
    turned = mm(swap_matrix(local_res, heads), rows)
    out_ref[...] = turned.reshape(heads, local_res, residues).astype(BF16)


def softmax_keys(scores):
    e = jnp.exp(scores - jnp.max(scores, axis=0, keepdims=True))
    return (e * (1.0 / jnp.sum(e, axis=0, keepdims=True))).astype(BF16)


def gate_of(values):
    return 0.5 * jnp.tanh(0.5 * values) + 0.5


def stack(parts, axis):
    return parts[0] if len(parts) == 1 else jnp.concatenate(parts, axis=axis)


def softmax_keys(scores):
    e = jnp.exp(scores - jnp.max(scores, axis=0, keepdims=True))
    return (e * (1.0 / jnp.sum(e, axis=0, keepdims=True))).astype(BF16)


def gate_of(values):
    return 0.5 * jnp.tanh(0.5 * values) + 0.5


def stack(parts, axis):
    return parts[0] if len(parts) == 1 else jnp.concatenate(parts, axis=axis)


def head_blocks(q, depth):
    heads = q.shape[0] // depth
    zero = jnp.zeros((depth, q.shape[1]), BF16)
    columns = []
    for h in range(heads):
        blocks = [q[h * depth : (h + 1) * depth] if i == h else zero for i in range(heads)]
        columns.append(jnp.concatenate(blocks, axis=0))
    return jnp.concatenate(columns, axis=1)


def start_copies(sources, targets, sems):
    copies = [
        pltpu.make_async_copy(source, target, sems.at[i])
        for i, (source, target) in enumerate(zip(sources, targets))
    ]
    for copy in copies:
        copy.start()
    return copies


def row_kernel(
    low, count, gap_ref, gain_ref, x_hbm, wk_hbm, wv_hbm, wqg_hbm, wout_hbm, bias_hbm, out_ref,
    x_ref, wk_ref, wv_ref, wqg_ref, wout_ref, bias_ref, sems,
    bias_scr, q_scr, k_scr, v_scr, gate_scr, gated_scr,
):
    copies = start_copies(
        [x_hbm, wk_hbm, wv_hbm, wqg_hbm, wout_hbm, bias_hbm],
        [x_ref, wk_ref, wv_ref, wqg_ref, wout_ref, bias_ref],
        sems,
    )
    groups, seqs, local_res, channels = x_ref.shape
    heads = bias_ref.shape[1]
    residues = groups * local_res
    queries = groups * count
    depth = channels // heads
    per = LANES // depth
    scale = depth ** (-0.5)
    pair = 2 if seqs % 2 == 0 else 1
    for copy in copies[:4]:
        copy.wait()

    def dense(i, carry):
        normed, mine = [], []
        for j in range(pair):
            x = x_ref[:, pl.ds(i * pair + j, 1)].reshape(residues, channels)
            n = layer_normalize(x.astype(F32), gain_ref[...]).astype(BF16)
            normed.append(n)
            if count != local_res:
                n = n.reshape(groups, local_res, channels)[:, low : low + count]
                n = n.reshape(queries, channels)
            mine.append(n)
        normed, mine = stack(normed, 0), stack(mine, 0)
        k = mm(normed, wk_ref[...]).astype(BF16)
        v = mm(wv_ref[...], normed.T).astype(BF16)
        qg = mm(wqg_ref[...], mine.T)
        q = (qg[:channels] * scale).astype(BF16)
        gates = gate_of(qg[channels:])
        for j in range(pair):
            s = i * pair + j
            q_scr[s] = q[:, j * queries : (j + 1) * queries]
            k_scr[s] = k[j * residues : (j + 1) * residues]
            v_scr[s] = v[:, j * residues : (j + 1) * residues]
            gate_scr[s] = gates[:, j * queries : (j + 1) * queries]
        return carry

    lax.fori_loop(0, seqs // pair, dense, 0)

    copies[5].wait()
    for h in range(heads):
        block = bias_ref[:, h, low : low + count].reshape(queries, residues)
        bias_scr[h] = block.T.astype(F32)
    bias_scr[heads] = jnp.full((residues, queries), MASKED_SCORE, F32)

    def attend(s, carry):
        gaps = [gap_ref[s, b] == 1 for b in range(residues // BLOCK)]
        attended = [None] * heads
        for g in range(heads // per):
            lanes = slice(g * LANES, (g + 1) * LANES)
            scores = mm(k_scr[s, :, lanes], head_blocks(q_scr[s, lanes], depth))
            weights = []
            for j in range(per):
                h = g * per + j
                bias = [
                    bias_scr[jnp.where(gap, heads, h), b * BLOCK : (b + 1) * BLOCK]
                    for b, gap in enumerate(gaps)
                ]
                own = scores[:, j * queries : (j + 1) * queries]
                weights.append(softmax_keys(own + stack(bias, 0)))
            for j in range(0, per, 2):
                h = g * per + j
                both = mm(
                    v_scr[s, h * depth : (h + 2) * depth],
                    jnp.concatenate(weights[j : j + 2], axis=1),
                )
                attended[h] = both[:depth, :queries]
                attended[h + 1] = both[depth:, queries:]
        gated = (jnp.concatenate(attended, axis=0) * gate_scr[s]).astype(BF16)
        gated_scr[s] = gated.T
        return carry

    lax.fori_loop(0, seqs, attend, 0)
    copies[4].wait()

    def finish(i, carry):
        gated = gated_scr[pl.ds(i * pair, pair)].reshape(pair * queries, channels)
        update = mm(gated, wout_ref[...])
        for j in range(pair):
            s = i * pair + j
            x = x_ref[:, pl.ds(s, 1), low : low + count].reshape(queries, channels)
            result = x.astype(F32) + update[j * queries : (j + 1) * queries]
            out_ref[:, pl.ds(s, 1)] = result.astype(BF16).reshape(groups, 1, count, channels)
        return carry

    lax.fori_loop(0, seqs // pair, finish, 0)


def column_kernel(
    heads, turn, earlier, gap_ref, gain_ref, gain2_ref, x_hbm, wk_hbm, wqvg_hbm, wout_hbm,
    widen_hbm, shrink_hbm, *refs,
):
    done_refs, refs = refs[:earlier], refs[earlier:]
    (out_ref, x_ref, wk_ref, wqvg_ref, wout_ref, widen_ref, shrink_ref, sems) = refs[:8]
    (turned_scr, q_scr, k_scr, v_scr, gate_scr, gated_scr, done_scr) = refs[8:]
    copies = start_copies(
        [x_hbm, wk_hbm, wqvg_hbm, wout_hbm, widen_hbm, shrink_hbm],
        [x_ref, wk_ref, wqvg_ref, wout_ref, widen_ref, shrink_ref],
        sems,
    )
    local_res, seqs, channels = turned_scr.shape
    depth = channels // heads
    per = LANES // depth
    scale = depth ** (-0.5)
    batch = min(4, local_res)
    slabs = local_res // SLAB if turn else 0
    swap = swap_matrix(SLAB, SLAB)
    base = 0
    for done_ref in done_refs:
        out_ref[:, base : base + done_ref.shape[1]] = done_ref[...]
        base += done_ref.shape[1]
    copies[0].wait()
    if not turn:
        turned_scr[...] = x_ref[...]
    for c in range(slabs):
        for g in range(seqs // SLAB):
            block = x_ref[g * SLAB : (g + 1) * SLAB, c * SLAB : (c + 1) * SLAB]
            turned = mm(swap, block.reshape(SLAB * SLAB, channels))
            turned_scr[c * SLAB : (c + 1) * SLAB, g * SLAB : (g + 1) * SLAB] = turned.astype(
                BF16
            ).reshape(SLAB, SLAB, channels)
    for copy in copies[1:3]:
        copy.wait()

    def dense(i, carry):
        x = turned_scr[pl.ds(i * batch, batch)].reshape(batch * seqs, channels)
        normed = layer_normalize(x.astype(F32), gain_ref[...]).astype(BF16)
        k = mm(normed, wk_ref[...]).astype(BF16)
        k_scr[pl.ds(i * batch, batch)] = k.reshape(batch, seqs, channels)
        qvg = mm(wqvg_ref[...], normed.T)
        q = (qvg[:channels] * scale).astype(BF16)
        v = qvg[channels : 2 * channels].astype(BF16)
        gates = gate_of(qvg[2 * channels :])
        for r in range(batch):
            q_scr[i * batch + r] = q[:, r * seqs : (r + 1) * seqs]
            v_scr[i * batch + r] = v[:, r * seqs : (r + 1) * seqs]
            gate_scr[i * batch + r] = gates[:, r * seqs : (r + 1) * seqs]
        return carry

    lax.fori_loop(0, local_res // batch, dense, 0)

    mask = jnp.broadcast_to(jnp.where(gap_ref[...] == 1, MASKED_SCORE, 0.0), (seqs, seqs))

    def attend(r, carry):
        attended = [None] * heads
        blank = jnp.zeros((2 * depth, seqs), BF16)
        for g in range(heads // per):
            lanes = slice(g * LANES, (g + 1) * LANES)
            scores = mm(k_scr[r, :, lanes], head_blocks(q_scr[r, lanes], depth))
            weights = [
                softmax_keys(scores[:, j * seqs : (j + 1) * seqs] + mask) for j in range(per)
            ]
            for j in range(0, per, 4):
                h = g * per + j
                v = v_scr[r, h * depth : (h + 4) * depth]
                left = jnp.concatenate(
                    [
                        jnp.concatenate([v[: 2 * depth], blank], axis=1),
                        jnp.concatenate([blank, v[2 * depth :]], axis=1),
                    ],
                    axis=0,
                )
                right = jnp.concatenate(
                    [
                        jnp.concatenate(weights[j : j + 2], axis=1),
                        jnp.concatenate(weights[j + 2 : j + 4], axis=1),
                    ],
                    axis=0,
                )
                both = mm(left, right)
                for e in range(4):
                    at = (e % 2) * seqs
                    attended[h + e] = both[e * depth : (e + 1) * depth, at : at + seqs]
        gated = (jnp.concatenate(attended, axis=0) * gate_scr[r]).astype(BF16)
        gated_scr[r] = gated.T
        return carry

    lax.fori_loop(0, local_res, attend, 0)
    for copy in copies[3:]:
        copy.wait()

    def finish(i, carry):
        x = turned_scr[pl.ds(i * batch, batch)].reshape(batch * seqs, channels)
        gated = gated_scr[pl.ds(i * batch, batch)].reshape(batch * seqs, channels)
        second = (x.astype(F32) + mm(gated, wout_ref[...])).astype(BF16)
        second_f = second.astype(F32)
        normed = layer_normalize(second_f, gain2_ref[...]).astype(BF16)
        hidden = jnp.maximum(mm(normed, widen_ref[...]), 0.0).astype(BF16)
        result = (second_f + mm(hidden, shrink_ref[...])).astype(BF16)
        done_scr[pl.ds(i * batch, batch)] = result.reshape(batch, seqs, channels)
        return carry

    lax.fori_loop(0, local_res // batch, finish, 0)
    if not turn:
        out_ref[...] = done_scr[...]
    for c in range(slabs):
        for g in range(seqs // SLAB):
            block = done_scr[c * SLAB : (c + 1) * SLAB, g * SLAB : (g + 1) * SLAB]
            turned = mm(swap, block.reshape(SLAB * SLAB, channels))
            start = base + c * SLAB
            out_ref[g * SLAB : (g + 1) * SLAB, start : start + SLAB] = turned.astype(
                BF16
            ).reshape(SLAB, SLAB, channels)


def gather_bias(block, groups):
    if groups != 8:
        return lax.all_gather(block, "res", axis=0, tiled=False)
    side, lines = 2, groups // 2
    here = lax.axis_index("res")
    across = lax.ppermute(block, "res", [(i, i ^ 1) for i in range(groups)])
    odd = here % side == 1
    own = jnp.stack([jnp.where(odd, across, block), jnp.where(odd, block, across)])
    up, down = [own], [own]
    for _ in range(lines - 1):
        up.append(lax.ppermute(up[-1], "res", [(i, i + side) for i in range(groups - side)]))
        down.append(lax.ppermute(down[-1], "res", [(i, i - side) for i in range(side, groups)]))
    line = here // side
    pairs = []
    for at in range(lines):
        pairs.append(
            lax.select_n(line, *[up[z - at] if z >= at else down[at - z] for z in range(lines)])
        )
    return jnp.concatenate(pairs, axis=0)


def in_vmem(count):
    return [pl.BlockSpec(memory_space=pltpu.VMEM)] * count


def anywhere(count):
    return [pl.BlockSpec(memory_space=pl.ANY)] * count


def like(*arrays):
    return [pltpu.VMEM(array.shape, array.dtype) for array in arrays]


def body(
    aligned_chain_features,
    pair_representation_state,
    gap_block_flags,
    pair_norm_gain,
    pair_head_weight,
    horizontal_scaling_factor,
    row_input_weight,
    horizontal_final_matrix,
    vertical_scaling_factor,
    column_input_weight,
    vertical_final_matrix,
    feedforward_scaling_factor,
    feedforward_widen_matrix,
    feedforward_shrink_matrix,
):
    groups = lax.axis_size("res")
    total_seqs, local_res, channels = aligned_chain_features.shape
    residues = pair_representation_state.shape[1]
    heads = pair_head_weight.shape[1]
    local_seqs = total_seqs // groups
    turn = local_res % SLAB == 0
    res_parts = local_res // SLAB if turn else 1
    part_res = local_res // res_parts
    here = lax.axis_index("res")

    def exchange(values):
        return lax.all_to_all(values, "res", split_axis=0, concat_axis=0, tiled=True)

    def kernel_call(kernel, name, micros, in_specs, out_shape, scratch):
        return pl.pallas_call(
            kernel,
            out_shape=jax.ShapeDtypeStruct(out_shape, BF16),
            in_specs=in_specs,
            out_specs=pl.BlockSpec(memory_space=pltpu.VMEM),
            scratch_shapes=scratch,
            compiler_params=pltpu.CompilerParams(vmem_limit_bytes=VMEM_BYTES),
            cost_estimate=pl.CostEstimate(
                flops=int(micros * 1e9), bytes_accessed=1 << 20, transcendentals=0
            ),
            name=name,
        )

    arrived = exchange(
        aligned_chain_features.reshape(groups, local_seqs, local_res, channels)
    )
    bias_local = kernel_call(
        bias_kernel, "pair_bias", 5, in_vmem(3), (heads, local_res, residues),
        [pltpu.VMEM((local_res, heads, residues), F32)],
    )(pair_representation_state, pair_norm_gain[None, :], pair_head_weight.T)
    bias_all = gather_bias(bias_local, groups)

    def slots(weight):
        return [weight[:, i * channels : (i + 1) * channels] for i in range(4)]

    rq, rk, rv, rg = slots(row_input_weight)
    row_weights = (rk, rv.T, jnp.concatenate([rq, rg], axis=1).T, horizontal_final_matrix)
    cq, ck, cv, cg = slots(column_input_weight)
    col_weights = (
        ck, jnp.concatenate([cq, cv, cg], axis=1).T, vertical_final_matrix,
        feedforward_widen_matrix, feedforward_shrink_matrix,
    )
    gap = lax.dynamic_slice_in_dim(gap_block_flags, here * local_seqs, local_seqs, 0)
    column_block = (here * local_res) // BLOCK
    col_gap = lax.dynamic_slice_in_dim(gap_block_flags, column_block, 1, 1)

    def row_attention(low, count):
        queries = groups * count
        operands = (arrived, *row_weights, bias_all)
        return kernel_call(
            functools.partial(row_kernel, low, count), "row_attention", 10,
            [pl.BlockSpec(memory_space=pltpu.SMEM)] + in_vmem(1) + anywhere(6),
            (groups, local_seqs, count, channels),
            like(*operands)
            + [
                pltpu.SemaphoreType.DMA((6,)),
                pltpu.VMEM((heads + 1, residues, queries), F32),
                pltpu.VMEM((local_seqs, channels, queries), BF16),
                pltpu.VMEM((local_seqs, residues, channels), BF16),
                pltpu.VMEM((local_seqs, channels, residues), BF16),
                pltpu.VMEM((local_seqs, channels, queries), F32),
                pltpu.VMEM((local_seqs, queries, channels), BF16),
            ],
        )(gap, horizontal_scaling_factor[None, :], *operands)

    finals = [exchange(row_attention(c * part_res, part_res)) for c in range(res_parts)]
    done = []
    for c in range(res_parts):
        piece = finals[c].reshape(total_seqs, part_res, channels)
        if not turn:
            piece = jnp.swapaxes(piece, 0, 1)
        before = done if c == res_parts - 1 else []
        if not turn:
            shape = (part_res, total_seqs, channels)
        else:
            shape = (total_seqs, part_res * (1 + len(before)), channels)
        operands = (piece, *col_weights)
        done.append(
            kernel_call(
                functools.partial(column_kernel, heads, turn, len(before)),
                "column_transition", 10,
                in_vmem(3) + anywhere(6) + in_vmem(len(before)), shape,
                like(*operands)
                + [
                    pltpu.SemaphoreType.DMA((6,)),
                    pltpu.VMEM((part_res, total_seqs, channels), BF16),
                    pltpu.VMEM((part_res, channels, total_seqs), BF16),
                    pltpu.VMEM((part_res, total_seqs, channels), BF16),
                    pltpu.VMEM((part_res, channels, total_seqs), BF16),
                    pltpu.VMEM((part_res, channels, total_seqs), F32),
                    pltpu.VMEM((part_res, total_seqs, channels), BF16),
                    pltpu.VMEM((part_res, total_seqs, channels), BF16),
                ],
            )(
                col_gap, vertical_scaling_factor[None, :], feedforward_scaling_factor[None, :],
                *operands, *before,
            )
        )
    return done[-1] if turn else jnp.swapaxes(done[-1], 0, 1)


def solution(mesh):
    placed = (
        P("dp", "res", None),
        P(("dp", "res"), None, None),
        P("dp", None),
    ) + (P(),) * 11
    return jax.shard_map(
        body, mesh=mesh, in_specs=placed, out_specs=P("dp", "res", None), check_vma=False
    )
```

```python
import functools

import jax
import jax.numpy as jnp
from jax import lax
from jax.experimental import pallas as pl
from jax.experimental.pallas import tpu as pltpu
from jax.sharding import PartitionSpec as P

BLOCK = 128
EPSILON = 1e-05
MASKED_SCORE = -1000000000.0
LANES = 128
SLAB = 16
F32 = jnp.float32
BF16 = jnp.bfloat16
VMEM_BYTES = 60 * 1024 * 1024
CHUNK = 64


def layer_normalize(values_f, scale_gain):
    centred = values_f - jnp.mean(values_f, axis=-1, keepdims=True)
    spread = jnp.mean(centred * centred, axis=-1, keepdims=True)
    return centred * lax.rsqrt(spread + EPSILON) * scale_gain


def mm(lhs, rhs):
    return jnp.dot(lhs, rhs, preferred_element_type=F32)


def mm_nt(lhs, rhs):
    return lax.dot_general(lhs, rhs, (((1,), (1,)), ((), ())), preferred_element_type=F32)


def swap_matrix(outer, inner):
    size = outer * inner
    to = lax.broadcasted_iota(jnp.int32, (size, size), 0)
    come = lax.broadcasted_iota(jnp.int32, (size, size), 1)
    source = lax.rem(to, outer) * inner + lax.div(to, outer)
    return jnp.where(come == source, 1.0, 0.0).astype(BF16)


def start_copies(sources, targets, sems):
    copies = [
        pltpu.make_async_copy(source, target, sems.at[i])
        for i, (source, target) in enumerate(zip(sources, targets))
    ]
    for copy in copies:
        copy.start()
    return copies


def payload_kernel(
    gain_ref, weight_ref, x_hbm, pair_hbm, out_hbm, pair_ref, normed_scr, bias_scr, sems, send_sems
):
    groups, seqs = x_hbm.shape[:2]
    local_res, residues, channels = pair_ref.shape
    heads = bias_scr.shape[0]
    step = normed_scr.shape[1] // channels
    parts = local_res // step
    copies = start_copies(
        [x_hbm] + [pair_hbm.at[p * step : (p + 1) * step] for p in range(parts)],
        [out_hbm.at[:, :seqs]] + [pair_ref.at[p * step : (p + 1) * step] for p in range(parts)],
        sems,
    )
    width = heads * step
    head_at = lax.broadcasted_iota(jnp.int32, (heads, width), 0)
    spread = jnp.where(lax.broadcasted_iota(jnp.int32, (heads, width), 1) // step == head_at, 1.0, 0.0)
    wide = mm(weight_ref[...], spread.astype(BF16))
    lane = lax.broadcasted_iota(jnp.int32, wide.shape, 1)
    weights = jnp.concatenate(
        [jnp.where(lane % step == i, wide, 0.0).astype(BF16) for i in range(step)], axis=0
    )
    rows = 2 * CHUNK
    for p in range(parts):
        copies[1 + p].wait()
        for i in range(step):
            for at in range(0, residues, rows):
                x = pair_ref[p * step + i, at : at + rows].astype(F32)
                normed_scr[at : at + rows, i * channels : (i + 1) * channels] = layer_normalize(
                    x, gain_ref[...]
                ).astype(BF16)
        projected = mm(normed_scr[...], weights)
        bias_scr[:, p * step : (p + 1) * step] = (
            projected.T.reshape(heads, step, residues).astype(BF16)
        )
    sends = start_copies(
        [bias_scr] * groups, [out_hbm.at[g, seqs:] for g in range(groups)], send_sems
    )
    for copy in sends:
        copy.wait()
    copies[0].wait()


def softmax_keys(scores):
    e = jnp.exp(scores - jnp.max(scores, axis=0, keepdims=True))
    return (e * (1.0 / jnp.sum(e, axis=0, keepdims=True))).astype(BF16)


def gate_of(values):
    return 0.5 * jnp.tanh(0.5 * values) + 0.5


def stack(parts, axis):
    return parts[0] if len(parts) == 1 else jnp.concatenate(parts, axis=axis)


def softmax_keys(scores):
    e = jnp.exp(scores - jnp.max(scores, axis=0, keepdims=True))
    return (e * (1.0 / jnp.sum(e, axis=0, keepdims=True))).astype(BF16)


def gate_of(values):
    return 0.5 * jnp.tanh(0.5 * values) + 0.5


def stack(parts, axis):
    return parts[0] if len(parts) == 1 else jnp.concatenate(parts, axis=axis)


def head_blocks(q, depth):
    heads = q.shape[0] // depth
    zero = jnp.zeros((depth, q.shape[1]), BF16)
    columns = []
    for h in range(heads):
        blocks = [q[h * depth : (h + 1) * depth] if i == h else zero for i in range(heads)]
        columns.append(jnp.concatenate(blocks, axis=0))
    return jnp.concatenate(columns, axis=1)


def row_kernel(
    low, count, gap_ref, gain_ref, payload_hbm, wk_hbm, wv_hbm, wqg_hbm, wout_hbm, out_ref,
    x_ref, bias_ref, wk_ref, wv_ref, wqg_ref, wout_ref, sems,
    bias_scr, q_scr, k_scr, v_scr, gate_scr, gated_scr, normed_scr, mine_scr,
):
    seqs = x_ref.shape[1]
    copies = start_copies(
        [payload_hbm.at[:, :seqs], wk_hbm, wv_hbm, wqg_hbm, wout_hbm, payload_hbm.at[:, seqs:]],
        [x_ref, wk_ref, wv_ref, wqg_ref, wout_ref, bias_ref],
        sems,
    )
    groups, seqs, local_res, channels = x_ref.shape
    heads = bias_ref.shape[1]
    residues = groups * local_res
    queries = groups * count
    depth = channels // heads
    per = LANES // depth
    scale = depth ** (-0.5)
    pair = 2 if seqs % 2 == 0 else 1
    for copy in copies[:4]:
        copy.wait()

    slabs = max(1, CHUNK // local_res)

    def dense(i, carry):
        for j in range(pair):
            for g in range(0, groups, slabs):
                x = x_ref[g : g + slabs, pl.ds(i * pair + j, 1)].reshape(slabs * local_res, channels)
                n = layer_normalize(x.astype(F32), gain_ref[...]).astype(BF16)
                at = j * residues + g * local_res
                normed_scr[at : at + slabs * local_res] = n
                if count != local_res:
                    n = n.reshape(slabs, local_res, channels)[:, low : low + count]
                    n = n.reshape(slabs * count, channels)
                at = j * queries + g * count
                mine_scr[at : at + slabs * count] = n
        for j in range(pair):
            s = i * pair + j
            normed = normed_scr[j * residues : (j + 1) * residues]
            k_scr[s] = mm(normed, wk_ref[...]).astype(BF16)
            v_scr[s] = mm(wv_ref[...], normed.T).astype(BF16)
        mine = mine_scr[...].T
        q = mm(wqg_ref[:channels], mine)
        for j in range(pair):
            q_scr[i * pair + j] = (q[:, j * queries : (j + 1) * queries] * scale).astype(BF16)
        gates = mm(wqg_ref[channels:], mine)
        for j in range(pair):
            for at in range(0, channels, CHUNK):
                gate_scr[i * pair + j, at : at + CHUNK] = gate_of(
                    gates[at : at + CHUNK, j * queries : (j + 1) * queries]
                )
        return carry

    lax.fori_loop(0, seqs // pair, dense, 0)

    copies[5].wait()
    for h in range(heads):
        block = bias_ref[:, h, low : low + count].reshape(queries, residues)
        bias_scr[h] = block.T.astype(F32)
    bias_scr[heads] = jnp.full((residues, queries), MASKED_SCORE, F32)

    def attend(s, carry):
        gaps = [gap_ref[s, b] == 1 for b in range(residues // BLOCK)]
        attended = [None] * heads
        for g in range(heads // per):
            lanes = slice(g * LANES, (g + 1) * LANES)
            scores = mm(k_scr[s, :, lanes], head_blocks(q_scr[s, lanes], depth))
            weights = []
            for j in range(per):
                h = g * per + j
                bias = [
                    bias_scr[jnp.where(gap, heads, h), b * BLOCK : (b + 1) * BLOCK]
                    for b, gap in enumerate(gaps)
                ]
                own = scores[:, j * queries : (j + 1) * queries]
                weights.append(softmax_keys(own + stack(bias, 0)))
            for j in range(0, per, 2):
                h = g * per + j
                both = mm(
                    v_scr[s, h * depth : (h + 2) * depth],
                    jnp.concatenate(weights[j : j + 2], axis=1),
                )
                attended[h] = both[:depth, :queries]
                attended[h + 1] = both[depth:, queries:]
        gated = (jnp.concatenate(attended, axis=0) * gate_scr[s]).astype(BF16)
        gated_scr[s] = gated.T
        return carry

    lax.fori_loop(0, seqs, attend, 0, unroll=pair)
    copies[4].wait()

    def finish(i, carry):
        gated = gated_scr[pl.ds(i * pair, pair)].reshape(pair * queries, channels)
        update = mm(gated, wout_ref[...])
        for j in range(pair):
            s = i * pair + j
            x = x_ref[:, pl.ds(s, 1), low : low + count].reshape(queries, channels)
            result = x.astype(F32) + update[j * queries : (j + 1) * queries]
            out_ref[:, pl.ds(s, 1)] = result.astype(BF16).reshape(groups, 1, count, channels)
        return carry

    lax.fori_loop(0, seqs // pair, finish, 0)


def column_kernel(
    heads, turn, earlier, gap_ref, gain_ref, gain2_ref, x_hbm, wk_hbm, wqvg_hbm, wout_hbm,
    widen_hbm, shrink_hbm, *refs,
):
    done_hbm, refs = refs[:earlier], refs[earlier:]
    (out_ref, x_ref, wk_ref, wqvg_ref, wout_ref, widen_ref, shrink_ref, sems) = refs[:8]
    (turned_scr, q_scr, k_scr, v_scr, gate_scr, gated_scr, done_scr, normed_scr) = refs[8:]
    base, places = 0, []
    for done in done_hbm:
        places.append(out_ref.at[:, base : base + done.shape[1]])
        base += done.shape[1]
    copies = start_copies(
        [x_hbm, wk_hbm, wqvg_hbm, wout_hbm, widen_hbm, shrink_hbm, *done_hbm],
        [x_ref, wk_ref, wqvg_ref, wout_ref, widen_ref, shrink_ref, *places],
        sems,
    )
    local_res, seqs, channels = turned_scr.shape
    depth = channels // heads
    per = LANES // depth
    scale = depth ** (-0.5)
    batch = min(4, local_res)
    slabs = local_res // SLAB if turn else 0
    swap = swap_matrix(SLAB, SLAB)
    copies[0].wait()
    if not turn:
        turned_scr[...] = x_ref[...]
    for c in range(slabs):
        for g in range(seqs // SLAB):
            block = x_ref[g * SLAB : (g + 1) * SLAB, c * SLAB : (c + 1) * SLAB]
            turned = mm(swap, block.reshape(SLAB * SLAB, channels))
            turned_scr[c * SLAB : (c + 1) * SLAB, g * SLAB : (g + 1) * SLAB] = turned.astype(
                BF16
            ).reshape(SLAB, SLAB, channels)
    for copy in copies[1:3]:
        copy.wait()

    def dense(i, carry):
        for r in range(batch):
            for at in range(0, seqs, CHUNK):
                x = turned_scr[i * batch + r, at : at + CHUNK].astype(F32)
                n = layer_normalize(x, gain_ref[...]).astype(BF16)
                normed_scr[r * seqs + at : r * seqs + at + CHUNK] = n
        k = mm(normed_scr[...], wk_ref[...]).astype(BF16)
        k_scr[pl.ds(i * batch, batch)] = k.reshape(batch, seqs, channels)
        normed = normed_scr[...].T
        q = mm(wqvg_ref[:channels], normed)
        for r in range(batch):
            q_scr[i * batch + r] = (q[:, r * seqs : (r + 1) * seqs] * scale).astype(BF16)
        v = mm(wqvg_ref[channels : 2 * channels], normed).astype(BF16)
        for r in range(batch):
            v_scr[i * batch + r] = v[:, r * seqs : (r + 1) * seqs]
        gates = mm(wqvg_ref[2 * channels :], normed)
        for r in range(batch):
            for at in range(0, channels, CHUNK):
                gate_scr[i * batch + r, at : at + CHUNK] = gate_of(
                    gates[at : at + CHUNK, r * seqs : (r + 1) * seqs]
                )
        return carry

    lax.fori_loop(0, local_res // batch, dense, 0)

    mask = jnp.broadcast_to(jnp.where(gap_ref[...] == 1, MASKED_SCORE, 0.0), (seqs, seqs))

    def attend(r, carry):
        attended = [None] * heads
        blank = jnp.zeros((2 * depth, seqs), BF16)
        for g in range(heads // per):
            lanes = slice(g * LANES, (g + 1) * LANES)
            scores = mm(k_scr[r, :, lanes], head_blocks(q_scr[r, lanes], depth))
            weights = [
                softmax_keys(scores[:, j * seqs : (j + 1) * seqs] + mask) for j in range(per)
            ]
            for j in range(0, per, 4):
                h = g * per + j
                v = v_scr[r, h * depth : (h + 4) * depth]
                left = jnp.concatenate(
                    [
                        jnp.concatenate([v[: 2 * depth], blank], axis=1),
                        jnp.concatenate([blank, v[2 * depth :]], axis=1),
                    ],
                    axis=0,
                )
                right = jnp.concatenate(
                    [
                        jnp.concatenate(weights[j : j + 2], axis=1),
                        jnp.concatenate(weights[j + 2 : j + 4], axis=1),
                    ],
                    axis=0,
                )
                both = mm(left, right)
                for e in range(4):
                    at = (e % 2) * seqs
                    attended[h + e] = both[e * depth : (e + 1) * depth, at : at + seqs]
        gated = (jnp.concatenate(attended, axis=0) * gate_scr[r]).astype(BF16)
        gated_scr[r] = gated.T
        return carry

    lax.fori_loop(0, local_res, attend, 0, unroll=2)
    for copy in copies[3:]:
        copy.wait()

    def finish(i, carry):
        gated = gated_scr[pl.ds(i * batch, batch)].reshape(batch * seqs, channels)
        update = mm(gated, wout_ref[...])
        for r in range(batch):
            for at in range(0, seqs, CHUNK):
                row = r * seqs + at
                x = turned_scr[i * batch + r, at : at + CHUNK].astype(F32)
                second = (x + update[row : row + CHUNK]).astype(BF16)
                gated_scr[i * batch + r, at : at + CHUNK] = second
                normed_scr[row : row + CHUNK] = layer_normalize(
                    second.astype(F32), gain2_ref[...]
                ).astype(BF16)
        hidden = jnp.maximum(mm(normed_scr[...], widen_ref[...]), 0.0).astype(BF16)
        update = mm(hidden, shrink_ref[...]).reshape(batch, seqs, channels)
        for r in range(batch):
            second = gated_scr[i * batch + r].astype(F32)
            done_scr[i * batch + r] = (second + update[r]).astype(BF16)
        return carry

    lax.fori_loop(0, local_res // batch, finish, 0)
    if not turn:
        out_ref[...] = done_scr[...]
    for c in range(slabs):
        for g in range(seqs // SLAB):
            block = done_scr[c * SLAB : (c + 1) * SLAB, g * SLAB : (g + 1) * SLAB]
            turned = mm(swap, block.reshape(SLAB * SLAB, channels))
            start = base + c * SLAB
            out_ref[g * SLAB : (g + 1) * SLAB, start : start + SLAB] = turned.astype(
                BF16
            ).reshape(SLAB, SLAB, channels)


def in_vmem(count):
    return [pl.BlockSpec(memory_space=pltpu.VMEM)] * count


def anywhere(count):
    return [pl.BlockSpec(memory_space=pl.ANY)] * count


def like(*arrays):
    return [pltpu.VMEM(array.shape, array.dtype) for array in arrays]


def body(
    aligned_chain_features,
    pair_representation_state,
    gap_block_flags,
    pair_norm_gain,
    pair_head_weight,
    horizontal_scaling_factor,
    row_input_weight,
    horizontal_final_matrix,
    vertical_scaling_factor,
    column_input_weight,
    vertical_final_matrix,
    feedforward_scaling_factor,
    feedforward_widen_matrix,
    feedforward_shrink_matrix,
):
    groups = lax.axis_size("res")
    total_seqs, local_res, channels = aligned_chain_features.shape
    residues = pair_representation_state.shape[1]
    heads = pair_head_weight.shape[1]
    local_seqs = total_seqs // groups
    turn = local_res % SLAB == 0
    res_parts = local_res // SLAB if turn else 1
    part_res = local_res // res_parts
    here = lax.axis_index("res")

    def exchange(values):
        return lax.all_to_all(values, "res", split_axis=0, concat_axis=0, tiled=True)

    def kernel_call(kernel, name, micros, in_specs, out_shape, scratch, space=pltpu.VMEM):
        return pl.pallas_call(
            kernel,
            out_shape=jax.ShapeDtypeStruct(out_shape, BF16),
            in_specs=in_specs,
            out_specs=pl.BlockSpec(memory_space=space),
            scratch_shapes=scratch,
            compiler_params=pltpu.CompilerParams(vmem_limit_bytes=VMEM_BYTES),
            cost_estimate=pl.CostEstimate(
                flops=int(micros * 1e9), bytes_accessed=1 << 20, transcendentals=0
            ),
            name=name,
        )

    step = min(SLAB, local_res)
    payload = kernel_call(
        payload_kernel, "payload", 5, in_vmem(2) + anywhere(2),
        (groups, local_seqs + heads, local_res, channels),
        [
            pltpu.VMEM(pair_representation_state.shape, BF16),
            pltpu.VMEM((residues, step * pair_representation_state.shape[2]), BF16),
            pltpu.VMEM((heads, local_res, residues), BF16),
            pltpu.SemaphoreType.DMA((1 + local_res // step,)),
            pltpu.SemaphoreType.DMA((groups,)),
        ],
        pl.ANY,
    )(
        pair_norm_gain[None, :], pair_head_weight,
        aligned_chain_features.reshape(groups, local_seqs, local_res, channels),
        pair_representation_state,
    )
    arrived = exchange(payload)

    def slots(weight):
        return [weight[:, i * channels : (i + 1) * channels] for i in range(4)]

    rq, rk, rv, rg = slots(row_input_weight)
    row_weights = (rk, rv.T, jnp.concatenate([rq, rg], axis=1).T, horizontal_final_matrix)
    cq, ck, cv, cg = slots(column_input_weight)
    col_weights = (
        ck, jnp.concatenate([cq, cv, cg], axis=1).T, vertical_final_matrix,
        feedforward_widen_matrix, feedforward_shrink_matrix,
    )
    gap = lax.dynamic_slice_in_dim(gap_block_flags, here * local_seqs, local_seqs, 0)
    column_block = (here * local_res) // BLOCK
    col_gap = lax.dynamic_slice_in_dim(gap_block_flags, column_block, 1, 1)

    def row_attention(low, count):
        queries = groups * count
        operands = (arrived, *row_weights)
        pair = 2 if local_seqs % 2 == 0 else 1
        return kernel_call(
            functools.partial(row_kernel, low, count), "row_attention", 10,
            [pl.BlockSpec(memory_space=pltpu.SMEM)] + in_vmem(1) + anywhere(5),
            (groups, local_seqs, count, channels),
            [
                pltpu.VMEM((groups, local_seqs, local_res, channels), BF16),
                pltpu.VMEM((groups, heads, local_res, residues), BF16),
            ]
            + like(*row_weights)
            + [
                pltpu.SemaphoreType.DMA((6,)),
                pltpu.VMEM((heads + 1, residues, queries), F32),
                pltpu.VMEM((local_seqs, channels, queries), BF16),
                pltpu.VMEM((local_seqs, residues, channels), BF16),
                pltpu.VMEM((local_seqs, channels, residues), BF16),
                pltpu.VMEM((local_seqs, channels, queries), F32),
                pltpu.VMEM((local_seqs, queries, channels), BF16),
                pltpu.VMEM((pair * residues, channels), BF16),
                pltpu.VMEM((pair * queries, channels), BF16),
            ],
        )(gap, horizontal_scaling_factor[None, :], *operands)

    finals = [exchange(row_attention(c * part_res, part_res)) for c in range(res_parts)]
    done = []
    for c in range(res_parts):
        piece = finals[c].reshape(total_seqs, part_res, channels)
        if not turn:
            piece = jnp.swapaxes(piece, 0, 1)
        before = done if c == res_parts - 1 else []
        if not turn:
            shape = (part_res, total_seqs, channels)
        else:
            shape = (total_seqs, part_res * (1 + len(before)), channels)
        operands = (piece, *col_weights)
        done.append(
            kernel_call(
                functools.partial(column_kernel, heads, turn, len(before)),
                "column_transition", 10,
                in_vmem(3) + anywhere(6 + len(before)), shape,
                like(*operands)
                + [
                    pltpu.SemaphoreType.DMA((6 + len(before),)),
                    pltpu.VMEM((part_res, total_seqs, channels), BF16),
                    pltpu.VMEM((part_res, channels, total_seqs), BF16),
                    pltpu.VMEM((part_res, total_seqs, channels), BF16),
                    pltpu.VMEM((part_res, channels, total_seqs), BF16),
                    pltpu.VMEM((part_res, channels, total_seqs), F32),
                    pltpu.VMEM((part_res, total_seqs, channels), BF16),
                    pltpu.VMEM((part_res, total_seqs, channels), BF16),
                    pltpu.VMEM((min(4, part_res) * total_seqs, channels), BF16),
                ],
            )(
                col_gap, vertical_scaling_factor[None, :], feedforward_scaling_factor[None, :],
                *operands, *before,
            )
        )
    return done[-1] if turn else jnp.swapaxes(done[-1], 0, 1)


def solution(mesh):
    placed = (
        P("dp", "res", None),
        P(("dp", "res"), None, None),
        P("dp", None),
    ) + (P(),) * 11
    return jax.shard_map(
        body, mesh=mesh, in_specs=placed, out_specs=P("dp", "res", None), check_vma=False
    )
```

```python
import functools

import jax
import jax.numpy as jnp
from jax import lax
from jax.experimental import pallas as pl
from jax.experimental.pallas import tpu as pltpu
from jax.sharding import PartitionSpec as P

BLOCK = 128
EPSILON = 1e-05
MASKED_SCORE = -1000000000.0
LANES = 128
SLAB = 16
F32 = jnp.float32
BF16 = jnp.bfloat16
VMEM_BYTES = 60 * 1024 * 1024
CHUNK = 64


def layer_normalize(values_f, scale_gain):
    centred = values_f - jnp.mean(values_f, axis=-1, keepdims=True)
    spread = jnp.mean(centred * centred, axis=-1, keepdims=True)
    return centred * lax.rsqrt(spread + EPSILON) * scale_gain


def mm(lhs, rhs):
    return jnp.dot(lhs, rhs, preferred_element_type=F32)


def mm_nt(lhs, rhs):
    return lax.dot_general(lhs, rhs, (((1,), (1,)), ((), ())), preferred_element_type=F32)


def swap_matrix(outer, inner):
    size = outer * inner
    to = lax.broadcasted_iota(jnp.int32, (size, size), 0)
    come = lax.broadcasted_iota(jnp.int32, (size, size), 1)
    source = lax.rem(to, outer) * inner + lax.div(to, outer)
    return jnp.where(come == source, 1.0, 0.0).astype(BF16)


def start_copies(sources, targets, sems):
    copies = [
        pltpu.make_async_copy(source, target, sems.at[i])
        for i, (source, target) in enumerate(zip(sources, targets))
    ]
    for copy in copies:
        copy.start()
    return copies


def bias_kernel(gain_ref, weight_ref, pair_hbm, out_ref, pair_ref, normed_scr, sems):
    local_res, residues, channels = pair_ref.shape
    heads = out_ref.shape[0]
    step = normed_scr.shape[1] // channels
    parts = local_res // step
    copies = start_copies(
        [pair_hbm.at[p * step : (p + 1) * step] for p in range(parts)],
        [pair_ref.at[p * step : (p + 1) * step] for p in range(parts)],
        sems,
    )
    width = heads * step
    head_at = lax.broadcasted_iota(jnp.int32, (heads, width), 0)
    spread = jnp.where(lax.broadcasted_iota(jnp.int32, (heads, width), 1) // step == head_at, 1.0, 0.0)
    wide = mm(weight_ref[...], spread.astype(BF16))
    lane = lax.broadcasted_iota(jnp.int32, wide.shape, 1)
    weights = jnp.concatenate(
        [jnp.where(lane % step == i, wide, 0.0).astype(BF16) for i in range(step)], axis=0
    )
    rows = 2 * CHUNK
    for p in range(parts):
        copies[p].wait()
        for i in range(step):
            for at in range(0, residues, rows):
                x = pair_ref[p * step + i, at : at + rows].astype(F32)
                normed_scr[at : at + rows, i * channels : (i + 1) * channels] = layer_normalize(
                    x, gain_ref[...]
                ).astype(BF16)
        projected = mm(normed_scr[...], weights)
        out_ref[:, p * step : (p + 1) * step] = (
            projected.T.reshape(heads, step, residues).astype(BF16)
        )


def softmax_lanes(scores):
    e = jnp.exp(scores - jnp.max(scores, axis=-1, keepdims=True))
    total = jnp.sum(e, axis=-1, keepdims=True)
    inverse = pl.reciprocal(total, approx=True)
    inverse = inverse * (2.0 - total * inverse)
    return (e * inverse).astype(BF16)


def gate_of(values):
    return 0.5 * jnp.tanh(0.5 * values) + 0.5


def pick_heads(parts, depth):
    lane = lax.broadcasted_iota(jnp.int32, parts[0].shape, 1)
    slot = lane // depth % len(parts)
    picked = parts[-1]
    for j in range(len(parts) - 2, -1, -1):
        picked = jnp.where(slot == j, parts[j], picked)
    return picked


def lane_mask(width, depth, slots, j):
    lane = lax.broadcasted_iota(jnp.int32, (1, width), 1)
    return jnp.where(lane // depth % slots == j, 1.0, 0.0).astype(BF16)


def row_kernel(
    low, count, gap_ref, gain_ref, x_hbm, win_hbm, wout_hbm, bias_hbm, out_ref,
    x_ref, win_ref, wout_ref, bias_ref, sems,
    bias_scr, q_scr, k_scr, v_scr, gate_scr, gated_scr, normed_scr, mine_scr, qm_scr, s_scr, p_scr,
):
    copies = start_copies(
        [x_hbm, win_hbm, wout_hbm, bias_hbm], [x_ref, win_ref, wout_ref, bias_ref], sems
    )
    groups, seqs, local_res, channels = x_ref.shape
    heads = bias_ref.shape[1]
    residues = groups * local_res
    queries = groups * count
    depth = channels // heads
    per = LANES // depth
    scale = depth ** (-0.5)
    block = normed_scr.shape[0] // residues
    slabs = max(1, CHUNK // local_res)
    qm_scr[...] = jnp.zeros(qm_scr.shape, BF16)
    copies[0].wait()
    copies[1].wait()

    def dense(i, carry):
        for j in range(block):
            for g in range(0, groups, slabs):
                x = x_ref[g : g + slabs, pl.ds(i * block + j, 1)].reshape(slabs * local_res, channels)
                n = layer_normalize(x.astype(F32), gain_ref[...]).astype(BF16)
                at = j * residues + g * local_res
                normed_scr[at : at + slabs * local_res] = n
                if count != local_res:
                    n = n.reshape(slabs, local_res, channels)[:, low : low + count]
                    n = n.reshape(slabs * count, channels)
                at = j * queries + g * count
                mine_scr[at : at + slabs * count] = n
        some = pl.ds(i * block, block)
        k = mm(normed_scr[...], win_ref[:, channels : 2 * channels])
        k_scr[some] = k.astype(BF16).reshape(block, residues, channels)
        v = mm(normed_scr[...], win_ref[:, 2 * channels : 3 * channels])
        v_scr[some] = v.astype(BF16).reshape(block, residues, channels)
        q = mm(mine_scr[...], win_ref[:, :channels]) * scale
        q_scr[some] = q.astype(BF16).reshape(block, queries, channels)
        gates = mm(mine_scr[...], win_ref[:, 3 * channels :])
        gate_scr[some] = gate_of(gates).reshape(block, queries, channels)
        return carry

    lax.fori_loop(0, seqs // block, dense, 0)

    copies[3].wait()
    for h in range(heads):
        bias_scr[h] = bias_ref[:, h, low : low + count].reshape(queries, residues).astype(F32)
    bias_scr[heads] = jnp.full((queries, residues), MASKED_SCORE, F32)
    chunk = min(CHUNK, queries)

    def attend(i, carry):
        for u in range(qm_scr.shape[0]):
            s = i * qm_scr.shape[0] + u
            gaps = [gap_ref[s, b] == 1 for b in range(residues // BLOCK)]
            for h in range(heads):
                lanes = slice(h // per * LANES, (h // per + 1) * LANES)
                qm_scr[u, h * queries : (h + 1) * queries, lanes] = q_scr[s, :, lanes] * lane_mask(
                    LANES, depth, per, h % per
                )
            s_scr[u] = mm_nt(qm_scr[u], k_scr[s])
            for h in range(heads):
                for at in range(0, queries, chunk):
                    row = h * queries + at
                    bias = [
                        bias_scr[
                            jnp.where(gap, heads, h), at : at + chunk, b * BLOCK : (b + 1) * BLOCK
                        ]
                        for b, gap in enumerate(gaps)
                    ]
                    scores = s_scr[u, row : row + chunk] + jnp.concatenate(bias, axis=1)
                    p_scr[u, row : row + chunk] = softmax_lanes(scores)
            attended = []
            for g in range(heads // per):
                parts = mm(
                    p_scr[u, g * per * queries : (g + 1) * per * queries],
                    v_scr[s, :, g * LANES : (g + 1) * LANES],
                )
                attended.append(
                    pick_heads([parts[j * queries : (j + 1) * queries] for j in range(per)], depth)
                )
            gated_scr[s] = (jnp.concatenate(attended, axis=1) * gate_scr[s]).astype(BF16)
        return carry

    lax.fori_loop(0, seqs // qm_scr.shape[0], attend, 0)
    copies[2].wait()

    def finish(i, carry):
        gated = gated_scr[pl.ds(i * block, block)].reshape(block * queries, channels)
        update = mm(gated, wout_ref[...])
        for j in range(block):
            s = i * block + j
            x = x_ref[:, pl.ds(s, 1), low : low + count].reshape(queries, channels)
            result = x.astype(F32) + update[j * queries : (j + 1) * queries]
            out_ref[:, pl.ds(s, 1)] = result.astype(BF16).reshape(groups, 1, count, channels)
        return carry

    lax.fori_loop(0, seqs // block, finish, 0)


def column_kernel(
    heads, turn, earlier, gap_ref, gain_ref, gain2_ref, x_hbm, win_hbm, wout_hbm,
    widen_hbm, shrink_hbm, *refs,
):
    done_hbm, refs = refs[:earlier], refs[earlier:]
    (out_ref, x_ref, win_ref, wout_ref, widen_ref, shrink_ref, sems) = refs[:7]
    (turned_scr, q_scr, k_scr, v_scr, gate_scr, gated_scr, done_scr, normed_scr) = refs[7:15]
    (qm_scr, kb_scr, vb_scr, s_scr, p_scr) = refs[15:]
    base, places = 0, []
    for done in done_hbm:
        places.append(out_ref.at[:, base : base + done.shape[1]])
        base += done.shape[1]
    copies = start_copies(
        [x_hbm, win_hbm, wout_hbm, widen_hbm, shrink_hbm, *done_hbm],
        [x_ref, win_ref, wout_ref, widen_ref, shrink_ref, *places],
        sems,
    )
    local_res, seqs, channels = turned_scr.shape
    depth = channels // heads
    per = LANES // depth
    halves = heads // per
    scale = depth ** (-0.5)
    batch = normed_scr.shape[0] // seqs
    slabs = local_res // SLAB if turn else 0
    swap = swap_matrix(SLAB, SLAB)
    kb_scr[...] = jnp.zeros(kb_scr.shape, BF16)
    vb_scr[...] = jnp.zeros(vb_scr.shape, BF16)
    copies[0].wait()
    if not turn:
        turned_scr[...] = x_ref[...]
    for c in range(slabs):
        for g in range(seqs // SLAB):
            block = x_ref[g * SLAB : (g + 1) * SLAB, c * SLAB : (c + 1) * SLAB]
            turned = mm(swap, block.reshape(SLAB * SLAB, channels))
            turned_scr[c * SLAB : (c + 1) * SLAB, g * SLAB : (g + 1) * SLAB] = turned.astype(
                BF16
            ).reshape(SLAB, SLAB, channels)
    copies[1].wait()

    def dense(i, carry):
        for r in range(batch):
            for at in range(0, seqs, CHUNK):
                x = turned_scr[i * batch + r, at : at + CHUNK].astype(F32)
                n = layer_normalize(x, gain_ref[...]).astype(BF16)
                normed_scr[r * seqs + at : r * seqs + at + CHUNK] = n
        some = pl.ds(i * batch, batch)
        q = mm(normed_scr[...], win_ref[:, :channels]) * scale
        q_scr[some] = q.astype(BF16).reshape(batch, seqs, channels)
        k = mm(normed_scr[...], win_ref[:, channels : 2 * channels])
        k_scr[some] = k.astype(BF16).reshape(batch, seqs, channels)
        v = mm(normed_scr[...], win_ref[:, 2 * channels : 3 * channels])
        v_scr[some] = v.astype(BF16).reshape(batch, seqs, channels)
        gates = mm(normed_scr[...], win_ref[:, 3 * channels :])
        gate_scr[some] = gate_of(gates).reshape(batch, seqs, channels)
        return carry

    lax.fori_loop(0, local_res // batch, dense, 0)

    mask = jnp.where(gap_ref[...] == 1, MASKED_SCORE, 0.0)

    def attend(i, carry):
        for u in range(qm_scr.shape[0]):
            r = i * qm_scr.shape[0] + u
            for j in range(per):
                qm_scr[u, j * seqs : (j + 1) * seqs] = q_scr[r] * lane_mask(channels, depth, per, j)
            for g in range(halves):
                lanes = slice(g * LANES, (g + 1) * LANES)
                kb_scr[u, g * seqs : (g + 1) * seqs, lanes] = k_scr[r, :, lanes]
                vb_scr[u, g * seqs : (g + 1) * seqs, lanes] = v_scr[r, :, lanes]
            s_scr[u] = mm_nt(qm_scr[u], kb_scr[u])
            for row in range(0, per * seqs, CHUNK):
                for g in range(halves):
                    lanes = slice(g * seqs, (g + 1) * seqs)
                    p_scr[u, row : row + CHUNK, lanes] = softmax_lanes(
                        s_scr[u, row : row + CHUNK, lanes] + mask
                    )
            parts = mm(p_scr[u], vb_scr[u])
            attended = pick_heads([parts[j * seqs : (j + 1) * seqs] for j in range(per)], depth)
            gated_scr[r] = (attended * gate_scr[r]).astype(BF16)
        return carry

    lax.fori_loop(0, local_res // qm_scr.shape[0], attend, 0)
    for copy in copies[2:]:
        copy.wait()

    def finish(i, carry):
        gated = gated_scr[pl.ds(i * batch, batch)].reshape(batch * seqs, channels)
        update = mm(gated, wout_ref[...])
        for r in range(batch):
            for at in range(0, seqs, CHUNK):
                row = r * seqs + at
                x = turned_scr[i * batch + r, at : at + CHUNK].astype(F32)
                second = (x + update[row : row + CHUNK]).astype(BF16)
                gated_scr[i * batch + r, at : at + CHUNK] = second
                normed_scr[row : row + CHUNK] = layer_normalize(
                    second.astype(F32), gain2_ref[...]
                ).astype(BF16)
        hidden = jnp.maximum(mm(normed_scr[...], widen_ref[...]), 0.0).astype(BF16)
        update = mm(hidden, shrink_ref[...]).reshape(batch, seqs, channels)
        for r in range(batch):
            second = gated_scr[i * batch + r].astype(F32)
            done_scr[i * batch + r] = (second + update[r]).astype(BF16)
        return carry

    lax.fori_loop(0, local_res // batch, finish, 0)
    if not turn:
        out_ref[...] = done_scr[...]
    for c in range(slabs):
        for g in range(seqs // SLAB):
            block = done_scr[c * SLAB : (c + 1) * SLAB, g * SLAB : (g + 1) * SLAB]
            turned = mm(swap, block.reshape(SLAB * SLAB, channels))
            start = base + c * SLAB
            out_ref[g * SLAB : (g + 1) * SLAB, start : start + SLAB] = turned.astype(
                BF16
            ).reshape(SLAB, SLAB, channels)


def largest(total, bound):
    return max(d for d in range(1, bound + 1) if total % d == 0)


def in_vmem(count):
    return [pl.BlockSpec(memory_space=pltpu.VMEM)] * count


def anywhere(count):
    return [pl.BlockSpec(memory_space=pl.ANY)] * count


def like(*arrays):
    return [pltpu.VMEM(array.shape, array.dtype) for array in arrays]


def body(
    aligned_chain_features,
    pair_representation_state,
    gap_block_flags,
    pair_norm_gain,
    pair_head_weight,
    horizontal_scaling_factor,
    row_input_weight,
    horizontal_final_matrix,
    vertical_scaling_factor,
    column_input_weight,
    vertical_final_matrix,
    feedforward_scaling_factor,
    feedforward_widen_matrix,
    feedforward_shrink_matrix,
):
    groups = lax.axis_size("res")
    total_seqs, local_res, channels = aligned_chain_features.shape
    residues = pair_representation_state.shape[1]
    heads = pair_head_weight.shape[1]
    local_seqs = total_seqs // groups
    turn = local_res % SLAB == 0
    res_parts = local_res // SLAB if turn else 1
    part_res = local_res // res_parts
    here = lax.axis_index("res")

    def exchange(values):
        return lax.all_to_all(values, "res", split_axis=0, concat_axis=0, tiled=True)

    def kernel_call(kernel, name, micros, in_specs, out_shape, scratch, space=pltpu.VMEM):
        return pl.pallas_call(
            kernel,
            out_shape=jax.ShapeDtypeStruct(out_shape, BF16),
            in_specs=in_specs,
            out_specs=pl.BlockSpec(memory_space=space),
            scratch_shapes=scratch,
            compiler_params=pltpu.CompilerParams(vmem_limit_bytes=VMEM_BYTES),
            cost_estimate=pl.CostEstimate(
                flops=int(micros * 1e9), bytes_accessed=1 << 20, transcendentals=0
            ),
            name=name,
        )

    step = min(SLAB, local_res)
    bias_local = kernel_call(
        bias_kernel, "pair_bias", 5, in_vmem(2) + anywhere(1), (heads, local_res, residues),
        [
            pltpu.VMEM(pair_representation_state.shape, BF16),
            pltpu.VMEM((residues, step * pair_representation_state.shape[2]), BF16),
            pltpu.SemaphoreType.DMA((local_res // step,)),
        ],
    )(pair_norm_gain[None, :], pair_head_weight, pair_representation_state)
    bias_local, features = lax.optimization_barrier((bias_local, aligned_chain_features))
    bias_all = lax.all_gather(bias_local, "res", axis=0, tiled=False)
    arrived = exchange(features.reshape(groups, local_seqs, local_res, channels))

    gap = lax.dynamic_slice_in_dim(gap_block_flags, here * local_seqs, local_seqs, 0)
    column_block = (here * local_res) // BLOCK
    col_gap = lax.dynamic_slice_in_dim(gap_block_flags, column_block, 1, 1).reshape(1, total_seqs)

    def row_attention(low, count):
        queries = groups * count
        operands = (arrived, row_input_weight, horizontal_final_matrix, bias_all)
        block, pair = largest(local_seqs, 4), largest(local_seqs, 2)
        return kernel_call(
            functools.partial(row_kernel, low, count), "row_attention", 10,
            [pl.BlockSpec(memory_space=pltpu.SMEM)] + in_vmem(1) + anywhere(4),
            (groups, local_seqs, count, channels),
            like(*operands)
            + [
                pltpu.SemaphoreType.DMA((4,)),
                pltpu.VMEM((heads + 1, queries, residues), F32),
                pltpu.VMEM((local_seqs, queries, channels), BF16),
                pltpu.VMEM((local_seqs, residues, channels), BF16),
                pltpu.VMEM((local_seqs, residues, channels), BF16),
                pltpu.VMEM((local_seqs, queries, channels), F32),
                pltpu.VMEM((local_seqs, queries, channels), BF16),
                pltpu.VMEM((block * residues, channels), BF16),
                pltpu.VMEM((block * queries, channels), BF16),
                pltpu.VMEM((pair, heads * queries, channels), BF16),
                pltpu.VMEM((pair, heads * queries, residues), F32),
                pltpu.VMEM((pair, heads * queries, residues), BF16),
            ],
        )(gap, horizontal_scaling_factor[None, :], *operands)

    finals = [exchange(row_attention(c * part_res, part_res)) for c in range(res_parts)]
    done = []
    rows, per = total_seqs, LANES * heads // channels
    batch, pair = largest(part_res, 8), largest(part_res, 2)
    for c in range(res_parts):
        piece = finals[c].reshape(total_seqs, part_res, channels)
        if not turn:
            piece = jnp.swapaxes(piece, 0, 1)
        before = done if c == res_parts - 1 else []
        if not turn:
            shape = (part_res, total_seqs, channels)
        else:
            shape = (total_seqs, part_res * (1 + len(before)), channels)
        operands = (
            piece, column_input_weight, vertical_final_matrix,
            feedforward_widen_matrix, feedforward_shrink_matrix,
        )
        done.append(
            kernel_call(
                functools.partial(column_kernel, heads, turn, len(before)),
                "column_transition", 10, in_vmem(3) + anywhere(5 + len(before)), shape,
                like(*operands)
                + [pltpu.SemaphoreType.DMA((5 + len(before),))]
                + [pltpu.VMEM((part_res, rows, channels), BF16)] * 4
                + [pltpu.VMEM((part_res, rows, channels), F32)]
                + [pltpu.VMEM((part_res, rows, channels), BF16)] * 2
                + [
                    pltpu.VMEM((batch * rows, channels), BF16),
                    pltpu.VMEM((pair, per * rows, channels), BF16),
                    pltpu.VMEM((pair, heads // per * rows, channels), BF16),
                    pltpu.VMEM((pair, heads // per * rows, channels), BF16),
                    pltpu.VMEM((pair, per * rows, heads // per * rows), F32),
                    pltpu.VMEM((pair, per * rows, heads // per * rows), BF16),
                ],
            )(
                col_gap, vertical_scaling_factor[None, :], feedforward_scaling_factor[None, :],
                *operands, *before,
            )
        )
    return done[-1] if turn else jnp.swapaxes(done[-1], 0, 1)


def solution(mesh):
    placed = (
        P("dp", "res", None),
        P(("dp", "res"), None, None),
        P("dp", None),
    ) + (P(),) * 11
    return jax.shard_map(
        body, mesh=mesh, in_specs=placed, out_specs=P("dp", "res", None), check_vma=False
    )
```

```python
import functools

import jax
import jax.numpy as jnp
from jax import lax
from jax.experimental import pallas as pl
from jax.experimental.pallas import tpu as pltpu
from jax.sharding import PartitionSpec as P

BLOCK = 128
EPSILON = 1e-05
MASKED_SCORE = -1000000000.0
LANES = 128
SLAB = 16
F32 = jnp.float32
BF16 = jnp.bfloat16
VMEM_BYTES = 44 * 1024 * 1024
CHUNK = 64


def layer_normalize(values_f, scale_gain):
    centred = values_f - jnp.mean(values_f, axis=-1, keepdims=True)
    spread = jnp.mean(centred * centred, axis=-1, keepdims=True)
    return centred * lax.rsqrt(spread + EPSILON) * scale_gain


def mm(lhs, rhs):
    return jnp.dot(lhs, rhs, preferred_element_type=F32)


def mm_nt(lhs, rhs):
    return lax.dot_general(lhs, rhs, (((1,), (1,)), ((), ())), preferred_element_type=F32)


def swap_matrix(outer, inner):
    size = outer * inner
    to = lax.broadcasted_iota(jnp.int32, (size, size), 0)
    come = lax.broadcasted_iota(jnp.int32, (size, size), 1)
    source = lax.rem(to, outer) * inner + lax.div(to, outer)
    return jnp.where(come == source, 1.0, 0.0).astype(BF16)


def bias_kernel(gain_ref, weight_ref, pair_ref, out_ref, normed_scr):
    local_res, residues, channels = pair_ref.shape
    heads = out_ref.shape[0]
    step = normed_scr.shape[1] // channels
    parts = local_res // step
    width = heads * step
    head_at = lax.broadcasted_iota(jnp.int32, (heads, width), 0)
    spread = jnp.where(lax.broadcasted_iota(jnp.int32, (heads, width), 1) // step == head_at, 1.0, 0.0)
    wide = mm(weight_ref[...], spread.astype(BF16))
    lane = lax.broadcasted_iota(jnp.int32, wide.shape, 1)
    weights = jnp.concatenate(
        [jnp.where(lane % step == i, wide, 0.0).astype(BF16) for i in range(step)], axis=0
    )
    rows = 2 * CHUNK
    for p in range(parts):
        for i in range(step):
            for at in range(0, residues, rows):
                x = pair_ref[p * step + i, at : at + rows].astype(F32)
                normed_scr[at : at + rows, i * channels : (i + 1) * channels] = layer_normalize(
                    x, gain_ref[...]
                ).astype(BF16)
        projected = mm(normed_scr[...], weights)
        out_ref[:, p * step : (p + 1) * step] = (
            projected.T.reshape(heads, step, residues).astype(BF16)
        )


def softmax_lanes(scores):
    e = jnp.exp(scores - jnp.max(scores, axis=-1, keepdims=True))
    total = jnp.sum(e, axis=-1, keepdims=True)
    inverse = pl.reciprocal(total, approx=True)
    inverse = inverse * (2.0 - total * inverse)
    return (e * inverse).astype(BF16)


def gate_of(values):
    return 0.5 * jnp.tanh(0.5 * values) + 0.5


def pick_heads(parts, depth):
    lane = lax.broadcasted_iota(jnp.int32, parts[0].shape, 1)
    slot = lane // depth % len(parts)
    picked = parts[-1]
    for j in range(len(parts) - 2, -1, -1):
        picked = jnp.where(slot == j, parts[j], picked)
    return picked


def lane_mask(width, depth, slots, j):
    lane = lax.broadcasted_iota(jnp.int32, (1, width), 1)
    return jnp.where(lane // depth % slots == j, 1.0, 0.0).astype(BF16)


def row_kernel(
    low, count, gap_ref, place_ref, gain_ref, x_ref, win_ref, wout_ref, *refs,
):
    bias_refs, refs = refs[:-12], refs[-12:]
    (out_ref, bias_scr, q_scr, k_scr, v_scr, gate_scr, gated_scr) = refs[:7]
    (normed_scr, mine_scr, qm_scr, s_scr, p_scr) = refs[7:]
    groups, seqs, local_res, channels = x_ref.shape
    heads = bias_scr.shape[0] - 1
    residues = groups * local_res
    queries = groups * count
    depth = channels // heads
    per = LANES // depth
    scale = depth ** (-0.5)
    block = normed_scr.shape[0] // residues
    slabs = max(1, CHUNK // local_res)
    qm_scr[...] = jnp.zeros(qm_scr.shape, BF16)

    def dense(i, carry):
        for j in range(block):
            for g in range(0, groups, slabs):
                x = x_ref[g : g + slabs, pl.ds(i * block + j, 1)].reshape(slabs * local_res, channels)
                n = layer_normalize(x.astype(F32), gain_ref[...]).astype(BF16)
                at = j * residues + g * local_res
                normed_scr[at : at + slabs * local_res] = n
                if count != local_res:
                    n = n.reshape(slabs, local_res, channels)[:, low : low + count]
                    n = n.reshape(slabs * count, channels)
                at = j * queries + g * count
                mine_scr[at : at + slabs * count] = n
        some = pl.ds(i * block, block)
        k = mm(normed_scr[...], win_ref[:, channels : 2 * channels])
        k_scr[some] = k.astype(BF16).reshape(block, residues, channels)
        v = mm(normed_scr[...], win_ref[:, 2 * channels : 3 * channels])
        v_scr[some] = v.astype(BF16).reshape(block, residues, channels)
        q = mm(mine_scr[...], win_ref[:, :channels]) * scale
        q_scr[some] = q.astype(BF16).reshape(block, queries, channels)
        gates = mm(mine_scr[...], win_ref[:, 3 * channels :])
        gate_scr[some] = gate_of(gates).reshape(block, queries, channels)
        return carry

    lax.fori_loop(0, seqs // block, dense, 0)

    for g in range(groups):
        if len(bias_refs) == 1:
            block_of = bias_refs[0][g, :, low : low + count]
        else:
            lines = groups // 2
            slot = lax.rem(place_ref[0, 0] - g // 2 + lines, lines)
            block_of = jnp.where(
                place_ref[0, 1] == g % 2,
                bias_refs[0][slot, :, low : low + count],
                bias_refs[1][slot, :, low : low + count],
            )
        bias_scr[:heads, g * count : (g + 1) * count] = block_of.astype(F32)
    bias_scr[heads] = jnp.full((queries, residues), MASKED_SCORE, F32)
    chunk = min(CHUNK, queries)

    def attend(i, carry):
        for u in range(qm_scr.shape[0]):
            s = i * qm_scr.shape[0] + u
            gaps = [gap_ref[s, b] == 1 for b in range(residues // BLOCK)]
            for h in range(heads):
                lanes = slice(h // per * LANES, (h // per + 1) * LANES)
                qm_scr[u, h * queries : (h + 1) * queries, lanes] = q_scr[s, :, lanes] * lane_mask(
                    LANES, depth, per, h % per
                )
            s_scr[u] = mm_nt(qm_scr[u], k_scr[s])
            for h in range(heads):
                for at in range(0, queries, chunk):
                    row = h * queries + at
                    bias = [
                        bias_scr[
                            jnp.where(gap, heads, h), at : at + chunk, b * BLOCK : (b + 1) * BLOCK
                        ]
                        for b, gap in enumerate(gaps)
                    ]
                    scores = s_scr[u, row : row + chunk] + jnp.concatenate(bias, axis=1)
                    p_scr[u, row : row + chunk] = softmax_lanes(scores)
            attended = []
            for g in range(heads // per):
                parts = mm(
                    p_scr[u, g * per * queries : (g + 1) * per * queries],
                    v_scr[s, :, g * LANES : (g + 1) * LANES],
                )
                attended.append(
                    pick_heads([parts[j * queries : (j + 1) * queries] for j in range(per)], depth)
                )
            gated_scr[s] = (jnp.concatenate(attended, axis=1) * gate_scr[s]).astype(BF16)
        return carry

    lax.fori_loop(0, seqs // qm_scr.shape[0], attend, 0)

    def finish(i, carry):
        gated = gated_scr[pl.ds(i * block, block)].reshape(block * queries, channels)
        update = mm(gated, wout_ref[...])
        for j in range(block):
            s = i * block + j
            x = x_ref[:, pl.ds(s, 1), low : low + count].reshape(queries, channels)
            result = x.astype(F32) + update[j * queries : (j + 1) * queries]
            out_ref[:, pl.ds(s, 1)] = result.astype(BF16).reshape(groups, 1, count, channels)
        return carry

    lax.fori_loop(0, seqs // block, finish, 0)


def column_kernel(
    heads, turn, earlier, gap_ref, gain_ref, gain2_ref, x_ref, win_ref, wout_ref,
    widen_ref, shrink_ref, *refs,
):
    done_refs, refs = refs[:earlier], refs[earlier:]
    (out_ref, turned_scr, q_scr, k_scr, v_scr, gate_scr, gated_scr, done_scr) = refs[:8]
    (normed_scr, qm_scr, kb_scr, vb_scr, s_scr, p_scr) = refs[8:]
    base = 0
    for done_ref in done_refs:
        out_ref[:, base : base + done_ref.shape[1]] = done_ref[...]
        base += done_ref.shape[1]
    local_res, seqs, channels = turned_scr.shape
    depth = channels // heads
    per = LANES // depth
    halves = heads // per
    scale = depth ** (-0.5)
    batch = normed_scr.shape[0] // seqs
    slabs = local_res // SLAB if turn else 0
    swap = swap_matrix(SLAB, SLAB)
    kb_scr[...] = jnp.zeros(kb_scr.shape, BF16)
    vb_scr[...] = jnp.zeros(vb_scr.shape, BF16)
    if not turn:
        turned_scr[...] = x_ref[...]
    for c in range(slabs):
        for g in range(seqs // SLAB):
            block = x_ref[g * SLAB : (g + 1) * SLAB, c * SLAB : (c + 1) * SLAB]
            turned = mm(swap, block.reshape(SLAB * SLAB, channels))
            turned_scr[c * SLAB : (c + 1) * SLAB, g * SLAB : (g + 1) * SLAB] = turned.astype(
                BF16
            ).reshape(SLAB, SLAB, channels)

    def dense(i, carry):
        for r in range(batch):
            for at in range(0, seqs, CHUNK):
                x = turned_scr[i * batch + r, at : at + CHUNK].astype(F32)
                n = layer_normalize(x, gain_ref[...]).astype(BF16)
                normed_scr[r * seqs + at : r * seqs + at + CHUNK] = n
        some = pl.ds(i * batch, batch)
        q = mm(normed_scr[...], win_ref[:, :channels]) * scale
        q_scr[some] = q.astype(BF16).reshape(batch, seqs, channels)
        k = mm(normed_scr[...], win_ref[:, channels : 2 * channels])
        k_scr[some] = k.astype(BF16).reshape(batch, seqs, channels)
        v = mm(normed_scr[...], win_ref[:, 2 * channels : 3 * channels])
        v_scr[some] = v.astype(BF16).reshape(batch, seqs, channels)
        gates = mm(normed_scr[...], win_ref[:, 3 * channels :])
        gate_scr[some] = gate_of(gates).reshape(batch, seqs, channels)
        return carry

    lax.fori_loop(0, local_res // batch, dense, 0)

    mask = jnp.where(gap_ref[...] == 1, MASKED_SCORE, 0.0)

    def attend(i, carry):
        for u in range(qm_scr.shape[0]):
            r = i * qm_scr.shape[0] + u
            for j in range(per):
                qm_scr[u, j * seqs : (j + 1) * seqs] = q_scr[r] * lane_mask(channels, depth, per, j)
            for g in range(halves):
                lanes = slice(g * LANES, (g + 1) * LANES)
                kb_scr[u, g * seqs : (g + 1) * seqs, lanes] = k_scr[r, :, lanes]
                vb_scr[u, g * seqs : (g + 1) * seqs, lanes] = v_scr[r, :, lanes]
            s_scr[u] = mm_nt(qm_scr[u], kb_scr[u])
            for row in range(0, per * seqs, CHUNK):
                for g in range(halves):
                    lanes = slice(g * seqs, (g + 1) * seqs)
                    p_scr[u, row : row + CHUNK, lanes] = softmax_lanes(
                        s_scr[u, row : row + CHUNK, lanes] + mask
                    )
            parts = mm(p_scr[u], vb_scr[u])
            attended = pick_heads([parts[j * seqs : (j + 1) * seqs] for j in range(per)], depth)
            gated_scr[r] = (attended * gate_scr[r]).astype(BF16)
        return carry

    lax.fori_loop(0, local_res // qm_scr.shape[0], attend, 0)

    def finish(i, carry):
        gated = gated_scr[pl.ds(i * batch, batch)].reshape(batch * seqs, channels)
        update = mm(gated, wout_ref[...])
        for r in range(batch):
            for at in range(0, seqs, CHUNK):
                row = r * seqs + at
                x = turned_scr[i * batch + r, at : at + CHUNK].astype(F32)
                second = (x + update[row : row + CHUNK]).astype(BF16)
                gated_scr[i * batch + r, at : at + CHUNK] = second
                normed_scr[row : row + CHUNK] = layer_normalize(
                    second.astype(F32), gain2_ref[...]
                ).astype(BF16)
        hidden = jnp.maximum(mm(normed_scr[...], widen_ref[...]), 0.0).astype(BF16)
        update = mm(hidden, shrink_ref[...]).reshape(batch, seqs, channels)
        for r in range(batch):
            second = gated_scr[i * batch + r].astype(F32)
            done_scr[i * batch + r] = (second + update[r]).astype(BF16)
        return carry

    lax.fori_loop(0, local_res // batch, finish, 0)
    if not turn:
        out_ref[...] = done_scr[...]
    for c in range(slabs):
        for g in range(seqs // SLAB):
            block = done_scr[c * SLAB : (c + 1) * SLAB, g * SLAB : (g + 1) * SLAB]
            turned = mm(swap, block.reshape(SLAB * SLAB, channels))
            start = base + c * SLAB
            out_ref[g * SLAB : (g + 1) * SLAB, start : start + SLAB] = turned.astype(
                BF16
            ).reshape(SLAB, SLAB, channels)


def largest(total, bound):
    return max(d for d in range(1, bound + 1) if total % d == 0)


def in_vmem(count):
    return [pl.BlockSpec(memory_space=pltpu.VMEM)] * count


def gather_bias(block, groups):
    if groups != 8:
        return (lax.all_gather(block, "res", axis=0, tiled=False),)
    line = [block]
    for k in range(2, groups, 2):
        line.append(lax.ppermute(block, "res", [(i, (i + k) % groups) for i in range(groups)]))
    line = jnp.stack(line)
    return line, lax.ppermute(line, "res", [(i, i ^ 1) for i in range(groups)])


def body(
    aligned_chain_features,
    pair_representation_state,
    gap_block_flags,
    pair_norm_gain,
    pair_head_weight,
    horizontal_scaling_factor,
    row_input_weight,
    horizontal_final_matrix,
    vertical_scaling_factor,
    column_input_weight,
    vertical_final_matrix,
    feedforward_scaling_factor,
    feedforward_widen_matrix,
    feedforward_shrink_matrix,
):
    groups = lax.axis_size("res")
    total_seqs, local_res, channels = aligned_chain_features.shape
    residues = pair_representation_state.shape[1]
    heads = pair_head_weight.shape[1]
    local_seqs = total_seqs // groups
    turn = local_res % SLAB == 0
    res_parts = local_res // SLAB if turn else 1
    part_res = local_res // res_parts
    here = lax.axis_index("res")

    def exchange(values):
        return lax.all_to_all(values, "res", split_axis=0, concat_axis=0, tiled=True)

    def kernel_call(kernel, name, micros, in_specs, out_shape, scratch, space=pltpu.VMEM):
        return pl.pallas_call(
            kernel,
            out_shape=jax.ShapeDtypeStruct(out_shape, BF16),
            in_specs=in_specs,
            out_specs=pl.BlockSpec(memory_space=space),
            scratch_shapes=scratch,
            compiler_params=pltpu.CompilerParams(vmem_limit_bytes=VMEM_BYTES),
            cost_estimate=pl.CostEstimate(
                flops=int(micros * 1e9), bytes_accessed=1 << 20, transcendentals=0
            ),
            name=name,
        )

    step = min(SLAB, local_res)
    bias_local = kernel_call(
        bias_kernel, "pair_bias", 5, in_vmem(3), (heads, local_res, residues),
        [
            pltpu.VMEM((residues, step * pair_representation_state.shape[2]), BF16),
        ],
    )(pair_norm_gain[None, :], pair_head_weight, pair_representation_state)
    bias_local, features = lax.optimization_barrier((bias_local, aligned_chain_features))
    bias_blocks = gather_bias(bias_local, groups)
    place = jnp.stack([here // 2, here % 2]).astype(jnp.int32)[None, :]
    arrived = exchange(features.reshape(groups, local_seqs, local_res, channels))

    gap = lax.dynamic_slice_in_dim(gap_block_flags, here * local_seqs, local_seqs, 0)
    column_block = (here * local_res) // BLOCK
    col_gap = lax.dynamic_slice_in_dim(gap_block_flags, column_block, 1, 1).reshape(1, total_seqs)

    def row_attention(low, count):
        queries = groups * count
        operands = (arrived, row_input_weight, horizontal_final_matrix, *bias_blocks)
        block, pair = largest(local_seqs, 4), largest(local_seqs, 2)
        return kernel_call(
            functools.partial(row_kernel, low, count), "row_attention", 10,
            [pl.BlockSpec(memory_space=pltpu.SMEM)] * 2 + in_vmem(1 + len(operands)),
            (groups, local_seqs, count, channels),
            [
                pltpu.VMEM((heads + 1, queries, residues), F32),
                pltpu.VMEM((local_seqs, queries, channels), BF16),
                pltpu.VMEM((local_seqs, residues, channels), BF16),
                pltpu.VMEM((local_seqs, residues, channels), BF16),
                pltpu.VMEM((local_seqs, queries, channels), F32),
                pltpu.VMEM((local_seqs, queries, channels), BF16),
                pltpu.VMEM((block * residues, channels), BF16),
                pltpu.VMEM((block * queries, channels), BF16),
                pltpu.VMEM((pair, heads * queries, channels), BF16),
                pltpu.VMEM((pair, heads * queries, residues), F32),
                pltpu.VMEM((pair, heads * queries, residues), BF16),
            ],
        )(gap, place, horizontal_scaling_factor[None, :], *operands)

    finals = [exchange(row_attention(c * part_res, part_res)) for c in range(res_parts)]
    done = []
    rows, per = total_seqs, LANES * heads // channels
    batch, pair = largest(part_res, 8), largest(part_res, 2)
    for c in range(res_parts):
        piece = finals[c].reshape(total_seqs, part_res, channels)
        if not turn:
            piece = jnp.swapaxes(piece, 0, 1)
        before = done if c == res_parts - 1 else []
        if not turn:
            shape = (part_res, total_seqs, channels)
        else:
            shape = (total_seqs, part_res * (1 + len(before)), channels)
        operands = (
            piece, column_input_weight, vertical_final_matrix,
            feedforward_widen_matrix, feedforward_shrink_matrix,
        )
        done.append(
            kernel_call(
                functools.partial(column_kernel, heads, turn, len(before)),
                "column_transition", 10, in_vmem(8 + len(before)), shape,
                [pltpu.VMEM((part_res, rows, channels), BF16)] * 4
                + [pltpu.VMEM((part_res, rows, channels), F32)]
                + [pltpu.VMEM((part_res, rows, channels), BF16)] * 2
                + [
                    pltpu.VMEM((batch * rows, channels), BF16),
                    pltpu.VMEM((pair, per * rows, channels), BF16),
                    pltpu.VMEM((pair, heads // per * rows, channels), BF16),
                    pltpu.VMEM((pair, heads // per * rows, channels), BF16),
                    pltpu.VMEM((pair, per * rows, heads // per * rows), F32),
                    pltpu.VMEM((pair, per * rows, heads // per * rows), BF16),
                ],
            )(
                col_gap, vertical_scaling_factor[None, :], feedforward_scaling_factor[None, :],
                *operands, *before,
            )
        )
    return done[-1] if turn else jnp.swapaxes(done[-1], 0, 1)


def solution(mesh):
    placed = (
        P("dp", "res", None),
        P(("dp", "res"), None, None),
        P("dp", None),
    ) + (P(),) * 11
    return jax.shard_map(
        body, mesh=mesh, in_specs=placed, out_specs=P("dp", "res", None), check_vma=False
    )
```

```python
import functools

import jax
import jax.numpy as jnp
from jax import lax
from jax.experimental import pallas as pl
from jax.experimental.pallas import tpu as pltpu
from jax.sharding import PartitionSpec as P

BLOCK = 128
EPSILON = 1e-05
MASKED_SCORE = -1000000000.0
LANES = 128
SLAB = 16
F32 = jnp.float32
BF16 = jnp.bfloat16
VMEM_BYTES = 44 * 1024 * 1024


def layer_normalize(values_f, scale_gain):
    centred = values_f - jnp.mean(values_f, axis=-1, keepdims=True)
    spread = jnp.mean(centred * centred, axis=-1, keepdims=True)
    return centred * lax.rsqrt(spread + EPSILON) * scale_gain


def mm(lhs, rhs):
    return jnp.dot(lhs, rhs, preferred_element_type=F32)


def mm_nt(lhs, rhs):
    return lax.dot_general(lhs, rhs, (((1,), (1,)), ((), ())), preferred_element_type=F32)


def swap_matrix(outer, inner):
    size = outer * inner
    to = lax.broadcasted_iota(jnp.int32, (size, size), 0)
    come = lax.broadcasted_iota(jnp.int32, (size, size), 1)
    source = lax.rem(to, outer) * inner + lax.div(to, outer)
    return jnp.where(come == source, 1.0, 0.0).astype(BF16)


def bias_kernel(gain_ref, weight_ref, pair_ref, out_ref):
    local_res, residues, channels = pair_ref.shape
    heads = out_ref.shape[0]
    step = min(SLAB, local_res)
    few = min(4, step)
    width = heads * step
    head_at = lax.broadcasted_iota(jnp.int32, (heads, width), 0)
    spread = jnp.where(lax.broadcasted_iota(jnp.int32, (heads, width), 1) // step == head_at, 1.0, 0.0)
    wide = mm(weight_ref[...], spread.astype(BF16))
    lane = lax.broadcasted_iota(jnp.int32, wide.shape, 1)
    weights = [jnp.where(lane % step == i, wide, 0.0).astype(BF16) for i in range(step)]
    for p in range(0, local_res, step):
        projected = None
        for i in range(0, step, few):
            x = pair_ref[p + i : p + i + few].reshape(few * residues, channels)
            normed = layer_normalize(x.astype(F32), gain_ref[...]).astype(BF16)
            left = [normed[j * residues : (j + 1) * residues] for j in range(few)]
            part = mm(jnp.concatenate(left, axis=1), jnp.concatenate(weights[i : i + few], axis=0))
            projected = part if projected is None else projected + part
        out_ref[:, p : p + step] = projected.T.reshape(heads, step, residues).astype(BF16)


def softmax_lanes(scores):
    e = jnp.exp(scores - jnp.max(scores, axis=-1, keepdims=True))
    total = jnp.sum(e, axis=-1, keepdims=True)
    inverse = pl.reciprocal(total, approx=True)
    inverse = inverse * (2.0 - total * inverse)
    return (e * inverse).astype(BF16)


def gate_of(values):
    return 0.5 * jnp.tanh(0.5 * values) + 0.5


def pick_heads(parts, depth):
    lane = lax.broadcasted_iota(jnp.int32, parts[0].shape, 1)
    slot = lane // depth % len(parts)
    picked = parts[-1]
    for j in range(len(parts) - 2, -1, -1):
        picked = jnp.where(slot == j, parts[j], picked)
    return picked


def lane_mask(width, depth, slots, j):
    lane = lax.broadcasted_iota(jnp.int32, (1, width), 1)
    return jnp.where(lane // depth % slots == j, 1.0, 0.0).astype(BF16)


def row_kernel(
    parts, blocks, gap_ref, place_ref, gain_ref, x_ref, win_ref, wout_ref, *refs
):
    bias_refs, refs = refs[:blocks], refs[blocks:]
    out_refs, refs = refs[:parts], refs[parts:]
    bias_scr, q_scr, k_scr, v_scr, gate_scr, gated_scr = refs
    groups, seqs, local_res, channels = x_ref.shape
    heads = bias_scr.shape[0] - 1
    residues = groups * local_res
    depth = channels // heads
    per = LANES // depth
    scale = depth ** (-0.5)
    batch = largest(seqs, 4)
    part_res = local_res // parts

    def some_x(i):
        x = [x_ref[:, pl.ds(i * batch + j, 1)].reshape(residues, channels) for j in range(batch)]
        return jnp.concatenate(x, axis=0).astype(F32)

    def dense(i, carry):
        normed = layer_normalize(some_x(i), gain_ref[...]).astype(BF16)
        q = (mm(normed, win_ref[:, :channels]) * scale).astype(BF16)
        k = mm(normed, win_ref[:, channels : 2 * channels]).astype(BF16)
        v = mm(normed, win_ref[:, 2 * channels : 3 * channels]).astype(BF16)
        gates = gate_of(mm(normed, win_ref[:, 3 * channels :]))
        shape = (batch, residues, channels)
        q_scr[pl.ds(i * batch, batch)] = q.reshape(shape)
        k_scr[pl.ds(i * batch, batch)] = k.reshape(shape)
        v_scr[pl.ds(i * batch, batch)] = v.reshape(shape)
        gate_scr[pl.ds(i * batch, batch)] = gates.reshape(shape)
        return carry

    lax.fori_loop(0, seqs // batch, dense, 0)

    for g in range(groups):
        if blocks == 1:
            block_of = bias_refs[0][g]
        else:
            lines = groups // 2
            slot = lax.rem(place_ref[0, 0] - g // 2 + lines, lines)
            block_of = jnp.where(
                place_ref[0, 1] == g % 2, bias_refs[0][slot], bias_refs[1][slot]
            )
        bias_scr[:heads, g * local_res : (g + 1) * local_res] = block_of.astype(F32)
    bias_scr[heads] = jnp.full((residues, residues), MASKED_SCORE, F32)
    masks = [lane_mask(LANES, depth, per, j) for j in range(per)]

    def attend(s, carry):
        gaps = [gap_ref[s, b] == 1 for b in range(residues // BLOCK)]
        attended = []
        for g in range(heads // per):
            lanes = slice(g * LANES, (g + 1) * LANES)
            q, k, v = q_scr[s, :, lanes], k_scr[s, :, lanes], v_scr[s, :, lanes]
            scores = mm_nt(jnp.concatenate([q * mask for mask in masks], axis=0), k)
            weights = []
            for j in range(per):
                bias = [
                    bias_scr[jnp.where(gap, heads, g * per + j), :, b * BLOCK : (b + 1) * BLOCK]
                    for b, gap in enumerate(gaps)
                ]
                own = scores[j * residues : (j + 1) * residues]
                weights.append(softmax_lanes(own + jnp.concatenate(bias, axis=1)))
            mixed = mm(jnp.concatenate(weights, axis=0), v)
            attended.append(
                pick_heads([mixed[j * residues : (j + 1) * residues] for j in range(per)], depth)
            )
        gated_scr[s] = (jnp.concatenate(attended, axis=1) * gate_scr[s]).astype(BF16)
        return carry

    lax.fori_loop(0, seqs, attend, 0)

    def finish(i, carry):
        gated = gated_scr[pl.ds(i * batch, batch)].reshape(batch * residues, channels)
        result = (some_x(i) + mm(gated, wout_ref[...])).astype(BF16)
        result = result.reshape(batch, groups, local_res, channels)
        for p, out_ref in enumerate(out_refs):
            for j in range(batch):
                out_ref[:, pl.ds(i * batch + j, 1)] = result[
                    j, :, p * part_res : (p + 1) * part_res
                ].reshape(groups, 1, part_res, channels)
        return carry

    lax.fori_loop(0, seqs // batch, finish, 0)


def column_kernel(
    heads, turn, lows, earlier, gap_ref, gain_ref, gain2_ref, win_ref, wout_ref,
    widen_ref, shrink_ref, *refs,
):
    pieces, refs = refs[: len(lows)], refs[len(lows) :]
    done_refs, refs = refs[:earlier], refs[earlier:]
    (out_ref, turned_scr, q_scr, k_scr, v_scr, gate_scr, gated_scr, done_scr) = refs
    local_res, seqs, channels = turned_scr.shape
    depth = channels // heads
    per = LANES // depth
    halves = heads // per
    scale = depth ** (-0.5)
    batch = largest(local_res, 8)
    pair = largest(local_res, 2)
    slabs = local_res // SLAB if turn else 0
    swap = swap_matrix(SLAB, SLAB)
    base = 0
    for done_ref in done_refs:
        out_ref[:, base : base + done_ref.shape[1]] = done_ref[...]
        base += done_ref.shape[1]
    if not turn:
        turned_scr[...] = pieces[0][...]
    for c in range(slabs):
        blocks = []
        for piece, low in zip(pieces, lows):
            start = low + c * SLAB
            for p in range(0, piece.shape[0], SLAB):
                block = piece[p : p + SLAB, start : start + SLAB]
                blocks.append(block.reshape(SLAB * SLAB, channels))
        turned = mm(swap, jnp.concatenate(blocks, axis=1)).astype(BF16)
        for g in range(seqs // SLAB):
            turned_scr[c * SLAB : (c + 1) * SLAB, g * SLAB : (g + 1) * SLAB] = turned[
                :, g * channels : (g + 1) * channels
            ].reshape(SLAB, SLAB, channels)

    def dense(i, carry):
        x = turned_scr[pl.ds(i * batch, batch)].reshape(batch * seqs, channels)
        normed = layer_normalize(x.astype(F32), gain_ref[...]).astype(BF16)
        q = (mm(normed, win_ref[:, :channels]) * scale).astype(BF16)
        k = mm(normed, win_ref[:, channels : 2 * channels]).astype(BF16)
        v = mm(normed, win_ref[:, 2 * channels : 3 * channels]).astype(BF16)
        gates = gate_of(mm(normed, win_ref[:, 3 * channels :]))
        shape = (batch, seqs, channels)
        q_scr[pl.ds(i * batch, batch)] = q.reshape(shape)
        k_scr[pl.ds(i * batch, batch)] = k.reshape(shape)
        v_scr[pl.ds(i * batch, batch)] = v.reshape(shape)
        gate_scr[pl.ds(i * batch, batch)] = gates.reshape(shape)
        return carry

    lax.fori_loop(0, local_res // batch, dense, 0)

    mask = jnp.where(gap_ref[...] == 1, MASKED_SCORE, 0.0)
    masks = [lane_mask(channels, depth, per, j) for j in range(per)]
    blank = jnp.zeros((seqs, LANES), BF16)

    def diagonal(values):
        rows = []
        for g in range(halves):
            own = values[:, g * LANES : (g + 1) * LANES]
            rows.append(jnp.concatenate([own if i == g else blank for i in range(halves)], axis=1))
        return jnp.concatenate(rows, axis=0)

    def attend(i, carry):
        at = [i * pair + u for u in range(pair)]
        entries = [(q_scr[r], k_scr[r], v_scr[r], gate_scr[r]) for r in at]
        results = []
        for q, k, v, gates in entries:
            scores = mm_nt(jnp.concatenate([q * m for m in masks], axis=0), diagonal(k))
            weights = [
                softmax_lanes(scores[:, g * seqs : (g + 1) * seqs] + mask) for g in range(halves)
            ]
            mixed = mm(jnp.concatenate(weights, axis=1), diagonal(v))
            attended = pick_heads([mixed[j * seqs : (j + 1) * seqs] for j in range(per)], depth)
            results.append((attended * gates).astype(BF16))
        for r, result in zip(at, results):
            gated_scr[r] = result
        return carry

    lax.fori_loop(0, local_res // pair, attend, 0)

    def finish(i, carry):
        x = turned_scr[pl.ds(i * batch, batch)].reshape(batch * seqs, channels)
        gated = gated_scr[pl.ds(i * batch, batch)].reshape(batch * seqs, channels)
        second = (x.astype(F32) + mm(gated, wout_ref[...])).astype(BF16)
        second_f = second.astype(F32)
        normed = layer_normalize(second_f, gain2_ref[...]).astype(BF16)
        hidden = jnp.maximum(mm(normed, widen_ref[...]), 0.0).astype(BF16)
        result = (second_f + mm(hidden, shrink_ref[...])).astype(BF16)
        done_scr[pl.ds(i * batch, batch)] = result.reshape(batch, seqs, channels)
        return carry

    lax.fori_loop(0, local_res // batch, finish, 0)
    if not turn:
        out_ref[...] = done_scr[...]
    for c in range(slabs):
        blocks = [
            done_scr[c * SLAB : (c + 1) * SLAB, g * SLAB : (g + 1) * SLAB].reshape(
                SLAB * SLAB, channels
            )
            for g in range(seqs // SLAB)
        ]
        turned = mm(swap, jnp.concatenate(blocks, axis=1)).astype(BF16)
        start = base + c * SLAB
        for g in range(seqs // SLAB):
            out_ref[g * SLAB : (g + 1) * SLAB, start : start + SLAB] = turned[
                :, g * channels : (g + 1) * channels
            ].reshape(SLAB, SLAB, channels)


def largest(total, bound):
    return max(d for d in range(1, bound + 1) if total % d == 0)


def in_vmem(count):
    return [pl.BlockSpec(memory_space=pltpu.VMEM)] * count


def shift_line(block, groups):
    line = [block]
    for k in range(2, groups, 2):
        line.append(lax.ppermute(block, "res", [(i, (i + k) % groups) for i in range(groups)]))
    return jnp.stack(line)


def body(
    aligned_chain_features,
    pair_representation_state,
    gap_block_flags,
    pair_norm_gain,
    pair_head_weight,
    horizontal_scaling_factor,
    row_input_weight,
    horizontal_final_matrix,
    vertical_scaling_factor,
    column_input_weight,
    vertical_final_matrix,
    feedforward_scaling_factor,
    feedforward_widen_matrix,
    feedforward_shrink_matrix,
):
    groups = lax.axis_size("res")
    total_seqs, local_res, channels = aligned_chain_features.shape
    residues = pair_representation_state.shape[1]
    heads = pair_head_weight.shape[1]
    local_seqs = total_seqs // groups
    turn = local_res % SLAB == 0
    seq_parts = 2 if turn and local_seqs % 2 == 0 else 1
    res_parts = local_res // SLAB if turn else 1
    part_seqs = local_seqs // seq_parts
    part_total = total_seqs // seq_parts
    part_res = local_res // res_parts
    here = lax.axis_index("res")

    def exchange(values):
        return lax.all_to_all(values, "res", split_axis=0, concat_axis=0, tiled=True)

    def kernel_call(kernel, name, micros, in_specs, out_shapes, scratch):
        return pl.pallas_call(
            kernel,
            out_shape=[jax.ShapeDtypeStruct(*shape) for shape in out_shapes],
            in_specs=in_specs,
            out_specs=in_vmem(len(out_shapes)),
            scratch_shapes=scratch,
            compiler_params=pltpu.CompilerParams(vmem_limit_bytes=VMEM_BYTES),
            cost_estimate=pl.CostEstimate(
                flops=int(micros * 1e9), bytes_accessed=1 << 20, transcendentals=0
            ),
            name=name,
        )

    halves = [
        aligned_chain_features[p * part_total : (p + 1) * part_total].reshape(
            groups, part_seqs, local_res, channels
        )
        for p in range(seq_parts)
    ]
    arrived = [exchange(halves[0])]
    (bias_local,) = kernel_call(
        bias_kernel, "pair_bias", 5, in_vmem(3), [((heads, local_res, residues), BF16)], [],
    )(pair_norm_gain[None, :], pair_head_weight, pair_representation_state)
    place = jnp.stack([here // 2, here % 2]).astype(jnp.int32)[None, :]
    if groups == 8:
        line = shift_line(bias_local, groups)
        line, *halves[1:] = lax.optimization_barrier((line, *halves[1:]))
        bias_blocks = (line, lax.ppermute(line, "res", [(i, i ^ 1) for i in range(groups)]))
    else:
        bias_blocks = (lax.all_gather(bias_local, "res", axis=0, tiled=False),)
    arrived += [exchange(half) for half in halves[1:]]

    column_block = (here * local_res) // BLOCK
    col_gap = lax.dynamic_slice_in_dim(gap_block_flags, column_block, 1, 1).reshape(1, total_seqs)

    def row_attention(part, parts):
        gap = lax.dynamic_slice_in_dim(
            gap_block_flags, part * part_total + here * part_seqs, part_seqs, 0
        )
        operands = (arrived[part], row_input_weight, horizontal_final_matrix, *bias_blocks)
        held = pltpu.VMEM((part_seqs, residues, channels), BF16)
        return kernel_call(
            functools.partial(row_kernel, parts, len(bias_blocks)), "row_attention", 10,
            [pl.BlockSpec(memory_space=pltpu.SMEM)] * 2 + in_vmem(1 + len(operands)),
            [((groups, part_seqs, local_res // parts, channels), BF16)] * parts,
            [
                pltpu.VMEM((heads + 1, residues, residues), F32),
                held, held, held,
                pltpu.VMEM((part_seqs, residues, channels), F32),
                held,
            ],
        )(gap, place, horizontal_scaling_factor[None, :], *operands)

    returned = []
    for p in range(seq_parts - 1):
        (first,) = row_attention(p, 1)
        returned.append(exchange(first).reshape(part_total, local_res, channels))
    finals = [exchange(first) for first in row_attention(seq_parts - 1, res_parts)]
    done = []
    for c in range(res_parts):
        pieces = returned + [finals[c].reshape(part_total, part_res, channels)]
        if not turn:
            pieces = [jnp.swapaxes(piece, 0, 1) for piece in pieces]
        lows = (c * part_res,) * len(returned) + (0,)
        before = done if c == res_parts - 1 else []
        if not turn:
            shape = (part_res, total_seqs, channels)
        else:
            shape = (total_seqs, part_res * (1 + len(before)), channels)
        held = pltpu.VMEM((part_res, total_seqs, channels), BF16)
        done += kernel_call(
            functools.partial(column_kernel, heads, turn, lows, len(before)),
            "column_transition", 10, in_vmem(7 + len(pieces) + len(before)), [(shape, BF16)],
            [
                held, held, held, held,
                pltpu.VMEM((part_res, total_seqs, channels), F32),
                held, held,
            ],
        )(
            col_gap, vertical_scaling_factor[None, :], feedforward_scaling_factor[None, :],
            column_input_weight, vertical_final_matrix, feedforward_widen_matrix,
            feedforward_shrink_matrix, *pieces, *before,
        )
    return done[-1] if turn else jnp.swapaxes(done[-1], 0, 1)


def solution(mesh):
    placed = (
        P("dp", "res", None),
        P(("dp", "res"), None, None),
        P("dp", None),
    ) + (P(),) * 11
    return jax.shard_map(
        body, mesh=mesh, in_specs=placed, out_specs=P("dp", "res", None), check_vma=False
    )
```

```python
import functools

import jax
import jax.numpy as jnp
from jax import lax
from jax.experimental import pallas as pl
from jax.experimental.pallas import tpu as pltpu
from jax.sharding import PartitionSpec as P

BLOCK = 128
EPSILON = 1e-05
MASKED_SCORE = -1000000000.0
LANES = 128
SLAB = 16
F32 = jnp.float32
BF16 = jnp.bfloat16
VMEM_BYTES = 28 * 1024 * 1024


def layer_normalize(values_f, scale_gain):
    centred = values_f - jnp.mean(values_f, axis=-1, keepdims=True)
    spread = jnp.mean(centred * centred, axis=-1, keepdims=True)
    return centred * lax.rsqrt(spread + EPSILON) * scale_gain


def mm(lhs, rhs):
    return jnp.dot(lhs, rhs, preferred_element_type=F32)


def mm_nt(lhs, rhs):
    return lax.dot_general(lhs, rhs, (((1,), (1,)), ((), ())), preferred_element_type=F32)


def swap_matrix(outer, inner):
    size = outer * inner
    to = lax.broadcasted_iota(jnp.int32, (size, size), 0)
    come = lax.broadcasted_iota(jnp.int32, (size, size), 1)
    source = lax.rem(to, outer) * inner + lax.div(to, outer)
    return jnp.where(come == source, 1.0, 0.0).astype(BF16)


def bias_kernel(gain_ref, weight_ref, pair_ref, out_ref):
    local_res, residues, channels = pair_ref.shape
    heads = out_ref.shape[0]
    step = min(SLAB, local_res)
    few = min(4, step)
    width = heads * step
    head_at = lax.broadcasted_iota(jnp.int32, (heads, width), 0)
    spread = jnp.where(lax.broadcasted_iota(jnp.int32, (heads, width), 1) // step == head_at, 1.0, 0.0)
    wide = mm(weight_ref[...], spread.astype(BF16))
    lane = lax.broadcasted_iota(jnp.int32, wide.shape, 1)
    weights = [jnp.where(lane % step == i, wide, 0.0).astype(BF16) for i in range(step)]
    for p in range(0, local_res, step):
        projected = None
        for i in range(0, step, few):
            x = pair_ref[p + i : p + i + few].reshape(few * residues, channels)
            normed = layer_normalize(x.astype(F32), gain_ref[...]).astype(BF16)
            left = [normed[j * residues : (j + 1) * residues] for j in range(few)]
            part = mm(jnp.concatenate(left, axis=1), jnp.concatenate(weights[i : i + few], axis=0))
            projected = part if projected is None else projected + part
        out_ref[:, p : p + step] = projected.T.reshape(heads, step, residues).astype(BF16)


def softmax_lanes(scores):
    e = jnp.exp(scores - jnp.max(scores, axis=-1, keepdims=True))
    total = jnp.sum(e, axis=-1, keepdims=True)
    inverse = pl.reciprocal(total, approx=True)
    inverse = inverse * (2.0 - total * inverse)
    return (e * inverse).astype(BF16)


def gate_of(values):
    return 0.5 * jnp.tanh(0.5 * values) + 0.5


def pick_heads(parts, depth):
    lane = lax.broadcasted_iota(jnp.int32, parts[0].shape, 1)
    slot = lane // depth % len(parts)
    picked = parts[-1]
    for j in range(len(parts) - 2, -1, -1):
        picked = jnp.where(slot == j, parts[j], picked)
    return picked


def lane_mask(width, depth, slots, j):
    lane = lax.broadcasted_iota(jnp.int32, (1, width), 1)
    return jnp.where(lane // depth % slots == j, 1.0, 0.0).astype(BF16)


def project_kernel(heads, gain_ref, x_ref, win_ref, q_ref, k_ref, v_ref, gate_ref):
    groups, seqs, local_res, channels = x_ref.shape
    scale = (channels // heads) ** (-0.5)
    batch = largest(seqs, 4)

    def dense(i, carry):
        x = [x_ref[:, pl.ds(i * batch + j, 1)].reshape(-1, channels) for j in range(batch)]
        x = jnp.concatenate(x, axis=0).astype(F32)
        normed = layer_normalize(x, gain_ref[...]).astype(BF16)
        some = pl.ds(i * batch, batch)
        q = (mm(normed, win_ref[:, :channels]) * scale).astype(BF16)
        q_ref[some] = q.reshape(batch, groups, local_res, channels)
        k = mm(normed, win_ref[:, channels : 2 * channels]).astype(BF16)
        k_ref[some] = k.reshape(batch, groups * local_res, channels)
        v = mm(normed, win_ref[:, 2 * channels : 3 * channels]).astype(BF16)
        v_ref[some] = v.reshape(batch, groups * local_res, channels)
        gates = gate_of(mm(normed, win_ref[:, 3 * channels :]))
        gate_ref[some] = gates.reshape(batch, groups, local_res, channels)
        return carry

    lax.fori_loop(0, seqs // batch, dense, 0)


def row_kernel(
    low, count, gap_ref, place_ref, x_ref, q_ref, k_ref, v_ref, gate_ref, wout_ref, *refs
):
    bias_refs, (out_ref, bias_scr, gated_scr) = refs[:-3], refs[-3:]
    groups, seqs, local_res, channels = x_ref.shape
    heads = bias_scr.shape[0] - 1
    residues = groups * local_res
    queries = groups * count
    depth = channels // heads
    per = LANES // depth
    batch = largest(seqs, 8)

    for g in range(groups):
        if len(bias_refs) > 1:
            shift = lax.rem(place_ref[0] - g + groups, groups)
            block_of = bias_refs[0][:, low : low + count]
            for k in range(1, groups):
                block_of = jnp.where(shift == k, bias_refs[k][:, low : low + count], block_of)
        else:
            block_of = bias_refs[0][g, :, low : low + count]
        bias_scr[:heads, g * count : (g + 1) * count] = block_of.astype(F32)
    bias_scr[heads] = jnp.full((queries, residues), MASKED_SCORE, F32)
    masks = [lane_mask(LANES, depth, per, j) for j in range(per)]

    def attend(s, carry):
        gaps = [gap_ref[s, b] == 1 for b in range(residues // BLOCK)]
        attended = []
        for g in range(heads // per):
            lanes = slice(g * LANES, (g + 1) * LANES)
            q = q_ref[s, :, low : low + count, lanes].reshape(queries, LANES)
            k, v = k_ref[s, :, lanes], v_ref[s, :, lanes]
            scores = mm_nt(jnp.concatenate([q * mask for mask in masks], axis=0), k)
            weights = []
            for j in range(per):
                bias = [
                    bias_scr[jnp.where(gap, heads, g * per + j), :, b * BLOCK : (b + 1) * BLOCK]
                    for b, gap in enumerate(gaps)
                ]
                own = scores[j * queries : (j + 1) * queries]
                weights.append(softmax_lanes(own + jnp.concatenate(bias, axis=1)))
            mixed = mm(jnp.concatenate(weights, axis=0), v)
            attended.append(
                pick_heads([mixed[j * queries : (j + 1) * queries] for j in range(per)], depth)
            )
        gates = gate_ref[s, :, low : low + count].reshape(queries, channels)
        gated_scr[s] = (jnp.concatenate(attended, axis=1) * gates).astype(BF16)
        return carry

    lax.fori_loop(0, seqs, attend, 0)

    def finish(i, carry):
        some = pl.ds(i * batch, batch)
        gated = gated_scr[some].reshape(batch * queries, channels)
        update = mm(gated, wout_ref[...])
        for j in range(batch):
            s = i * batch + j
            x = x_ref[:, pl.ds(s, 1), low : low + count].reshape(queries, channels)
            result = x.astype(F32) + update[j * queries : (j + 1) * queries]
            out_ref[:, pl.ds(s, 1)] = result.astype(BF16).reshape(groups, 1, count, channels)
        return carry

    lax.fori_loop(0, seqs // batch, finish, 0)


def column_kernel(
    heads, turn, lows, earlier, gap_ref, gain_ref, gain2_ref, win_ref, wout_ref,
    widen_ref, shrink_ref, *refs,
):
    pieces, refs = refs[: len(lows)], refs[len(lows) :]
    done_refs, refs = refs[:earlier], refs[earlier:]
    (out_ref, turned_scr, q_scr, k_scr, v_scr, gate_scr, gated_scr, done_scr) = refs
    local_res, seqs, channels = turned_scr.shape
    depth = channels // heads
    per = LANES // depth
    halves = heads // per
    scale = depth ** (-0.5)
    batch = largest(local_res, 8)
    pair = largest(local_res, 2)
    slabs = local_res // SLAB if turn else 0
    swap = swap_matrix(SLAB, SLAB)
    base = 0
    for done_ref in done_refs:
        out_ref[:, base : base + done_ref.shape[1]] = done_ref[...]
        base += done_ref.shape[1]
    if not turn:
        turned_scr[...] = pieces[0][...]
    for c in range(slabs):
        blocks = []
        for piece, low in zip(pieces, lows):
            start = low + c * SLAB
            for p in range(0, piece.shape[0], SLAB):
                block = piece[p : p + SLAB, start : start + SLAB]
                blocks.append(block.reshape(SLAB * SLAB, channels))
        turned = mm(swap, jnp.concatenate(blocks, axis=1)).astype(BF16)
        for g in range(seqs // SLAB):
            turned_scr[c * SLAB : (c + 1) * SLAB, g * SLAB : (g + 1) * SLAB] = turned[
                :, g * channels : (g + 1) * channels
            ].reshape(SLAB, SLAB, channels)

    def dense(i, carry):
        x = turned_scr[pl.ds(i * batch, batch)].reshape(batch * seqs, channels)
        normed = layer_normalize(x.astype(F32), gain_ref[...]).astype(BF16)
        q = (mm(normed, win_ref[:, :channels]) * scale).astype(BF16)
        k = mm(normed, win_ref[:, channels : 2 * channels]).astype(BF16)
        v = mm(normed, win_ref[:, 2 * channels : 3 * channels]).astype(BF16)
        gates = gate_of(mm(normed, win_ref[:, 3 * channels :]))
        shape = (batch, seqs, channels)
        q_scr[pl.ds(i * batch, batch)] = q.reshape(shape)
        k_scr[pl.ds(i * batch, batch)] = k.reshape(shape)
        v_scr[pl.ds(i * batch, batch)] = v.reshape(shape)
        gate_scr[pl.ds(i * batch, batch)] = gates.reshape(shape)
        return carry

    lax.fori_loop(0, local_res // batch, dense, 0)

    mask = jnp.where(gap_ref[...] == 1, MASKED_SCORE, 0.0)
    masks = [lane_mask(channels, depth, per, j) for j in range(per)]
    blank = jnp.zeros((seqs, LANES), BF16)

    def diagonal(values):
        rows = []
        for g in range(halves):
            own = values[:, g * LANES : (g + 1) * LANES]
            rows.append(jnp.concatenate([own if i == g else blank for i in range(halves)], axis=1))
        return jnp.concatenate(rows, axis=0)

    def attend(i, carry):
        at = [i * pair + u for u in range(pair)]
        entries = [(q_scr[r], k_scr[r], v_scr[r], gate_scr[r]) for r in at]
        results = []
        for q, k, v, gates in entries:
            scores = mm_nt(jnp.concatenate([q * m for m in masks], axis=0), diagonal(k))
            weights = [
                softmax_lanes(scores[:, g * seqs : (g + 1) * seqs] + mask) for g in range(halves)
            ]
            mixed = mm(jnp.concatenate(weights, axis=1), diagonal(v))
            attended = pick_heads([mixed[j * seqs : (j + 1) * seqs] for j in range(per)], depth)
            results.append((attended * gates).astype(BF16))
        for r, result in zip(at, results):
            gated_scr[r] = result
        return carry

    lax.fori_loop(0, local_res // pair, attend, 0)

    def finish(i, carry):
        x = turned_scr[pl.ds(i * batch, batch)].reshape(batch * seqs, channels)
        gated = gated_scr[pl.ds(i * batch, batch)].reshape(batch * seqs, channels)
        second = (x.astype(F32) + mm(gated, wout_ref[...])).astype(BF16)
        second_f = second.astype(F32)
        normed = layer_normalize(second_f, gain2_ref[...]).astype(BF16)
        hidden = jnp.maximum(mm(normed, widen_ref[...]), 0.0).astype(BF16)
        result = (second_f + mm(hidden, shrink_ref[...])).astype(BF16)
        done_scr[pl.ds(i * batch, batch)] = result.reshape(batch, seqs, channels)
        return carry

    lax.fori_loop(0, local_res // batch, finish, 0)
    if not turn:
        out_ref[...] = done_scr[...]
    for c in range(slabs):
        blocks = [
            done_scr[c * SLAB : (c + 1) * SLAB, g * SLAB : (g + 1) * SLAB].reshape(
                SLAB * SLAB, channels
            )
            for g in range(seqs // SLAB)
        ]
        turned = mm(swap, jnp.concatenate(blocks, axis=1)).astype(BF16)
        start = base + c * SLAB
        for g in range(seqs // SLAB):
            out_ref[g * SLAB : (g + 1) * SLAB, start : start + SLAB] = turned[
                :, g * channels : (g + 1) * channels
            ].reshape(SLAB, SLAB, channels)


def largest(total, bound):
    return max(d for d in range(1, bound + 1) if total % d == 0)


def in_vmem(count):
    return [pl.BlockSpec(memory_space=pltpu.VMEM)] * count


def gather_bias(block, groups):
    if groups != 8:
        return (lax.all_gather(block, "res", axis=0, tiled=False),)
    return (block,) + tuple(
        lax.ppermute(block, "res", [(i, (i + k) % groups) for i in range(groups)])
        for k in range(1, groups)
    )


def body(
    aligned_chain_features,
    pair_representation_state,
    gap_block_flags,
    pair_norm_gain,
    pair_head_weight,
    horizontal_scaling_factor,
    row_input_weight,
    horizontal_final_matrix,
    vertical_scaling_factor,
    column_input_weight,
    vertical_final_matrix,
    feedforward_scaling_factor,
    feedforward_widen_matrix,
    feedforward_shrink_matrix,
):
    groups = lax.axis_size("res")
    total_seqs, local_res, channels = aligned_chain_features.shape
    residues = pair_representation_state.shape[1]
    heads = pair_head_weight.shape[1]
    local_seqs = total_seqs // groups
    turn = local_res % SLAB == 0
    res_parts = local_res // SLAB if turn else 1
    part_res = local_res // res_parts
    here = lax.axis_index("res")

    def exchange(values):
        return lax.all_to_all(values, "res", split_axis=0, concat_axis=0, tiled=True)

    def kernel_call(kernel, name, micros, in_specs, out_shapes, scratch):
        return pl.pallas_call(
            kernel,
            out_shape=[jax.ShapeDtypeStruct(*shape) for shape in out_shapes],
            in_specs=in_specs,
            out_specs=in_vmem(len(out_shapes)),
            scratch_shapes=scratch,
            compiler_params=pltpu.CompilerParams(vmem_limit_bytes=VMEM_BYTES),
            cost_estimate=pl.CostEstimate(
                flops=int(micros * 1e9), bytes_accessed=1 << 20, transcendentals=0
            ),
            name=name,
        )

    arrived = exchange(
        aligned_chain_features.reshape(groups, local_seqs, local_res, channels)
    )
    (bias_local,) = kernel_call(
        bias_kernel, "pair_bias", 5, in_vmem(3), [((heads, local_res, residues), BF16)], [],
    )(pair_norm_gain[None, :], pair_head_weight, pair_representation_state)
    bias_local, arrived = lax.optimization_barrier((bias_local, arrived))
    bias_blocks = gather_bias(bias_local, groups)

    column_block = (here * local_res) // BLOCK
    col_gap = lax.dynamic_slice_in_dim(gap_block_flags, column_block, 1, 1).reshape(1, total_seqs)

    gap = lax.dynamic_slice_in_dim(gap_block_flags, here * local_seqs, local_seqs, 0)
    by_group = (local_seqs, groups, local_res, channels)
    by_row = (local_seqs, residues, channels)
    projected = kernel_call(
        functools.partial(project_kernel, heads), "row_project", 10, in_vmem(3),
        [(by_group, BF16), (by_row, BF16), (by_row, BF16), (by_group, F32)], [],
    )(horizontal_scaling_factor[None, :], arrived, row_input_weight)

    def row_attention(low, count):
        queries = groups * count
        operands = (arrived, *projected, horizontal_final_matrix, *bias_blocks)
        (first,) = kernel_call(
            functools.partial(row_kernel, low, count), "row_attention", 10,
            [pl.BlockSpec(memory_space=pltpu.SMEM)] * 2 + in_vmem(len(operands)),
            [((groups, local_seqs, count, channels), BF16)],
            [
                pltpu.VMEM((heads + 1, queries, residues), F32),
                pltpu.VMEM((local_seqs, queries, channels), BF16),
            ],
        )(gap, here.astype(jnp.int32)[None], *operands)
        return first

    finals = [exchange(row_attention(c * part_res, part_res)) for c in range(res_parts)]
    done = []
    for c in range(res_parts):
        pieces = [finals[c].reshape(total_seqs, part_res, channels)]
        if not turn:
            pieces = [jnp.swapaxes(piece, 0, 1) for piece in pieces]
        lows = (0,)
        before = done if c == res_parts - 1 else []
        if not turn:
            shape = (part_res, total_seqs, channels)
        else:
            shape = (total_seqs, part_res * (1 + len(before)), channels)
        held = pltpu.VMEM((part_res, total_seqs, channels), BF16)
        done += kernel_call(
            functools.partial(column_kernel, heads, turn, lows, len(before)),
            "column_transition", 10, in_vmem(7 + len(pieces) + len(before)), [(shape, BF16)],
            [
                held, held, held, held,
                pltpu.VMEM((part_res, total_seqs, channels), F32),
                held, held,
            ],
        )(
            col_gap, vertical_scaling_factor[None, :], feedforward_scaling_factor[None, :],
            column_input_weight, vertical_final_matrix, feedforward_widen_matrix,
            feedforward_shrink_matrix, *pieces, *before,
        )
    return done[-1] if turn else jnp.swapaxes(done[-1], 0, 1)


def solution(mesh):
    placed = (
        P("dp", "res", None),
        P(("dp", "res"), None, None),
        P("dp", None),
    ) + (P(),) * 11
    return jax.shard_map(
        body, mesh=mesh, in_specs=placed, out_specs=P("dp", "res", None), check_vma=False
    )
```

```python
import functools

import jax
import jax.numpy as jnp
from jax import lax
from jax.experimental import pallas as pl
from jax.experimental.pallas import tpu as pltpu
from jax.sharding import PartitionSpec as P

BLOCK = 128
EPSILON = 1e-05
MASKED_SCORE = -1000000000.0
LANES = 128
SLAB = 16
F32 = jnp.float32
BF16 = jnp.bfloat16
VMEM_BYTES = 28 * 1024 * 1024


def layer_normalize(values_f, scale_gain):
    centred = values_f - jnp.mean(values_f, axis=-1, keepdims=True)
    spread = jnp.mean(centred * centred, axis=-1, keepdims=True)
    return centred * lax.rsqrt(spread + EPSILON) * scale_gain


def mm(lhs, rhs):
    return jnp.dot(lhs, rhs, preferred_element_type=F32)


def mm_nt(lhs, rhs):
    return lax.dot_general(lhs, rhs, (((1,), (1,)), ((), ())), preferred_element_type=F32)


def swap_matrix(outer, inner):
    size = outer * inner
    to = lax.broadcasted_iota(jnp.int32, (size, size), 0)
    come = lax.broadcasted_iota(jnp.int32, (size, size), 1)
    source = lax.rem(to, outer) * inner + lax.div(to, outer)
    return jnp.where(come == source, 1.0, 0.0).astype(BF16)


def bias_kernel(gain_ref, weight_ref, pair_ref, out_ref):
    local_res, residues, channels = pair_ref.shape
    heads = out_ref.shape[0]
    step = min(SLAB, local_res)
    few = min(4, step)
    width = heads * step
    head_at = lax.broadcasted_iota(jnp.int32, (heads, width), 0)
    spread = jnp.where(lax.broadcasted_iota(jnp.int32, (heads, width), 1) // step == head_at, 1.0, 0.0)
    wide = mm(weight_ref[...], spread.astype(BF16))
    lane = lax.broadcasted_iota(jnp.int32, wide.shape, 1)
    weights = [jnp.where(lane % step == i, wide, 0.0).astype(BF16) for i in range(step)]
    for p in range(0, local_res, step):
        projected = None
        for i in range(0, step, few):
            x = pair_ref[p + i : p + i + few].reshape(few * residues, channels)
            normed = layer_normalize(x.astype(F32), gain_ref[...]).astype(BF16)
            left = [normed[j * residues : (j + 1) * residues] for j in range(few)]
            part = mm(jnp.concatenate(left, axis=1), jnp.concatenate(weights[i : i + few], axis=0))
            projected = part if projected is None else projected + part
        out_ref[:, p : p + step] = projected.T.reshape(heads, step, residues).astype(BF16)


def softmax_lanes(scores):
    e = jnp.exp(scores - jnp.max(scores, axis=-1, keepdims=True))
    total = jnp.sum(e, axis=-1, keepdims=True)
    inverse = pl.reciprocal(total, approx=True)
    inverse = inverse * (2.0 - total * inverse)
    return (e * inverse).astype(BF16)


def gate_of(values):
    return 0.5 * jnp.tanh(0.5 * values) + 0.5


def pick_heads(parts, depth):
    lane = lax.broadcasted_iota(jnp.int32, parts[0].shape, 1)
    slot = lane // depth % len(parts)
    picked = parts[-1]
    for j in range(len(parts) - 2, -1, -1):
        picked = jnp.where(slot == j, parts[j], picked)
    return picked


def lane_mask(width, depth, slots, j):
    lane = lax.broadcasted_iota(jnp.int32, (1, width), 1)
    return jnp.where(lane // depth % slots == j, 1.0, 0.0).astype(BF16)


def project_kernel(heads, gain_ref, x_ref, win_ref, q_ref, k_ref, v_ref, gate_ref):
    groups, seqs, local_res, channels = x_ref.shape
    scale = (channels // heads) ** (-0.5)
    batch = largest(seqs, 4)

    def dense(i, carry):
        x = [x_ref[:, pl.ds(i * batch + j, 1)].reshape(-1, channels) for j in range(batch)]
        x = jnp.concatenate(x, axis=0).astype(F32)
        normed = layer_normalize(x, gain_ref[...]).astype(BF16)
        some = pl.ds(i * batch, batch)
        q = (mm(normed, win_ref[:, :channels]) * scale).astype(BF16)
        q_ref[some] = q.reshape(batch, groups * local_res, channels)
        k = mm(normed, win_ref[:, channels : 2 * channels]).astype(BF16)
        k_ref[some] = k.reshape(batch, groups * local_res, channels)
        v = mm(normed, win_ref[:, 2 * channels : 3 * channels]).astype(BF16)
        v_ref[some] = v.reshape(batch, groups * local_res, channels)
        gates = gate_of(mm(normed, win_ref[:, 3 * channels :]))
        gate_ref[some] = gates.reshape(batch, groups * local_res, channels)
        return carry

    lax.fori_loop(0, seqs // batch, dense, 0)


def in_turn(tasks, scores_of, weights_of, mixed_of):
    results, scores = [], scores_of(tasks[0])
    for at, task in enumerate(tasks):
        ahead = scores_of(tasks[at + 1]) if at + 1 < len(tasks) else None
        results.append(mixed_of(task, weights_of(task, scores)))
        scores = ahead
    return results


def row_kernel(
    parts, gap_ref, place_ref, x_ref, q_ref, k_ref, v_ref, gate_ref, wout_ref, *refs
):
    refs, (bias_scr, gated_scr) = refs[:-2], refs[-2:]
    bias_refs, out_refs = refs[:-parts], refs[-parts:]
    groups, seqs, local_res, channels = x_ref.shape
    heads = bias_scr.shape[0] - 1
    residues = groups * local_res
    depth = channels // heads
    per = LANES // depth
    batch = largest(seqs, 4)
    part_res = local_res // parts

    for g in range(groups):
        if len(bias_refs) == 1:
            block_of = bias_refs[0][g]
        else:
            lines = groups // 2
            slot = lax.rem(place_ref[0, 0] - g // 2 + lines, lines)
            block_of = jnp.where(
                place_ref[0, 1] == g % 2, bias_refs[0][slot], bias_refs[1][slot]
            )
        bias_scr[:heads, g * local_res : (g + 1) * local_res] = block_of.astype(F32)
    bias_scr[heads] = jnp.full((residues, residues), MASKED_SCORE, F32)
    masks = [lane_mask(LANES, depth, per, j) for j in range(per)]

    def attend(i, carry):
        tasks = [(u, g) for u in range(batch) for g in range(heads // per)]
        at = [i * batch + u for u in range(batch)]
        gaps = [[gap_ref[s, b] == 1 for b in range(residues // BLOCK)] for s in at]
        gates = [gate_ref[s] for s in at]

        def lanes(ref, task):
            return ref[at[task[0]], :, task[1] * LANES : (task[1] + 1) * LANES]

        def scores_of(task):
            q = lanes(q_ref, task)
            return mm_nt(
                jnp.concatenate([q * mask for mask in masks], axis=0), lanes(k_ref, task)
            )

        def weights_of(task, scores):
            weights = []
            for j in range(per):
                bias = [
                    bias_scr[
                        jnp.where(gap, heads, task[1] * per + j), :, b * BLOCK : (b + 1) * BLOCK
                    ]
                    for b, gap in enumerate(gaps[task[0]])
                ]
                own = scores[j * residues : (j + 1) * residues]
                weights.append(softmax_lanes(own + jnp.concatenate(bias, axis=1)))
            return jnp.concatenate(weights, axis=0)

        def mixed_of(task, weights):
            mixed = mm(weights, lanes(v_ref, task))
            return pick_heads([mixed[j * residues : (j + 1) * residues] for j in range(per)], depth)

        attended = in_turn(tasks, scores_of, weights_of, mixed_of)
        halves = heads // per
        for u in range(batch):
            whole = jnp.concatenate(attended[u * halves : (u + 1) * halves], axis=1)
            gated_scr[at[u]] = (whole * gates[u]).astype(BF16)
        return carry

    lax.fori_loop(0, seqs // batch, attend, 0)

    def finish(i, carry):
        x = [x_ref[:, pl.ds(i * batch + j, 1)].reshape(residues, channels) for j in range(batch)]
        gated = gated_scr[pl.ds(i * batch, batch)].reshape(batch * residues, channels)
        result = jnp.concatenate(x, axis=0).astype(F32) + mm(gated, wout_ref[...])
        result = result.astype(BF16).reshape(batch, groups, local_res, channels)
        for p, out_ref in enumerate(out_refs):
            for j in range(batch):
                out_ref[:, pl.ds(i * batch + j, 1)] = result[
                    j, :, p * part_res : (p + 1) * part_res
                ].reshape(groups, 1, part_res, channels)
        return carry

    lax.fori_loop(0, seqs // batch, finish, 0)


def column_kernel(
    heads, turn, lows, earlier, gap_ref, gain_ref, gain2_ref, win_ref, wout_ref,
    widen_ref, shrink_ref, *refs,
):
    pieces, refs = refs[: len(lows)], refs[len(lows) :]
    done_refs, refs = refs[:earlier], refs[earlier:]
    (out_ref, turned_scr, q_scr, k_scr, v_scr, gate_scr, gated_scr, done_scr) = refs
    local_res, seqs, channels = turned_scr.shape
    depth = channels // heads
    per = LANES // depth
    halves = heads // per
    scale = depth ** (-0.5)
    batch = largest(local_res, 8)
    pair = largest(local_res, 4)
    slabs = local_res // SLAB if turn else 0
    swap = swap_matrix(SLAB, SLAB)
    base = 0
    for done_ref in done_refs:
        out_ref[:, base : base + done_ref.shape[1]] = done_ref[...]
        base += done_ref.shape[1]
    if not turn:
        turned_scr[...] = pieces[0][...]
    for c in range(slabs):
        blocks = []
        for piece, low in zip(pieces, lows):
            start = low + c * SLAB
            for p in range(0, piece.shape[0], SLAB):
                block = piece[p : p + SLAB, start : start + SLAB]
                blocks.append(block.reshape(SLAB * SLAB, channels))
        turned = mm(swap, jnp.concatenate(blocks, axis=1)).astype(BF16)
        for g in range(seqs // SLAB):
            turned_scr[c * SLAB : (c + 1) * SLAB, g * SLAB : (g + 1) * SLAB] = turned[
                :, g * channels : (g + 1) * channels
            ].reshape(SLAB, SLAB, channels)

    def dense(i, carry):
        x = turned_scr[pl.ds(i * batch, batch)].reshape(batch * seqs, channels)
        normed = layer_normalize(x.astype(F32), gain_ref[...]).astype(BF16)
        q = (mm(normed, win_ref[:, :channels]) * scale).astype(BF16)
        k = mm(normed, win_ref[:, channels : 2 * channels]).astype(BF16)
        v = mm(normed, win_ref[:, 2 * channels : 3 * channels]).astype(BF16)
        gates = gate_of(mm(normed, win_ref[:, 3 * channels :]))
        shape = (batch, seqs, channels)
        q_scr[pl.ds(i * batch, batch)] = q.reshape(shape)
        k_scr[pl.ds(i * batch, batch)] = k.reshape(shape)
        v_scr[pl.ds(i * batch, batch)] = v.reshape(shape)
        gate_scr[pl.ds(i * batch, batch)] = gates.reshape(shape)
        return carry

    lax.fori_loop(0, local_res // batch, dense, 0)

    mask = jnp.where(gap_ref[...] == 1, MASKED_SCORE, 0.0)
    masks = [lane_mask(channels, depth, per, j) for j in range(per)]
    blank = jnp.zeros((seqs, LANES), BF16)

    def diagonal(values):
        rows = []
        for g in range(halves):
            own = values[:, g * LANES : (g + 1) * LANES]
            rows.append(jnp.concatenate([own if i == g else blank for i in range(halves)], axis=1))
        return jnp.concatenate(rows, axis=0)

    def attend(i, carry):
        at = [i * pair + u for u in range(pair)]
        gates = [gate_scr[r] for r in at]

        def scores_of(u):
            q = q_scr[at[u]]
            return mm_nt(jnp.concatenate([q * m for m in masks], axis=0), diagonal(k_scr[at[u]]))

        def weights_of(u, scores):
            weights = [
                softmax_lanes(scores[:, g * seqs : (g + 1) * seqs] + mask) for g in range(halves)
            ]
            return jnp.concatenate(weights, axis=1)

        def mixed_of(u, weights):
            mixed = mm(weights, diagonal(v_scr[at[u]]))
            return pick_heads([mixed[j * seqs : (j + 1) * seqs] for j in range(per)], depth)

        attended = in_turn(list(range(pair)), scores_of, weights_of, mixed_of)
        for u in range(pair):
            gated_scr[at[u]] = (attended[u] * gates[u]).astype(BF16)
        return carry

    lax.fori_loop(0, local_res // pair, attend, 0)

    def finish(i, carry):
        x = turned_scr[pl.ds(i * batch, batch)].reshape(batch * seqs, channels)
        gated = gated_scr[pl.ds(i * batch, batch)].reshape(batch * seqs, channels)
        second = (x.astype(F32) + mm(gated, wout_ref[...])).astype(BF16)
        second_f = second.astype(F32)
        normed = layer_normalize(second_f, gain2_ref[...]).astype(BF16)
        hidden = jnp.maximum(mm(normed, widen_ref[...]), 0.0).astype(BF16)
        result = (second_f + mm(hidden, shrink_ref[...])).astype(BF16)
        done_scr[pl.ds(i * batch, batch)] = result.reshape(batch, seqs, channels)
        return carry

    lax.fori_loop(0, local_res // batch, finish, 0)
    if not turn:
        out_ref[...] = done_scr[...]
    for c in range(slabs):
        blocks = [
            done_scr[c * SLAB : (c + 1) * SLAB, g * SLAB : (g + 1) * SLAB].reshape(
                SLAB * SLAB, channels
            )
            for g in range(seqs // SLAB)
        ]
        turned = mm(swap, jnp.concatenate(blocks, axis=1)).astype(BF16)
        start = base + c * SLAB
        for g in range(seqs // SLAB):
            out_ref[g * SLAB : (g + 1) * SLAB, start : start + SLAB] = turned[
                :, g * channels : (g + 1) * channels
            ].reshape(SLAB, SLAB, channels)


def largest(total, bound):
    return max(d for d in range(1, bound + 1) if total % d == 0)


def in_vmem(count):
    return [pl.BlockSpec(memory_space=pltpu.VMEM)] * count


def shift_line(block, groups):
    return [
        lax.ppermute(block, "res", [(i, (i + k) % groups) for i in range(groups)])
        for k in range(2, groups, 2)
    ]


def body(
    aligned_chain_features,
    pair_representation_state,
    gap_block_flags,
    pair_norm_gain,
    pair_head_weight,
    horizontal_scaling_factor,
    row_input_weight,
    horizontal_final_matrix,
    vertical_scaling_factor,
    column_input_weight,
    vertical_final_matrix,
    feedforward_scaling_factor,
    feedforward_widen_matrix,
    feedforward_shrink_matrix,
):
    groups = lax.axis_size("res")
    total_seqs, local_res, channels = aligned_chain_features.shape
    residues = pair_representation_state.shape[1]
    heads = pair_head_weight.shape[1]
    local_seqs = total_seqs // groups
    turn = local_res % SLAB == 0
    res_parts = local_res // SLAB if turn else 1
    part_res = local_res // res_parts
    here = lax.axis_index("res")

    def exchange(values):
        return lax.all_to_all(values, "res", split_axis=0, concat_axis=0, tiled=True)

    def kernel_call(kernel, name, micros, in_specs, out_shapes, scratch):
        return pl.pallas_call(
            kernel,
            out_shape=[jax.ShapeDtypeStruct(*shape) for shape in out_shapes],
            in_specs=in_specs,
            out_specs=in_vmem(len(out_shapes)),
            scratch_shapes=scratch,
            compiler_params=pltpu.CompilerParams(vmem_limit_bytes=VMEM_BYTES),
            cost_estimate=pl.CostEstimate(
                flops=int(micros * 1e9), bytes_accessed=1 << 20, transcendentals=0
            ),
            name=name,
        )

    (bias_local,) = kernel_call(
        bias_kernel, "pair_bias", 5, in_vmem(3), [((heads, local_res, residues), BF16)], [],
    )(pair_norm_gain[None, :], pair_head_weight, pair_representation_state)
    features = aligned_chain_features
    if groups == 8:
        line = shift_line(bias_local, groups)
        line[0], features = lax.optimization_barrier((line[0], features))
        line = jnp.stack([bias_local, *line])
        bias_blocks = (line, lax.ppermute(line, "res", [(i, i ^ 1) for i in range(groups)]))
    else:
        bias_blocks = (lax.all_gather(bias_local, "res", axis=0, tiled=False),)
    arrived = exchange(features.reshape(groups, local_seqs, local_res, channels))

    column_block = (here * local_res) // BLOCK
    col_gap = lax.dynamic_slice_in_dim(gap_block_flags, column_block, 1, 1).reshape(1, total_seqs)

    gap = lax.dynamic_slice_in_dim(gap_block_flags, here * local_seqs, local_seqs, 0)
    by_row = (local_seqs, residues, channels)
    projected = kernel_call(
        functools.partial(project_kernel, heads), "row_project", 10, in_vmem(3),
        [(by_row, BF16), (by_row, BF16), (by_row, BF16), (by_row, F32)], [],
    )(horizontal_scaling_factor[None, :], arrived, row_input_weight)

    place = jnp.stack([here // 2, here % 2]).astype(jnp.int32)[None, :]
    operands = (arrived, *projected, horizontal_final_matrix, *bias_blocks)
    firsts = kernel_call(
        functools.partial(row_kernel, res_parts), "row_attention", 20,
        [pl.BlockSpec(memory_space=pltpu.SMEM)] * 2 + in_vmem(len(operands)),
        [((groups, local_seqs, part_res, channels), BF16)] * res_parts,
        [
            pltpu.VMEM((heads + 1, residues, residues), F32),
            pltpu.VMEM((local_seqs, residues, channels), BF16),
        ],
    )(gap, place, *operands)
    finals = [exchange(first) for first in firsts]
    done = []
    for c in range(res_parts):
        pieces = [finals[c].reshape(total_seqs, part_res, channels)]
        if not turn:
            pieces = [jnp.swapaxes(piece, 0, 1) for piece in pieces]
        lows = (0,)
        before = done if c == res_parts - 1 else []
        if not turn:
            shape = (part_res, total_seqs, channels)
        else:
            shape = (total_seqs, part_res * (1 + len(before)), channels)
        held = pltpu.VMEM((part_res, total_seqs, channels), BF16)
        done += kernel_call(
            functools.partial(column_kernel, heads, turn, lows, len(before)),
            "column_transition", 10, in_vmem(7 + len(pieces) + len(before)), [(shape, BF16)],
            [
                held, held, held, held,
                pltpu.VMEM((part_res, total_seqs, channels), F32),
                held, held,
            ],
        )(
            col_gap, vertical_scaling_factor[None, :], feedforward_scaling_factor[None, :],
            column_input_weight, vertical_final_matrix, feedforward_widen_matrix,
            feedforward_shrink_matrix, *pieces, *before,
        )
    return done[-1] if turn else jnp.swapaxes(done[-1], 0, 1)


def solution(mesh):
    placed = (
        P("dp", "res", None),
        P(("dp", "res"), None, None),
        P("dp", None),
    ) + (P(),) * 11
    return jax.shard_map(
        body, mesh=mesh, in_specs=placed, out_specs=P("dp", "res", None), check_vma=False
    )
```

```python
import functools

import jax
import jax.numpy as jnp
from jax import lax
from jax.experimental import pallas as pl
from jax.experimental.pallas import tpu as pltpu
from jax.sharding import PartitionSpec as P

BLOCK = 128
EPSILON = 1e-05
MASKED_SCORE = -1000000000.0
LANES = 128
SLAB = 16
F32 = jnp.float32
BF16 = jnp.bfloat16
VMEM_BYTES = 28 * 1024 * 1024


def layer_normalize(values_f, scale_gain):
    centred = values_f - jnp.mean(values_f, axis=-1, keepdims=True)
    spread = jnp.mean(centred * centred, axis=-1, keepdims=True)
    return centred * lax.rsqrt(spread + EPSILON) * scale_gain


def mm(lhs, rhs):
    return jnp.dot(lhs, rhs, preferred_element_type=F32)


def mm_nt(lhs, rhs):
    return lax.dot_general(lhs, rhs, (((1,), (1,)), ((), ())), preferred_element_type=F32)


def swap_matrix(outer, inner):
    size = outer * inner
    to = lax.broadcasted_iota(jnp.int32, (size, size), 0)
    come = lax.broadcasted_iota(jnp.int32, (size, size), 1)
    source = lax.rem(to, outer) * inner + lax.div(to, outer)
    return jnp.where(come == source, 1.0, 0.0).astype(BF16)


def bias_kernel(gain_ref, weight_ref, pair_ref, out_ref):
    local_res, residues, channels = pair_ref.shape
    heads = out_ref.shape[0]
    step = min(SLAB, local_res)
    few = min(4, step)
    width = heads * step
    head_at = lax.broadcasted_iota(jnp.int32, (heads, width), 0)
    spread = jnp.where(lax.broadcasted_iota(jnp.int32, (heads, width), 1) // step == head_at, 1.0, 0.0)
    wide = mm(weight_ref[...], spread.astype(BF16))
    lane = lax.broadcasted_iota(jnp.int32, wide.shape, 1)
    weights = [jnp.where(lane % step == i, wide, 0.0).astype(BF16) for i in range(step)]
    for p in range(0, local_res, step):
        projected = None
        for i in range(0, step, few):
            x = pair_ref[p + i : p + i + few].reshape(few * residues, channels)
            normed = layer_normalize(x.astype(F32), gain_ref[...]).astype(BF16)
            left = [normed[j * residues : (j + 1) * residues] for j in range(few)]
            part = mm(jnp.concatenate(left, axis=1), jnp.concatenate(weights[i : i + few], axis=0))
            projected = part if projected is None else projected + part
        out_ref[:, p : p + step] = projected.T.reshape(heads, step, residues).astype(BF16)


def softmax_lanes(scores):
    e = jnp.exp(scores - jnp.max(scores, axis=-1, keepdims=True))
    total = jnp.sum(e, axis=-1, keepdims=True)
    inverse = pl.reciprocal(total, approx=True)
    inverse = inverse * (2.0 - total * inverse)
    return (e * inverse).astype(BF16)


def gate_of(values):
    return 0.5 * jnp.tanh(0.5 * values) + 0.5


def pick_heads(parts, depth):
    lane = lax.broadcasted_iota(jnp.int32, parts[0].shape, 1)
    slot = lane // depth % len(parts)
    picked = parts[-1]
    for j in range(len(parts) - 2, -1, -1):
        picked = jnp.where(slot == j, parts[j], picked)
    return picked


def lane_mask(width, depth, slots, j):
    lane = lax.broadcasted_iota(jnp.int32, (1, width), 1)
    return jnp.where(lane // depth % slots == j, 1.0, 0.0).astype(BF16)


def project_kernel(heads, gain_ref, x_ref, win_ref, q_ref, k_ref, v_ref, gate_ref):
    groups, seqs, local_res, channels = x_ref.shape
    scale = (channels // heads) ** (-0.5)
    batch = largest(seqs, 4)

    def dense(i, carry):
        x = [x_ref[:, pl.ds(i * batch + j, 1)].reshape(-1, channels) for j in range(batch)]
        x = jnp.concatenate(x, axis=0).astype(F32)
        normed = layer_normalize(x, gain_ref[...]).astype(BF16)
        some = pl.ds(i * batch, batch)
        q = (mm(normed, win_ref[:, :channels]) * scale).astype(BF16)
        q_ref[some] = q.reshape(batch, groups * local_res, channels)
        k = mm(normed, win_ref[:, channels : 2 * channels]).astype(BF16)
        k_ref[some] = k.reshape(batch, groups * local_res, channels)
        v = mm(normed, win_ref[:, 2 * channels : 3 * channels]).astype(BF16)
        v_ref[some] = v.reshape(batch, groups * local_res, channels)
        gates = gate_of(mm(normed, win_ref[:, 3 * channels :]))
        gate_ref[some] = gates.reshape(batch, groups * local_res, channels)
        return carry

    lax.fori_loop(0, seqs // batch, dense, 0)


def in_turn(tasks, scores_of, weights_of, mixed_of):
    results, scores = [], scores_of(tasks[0])
    for at, task in enumerate(tasks):
        ahead = scores_of(tasks[at + 1]) if at + 1 < len(tasks) else None
        results.append(mixed_of(task, weights_of(task, scores)))
        scores = ahead
    return results


def row_kernel(
    parts, ordered, gap_ref, place_ref, x_ref, q_ref, k_ref, v_ref, gate_ref, wout_ref, bias_ref,
    *refs,
):
    refs, (bias_scr, gated_scr) = refs[:-2], refs[-2:]
    out_refs = refs[-parts:]
    groups, seqs, local_res, channels = x_ref.shape
    heads = bias_scr.shape[0] - 1
    residues = groups * local_res
    depth = channels // heads
    per = LANES // depth
    batch = largest(seqs, 4)
    part_res = local_res // parts

    for g in range(groups):
        block_of = bias_ref[g if ordered else lax.rem(place_ref[0] - g + groups, groups)]
        bias_scr[:heads, g * local_res : (g + 1) * local_res] = block_of.astype(F32)
    bias_scr[heads] = jnp.full((residues, residues), MASKED_SCORE, F32)
    masks = [lane_mask(LANES, depth, per, j) for j in range(per)]

    def attend(i, carry):
        tasks = [(u, g) for u in range(batch) for g in range(heads // per)]
        at = [i * batch + u for u in range(batch)]
        gaps = [[gap_ref[s, b] == 1 for b in range(residues // BLOCK)] for s in at]
        gates = [gate_ref[s] for s in at]

        def lanes(ref, task):
            return ref[at[task[0]], :, task[1] * LANES : (task[1] + 1) * LANES]

        def scores_of(task):
            q = lanes(q_ref, task)
            return mm_nt(
                jnp.concatenate([q * mask for mask in masks], axis=0), lanes(k_ref, task)
            )

        def weights_of(task, scores):
            weights = []
            for j in range(per):
                bias = [
                    bias_scr[
                        jnp.where(gap, heads, task[1] * per + j), :, b * BLOCK : (b + 1) * BLOCK
                    ]
                    for b, gap in enumerate(gaps[task[0]])
                ]
                own = scores[j * residues : (j + 1) * residues]
                weights.append(softmax_lanes(own + jnp.concatenate(bias, axis=1)))
            return jnp.concatenate(weights, axis=0)

        def mixed_of(task, weights):
            mixed = mm(weights, lanes(v_ref, task))
            return pick_heads([mixed[j * residues : (j + 1) * residues] for j in range(per)], depth)

        attended = in_turn(tasks, scores_of, weights_of, mixed_of)
        halves = heads // per
        for u in range(batch):
            whole = jnp.concatenate(attended[u * halves : (u + 1) * halves], axis=1)
            gated_scr[at[u]] = (whole * gates[u]).astype(BF16)
        return carry

    lax.fori_loop(0, seqs // batch, attend, 0)

    def finish(i, carry):
        x = [x_ref[:, pl.ds(i * batch + j, 1)].reshape(residues, channels) for j in range(batch)]
        gated = gated_scr[pl.ds(i * batch, batch)].reshape(batch * residues, channels)
        result = jnp.concatenate(x, axis=0).astype(F32) + mm(gated, wout_ref[...])
        result = result.astype(BF16).reshape(batch, groups, local_res, channels)
        for p, out_ref in enumerate(out_refs):
            for j in range(batch):
                out_ref[:, pl.ds(i * batch + j, 1)] = result[
                    j, :, p * part_res : (p + 1) * part_res
                ].reshape(groups, 1, part_res, channels)
        return carry

    lax.fori_loop(0, seqs // batch, finish, 0)


def column_kernel(
    heads, turn, lows, earlier, gap_ref, gain_ref, gain2_ref, win_ref, wout_ref,
    widen_ref, shrink_ref, *refs,
):
    pieces, refs = refs[: len(lows)], refs[len(lows) :]
    done_refs, refs = refs[:earlier], refs[earlier:]
    (out_ref, turned_scr, q_scr, k_scr, v_scr, gate_scr, gated_scr, done_scr) = refs
    local_res, seqs, channels = turned_scr.shape
    depth = channels // heads
    per = LANES // depth
    halves = heads // per
    scale = depth ** (-0.5)
    batch = largest(local_res, 8)
    pair = largest(local_res, 4)
    slabs = local_res // SLAB if turn else 0
    swap = swap_matrix(SLAB, SLAB)
    base = 0
    for done_ref in done_refs:
        out_ref[:, base : base + done_ref.shape[1]] = done_ref[...]
        base += done_ref.shape[1]
    if not turn:
        turned_scr[...] = pieces[0][...]
    for c in range(slabs):
        blocks = []
        for piece, low in zip(pieces, lows):
            start = low + c * SLAB
            for p in range(0, piece.shape[0], SLAB):
                block = piece[p : p + SLAB, start : start + SLAB]
                blocks.append(block.reshape(SLAB * SLAB, channels))
        turned = mm(swap, jnp.concatenate(blocks, axis=1)).astype(BF16)
        for g in range(seqs // SLAB):
            turned_scr[c * SLAB : (c + 1) * SLAB, g * SLAB : (g + 1) * SLAB] = turned[
                :, g * channels : (g + 1) * channels
            ].reshape(SLAB, SLAB, channels)

    def dense(i, carry):
        x = turned_scr[pl.ds(i * batch, batch)].reshape(batch * seqs, channels)
        normed = layer_normalize(x.astype(F32), gain_ref[...]).astype(BF16)
        q = (mm(normed, win_ref[:, :channels]) * scale).astype(BF16)
        k = mm(normed, win_ref[:, channels : 2 * channels]).astype(BF16)
        v = mm(normed, win_ref[:, 2 * channels : 3 * channels]).astype(BF16)
        gates = gate_of(mm(normed, win_ref[:, 3 * channels :]))
        shape = (batch, seqs, channels)
        q_scr[pl.ds(i * batch, batch)] = q.reshape(shape)
        k_scr[pl.ds(i * batch, batch)] = k.reshape(shape)
        v_scr[pl.ds(i * batch, batch)] = v.reshape(shape)
        gate_scr[pl.ds(i * batch, batch)] = gates.reshape(shape)
        return carry

    lax.fori_loop(0, local_res // batch, dense, 0)

    mask = jnp.where(gap_ref[...] == 1, MASKED_SCORE, 0.0)
    masks = [lane_mask(channels, depth, per, j) for j in range(per)]
    blank = jnp.zeros((seqs, LANES), BF16)

    def diagonal(values):
        rows = []
        for g in range(halves):
            own = values[:, g * LANES : (g + 1) * LANES]
            rows.append(jnp.concatenate([own if i == g else blank for i in range(halves)], axis=1))
        return jnp.concatenate(rows, axis=0)

    def attend(i, carry):
        at = [i * pair + u for u in range(pair)]
        gates = [gate_scr[r] for r in at]

        def scores_of(u):
            q = q_scr[at[u]]
            return mm_nt(jnp.concatenate([q * m for m in masks], axis=0), diagonal(k_scr[at[u]]))

        def weights_of(u, scores):
            weights = [
                softmax_lanes(scores[:, g * seqs : (g + 1) * seqs] + mask) for g in range(halves)
            ]
            return jnp.concatenate(weights, axis=1)

        def mixed_of(u, weights):
            mixed = mm(weights, diagonal(v_scr[at[u]]))
            return pick_heads([mixed[j * seqs : (j + 1) * seqs] for j in range(per)], depth)

        attended = in_turn(list(range(pair)), scores_of, weights_of, mixed_of)
        for u in range(pair):
            gated_scr[at[u]] = (attended[u] * gates[u]).astype(BF16)
        return carry

    lax.fori_loop(0, local_res // pair, attend, 0)

    def finish(i, carry):
        x = turned_scr[pl.ds(i * batch, batch)].reshape(batch * seqs, channels)
        gated = gated_scr[pl.ds(i * batch, batch)].reshape(batch * seqs, channels)
        second = (x.astype(F32) + mm(gated, wout_ref[...])).astype(BF16)
        second_f = second.astype(F32)
        normed = layer_normalize(second_f, gain2_ref[...]).astype(BF16)
        hidden = jnp.maximum(mm(normed, widen_ref[...]), 0.0).astype(BF16)
        result = (second_f + mm(hidden, shrink_ref[...])).astype(BF16)
        done_scr[pl.ds(i * batch, batch)] = result.reshape(batch, seqs, channels)
        return carry

    lax.fori_loop(0, local_res // batch, finish, 0)
    if not turn:
        out_ref[...] = done_scr[...]
    for c in range(slabs):
        blocks = [
            done_scr[c * SLAB : (c + 1) * SLAB, g * SLAB : (g + 1) * SLAB].reshape(
                SLAB * SLAB, channels
            )
            for g in range(seqs // SLAB)
        ]
        turned = mm(swap, jnp.concatenate(blocks, axis=1)).astype(BF16)
        start = base + c * SLAB
        for g in range(seqs // SLAB):
            out_ref[g * SLAB : (g + 1) * SLAB, start : start + SLAB] = turned[
                :, g * channels : (g + 1) * channels
            ].reshape(SLAB, SLAB, channels)


def largest(total, bound):
    return max(d for d in range(1, bound + 1) if total % d == 0)


def in_vmem(count):
    return [pl.BlockSpec(memory_space=pltpu.VMEM)] * count


def gather_bias(block, groups):
    if groups != 8:
        return lax.all_gather(block, "res", axis=0, tiled=False)
    blocks = [block] + [
        lax.ppermute(block, "res", [(i, (i + k) % groups) for i in range(groups)])
        for k in range(1, groups)
    ]
    return jnp.stack(blocks)


def body(
    aligned_chain_features,
    pair_representation_state,
    gap_block_flags,
    pair_norm_gain,
    pair_head_weight,
    horizontal_scaling_factor,
    row_input_weight,
    horizontal_final_matrix,
    vertical_scaling_factor,
    column_input_weight,
    vertical_final_matrix,
    feedforward_scaling_factor,
    feedforward_widen_matrix,
    feedforward_shrink_matrix,
):
    groups = lax.axis_size("res")
    total_seqs, local_res, channels = aligned_chain_features.shape
    residues = pair_representation_state.shape[1]
    heads = pair_head_weight.shape[1]
    local_seqs = total_seqs // groups
    turn = local_res % SLAB == 0
    seq_parts = 2 if turn and local_seqs % 2 == 0 else 1
    res_parts = local_res // SLAB if turn else 1
    part_seqs = local_seqs // seq_parts
    part_total = total_seqs // seq_parts
    part_res = local_res // res_parts
    here = lax.axis_index("res")

    def exchange(values):
        return lax.all_to_all(values, "res", split_axis=0, concat_axis=0, tiled=True)

    def kernel_call(kernel, name, micros, in_specs, out_shapes, scratch):
        return pl.pallas_call(
            kernel,
            out_shape=[jax.ShapeDtypeStruct(*shape) for shape in out_shapes],
            in_specs=in_specs,
            out_specs=in_vmem(len(out_shapes)),
            scratch_shapes=scratch,
            compiler_params=pltpu.CompilerParams(vmem_limit_bytes=VMEM_BYTES),
            cost_estimate=pl.CostEstimate(
                flops=int(micros * 1e9), bytes_accessed=1 << 20, transcendentals=0
            ),
            name=name,
        )

    halves = [
        aligned_chain_features[p * part_total : (p + 1) * part_total].reshape(
            groups, part_seqs, local_res, channels
        )
        for p in range(seq_parts)
    ]
    arrived = [exchange(halves[0])]
    (bias_local,) = kernel_call(
        bias_kernel, "pair_bias", 5, in_vmem(3), [((heads, local_res, residues), BF16)], [],
    )(pair_norm_gain[None, :], pair_head_weight, pair_representation_state)
    bias_local, arrived[0] = lax.optimization_barrier((bias_local, arrived[0]))
    bias_all = gather_bias(bias_local, groups)
    if seq_parts > 1:
        bias_all, *halves[1:] = lax.optimization_barrier((bias_all, *halves[1:]))
    arrived += [exchange(half) for half in halves[1:]]

    column_block = (here * local_res) // BLOCK
    col_gap = lax.dynamic_slice_in_dim(gap_block_flags, column_block, 1, 1).reshape(1, total_seqs)
    place = here.astype(jnp.int32)[None]

    def row_attention(part, parts, *after):
        gap = lax.dynamic_slice_in_dim(
            gap_block_flags, part * part_total + here * part_seqs, part_seqs, 0
        )
        by_row = (part_seqs, residues, channels)
        projected = kernel_call(
            functools.partial(project_kernel, heads), "row_project", 3, in_vmem(3),
            [(by_row, BF16), (by_row, BF16), (by_row, BF16), (by_row, F32)], [],
        )(horizontal_scaling_factor[None, :], arrived[part], row_input_weight)
        operands = (arrived[part], *projected, horizontal_final_matrix, bias_all)
        return kernel_call(
            functools.partial(row_kernel, parts, groups != 8), "row_attention", 10,
            [pl.BlockSpec(memory_space=pltpu.SMEM)] * 2
            + in_vmem(len(operands))
            + [pl.BlockSpec(memory_space=pl.ANY)] * len(after),
            [((groups, part_seqs, local_res // parts, channels), BF16)] * parts,
            [
                pltpu.VMEM((heads + 1, residues, residues), F32),
                pltpu.VMEM((part_seqs, residues, channels), BF16),
            ],
        )(gap, place, *operands, *after)

    returned, after = [], []
    for p in range(seq_parts - 1):
        after = row_attention(p, 1, *after)
        returned.append(exchange(after[0]).reshape(part_total, local_res, channels))
    finals = [exchange(first) for first in row_attention(seq_parts - 1, res_parts, *after)]
    done = []
    for c in range(res_parts):
        pieces = returned + [finals[c].reshape(part_total, part_res, channels)]
        if not turn:
            pieces = [jnp.swapaxes(piece, 0, 1) for piece in pieces]
        lows = (c * part_res,) * len(returned) + (0,)
        before = done if c == res_parts - 1 else []
        if not turn:
            shape = (part_res, total_seqs, channels)
        else:
            shape = (total_seqs, part_res * (1 + len(before)), channels)
        held = pltpu.VMEM((part_res, total_seqs, channels), BF16)
        done += kernel_call(
            functools.partial(column_kernel, heads, turn, lows, len(before)),
            "column_transition", 10, in_vmem(7 + len(pieces) + len(before)), [(shape, BF16)],
            [
                held, held, held, held,
                pltpu.VMEM((part_res, total_seqs, channels), F32),
                held, held,
            ],
        )(
            col_gap, vertical_scaling_factor[None, :], feedforward_scaling_factor[None, :],
            column_input_weight, vertical_final_matrix, feedforward_widen_matrix,
            feedforward_shrink_matrix, *pieces, *before,
        )
    return done[-1] if turn else jnp.swapaxes(done[-1], 0, 1)


def solution(mesh):
    placed = (
        P("dp", "res", None),
        P(("dp", "res"), None, None),
        P("dp", None),
    ) + (P(),) * 11
    return jax.shard_map(
        body, mesh=mesh, in_specs=placed, out_specs=P("dp", "res", None), check_vma=False
    )
```

```python
import functools

import jax
import jax.numpy as jnp
from jax import lax
from jax.experimental import pallas as pl
from jax.experimental.pallas import tpu as pltpu
from jax.sharding import PartitionSpec as P

BLOCK = 128
EPSILON = 1e-05
MASKED_SCORE = -1000000000.0
LANES = 128
SLAB = 16
SLOTS = 8
F32 = jnp.float32
BF16 = jnp.bfloat16
VMEM_BYTES = 28 * 1024 * 1024


def layer_normalize(values_f, scale_gain):
    centred = values_f - jnp.mean(values_f, axis=-1, keepdims=True)
    spread = jnp.mean(centred * centred, axis=-1, keepdims=True)
    return centred * lax.rsqrt(spread + EPSILON) * scale_gain


def mm(lhs, rhs):
    return jnp.dot(lhs, rhs, preferred_element_type=F32)


def mm_nt(lhs, rhs):
    return lax.dot_general(lhs, rhs, (((1,), (1,)), ((), ())), preferred_element_type=F32)


def swap_matrix(outer, inner):
    size = outer * inner
    to = lax.broadcasted_iota(jnp.int32, (size, size), 0)
    come = lax.broadcasted_iota(jnp.int32, (size, size), 1)
    source = lax.rem(to, outer) * inner + lax.div(to, outer)
    return jnp.where(come == source, 1.0, 0.0).astype(BF16)


def bias_kernel(gain_ref, weight_ref, pair_ref, out_ref):
    local_res, residues, channels = pair_ref.shape
    heads = out_ref.shape[0]
    step = min(SLAB, local_res)
    few = min(4, step)
    width = heads * step
    head_at = lax.broadcasted_iota(jnp.int32, (heads, width), 0)
    spread = jnp.where(lax.broadcasted_iota(jnp.int32, (heads, width), 1) // step == head_at, 1.0, 0.0)
    wide = mm(weight_ref[...], spread.astype(BF16))
    lane = lax.broadcasted_iota(jnp.int32, wide.shape, 1)
    weights = [jnp.where(lane % step == i, wide, 0.0).astype(BF16) for i in range(step)]
    for p in range(0, local_res, step):
        projected = None
        for i in range(0, step, few):
            x = pair_ref[p + i : p + i + few].reshape(few * residues, channels)
            normed = layer_normalize(x.astype(F32), gain_ref[...]).astype(BF16)
            left = [normed[j * residues : (j + 1) * residues] for j in range(few)]
            part = mm(jnp.concatenate(left, axis=1), jnp.concatenate(weights[i : i + few], axis=0))
            projected = part if projected is None else projected + part
        out_ref[:, p : p + step] = projected.T.reshape(heads, step, residues).astype(BF16)


def softmax_lanes(scores):
    e = jnp.exp(scores - jnp.max(scores, axis=-1, keepdims=True))
    total = jnp.sum(e, axis=-1, keepdims=True)
    inverse = pl.reciprocal(total, approx=True)
    inverse = inverse * (2.0 - total * inverse)
    return (e * inverse).astype(BF16)


def gate_of(values):
    return 0.5 * jnp.tanh(0.5 * values) + 0.5


def pick_heads(parts, depth):
    lane = lax.broadcasted_iota(jnp.int32, parts[0].shape, 1)
    slot = lane // depth % len(parts)
    picked = parts[-1]
    for j in range(len(parts) - 2, -1, -1):
        picked = jnp.where(slot == j, parts[j], picked)
    return picked


def lane_mask(width, depth, slots, j):
    lane = lax.broadcasted_iota(jnp.int32, (1, width), 1)
    return jnp.where(lane // depth % slots == j, 1.0, 0.0).astype(BF16)


def rows_of(refs, slot, at):
    ref = refs[0].at[slot] if len(refs) == 1 else refs[slot]
    return ref[pl.ds(at, 1)].reshape(ref.shape[1:])


def project_kernel(heads, groups, gain_ref, win_ref, *refs):
    x_refs, (q_ref, k_ref, v_ref, gate_ref) = refs[:-4], refs[-4:]
    seqs, residues, channels = q_ref.shape
    scale = (channels // heads) ** (-0.5)
    batch = largest(seqs, 4)

    def dense(i, carry):
        x = [rows_of(x_refs, t, i * batch + j) for j in range(batch) for t in range(groups)]
        x = jnp.concatenate(x, axis=0).astype(F32)
        normed = layer_normalize(x, gain_ref[...]).astype(BF16)
        some = pl.ds(i * batch, batch)
        shape = (batch, residues, channels)
        q = (mm(normed, win_ref[:, :channels]) * scale).astype(BF16)
        q_ref[some] = q.reshape(shape)
        k_ref[some] = mm(normed, win_ref[:, channels : 2 * channels]).astype(BF16).reshape(shape)
        v_ref[some] = mm(normed, win_ref[:, 2 * channels : 3 * channels]).astype(BF16).reshape(shape)
        gate_ref[some] = gate_of(mm(normed, win_ref[:, 3 * channels :])).reshape(shape)
        return carry

    lax.fori_loop(0, seqs // batch, dense, 0)


def in_turn(tasks, scores_of, weights_of, mixed_of):
    results, scores = [], scores_of(tasks[0])
    for at, task in enumerate(tasks):
        ahead = scores_of(tasks[at + 1]) if at + 1 < len(tasks) else None
        results.append(mixed_of(task, weights_of(task, scores)))
        scores = ahead
    return results


def row_kernel(
    blocks, outs, gap_ref, place_ref, q_ref, k_ref, v_ref, gate_ref, wout_ref, bias_ref, *refs
):
    x_refs, refs, (bias_scr, gated_scr) = refs[:blocks], refs[blocks:-2], refs[-2:]
    out_refs = refs[-outs:]
    groups, heads, local_res, residues = bias_ref.shape
    seqs, _, channels = q_ref.shape
    depth = channels // heads
    per = LANES // depth
    batch = largest(seqs, 4)
    parts = 1 if blocks == 1 else outs // groups
    part_res = local_res // parts

    def home(place):
        if blocks == 1:
            return place
        slot = lax.rem(place_ref[0] - place // local_res + groups, groups)
        return slot * local_res + place % local_res

    square = (residues, residues)
    residue = lax.broadcasted_iota(jnp.int32, square, 0)
    order = jnp.where(residue == home(lax.broadcasted_iota(jnp.int32, square, 1)), 1.0, 0.0)
    order = order.astype(BF16)
    for h in range(heads):
        bias_scr[h] = mm(bias_ref[:, h].reshape(residues, residues), order)
    masks = [lane_mask(LANES, depth, per, j) for j in range(per)]
    block_at = home(lax.broadcasted_iota(jnp.int32, (1, residues), 1)) // BLOCK

    def attend(i, carry):
        tasks = [(u, g) for u in range(batch) for g in range(heads // per)]
        at = [i * batch + u for u in range(batch)]
        gaps = []
        for s in at:
            gap = jnp.zeros((1, residues), F32)
            for b in range(residues // BLOCK):
                closed = jnp.where(gap_ref[s, b] == 1, MASKED_SCORE, 0.0)
                gap = jnp.where(block_at == b, closed, gap)
            gaps.append(gap)
        gates = [gate_ref[s] for s in at]

        def lanes(ref, task):
            return ref[at[task[0]], :, task[1] * LANES : (task[1] + 1) * LANES]

        def scores_of(task):
            q = lanes(q_ref, task)
            return mm_nt(
                jnp.concatenate([q * mask for mask in masks], axis=0), lanes(k_ref, task)
            )

        def weights_of(task, scores):
            weights = []
            for j in range(per):
                own = scores[j * residues : (j + 1) * residues]
                own = own + bias_scr[task[1] * per + j] + gaps[task[0]]
                weights.append(softmax_lanes(own))
            return jnp.concatenate(weights, axis=0)

        def mixed_of(task, weights):
            mixed = mm(weights, lanes(v_ref, task))
            return pick_heads([mixed[j * residues : (j + 1) * residues] for j in range(per)], depth)

        attended = in_turn(tasks, scores_of, weights_of, mixed_of)
        halves = heads // per
        for u in range(batch):
            whole = jnp.concatenate(attended[u * halves : (u + 1) * halves], axis=1)
            gated_scr[at[u]] = (whole * gates[u]).astype(BF16)
        return carry

    lax.fori_loop(0, seqs // batch, attend, 0)

    def finish(i, carry):
        x = [rows_of(x_refs, t, i * batch + j) for j in range(batch) for t in range(groups)]
        gated = gated_scr[pl.ds(i * batch, batch)].reshape(batch * residues, channels)
        result = jnp.concatenate(x, axis=0).astype(F32) + mm(gated, wout_ref[...])
        result = result.astype(BF16).reshape(batch, groups, local_res, channels)
        for j in range(batch):
            s = i * batch + j
            if blocks == 1:
                out_refs[0][:, pl.ds(s, 1)] = result[j].reshape(groups, 1, local_res, channels)
                continue
            for p in range(parts):
                for t in range(groups):
                    out_refs[p * groups + t][s] = result[j, t, p * part_res : (p + 1) * part_res]
        return carry

    lax.fori_loop(0, seqs // batch, finish, 0)


def column_kernel(
    heads, turn, lows, earlier, place_ref, gap_ref, gain_ref, gain2_ref, win_ref, wout_ref,
    widen_ref, shrink_ref, *refs,
):
    pieces, refs = refs[: len(lows)], refs[len(lows) :]
    done_refs, refs = refs[:earlier], refs[earlier:]
    (out_ref, turned_scr, q_scr, k_scr, v_scr, gate_scr, gated_scr, done_scr) = refs
    local_res, seqs, channels = turned_scr.shape
    depth = channels // heads
    per = LANES // depth
    halves = heads // per
    scale = depth ** (-0.5)
    batch = largest(local_res, 8)
    pair = largest(local_res, 4)
    slabs = local_res // SLAB if turn else 0
    swap = swap_matrix(SLAB, SLAB)
    base = 0
    for done_ref in done_refs:
        out_ref[:, base : base + done_ref.shape[1]] = done_ref[...]
        base += done_ref.shape[1]
    if not turn:
        turned_scr[...] = pieces[0][...]
    each = pieces[0].shape[0]
    fold = SLAB // each if turn else 1
    for c in range(slabs):
        parts = [
            piece[:, low + c * SLAB : low + (c + 1) * SLAB] for piece, low in zip(pieces, lows)
        ]
        blocks = [
            jnp.concatenate(parts[i : i + fold], axis=0).reshape(SLAB * SLAB, channels)
            for i in range(0, len(parts), fold)
        ]
        turned = mm(swap, jnp.concatenate(blocks, axis=1)).astype(BF16)
        for g in range(seqs // SLAB):
            turned_scr[c * SLAB : (c + 1) * SLAB, g * SLAB : (g + 1) * SLAB] = turned[
                :, g * channels : (g + 1) * channels
            ].reshape(SLAB, SLAB, channels)

    def dense(i, carry):
        x = turned_scr[pl.ds(i * batch, batch)].reshape(batch * seqs, channels)
        normed = layer_normalize(x.astype(F32), gain_ref[...]).astype(BF16)
        q = (mm(normed, win_ref[:, :channels]) * scale).astype(BF16)
        k = mm(normed, win_ref[:, channels : 2 * channels]).astype(BF16)
        v = mm(normed, win_ref[:, 2 * channels : 3 * channels]).astype(BF16)
        gates = gate_of(mm(normed, win_ref[:, 3 * channels :]))
        shape = (batch, seqs, channels)
        q_scr[pl.ds(i * batch, batch)] = q.reshape(shape)
        k_scr[pl.ds(i * batch, batch)] = k.reshape(shape)
        v_scr[pl.ds(i * batch, batch)] = v.reshape(shape)
        gate_scr[pl.ds(i * batch, batch)] = gates.reshape(shape)
        return carry

    lax.fori_loop(0, local_res // batch, dense, 0)

    mask = jnp.where(gap_ref[...] == 1, MASKED_SCORE, 0.0)
    masks = [lane_mask(channels, depth, per, j) for j in range(per)]
    blank = jnp.zeros((seqs, LANES), BF16)

    def diagonal(values):
        rows = []
        for g in range(halves):
            own = values[:, g * LANES : (g + 1) * LANES]
            rows.append(jnp.concatenate([own if i == g else blank for i in range(halves)], axis=1))
        return jnp.concatenate(rows, axis=0)

    def attend(i, carry):
        at = [i * pair + u for u in range(pair)]
        gates = [gate_scr[r] for r in at]

        def scores_of(u):
            q = q_scr[at[u]]
            return mm_nt(jnp.concatenate([q * m for m in masks], axis=0), diagonal(k_scr[at[u]]))

        def weights_of(u, scores):
            weights = [
                softmax_lanes(scores[:, g * seqs : (g + 1) * seqs] + mask) for g in range(halves)
            ]
            return jnp.concatenate(weights, axis=1)

        def mixed_of(u, weights):
            mixed = mm(weights, diagonal(v_scr[at[u]]))
            return pick_heads([mixed[j * seqs : (j + 1) * seqs] for j in range(per)], depth)

        attended = in_turn(list(range(pair)), scores_of, weights_of, mixed_of)
        for u in range(pair):
            gated_scr[at[u]] = (attended[u] * gates[u]).astype(BF16)
        return carry

    lax.fori_loop(0, local_res // pair, attend, 0)

    def finish(i, carry):
        x = turned_scr[pl.ds(i * batch, batch)].reshape(batch * seqs, channels)
        gated = gated_scr[pl.ds(i * batch, batch)].reshape(batch * seqs, channels)
        second = (x.astype(F32) + mm(gated, wout_ref[...])).astype(BF16)
        second_f = second.astype(F32)
        normed = layer_normalize(second_f, gain2_ref[...]).astype(BF16)
        hidden = jnp.maximum(mm(normed, widen_ref[...]), 0.0).astype(BF16)
        result = (second_f + mm(hidden, shrink_ref[...])).astype(BF16)
        done_scr[pl.ds(i * batch, batch)] = result.reshape(batch, seqs, channels)
        return carry

    lax.fori_loop(0, local_res // batch, finish, 0)
    if not turn:
        out_ref[...] = done_scr[...]
    for c in range(slabs):
        blocks = [
            done_scr[c * SLAB : (c + 1) * SLAB, g * SLAB : (g + 1) * SLAB].reshape(
                SLAB * SLAB, channels
            )
            for g in range(seqs // SLAB)
        ]
        turned = mm(swap, jnp.concatenate(blocks, axis=1)).astype(BF16)
        start = base + c * SLAB
        for g in range(seqs // SLAB):
            own = turned[:, g * channels : (g + 1) * channels].reshape(SLAB, SLAB, channels)
            for e in range(fold):
                slot = g * fold + e
                around = SLOTS * (slot // SLOTS)
                place = around + lax.rem(place_ref[0] + slot % SLOTS, SLOTS)
                out_ref[pl.ds(place * each, each), start : start + SLAB] = own[
                    e * each : (e + 1) * each
                ]


def largest(total, bound):
    return max(d for d in range(1, bound + 1) if total % d == 0)


def in_vmem(count):
    return [pl.BlockSpec(memory_space=pltpu.VMEM)] * count


def shifts(blocks, sign):
    arrived = [blocks[0]]
    for k in range(1, SLOTS):
        to = [(i, (i + sign * k) % SLOTS) for i in range(SLOTS)]
        arrived.append(lax.ppermute(blocks[k], "res", to))
    return arrived


def body(
    aligned_chain_features,
    pair_representation_state,
    gap_block_flags,
    pair_norm_gain,
    pair_head_weight,
    horizontal_scaling_factor,
    row_input_weight,
    horizontal_final_matrix,
    vertical_scaling_factor,
    column_input_weight,
    vertical_final_matrix,
    feedforward_scaling_factor,
    feedforward_widen_matrix,
    feedforward_shrink_matrix,
):
    groups = lax.axis_size("res")
    total_seqs, local_res, channels = aligned_chain_features.shape
    residues = pair_representation_state.shape[1]
    heads = pair_head_weight.shape[1]
    local_seqs = total_seqs // groups
    by_shifts = groups == SLOTS and local_res % SLAB == 0 and local_seqs % SLAB == 0
    seq_parts = 2 if by_shifts else 1
    res_parts = local_res // SLAB if by_shifts else 1
    part_seqs = local_seqs // seq_parts
    part_total = total_seqs // seq_parts
    part_res = local_res // res_parts
    here = lax.axis_index("res")

    def exchange(values):
        return lax.all_to_all(values, "res", split_axis=0, concat_axis=0, tiled=True)

    def kernel_call(kernel, name, micros, in_specs, out_shapes, scratch):
        return pl.pallas_call(
            kernel,
            out_shape=[jax.ShapeDtypeStruct(*shape) for shape in out_shapes],
            in_specs=in_specs,
            out_specs=in_vmem(len(out_shapes)),
            scratch_shapes=scratch,
            compiler_params=pltpu.CompilerParams(vmem_limit_bytes=VMEM_BYTES),
            cost_estimate=pl.CostEstimate(
                flops=int(micros * 1e9), bytes_accessed=1 << 20, transcendentals=0
            ),
            name=name,
        )

    def entering(half):
        values = aligned_chain_features[half * part_total : (half + 1) * part_total].reshape(
            groups, part_seqs, local_res, channels
        )
        if not by_shifts:
            return [values]
        return [
            lax.dynamic_index_in_dim(values, lax.rem(here + k, groups), 0, keepdims=False)
            for k in range(groups)
        ]

    def enter(blocks):
        return shifts(blocks, 1) if by_shifts else [exchange(blocks[0])]

    arrived = [enter(entering(0))]
    (bias_local,) = kernel_call(
        bias_kernel, "pair_bias", 5, in_vmem(3), [((heads, local_res, residues), BF16)], [],
    )(pair_norm_gain[None, :], pair_head_weight, pair_representation_state)
    if by_shifts:
        bias_local, *arrived[0] = lax.optimization_barrier((bias_local, *arrived[0]))
        bias_all = jnp.stack(shifts([bias_local] * groups, 1))
    else:
        bias_all = lax.all_gather(bias_local, "res", axis=0, tiled=False)
    for half in range(1, seq_parts):
        bias_all, *blocks = lax.optimization_barrier((bias_all, *entering(half)))
        arrived.append(enter(blocks))

    column_block = (here * local_res) // BLOCK
    col_gap = lax.dynamic_slice_in_dim(gap_block_flags, column_block, 1, 1)
    if by_shifts:
        col_gap = jnp.roll(col_gap.reshape(seq_parts, groups, part_seqs), -here, axis=1)
    col_gap = col_gap.reshape(1, total_seqs)
    place = here.astype(jnp.int32)[None]

    def row_attention(part, parts, *after):
        gap = lax.dynamic_slice_in_dim(
            gap_block_flags, part * part_total + here * part_seqs, part_seqs, 0
        )
        by_row = (part_seqs, residues, channels)
        blocks = arrived[part]
        projected = kernel_call(
            functools.partial(project_kernel, heads, groups), "row_project", 3,
            in_vmem(2 + len(blocks)),
            [(by_row, BF16), (by_row, BF16), (by_row, BF16), (by_row, F32)], [],
        )(horizontal_scaling_factor[None, :], row_input_weight, *blocks)
        operands = (*projected, horizontal_final_matrix, bias_all, *blocks)
        if by_shifts:
            outs = [((part_seqs, local_res // parts, channels), BF16)] * (groups * parts)
        else:
            outs = [((groups, part_seqs, local_res, channels), BF16)]
        return kernel_call(
            functools.partial(row_kernel, len(blocks), len(outs)), "row_attention", 10,
            [pl.BlockSpec(memory_space=pltpu.SMEM)] * 2
            + in_vmem(len(operands))
            + [pl.BlockSpec(memory_space=pl.ANY)] * len(after),
            outs,
            [
                pltpu.VMEM((heads, residues, residues), F32),
                pltpu.VMEM((part_seqs, residues, channels), BF16),
            ],
        )(gap, place, *operands, *after)

    if by_shifts:
        first = row_attention(0, 1)
        returned = shifts(first, -1)
        second = row_attention(1, res_parts, first[0])
        finals = [
            shifts(second[c * groups : (c + 1) * groups], -1) for c in range(res_parts)
        ]
    else:
        returned, (first,) = [], row_attention(0, 1)
        back = exchange(first).reshape(total_seqs, local_res, channels)
        finals = [[jnp.swapaxes(back, 0, 1)]]
    done = []
    for c in range(res_parts):
        pieces = returned + finals[c]
        lows = (c * part_res,) * len(returned) + (0,) * len(finals[c])
        before = done if c == res_parts - 1 else []
        if not by_shifts:
            shape = (part_res, total_seqs, channels)
        else:
            shape = (total_seqs, part_res * (1 + len(before)), channels)
        held = pltpu.VMEM((part_res, total_seqs, channels), BF16)
        done += kernel_call(
            functools.partial(column_kernel, heads, by_shifts, lows, len(before)),
            "column_transition", 10,
            [pl.BlockSpec(memory_space=pltpu.SMEM)] + in_vmem(7 + len(pieces) + len(before)),
            [(shape, BF16)],
            [
                held, held, held, held,
                pltpu.VMEM((part_res, total_seqs, channels), F32),
                held, held,
            ],
        )(
            place, col_gap, vertical_scaling_factor[None, :], feedforward_scaling_factor[None, :],
            column_input_weight, vertical_final_matrix, feedforward_widen_matrix,
            feedforward_shrink_matrix, *pieces, *before,
        )
    return done[-1] if by_shifts else jnp.swapaxes(done[-1], 0, 1)


def solution(mesh):
    placed = (
        P("dp", "res", None),
        P(("dp", "res"), None, None),
        P("dp", None),
    ) + (P(),) * 11
    return jax.shard_map(
        body, mesh=mesh, in_specs=placed, out_specs=P("dp", "res", None), check_vma=False
    )
```

```python
import functools

import jax
import jax.numpy as jnp
from jax import lax
from jax.experimental import pallas as pl
from jax.experimental.pallas import tpu as pltpu
from jax.sharding import PartitionSpec as P

BLOCK = 128
EPSILON = 1e-05
MASKED_SCORE = -1000000000.0
LANES = 128
SLAB = 16
SLOTS = 8
F32 = jnp.float32
BF16 = jnp.bfloat16
VMEM_BYTES = 28 * 1024 * 1024


def layer_normalize(values_f, scale_gain):
    centred = values_f - jnp.mean(values_f, axis=-1, keepdims=True)
    spread = jnp.mean(centred * centred, axis=-1, keepdims=True)
    return centred * lax.rsqrt(spread + EPSILON) * scale_gain


def mm(lhs, rhs):
    return jnp.dot(lhs, rhs, preferred_element_type=F32)


def mm_nt(lhs, rhs):
    return lax.dot_general(lhs, rhs, (((1,), (1,)), ((), ())), preferred_element_type=F32)


def swap_matrix(outer, inner):
    size = outer * inner
    to = lax.broadcasted_iota(jnp.int32, (size, size), 0)
    come = lax.broadcasted_iota(jnp.int32, (size, size), 1)
    source = lax.rem(to, outer) * inner + lax.div(to, outer)
    return jnp.where(come == source, 1.0, 0.0).astype(BF16)


def bias_kernel(gain_ref, weight_ref, pair_ref, out_ref):
    local_res, residues, channels = pair_ref.shape
    heads = out_ref.shape[0]
    step = min(SLAB, local_res)
    few = min(4, step)
    width = heads * step
    head_at = lax.broadcasted_iota(jnp.int32, (heads, width), 0)
    spread = jnp.where(lax.broadcasted_iota(jnp.int32, (heads, width), 1) // step == head_at, 1.0, 0.0)
    wide = mm(weight_ref[...], spread.astype(BF16))
    lane = lax.broadcasted_iota(jnp.int32, wide.shape, 1)
    weights = [jnp.where(lane % step == i, wide, 0.0).astype(BF16) for i in range(step)]
    for p in range(0, local_res, step):
        projected = None
        for i in range(0, step, few):
            x = pair_ref[p + i : p + i + few].reshape(few * residues, channels)
            normed = layer_normalize(x.astype(F32), gain_ref[...]).astype(BF16)
            left = [normed[j * residues : (j + 1) * residues] for j in range(few)]
            part = mm(jnp.concatenate(left, axis=1), jnp.concatenate(weights[i : i + few], axis=0))
            projected = part if projected is None else projected + part
        out_ref[:, p : p + step] = projected.T.reshape(heads, step, residues).astype(BF16)


def softmax_lanes(scores):
    e = jnp.exp(scores - jnp.max(scores, axis=-1, keepdims=True))
    total = jnp.sum(e, axis=-1, keepdims=True)
    inverse = pl.reciprocal(total, approx=True)
    inverse = inverse * (2.0 - total * inverse)
    return (e * inverse).astype(BF16)


def gate_of(values):
    return 0.5 * jnp.tanh(0.5 * values) + 0.5


def pick_heads(parts, depth):
    lane = lax.broadcasted_iota(jnp.int32, parts[0].shape, 1)
    slot = lane // depth % len(parts)
    picked = parts[-1]
    for j in range(len(parts) - 2, -1, -1):
        picked = jnp.where(slot == j, parts[j], picked)
    return picked


def lane_mask(width, depth, slots, j):
    lane = lax.broadcasted_iota(jnp.int32, (1, width), 1)
    return jnp.where(lane // depth % slots == j, 1.0, 0.0).astype(BF16)


def rows_of(refs, slot, at):
    ref = refs[0].at[slot] if len(refs) == 1 else refs[slot]
    return ref[pl.ds(at, 1)].reshape(ref.shape[1:])


def project_kernel(heads, groups, gain_ref, win_ref, *refs):
    x_refs, (q_ref, k_ref, v_ref, gate_ref) = refs[:-4], refs[-4:]
    seqs, residues, channels = q_ref.shape
    scale = (channels // heads) ** (-0.5)
    batch = largest(seqs, 4)

    def dense(i, carry):
        x = [rows_of(x_refs, t, i * batch + j) for j in range(batch) for t in range(groups)]
        x = jnp.concatenate(x, axis=0).astype(F32)
        normed = layer_normalize(x, gain_ref[...]).astype(BF16)
        some = pl.ds(i * batch, batch)
        shape = (batch, residues, channels)
        q = (mm(normed, win_ref[:, :channels]) * scale).astype(BF16)
        q_ref[some] = q.reshape(shape)
        k_ref[some] = mm(normed, win_ref[:, channels : 2 * channels]).astype(BF16).reshape(shape)
        v_ref[some] = mm(normed, win_ref[:, 2 * channels : 3 * channels]).astype(BF16).reshape(shape)
        gate_ref[some] = gate_of(mm(normed, win_ref[:, 3 * channels :])).reshape(shape)
        return carry

    lax.fori_loop(0, seqs // batch, dense, 0)


def in_turn(tasks, scores_of, weights_of, mixed_of):
    results, scores = [], scores_of(tasks[0])
    for at, task in enumerate(tasks):
        ahead = scores_of(tasks[at + 1]) if at + 1 < len(tasks) else None
        results.append(mixed_of(task, weights_of(task, scores)))
        scores = ahead
    return results


def row_kernel(
    blocks, outs, gap_ref, place_ref, q_ref, k_ref, v_ref, gate_ref, wout_ref, bias_ref, *refs
):
    x_refs, out_refs, (bias_scr, gated_scr) = refs[:blocks], refs[blocks:-2], refs[-2:]
    groups, heads, local_res, residues = bias_ref.shape
    seqs, _, channels = q_ref.shape
    depth = channels // heads
    per = LANES // depth
    batch = largest(seqs, 4)
    parts = 1 if blocks == 1 else outs // groups
    part_res = local_res // parts

    def home(place):
        if blocks == 1:
            return place
        slot = lax.rem(place_ref[0] - place // local_res + groups, groups)
        return slot * local_res + place % local_res

    square = (residues, residues)
    residue = lax.broadcasted_iota(jnp.int32, square, 0)
    order = jnp.where(residue == home(lax.broadcasted_iota(jnp.int32, square, 1)), 1.0, 0.0)
    order = order.astype(BF16)
    for h in range(heads):
        bias_scr[h] = mm(bias_ref[:, h].reshape(residues, residues), order)
    masks = [lane_mask(LANES, depth, per, j) for j in range(per)]
    block_at = home(lax.broadcasted_iota(jnp.int32, (1, residues), 1)) // BLOCK

    def attend(i, carry):
        tasks = [(u, g) for u in range(batch) for g in range(heads // per)]
        at = [i * batch + u for u in range(batch)]
        gaps = []
        for s in at:
            gap = jnp.zeros((1, residues), F32)
            for b in range(residues // BLOCK):
                closed = jnp.where(gap_ref[s, b] == 1, MASKED_SCORE, 0.0)
                gap = jnp.where(block_at == b, closed, gap)
            gaps.append(gap)
        gates = [gate_ref[s] for s in at]

        def lanes(ref, task):
            return ref[at[task[0]], :, task[1] * LANES : (task[1] + 1) * LANES]

        def scores_of(task):
            q = lanes(q_ref, task)
            return mm_nt(
                jnp.concatenate([q * mask for mask in masks], axis=0), lanes(k_ref, task)
            )

        def weights_of(task, scores):
            weights = []
            for j in range(per):
                own = scores[j * residues : (j + 1) * residues]
                own = own + bias_scr[task[1] * per + j] + gaps[task[0]]
                weights.append(softmax_lanes(own))
            return jnp.concatenate(weights, axis=0)

        def mixed_of(task, weights):
            mixed = mm(weights, lanes(v_ref, task))
            return pick_heads([mixed[j * residues : (j + 1) * residues] for j in range(per)], depth)

        attended = in_turn(tasks, scores_of, weights_of, mixed_of)
        halves = heads // per
        for u in range(batch):
            whole = jnp.concatenate(attended[u * halves : (u + 1) * halves], axis=1)
            gated_scr[at[u]] = (whole * gates[u]).astype(BF16)
        return carry

    lax.fori_loop(0, seqs // batch, attend, 0)

    def finish(i, carry):
        x = [rows_of(x_refs, t, i * batch + j) for j in range(batch) for t in range(groups)]
        gated = gated_scr[pl.ds(i * batch, batch)].reshape(batch * residues, channels)
        result = jnp.concatenate(x, axis=0).astype(F32) + mm(gated, wout_ref[...])
        result = result.astype(BF16).reshape(batch, groups, local_res, channels)
        for j in range(batch):
            s = i * batch + j
            if blocks == 1:
                out_refs[0][:, pl.ds(s, 1)] = result[j].reshape(groups, 1, local_res, channels)
                continue
            for p in range(parts):
                for t in range(groups):
                    out_refs[p * groups + t][s] = result[j, t, p * part_res : (p + 1) * part_res]
        return carry

    lax.fori_loop(0, seqs // batch, finish, 0)


def column_kernel(
    heads, turn, lows, earlier, place_ref, gap_ref, gain_ref, gain2_ref, win_ref, wout_ref,
    widen_ref, shrink_ref, *refs,
):
    pieces, refs = refs[: len(lows)], refs[len(lows) :]
    done_refs, refs = refs[:earlier], refs[earlier:]
    (out_ref, turned_scr, q_scr, k_scr, v_scr, gate_scr, gated_scr, done_scr) = refs
    local_res, seqs, channels = turned_scr.shape
    depth = channels // heads
    per = LANES // depth
    halves = heads // per
    scale = depth ** (-0.5)
    batch = largest(local_res, 8)
    pair = largest(local_res, 4)
    slabs = local_res // SLAB if turn else 0
    swap = swap_matrix(SLAB, SLAB)
    base = 0
    for done_ref in done_refs:
        out_ref[:, base : base + done_ref.shape[1]] = done_ref[...]
        base += done_ref.shape[1]
    if not turn:
        turned_scr[...] = pieces[0][...]
    each = pieces[0].shape[0]
    fold = SLAB // each if turn else 1
    for c in range(slabs):
        parts = [
            piece[:, low + c * SLAB : low + (c + 1) * SLAB] for piece, low in zip(pieces, lows)
        ]
        blocks = [
            jnp.concatenate(parts[i : i + fold], axis=0).reshape(SLAB * SLAB, channels)
            for i in range(0, len(parts), fold)
        ]
        turned = mm(swap, jnp.concatenate(blocks, axis=1)).astype(BF16)
        for g in range(seqs // SLAB):
            turned_scr[c * SLAB : (c + 1) * SLAB, g * SLAB : (g + 1) * SLAB] = turned[
                :, g * channels : (g + 1) * channels
            ].reshape(SLAB, SLAB, channels)

    def dense(i, carry):
        x = turned_scr[pl.ds(i * batch, batch)].reshape(batch * seqs, channels)
        normed = layer_normalize(x.astype(F32), gain_ref[...]).astype(BF16)
        q = (mm(normed, win_ref[:, :channels]) * scale).astype(BF16)
        k = mm(normed, win_ref[:, channels : 2 * channels]).astype(BF16)
        v = mm(normed, win_ref[:, 2 * channels : 3 * channels]).astype(BF16)
        gates = gate_of(mm(normed, win_ref[:, 3 * channels :]))
        shape = (batch, seqs, channels)
        q_scr[pl.ds(i * batch, batch)] = q.reshape(shape)
        k_scr[pl.ds(i * batch, batch)] = k.reshape(shape)
        v_scr[pl.ds(i * batch, batch)] = v.reshape(shape)
        gate_scr[pl.ds(i * batch, batch)] = gates.reshape(shape)
        return carry

    lax.fori_loop(0, local_res // batch, dense, 0)

    mask = jnp.where(gap_ref[...] == 1, MASKED_SCORE, 0.0)
    masks = [lane_mask(channels, depth, per, j) for j in range(per)]
    blank = jnp.zeros((seqs, LANES), BF16)

    def diagonal(values):
        rows = []
        for g in range(halves):
            own = values[:, g * LANES : (g + 1) * LANES]
            rows.append(jnp.concatenate([own if i == g else blank for i in range(halves)], axis=1))
        return jnp.concatenate(rows, axis=0)

    def attend(i, carry):
        at = [i * pair + u for u in range(pair)]
        gates = [gate_scr[r] for r in at]

        def scores_of(u):
            q = q_scr[at[u]]
            return mm_nt(jnp.concatenate([q * m for m in masks], axis=0), diagonal(k_scr[at[u]]))

        def weights_of(u, scores):
            weights = [
                softmax_lanes(scores[:, g * seqs : (g + 1) * seqs] + mask) for g in range(halves)
            ]
            return jnp.concatenate(weights, axis=1)

        def mixed_of(u, weights):
            mixed = mm(weights, diagonal(v_scr[at[u]]))
            return pick_heads([mixed[j * seqs : (j + 1) * seqs] for j in range(per)], depth)

        attended = in_turn(list(range(pair)), scores_of, weights_of, mixed_of)
        for u in range(pair):
            gated_scr[at[u]] = (attended[u] * gates[u]).astype(BF16)
        return carry

    lax.fori_loop(0, local_res // pair, attend, 0)

    def finish(i, carry):
        x = turned_scr[pl.ds(i * batch, batch)].reshape(batch * seqs, channels)
        gated = gated_scr[pl.ds(i * batch, batch)].reshape(batch * seqs, channels)
        second = (x.astype(F32) + mm(gated, wout_ref[...])).astype(BF16)
        second_f = second.astype(F32)
        normed = layer_normalize(second_f, gain2_ref[...]).astype(BF16)
        hidden = jnp.maximum(mm(normed, widen_ref[...]), 0.0).astype(BF16)
        result = (second_f + mm(hidden, shrink_ref[...])).astype(BF16)
        done_scr[pl.ds(i * batch, batch)] = result.reshape(batch, seqs, channels)
        return carry

    lax.fori_loop(0, local_res // batch, finish, 0)
    if not turn:
        out_ref[...] = done_scr[...]
    for c in range(slabs):
        blocks = [
            done_scr[c * SLAB : (c + 1) * SLAB, g * SLAB : (g + 1) * SLAB].reshape(
                SLAB * SLAB, channels
            )
            for g in range(seqs // SLAB)
        ]
        turned = mm(swap, jnp.concatenate(blocks, axis=1)).astype(BF16)
        start = base + c * SLAB
        for g in range(seqs // SLAB):
            own = turned[:, g * channels : (g + 1) * channels].reshape(SLAB, SLAB, channels)
            for e in range(fold):
                slot = g * fold + e
                around = SLOTS * (slot // SLOTS)
                place = around + lax.rem(place_ref[0] + slot % SLOTS, SLOTS)
                out_ref[pl.ds(place * each, each), start : start + SLAB] = own[
                    e * each : (e + 1) * each
                ]


def largest(total, bound):
    return max(d for d in range(1, bound + 1) if total % d == 0)


def in_vmem(count):
    return [pl.BlockSpec(memory_space=pltpu.VMEM)] * count


def shifts(blocks, sign):
    arrived = [blocks[0]]
    for k in range(1, SLOTS):
        to = [(i, (i + sign * k) % SLOTS) for i in range(SLOTS)]
        arrived.append(lax.ppermute(blocks[k], "res", to))
    return arrived


def body(
    aligned_chain_features,
    pair_representation_state,
    gap_block_flags,
    pair_norm_gain,
    pair_head_weight,
    horizontal_scaling_factor,
    row_input_weight,
    horizontal_final_matrix,
    vertical_scaling_factor,
    column_input_weight,
    vertical_final_matrix,
    feedforward_scaling_factor,
    feedforward_widen_matrix,
    feedforward_shrink_matrix,
):
    groups = lax.axis_size("res")
    total_seqs, local_res, channels = aligned_chain_features.shape
    residues = pair_representation_state.shape[1]
    heads = pair_head_weight.shape[1]
    local_seqs = total_seqs // groups
    by_shifts = groups == SLOTS and local_res % SLAB == 0 and local_seqs % SLAB == 0
    res_parts = local_res // SLAB if by_shifts else 1
    part_res = local_res // res_parts
    here = lax.axis_index("res")

    def exchange(values):
        return lax.all_to_all(values, "res", split_axis=0, concat_axis=0, tiled=True)

    def kernel_call(kernel, name, micros, in_specs, out_shapes, scratch):
        return pl.pallas_call(
            kernel,
            out_shape=[jax.ShapeDtypeStruct(*shape) for shape in out_shapes],
            in_specs=in_specs,
            out_specs=in_vmem(len(out_shapes)),
            scratch_shapes=scratch,
            compiler_params=pltpu.CompilerParams(vmem_limit_bytes=VMEM_BYTES),
            cost_estimate=pl.CostEstimate(
                flops=int(micros * 1e9), bytes_accessed=1 << 20, transcendentals=0
            ),
            name=name,
        )

    values = aligned_chain_features.reshape(groups, local_seqs, local_res, channels)
    if by_shifts:
        arrived = shifts(
            [
                lax.dynamic_index_in_dim(values, lax.rem(here + k, groups), 0, keepdims=False)
                for k in range(groups)
            ],
            1,
        )
    else:
        arrived = [exchange(values)]
    (bias_local,) = kernel_call(
        bias_kernel, "pair_bias", 5, in_vmem(3), [((heads, local_res, residues), BF16)], [],
    )(pair_norm_gain[None, :], pair_head_weight, pair_representation_state)
    if by_shifts:
        bias_local, arrived[1] = lax.optimization_barrier((bias_local, arrived[1]))
        bias_all = jnp.stack(shifts([bias_local] * groups, 1))
    else:
        bias_all = lax.all_gather(bias_local, "res", axis=0, tiled=False)

    column_block = (here * local_res) // BLOCK
    col_gap = lax.dynamic_slice_in_dim(gap_block_flags, column_block, 1, 1)
    if by_shifts:
        col_gap = jnp.roll(col_gap.reshape(groups, local_seqs), -here, axis=0)
    col_gap = col_gap.reshape(1, total_seqs)
    place = here.astype(jnp.int32)[None]

    gap = lax.dynamic_slice_in_dim(gap_block_flags, here * local_seqs, local_seqs, 0)
    by_row = (local_seqs, residues, channels)
    projected = kernel_call(
        functools.partial(project_kernel, heads, groups), "row_project", 5,
        in_vmem(2 + len(arrived)),
        [(by_row, BF16), (by_row, BF16), (by_row, BF16), (by_row, F32)], [],
    )(horizontal_scaling_factor[None, :], row_input_weight, *arrived)
    operands = (*projected, horizontal_final_matrix, bias_all, *arrived)
    if by_shifts:
        outs = [((local_seqs, part_res, channels), BF16)] * (groups * res_parts)
    else:
        outs = [((groups, local_seqs, local_res, channels), BF16)]
    first = kernel_call(
        functools.partial(row_kernel, len(arrived), len(outs)), "row_attention", 20,
        [pl.BlockSpec(memory_space=pltpu.SMEM)] * 2 + in_vmem(len(operands)),
        outs,
        [
            pltpu.VMEM((heads, residues, residues), F32),
            pltpu.VMEM((local_seqs, residues, channels), BF16),
        ],
    )(gap, place, *operands)
    if by_shifts:
        finals = [shifts(first[c * groups : (c + 1) * groups], -1) for c in range(res_parts)]
    else:
        back = exchange(first[0]).reshape(total_seqs, local_res, channels)
        finals = [[jnp.swapaxes(back, 0, 1)]]
    done = []
    for c in range(res_parts):
        pieces = finals[c]
        lows = (0,) * len(pieces)
        before = done if c == res_parts - 1 else []
        if not by_shifts:
            shape = (part_res, total_seqs, channels)
        else:
            shape = (total_seqs, part_res * (1 + len(before)), channels)
        held = pltpu.VMEM((part_res, total_seqs, channels), BF16)
        done += kernel_call(
            functools.partial(column_kernel, heads, by_shifts, lows, len(before)),
            "column_transition", 10,
            [pl.BlockSpec(memory_space=pltpu.SMEM)] + in_vmem(7 + len(pieces) + len(before)),
            [(shape, BF16)],
            [
                held, held, held, held,
                pltpu.VMEM((part_res, total_seqs, channels), F32),
                held, held,
            ],
        )(
            place, col_gap, vertical_scaling_factor[None, :], feedforward_scaling_factor[None, :],
            column_input_weight, vertical_final_matrix, feedforward_widen_matrix,
            feedforward_shrink_matrix, *pieces, *before,
        )
    return done[-1] if by_shifts else jnp.swapaxes(done[-1], 0, 1)


def solution(mesh):
    placed = (
        P("dp", "res", None),
        P(("dp", "res"), None, None),
        P("dp", None),
    ) + (P(),) * 11
    return jax.shard_map(
        body, mesh=mesh, in_specs=placed, out_specs=P("dp", "res", None), check_vma=False
    )
```

```python
import functools

import jax
import jax.numpy as jnp
from jax import lax
from jax.experimental import pallas as pl
from jax.experimental.pallas import tpu as pltpu
from jax.sharding import PartitionSpec as P

BLOCK = 128
EPSILON = 1e-05
MASKED_SCORE = -1000000000.0
LANES = 128
SLAB = 16
SLOTS = 8
STACKED, LISTED = 0, 1
F32 = jnp.float32
BF16 = jnp.bfloat16
VMEM_BYTES = 28 * 1024 * 1024


def layer_normalize(values_f, scale_gain):
    centred = values_f - jnp.mean(values_f, axis=-1, keepdims=True)
    spread = jnp.mean(centred * centred, axis=-1, keepdims=True)
    return centred * lax.rsqrt(spread + EPSILON) * scale_gain


def mm(lhs, rhs):
    return jnp.dot(lhs, rhs, preferred_element_type=F32)


def mm_nt(lhs, rhs):
    return lax.dot_general(lhs, rhs, (((1,), (1,)), ((), ())), preferred_element_type=F32)


def swap_matrix(outer, inner):
    size = outer * inner
    to = lax.broadcasted_iota(jnp.int32, (size, size), 0)
    come = lax.broadcasted_iota(jnp.int32, (size, size), 1)
    source = lax.rem(to, outer) * inner + lax.div(to, outer)
    return jnp.where(come == source, 1.0, 0.0).astype(BF16)


def bias_kernel(gain_ref, weight_ref, pair_ref, out_ref):
    local_res, residues, channels = pair_ref.shape
    heads = out_ref.shape[0]
    step = min(SLAB, local_res)
    few = min(4, step)
    width = heads * step
    head_at = lax.broadcasted_iota(jnp.int32, (heads, width), 0)
    spread = jnp.where(lax.broadcasted_iota(jnp.int32, (heads, width), 1) // step == head_at, 1.0, 0.0)
    wide = mm(weight_ref[...], spread.astype(BF16))
    lane = lax.broadcasted_iota(jnp.int32, wide.shape, 1)
    weights = [jnp.where(lane % step == i, wide, 0.0).astype(BF16) for i in range(step)]
    for p in range(0, local_res, step):
        projected = None
        for i in range(0, step, few):
            x = pair_ref[p + i : p + i + few].reshape(few * residues, channels)
            normed = layer_normalize(x.astype(F32), gain_ref[...]).astype(BF16)
            left = [normed[j * residues : (j + 1) * residues] for j in range(few)]
            part = mm(jnp.concatenate(left, axis=1), jnp.concatenate(weights[i : i + few], axis=0))
            projected = part if projected is None else projected + part
        out_ref[:, p : p + step] = projected.T.reshape(heads, step, residues).astype(BF16)


def softmax_lanes(scores):
    e = jnp.exp(scores - jnp.max(scores, axis=-1, keepdims=True))
    total = jnp.sum(e, axis=-1, keepdims=True)
    inverse = pl.reciprocal(total, approx=True)
    inverse = inverse * (2.0 - total * inverse)
    return (e * inverse).astype(BF16)


def gate_of(values):
    return 0.5 * jnp.tanh(0.5 * values) + 0.5


def pick_heads(parts, depth):
    lane = lax.broadcasted_iota(jnp.int32, parts[0].shape, 1)
    slot = lane // depth % len(parts)
    picked = parts[-1]
    for j in range(len(parts) - 2, -1, -1):
        picked = jnp.where(slot == j, parts[j], picked)
    return picked


def lane_mask(width, depth, slots, j):
    lane = lax.broadcasted_iota(jnp.int32, (1, width), 1)
    return jnp.where(lane // depth % slots == j, 1.0, 0.0).astype(BF16)


def rows_of(refs, slot, at):
    ref = refs[0].at[slot] if len(refs) == 1 else refs[slot]
    return ref[pl.ds(at, 1)].reshape(ref.shape[1:])


def project_kernel(heads, groups, gain_ref, win_ref, *refs):
    x_refs, (q_ref, k_ref, v_ref, gate_ref) = refs[:-4], refs[-4:]
    seqs, residues, channels = q_ref.shape
    scale = (channels // heads) ** (-0.5)
    batch = largest(seqs, 4)

    def dense(i, carry):
        x = [rows_of(x_refs, t, i * batch + j) for j in range(batch) for t in range(groups)]
        x = jnp.concatenate(x, axis=0).astype(F32)
        normed = layer_normalize(x, gain_ref[...]).astype(BF16)
        some = pl.ds(i * batch, batch)
        shape = (batch, residues, channels)
        q = (mm(normed, win_ref[:, :channels]) * scale).astype(BF16)
        q_ref[some] = q.reshape(shape)
        k_ref[some] = mm(normed, win_ref[:, channels : 2 * channels]).astype(BF16).reshape(shape)
        v_ref[some] = mm(normed, win_ref[:, 2 * channels : 3 * channels]).astype(BF16).reshape(shape)
        gate_ref[some] = gate_of(mm(normed, win_ref[:, 3 * channels :])).reshape(shape)
        return carry

    lax.fori_loop(0, seqs // batch, dense, 0)


def in_turn(tasks, scores_of, weights_of, mixed_of):
    results, scores = [], scores_of(tasks[0])
    for at, task in enumerate(tasks):
        ahead = scores_of(tasks[at + 1]) if at + 1 < len(tasks) else None
        results.append(mixed_of(task, weights_of(task, scores)))
        scores = ahead
    return results


def row_kernel(
    blocks, kinds, gap_ref, place_ref, q_ref, k_ref, v_ref, gate_ref, wout_ref, bias_ref, *refs
):
    x_refs, refs, (bias_scr, gated_scr) = refs[:blocks], refs[blocks:-2], refs[-2:]
    groups, heads, local_res, residues = bias_ref.shape
    out_refs = []
    for kind in kinds[::-1]:
        count = 1 if kind == STACKED else groups
        out_refs.insert(0, refs[-count:])
        refs = refs[:-count]
    seqs, _, channels = q_ref.shape
    depth = channels // heads
    per = LANES // depth
    batch = largest(seqs, 4)
    part_res = local_res // len(kinds)

    def home(place):
        if blocks == 1:
            return place
        slot = lax.rem(place_ref[0] - place // local_res + groups, groups)
        return slot * local_res + place % local_res

    square = (residues, residues)
    residue = lax.broadcasted_iota(jnp.int32, square, 0)
    order = jnp.where(residue == home(lax.broadcasted_iota(jnp.int32, square, 1)), 1.0, 0.0)
    order = order.astype(BF16)
    for h in range(heads):
        bias_scr[h] = mm(bias_ref[:, h].reshape(residues, residues), order)
    masks = [lane_mask(LANES, depth, per, j) for j in range(per)]
    block_at = home(lax.broadcasted_iota(jnp.int32, (1, residues), 1)) // BLOCK

    def attend(i, carry):
        tasks = [(u, g) for u in range(batch) for g in range(heads // per)]
        at = [i * batch + u for u in range(batch)]
        gaps = []
        for s in at:
            gap = jnp.zeros((1, residues), F32)
            for b in range(residues // BLOCK):
                closed = jnp.where(gap_ref[s, b] == 1, MASKED_SCORE, 0.0)
                gap = jnp.where(block_at == b, closed, gap)
            gaps.append(gap)
        gates = [gate_ref[s] for s in at]

        def lanes(ref, task):
            return ref[at[task[0]], :, task[1] * LANES : (task[1] + 1) * LANES]

        def scores_of(task):
            q = lanes(q_ref, task)
            return mm_nt(
                jnp.concatenate([q * mask for mask in masks], axis=0), lanes(k_ref, task)
            )

        def weights_of(task, scores):
            weights = []
            for j in range(per):
                own = scores[j * residues : (j + 1) * residues]
                own = own + bias_scr[task[1] * per + j] + gaps[task[0]]
                weights.append(softmax_lanes(own))
            return jnp.concatenate(weights, axis=0)

        def mixed_of(task, weights):
            mixed = mm(weights, lanes(v_ref, task))
            return pick_heads([mixed[j * residues : (j + 1) * residues] for j in range(per)], depth)

        attended = in_turn(tasks, scores_of, weights_of, mixed_of)
        halves = heads // per
        for u in range(batch):
            whole = jnp.concatenate(attended[u * halves : (u + 1) * halves], axis=1)
            gated_scr[at[u]] = (whole * gates[u]).astype(BF16)
        return carry

    lax.fori_loop(0, seqs // batch, attend, 0)

    def finish(i, carry):
        x = [rows_of(x_refs, t, i * batch + j) for j in range(batch) for t in range(groups)]
        gated = gated_scr[pl.ds(i * batch, batch)].reshape(batch * residues, channels)
        result = jnp.concatenate(x, axis=0).astype(F32) + mm(gated, wout_ref[...])
        result = result.astype(BF16).reshape(batch, groups, local_res, channels)
        for j in range(batch):
            s = i * batch + j
            for p, (kind, outs) in enumerate(zip(kinds, out_refs)):
                for t in range(groups):
                    rows = result[j, t, p * part_res : (p + 1) * part_res]
                    if kind != STACKED:
                        outs[t][s] = rows
                    elif blocks == 1:
                        outs[0][t, s] = rows
                    else:
                        outs[0][lax.rem(place_ref[0] - t + groups, groups), s] = rows
        return carry

    lax.fori_loop(0, seqs // batch, finish, 0)


def column_kernel(
    heads, turn, lows, earlier, place_ref, gap_ref, gain_ref, gain2_ref, win_ref, wout_ref,
    widen_ref, shrink_ref, *refs,
):
    pieces, places = [], []
    for kind, low in lows:
        if kind == STACKED:
            pieces += [(refs[0].at[g] if turn else refs[0], low) for g in range(SLOTS if turn else 1)]
            places += [len(places) + g for g in range(SLOTS)]
            refs = refs[1:]
        else:
            pieces += [(ref, low) for ref in refs[:SLOTS]]
            places += [len(places) + lax.rem(place_ref[0] + t, SLOTS) for t in range(SLOTS)]
            refs = refs[SLOTS:]
    done_refs, refs = refs[:earlier], refs[earlier:]
    (out_ref, turned_scr, q_scr, k_scr, v_scr, gate_scr, gated_scr, done_scr) = refs
    local_res, seqs, channels = turned_scr.shape
    depth = channels // heads
    per = LANES // depth
    halves = heads // per
    scale = depth ** (-0.5)
    batch = largest(local_res, 8)
    pair = largest(local_res, 4)
    slabs = local_res // SLAB if turn else 0
    swap = swap_matrix(SLAB, SLAB)
    base = 0
    for done_ref in done_refs:
        out_ref[:, base : base + done_ref.shape[1]] = done_ref[...]
        base += done_ref.shape[1]
    if not turn:
        turned_scr[...] = pieces[0][0][...]
    each = pieces[0][0].shape[0]
    fold = SLAB // each if turn else 1
    for c in range(slabs):
        parts = [
            piece[:, low + c * SLAB : low + (c + 1) * SLAB] for piece, low in pieces
        ]
        blocks = [
            jnp.concatenate(parts[i : i + fold], axis=0).reshape(SLAB * SLAB, channels)
            for i in range(0, len(parts), fold)
        ]
        turned = mm(swap, jnp.concatenate(blocks, axis=1)).astype(BF16)
        for g in range(seqs // SLAB):
            turned_scr[c * SLAB : (c + 1) * SLAB, g * SLAB : (g + 1) * SLAB] = turned[
                :, g * channels : (g + 1) * channels
            ].reshape(SLAB, SLAB, channels)

    def dense(i, carry):
        x = turned_scr[pl.ds(i * batch, batch)].reshape(batch * seqs, channels)
        normed = layer_normalize(x.astype(F32), gain_ref[...]).astype(BF16)
        q = (mm(normed, win_ref[:, :channels]) * scale).astype(BF16)
        k = mm(normed, win_ref[:, channels : 2 * channels]).astype(BF16)
        v = mm(normed, win_ref[:, 2 * channels : 3 * channels]).astype(BF16)
        gates = gate_of(mm(normed, win_ref[:, 3 * channels :]))
        shape = (batch, seqs, channels)
        q_scr[pl.ds(i * batch, batch)] = q.reshape(shape)
        k_scr[pl.ds(i * batch, batch)] = k.reshape(shape)
        v_scr[pl.ds(i * batch, batch)] = v.reshape(shape)
        gate_scr[pl.ds(i * batch, batch)] = gates.reshape(shape)
        return carry

    lax.fori_loop(0, local_res // batch, dense, 0)

    mask = jnp.where(gap_ref[...] == 1, MASKED_SCORE, 0.0)
    masks = [lane_mask(channels, depth, per, j) for j in range(per)]
    blank = jnp.zeros((seqs, LANES), BF16)

    def diagonal(values):
        rows = []
        for g in range(halves):
            own = values[:, g * LANES : (g + 1) * LANES]
            rows.append(jnp.concatenate([own if i == g else blank for i in range(halves)], axis=1))
        return jnp.concatenate(rows, axis=0)

    def attend(i, carry):
        at = [i * pair + u for u in range(pair)]
        gates = [gate_scr[r] for r in at]

        def scores_of(u):
            q = q_scr[at[u]]
            return mm_nt(jnp.concatenate([q * m for m in masks], axis=0), diagonal(k_scr[at[u]]))

        def weights_of(u, scores):
            weights = [
                softmax_lanes(scores[:, g * seqs : (g + 1) * seqs] + mask) for g in range(halves)
            ]
            return jnp.concatenate(weights, axis=1)

        def mixed_of(u, weights):
            mixed = mm(weights, diagonal(v_scr[at[u]]))
            return pick_heads([mixed[j * seqs : (j + 1) * seqs] for j in range(per)], depth)

        attended = in_turn(list(range(pair)), scores_of, weights_of, mixed_of)
        for u in range(pair):
            gated_scr[at[u]] = (attended[u] * gates[u]).astype(BF16)
        return carry

    lax.fori_loop(0, local_res // pair, attend, 0)

    def finish(i, carry):
        x = turned_scr[pl.ds(i * batch, batch)].reshape(batch * seqs, channels)
        gated = gated_scr[pl.ds(i * batch, batch)].reshape(batch * seqs, channels)
        second = (x.astype(F32) + mm(gated, wout_ref[...])).astype(BF16)
        second_f = second.astype(F32)
        normed = layer_normalize(second_f, gain2_ref[...]).astype(BF16)
        hidden = jnp.maximum(mm(normed, widen_ref[...]), 0.0).astype(BF16)
        result = (second_f + mm(hidden, shrink_ref[...])).astype(BF16)
        done_scr[pl.ds(i * batch, batch)] = result.reshape(batch, seqs, channels)
        return carry

    lax.fori_loop(0, local_res // batch, finish, 0)
    if not turn:
        out_ref[...] = done_scr[...]
    for c in range(slabs):
        blocks = [
            done_scr[c * SLAB : (c + 1) * SLAB, g * SLAB : (g + 1) * SLAB].reshape(
                SLAB * SLAB, channels
            )
            for g in range(seqs // SLAB)
        ]
        turned = mm(swap, jnp.concatenate(blocks, axis=1)).astype(BF16)
        start = base + c * SLAB
        for g in range(seqs // SLAB):
            own = turned[:, g * channels : (g + 1) * channels].reshape(SLAB, SLAB, channels)
            for e in range(fold):
                place = places[g * fold + e]
                out_ref[pl.ds(place * each, each), start : start + SLAB] = own[
                    e * each : (e + 1) * each
                ]


def largest(total, bound):
    return max(d for d in range(1, bound + 1) if total % d == 0)


def in_vmem(count):
    return [pl.BlockSpec(memory_space=pltpu.VMEM)] * count


def shifts(blocks, sign):
    arrived = [blocks[0]]
    for k in range(1, SLOTS):
        to = [(i, (i + sign * k) % SLOTS) for i in range(SLOTS)]
        arrived.append(lax.ppermute(blocks[k], "res", to))
    return arrived


def body(
    aligned_chain_features,
    pair_representation_state,
    gap_block_flags,
    pair_norm_gain,
    pair_head_weight,
    horizontal_scaling_factor,
    row_input_weight,
    horizontal_final_matrix,
    vertical_scaling_factor,
    column_input_weight,
    vertical_final_matrix,
    feedforward_scaling_factor,
    feedforward_widen_matrix,
    feedforward_shrink_matrix,
):
    groups = lax.axis_size("res")
    total_seqs, local_res, channels = aligned_chain_features.shape
    residues = pair_representation_state.shape[1]
    heads = pair_head_weight.shape[1]
    local_seqs = total_seqs // groups
    by_shifts = groups == SLOTS and local_res % SLAB == 0 and local_seqs % SLAB == 0
    seq_parts = 2 if by_shifts else 1
    res_parts = local_res // SLAB if by_shifts else 1
    part_seqs = local_seqs // seq_parts
    part_total = total_seqs // seq_parts
    part_res = local_res // res_parts
    here = lax.axis_index("res")

    def exchange(values):
        return lax.all_to_all(values, "res", split_axis=0, concat_axis=0, tiled=True)

    def kernel_call(kernel, name, micros, in_specs, out_shapes, scratch):
        return pl.pallas_call(
            kernel,
            out_shape=[jax.ShapeDtypeStruct(*shape) for shape in out_shapes],
            in_specs=in_specs,
            out_specs=in_vmem(len(out_shapes)),
            scratch_shapes=scratch,
            compiler_params=pltpu.CompilerParams(vmem_limit_bytes=VMEM_BYTES),
            cost_estimate=pl.CostEstimate(
                flops=int(micros * 1e9), bytes_accessed=1 << 20, transcendentals=0
            ),
            name=name,
        )

    def entering(half):
        values = aligned_chain_features[half * part_total : (half + 1) * part_total].reshape(
            groups, part_seqs, local_res, channels
        )
        if not by_shifts:
            return [values]
        return [
            lax.dynamic_index_in_dim(values, lax.rem(here + k, groups), 0, keepdims=False)
            for k in range(groups)
        ]

    def enter(blocks):
        return shifts(blocks, 1) if by_shifts else [exchange(blocks[0])]

    arrived = [enter(entering(0))]
    (bias_local,) = kernel_call(
        bias_kernel, "pair_bias", 5, in_vmem(3), [((heads, local_res, residues), BF16)], [],
    )(pair_norm_gain[None, :], pair_head_weight, pair_representation_state)
    if by_shifts:
        bias_local, *arrived[0] = lax.optimization_barrier((bias_local, *arrived[0]))
        bias_all = jnp.stack(shifts([bias_local] * groups, 1))
    else:
        bias_all = lax.all_gather(bias_local, "res", axis=0, tiled=False)
    for half in range(1, seq_parts):
        bias_all, *blocks = lax.optimization_barrier((bias_all, *entering(half)))
        arrived.append(enter(blocks))

    column_block = (here * local_res) // BLOCK
    col_gap = lax.dynamic_slice_in_dim(gap_block_flags, column_block, 1, 1).reshape(1, total_seqs)
    place = here.astype(jnp.int32)[None]

    def row_attention(part, kinds, *after):
        gap = lax.dynamic_slice_in_dim(
            gap_block_flags, part * part_total + here * part_seqs, part_seqs, 0
        )
        by_row = (part_seqs, residues, channels)
        blocks = arrived[part]
        projected = kernel_call(
            functools.partial(project_kernel, heads, groups), "row_project", 3,
            in_vmem(2 + len(blocks)),
            [(by_row, BF16), (by_row, BF16), (by_row, BF16), (by_row, F32)], [],
        )(horizontal_scaling_factor[None, :], row_input_weight, *blocks)
        operands = (*projected, horizontal_final_matrix, bias_all, *blocks)
        count = local_res // len(kinds)
        outs = []
        for kind in kinds:
            if kind == STACKED:
                outs += [((groups, part_seqs, count, channels), BF16)]
            else:
                outs += [((part_seqs, count, channels), BF16)] * groups
        return kernel_call(
            functools.partial(row_kernel, len(blocks), kinds), "row_attention", 10,
            [pl.BlockSpec(memory_space=pltpu.SMEM)] * 2
            + in_vmem(len(operands))
            + [pl.BlockSpec(memory_space=pl.ANY)] * len(after),
            outs,
            [
                pltpu.VMEM((heads, residues, residues), F32),
                pltpu.VMEM((part_seqs, residues, channels), BF16),
            ],
        )(gap, place, *operands, *after)

    if by_shifts:
        first = row_attention(0, (STACKED,))
        returned = exchange(first[0])
        kinds = (LISTED,) * (res_parts - 1) + (STACKED,)
        second = row_attention(1, kinds, first[0])
        finals = [shifts(second[c * groups : (c + 1) * groups], -1) for c in range(res_parts - 1)]
        finals.append([exchange(second[-1])])
    else:
        (first,) = row_attention(0, (STACKED,))
        back = exchange(first).reshape(total_seqs, local_res, channels)
        kinds, finals = (STACKED,), [[jnp.swapaxes(back, 0, 1)]]
    done = []
    for c in range(res_parts):
        pieces, lows, own_gap = finals[c], ((kinds[c], 0),), col_gap
        if by_shifts:
            pieces, lows = [returned] + pieces, ((STACKED, c * part_res),) + lows
        if kinds[c] == LISTED:
            second = col_gap[:, part_total:].reshape(groups, part_seqs)
            second = jnp.roll(second, -here, axis=0).reshape(1, part_total)
            own_gap = jnp.concatenate([col_gap[:, :part_total], second], axis=1)
        before = done if c == res_parts - 1 else []
        if not by_shifts:
            shape = (part_res, total_seqs, channels)
        else:
            shape = (total_seqs, part_res * (1 + len(before)), channels)
        held = pltpu.VMEM((part_res, total_seqs, channels), BF16)
        done += kernel_call(
            functools.partial(column_kernel, heads, by_shifts, lows, len(before)),
            "column_transition", 10,
            [pl.BlockSpec(memory_space=pltpu.SMEM)] + in_vmem(7 + len(pieces) + len(before)),
            [(shape, BF16)],
            [
                held, held, held, held,
                pltpu.VMEM((part_res, total_seqs, channels), F32),
                held, held,
            ],
        )(
            place, own_gap, vertical_scaling_factor[None, :], feedforward_scaling_factor[None, :],
            column_input_weight, vertical_final_matrix, feedforward_widen_matrix,
            feedforward_shrink_matrix, *pieces, *before,
        )
    return done[-1] if by_shifts else jnp.swapaxes(done[-1], 0, 1)


def solution(mesh):
    placed = (
        P("dp", "res", None),
        P(("dp", "res"), None, None),
        P("dp", None),
    ) + (P(),) * 11
    return jax.shard_map(
        body, mesh=mesh, in_specs=placed, out_specs=P("dp", "res", None), check_vma=False
    )
```

```python
import functools

import jax
import jax.numpy as jnp
from jax import lax
from jax.experimental import pallas as pl
from jax.experimental.pallas import tpu as pltpu
from jax.sharding import PartitionSpec as P

BLOCK = 128
EPSILON = 1e-05
MASKED_SCORE = -1000000000.0
LANES = 128
SLAB = 16
SLOTS = 8
STACKED, LISTED = 0, 1
F32 = jnp.float32
BF16 = jnp.bfloat16
VMEM_BYTES = 28 * 1024 * 1024


def layer_normalize(values_f, scale_gain):
    centred = values_f - jnp.mean(values_f, axis=-1, keepdims=True)
    spread = jnp.mean(centred * centred, axis=-1, keepdims=True)
    return centred * lax.rsqrt(spread + EPSILON) * scale_gain


def mm(lhs, rhs):
    return jnp.dot(lhs, rhs, preferred_element_type=F32)


def mm_nt(lhs, rhs):
    return lax.dot_general(lhs, rhs, (((1,), (1,)), ((), ())), preferred_element_type=F32)


def swap_matrix(outer, inner):
    size = outer * inner
    to = lax.broadcasted_iota(jnp.int32, (size, size), 0)
    come = lax.broadcasted_iota(jnp.int32, (size, size), 1)
    source = lax.rem(to, outer) * inner + lax.div(to, outer)
    return jnp.where(come == source, 1.0, 0.0).astype(BF16)


def bias_kernel(gain_ref, weight_ref, pair_ref, out_ref):
    local_res, residues, channels = pair_ref.shape
    heads = out_ref.shape[0]
    step = min(SLAB, local_res)
    few = min(4, step)
    width = heads * step
    head_at = lax.broadcasted_iota(jnp.int32, (heads, width), 0)
    spread = jnp.where(lax.broadcasted_iota(jnp.int32, (heads, width), 1) // step == head_at, 1.0, 0.0)
    wide = mm(weight_ref[...], spread.astype(BF16))
    lane = lax.broadcasted_iota(jnp.int32, wide.shape, 1)
    weights = [jnp.where(lane % step == i, wide, 0.0).astype(BF16) for i in range(step)]
    for p in range(0, local_res, step):
        projected = None
        for i in range(0, step, few):
            x = pair_ref[p + i : p + i + few].reshape(few * residues, channels)
            normed = layer_normalize(x.astype(F32), gain_ref[...]).astype(BF16)
            left = [normed[j * residues : (j + 1) * residues] for j in range(few)]
            part = mm(jnp.concatenate(left, axis=1), jnp.concatenate(weights[i : i + few], axis=0))
            projected = part if projected is None else projected + part
        out_ref[:, p : p + step] = projected.T.reshape(heads, step, residues).astype(BF16)


def softmax_lanes(scores):
    e = jnp.exp(scores - jnp.max(scores, axis=-1, keepdims=True))
    total = jnp.sum(e, axis=-1, keepdims=True)
    inverse = pl.reciprocal(total, approx=True)
    inverse = inverse * (2.0 - total * inverse)
    return (e * inverse).astype(BF16)


def gate_of(values):
    return 0.5 * jnp.tanh(0.5 * values) + 0.5


def pick_heads(parts, depth):
    lane = lax.broadcasted_iota(jnp.int32, parts[0].shape, 1)
    slot = lane // depth % len(parts)
    picked = parts[-1]
    for j in range(len(parts) - 2, -1, -1):
        picked = jnp.where(slot == j, parts[j], picked)
    return picked


def lane_mask(width, depth, slots, j):
    lane = lax.broadcasted_iota(jnp.int32, (1, width), 1)
    return jnp.where(lane // depth % slots == j, 1.0, 0.0).astype(BF16)


def rows_of(refs, slot, at):
    ref = refs[0].at[slot] if len(refs) == 1 else refs[slot]
    return ref[pl.ds(at, 1)].reshape(ref.shape[1:])


def project_kernel(heads, groups, gain_ref, win_ref, *refs):
    x_refs, (q_ref, k_ref, v_ref, gate_ref) = refs[:-4], refs[-4:]
    seqs, residues, channels = q_ref.shape
    scale = (channels // heads) ** (-0.5)
    batch = largest(seqs, 4)

    def dense(i, carry):
        x = [rows_of(x_refs, t, i * batch + j) for j in range(batch) for t in range(groups)]
        x = jnp.concatenate(x, axis=0).astype(F32)
        normed = layer_normalize(x, gain_ref[...]).astype(BF16)
        some = pl.ds(i * batch, batch)
        shape = (batch, residues, channels)
        q = (mm(normed, win_ref[:, :channels]) * scale).astype(BF16)
        q_ref[some] = q.reshape(shape)
        k_ref[some] = mm(normed, win_ref[:, channels : 2 * channels]).astype(BF16).reshape(shape)
        v_ref[some] = mm(normed, win_ref[:, 2 * channels : 3 * channels]).astype(BF16).reshape(shape)
        gate_ref[some] = gate_of(mm(normed, win_ref[:, 3 * channels :])).reshape(shape)
        return carry

    lax.fori_loop(0, seqs // batch, dense, 0)


def in_turn(tasks, scores_of, weights_of, mixed_of):
    results, scores = [], scores_of(tasks[0])
    for at, task in enumerate(tasks):
        ahead = scores_of(tasks[at + 1]) if at + 1 < len(tasks) else None
        results.append(mixed_of(task, weights_of(task, scores)))
        scores = ahead
    return results


def row_kernel(
    blocks, kinds, by_shifts, gap_ref, place_ref, q_ref, k_ref, v_ref, gate_ref, wout_ref, bias_ref, *refs
):
    x_refs, refs, (bias_scr, gated_scr) = refs[:blocks], refs[blocks:-2], refs[-2:]
    groups, heads, local_res, residues = bias_ref.shape
    out_refs = []
    for kind in kinds[::-1]:
        out_refs.insert(0, refs[-1:])
        refs = refs[:-1]
    seqs, _, channels = q_ref.shape
    depth = channels // heads
    per = LANES // depth
    batch = largest(seqs, 4)
    part_res = local_res // len(kinds)

    def home(slot):
        return slot if blocks == 1 else lax.rem(place_ref[0] - slot + groups, groups)

    def residue_at(place):
        return home(place // local_res) * local_res + place % local_res

    square = (residues, residues)
    residue = lax.broadcasted_iota(jnp.int32, square, 0)
    order = jnp.where(residue == residue_at(lax.broadcasted_iota(jnp.int32, square, 1)), 1.0, 0.0)
    order = order.astype(BF16)
    slots = list(range(groups))
    if by_shifts and blocks == 1:
        slots = [lax.rem(place_ref[0] - t + groups, groups) for t in range(groups)]
    for h in range(heads):
        rows = jnp.concatenate([bias_ref[slot, h] for slot in slots], axis=0)
        bias_scr[h] = mm(rows, order)
    masks = [lane_mask(LANES, depth, per, j) for j in range(per)]
    block_at = residue_at(lax.broadcasted_iota(jnp.int32, (1, residues), 1)) // BLOCK

    def attend(i, carry):
        tasks = [(u, g) for u in range(batch) for g in range(heads // per)]
        at = [i * batch + u for u in range(batch)]
        gaps = []
        for s in at:
            gap = jnp.zeros((1, residues), F32)
            for b in range(residues // BLOCK):
                closed = jnp.where(gap_ref[s, b] == 1, MASKED_SCORE, 0.0)
                gap = jnp.where(block_at == b, closed, gap)
            gaps.append(gap)
        gates = [gate_ref[s] for s in at]

        def lanes(ref, task):
            return ref[at[task[0]], :, task[1] * LANES : (task[1] + 1) * LANES]

        def scores_of(task):
            q = lanes(q_ref, task)
            return mm_nt(
                jnp.concatenate([q * mask for mask in masks], axis=0), lanes(k_ref, task)
            )

        def weights_of(task, scores):
            weights = []
            for j in range(per):
                own = scores[j * residues : (j + 1) * residues]
                own = own + bias_scr[task[1] * per + j] + gaps[task[0]]
                weights.append(softmax_lanes(own))
            return jnp.concatenate(weights, axis=0)

        def mixed_of(task, weights):
            mixed = mm(weights, lanes(v_ref, task))
            return pick_heads([mixed[j * residues : (j + 1) * residues] for j in range(per)], depth)

        attended = in_turn(tasks, scores_of, weights_of, mixed_of)
        halves = heads // per
        for u in range(batch):
            whole = jnp.concatenate(attended[u * halves : (u + 1) * halves], axis=1)
            gated_scr[at[u]] = (whole * gates[u]).astype(BF16)
        return carry

    lax.fori_loop(0, seqs // batch, attend, 0)

    def finish(i, carry):
        x = [rows_of(x_refs, t, i * batch + j) for j in range(batch) for t in range(groups)]
        gated = gated_scr[pl.ds(i * batch, batch)].reshape(batch * residues, channels)
        result = jnp.concatenate(x, axis=0).astype(F32) + mm(gated, wout_ref[...])
        result = result.astype(BF16).reshape(batch, groups, local_res, channels)
        for j in range(batch):
            s = i * batch + j
            for p, (kind, outs) in enumerate(zip(kinds, out_refs)):
                for t in range(groups):
                    rows = result[j, t, p * part_res : (p + 1) * part_res]
                    if kind == STACKED:
                        outs[0][home(t), s] = rows
                    elif blocks == 1:
                        outs[0][lax.rem(place_ref[0] - t + groups, groups), s] = rows
                    else:
                        outs[0][t, s] = rows
        return carry

    lax.fori_loop(0, seqs // batch, finish, 0)


def column_kernel(
    heads, turn, lows, earlier, place_ref, gap_ref, gain_ref, gain2_ref, win_ref, wout_ref,
    widen_ref, shrink_ref, *refs,
):
    pieces, places = [], []
    for kind, low in lows:
        if kind == STACKED:
            pieces += [(refs[0].at[g] if turn else refs[0], low) for g in range(SLOTS if turn else 1)]
            places += [len(places) + g for g in range(SLOTS)]
            refs = refs[1:]
        else:
            pieces += [(ref, low) for ref in refs[:SLOTS]]
            places += [len(places) + lax.rem(place_ref[0] + t, SLOTS) for t in range(SLOTS)]
            refs = refs[SLOTS:]
    done_refs, refs = refs[:earlier], refs[earlier:]
    (out_ref, turned_scr, q_scr, k_scr, v_scr, gate_scr, gated_scr, done_scr) = refs
    local_res, seqs, channels = turned_scr.shape
    depth = channels // heads
    per = LANES // depth
    halves = heads // per
    scale = depth ** (-0.5)
    batch = largest(local_res, 8)
    pair = largest(local_res, 4)
    slabs = local_res // SLAB if turn else 0
    swap = swap_matrix(SLAB, SLAB)
    base = 0
    for done_ref in done_refs:
        out_ref[:, base : base + done_ref.shape[1]] = done_ref[...]
        base += done_ref.shape[1]
    if not turn:
        turned_scr[...] = pieces[0][0][...]
    each = pieces[0][0].shape[0]
    fold = SLAB // each if turn else 1
    for c in range(slabs):
        parts = [
            piece[:, low + c * SLAB : low + (c + 1) * SLAB] for piece, low in pieces
        ]
        blocks = [
            jnp.concatenate(parts[i : i + fold], axis=0).reshape(SLAB * SLAB, channels)
            for i in range(0, len(parts), fold)
        ]
        turned = mm(swap, jnp.concatenate(blocks, axis=1)).astype(BF16)
        for g in range(seqs // SLAB):
            turned_scr[c * SLAB : (c + 1) * SLAB, g * SLAB : (g + 1) * SLAB] = turned[
                :, g * channels : (g + 1) * channels
            ].reshape(SLAB, SLAB, channels)

    def dense(i, carry):
        x = turned_scr[pl.ds(i * batch, batch)].reshape(batch * seqs, channels)
        normed = layer_normalize(x.astype(F32), gain_ref[...]).astype(BF16)
        q = (mm(normed, win_ref[:, :channels]) * scale).astype(BF16)
        k = mm(normed, win_ref[:, channels : 2 * channels]).astype(BF16)
        v = mm(normed, win_ref[:, 2 * channels : 3 * channels]).astype(BF16)
        gates = gate_of(mm(normed, win_ref[:, 3 * channels :]))
        shape = (batch, seqs, channels)
        q_scr[pl.ds(i * batch, batch)] = q.reshape(shape)
        k_scr[pl.ds(i * batch, batch)] = k.reshape(shape)
        v_scr[pl.ds(i * batch, batch)] = v.reshape(shape)
        gate_scr[pl.ds(i * batch, batch)] = gates.reshape(shape)
        return carry

    lax.fori_loop(0, local_res // batch, dense, 0)

    mask = jnp.broadcast_to(
        jnp.where(gap_ref[...] == 1, MASKED_SCORE, 0.0), (seqs, halves * seqs)
    )
    masks = [lane_mask(channels, depth, per, j) for j in range(per)]
    blank = jnp.zeros((seqs, LANES), BF16)

    def diagonal(values):
        rows = []
        for g in range(halves):
            own = values[:, g * LANES : (g + 1) * LANES]
            rows.append(jnp.concatenate([own if i == g else blank for i in range(halves)], axis=1))
        return jnp.concatenate(rows, axis=0)

    def attend(i, carry):
        at = [i * pair + u for u in range(pair)]
        gates = [gate_scr[r] for r in at]

        def scores_of(u):
            k = k_scr[at[u]]
            return mm_nt(jnp.concatenate([k * m for m in masks], axis=0), diagonal(q_scr[at[u]]))

        def weights_of(u, scores):
            weights = []
            for j in range(per):
                own = scores[j * seqs : (j + 1) * seqs] + mask
                e = jnp.exp(own - jnp.max(own, axis=0, keepdims=True))
                weights.append((e * (1.0 / jnp.sum(e, axis=0, keepdims=True))).astype(BF16))
            return weights

        def mixed_of(u, weights):
            v = v_scr[at[u]].T
            mixed = [None] * heads
            for j in range(per):
                left = [v[(g * per + j) * depth : (g * per + j + 1) * depth] for g in range(halves)]
                both = mm(jnp.concatenate(left, axis=0), weights[j])
                for g in range(halves):
                    mixed[g * per + j] = both[
                        g * depth : (g + 1) * depth, g * seqs : (g + 1) * seqs
                    ]
            return jnp.concatenate(mixed, axis=0).T

        attended = in_turn(list(range(pair)), scores_of, weights_of, mixed_of)
        for u in range(pair):
            gated_scr[at[u]] = (attended[u] * gates[u]).astype(BF16)
        return carry

    lax.fori_loop(0, local_res // pair, attend, 0)

    def finish(i, carry):
        x = turned_scr[pl.ds(i * batch, batch)].reshape(batch * seqs, channels)
        gated = gated_scr[pl.ds(i * batch, batch)].reshape(batch * seqs, channels)
        second = (x.astype(F32) + mm(gated, wout_ref[...])).astype(BF16)
        second_f = second.astype(F32)
        normed = layer_normalize(second_f, gain2_ref[...]).astype(BF16)
        hidden = jnp.maximum(mm(normed, widen_ref[...]), 0.0).astype(BF16)
        result = (second_f + mm(hidden, shrink_ref[...])).astype(BF16)
        done_scr[pl.ds(i * batch, batch)] = result.reshape(batch, seqs, channels)
        return carry

    lax.fori_loop(0, local_res // batch, finish, 0)
    if not turn:
        out_ref[...] = done_scr[...]
    for c in range(slabs):
        blocks = [
            done_scr[c * SLAB : (c + 1) * SLAB, g * SLAB : (g + 1) * SLAB].reshape(
                SLAB * SLAB, channels
            )
            for g in range(seqs // SLAB)
        ]
        turned = mm(swap, jnp.concatenate(blocks, axis=1)).astype(BF16)
        start = base + c * SLAB
        for g in range(seqs // SLAB):
            own = turned[:, g * channels : (g + 1) * channels].reshape(SLAB, SLAB, channels)
            for e in range(fold):
                place = places[g * fold + e]
                out_ref[pl.ds(place * each, each), start : start + SLAB] = own[
                    e * each : (e + 1) * each
                ]


def largest(total, bound):
    return max(d for d in range(1, bound + 1) if total % d == 0)


def in_vmem(count):
    return [pl.BlockSpec(memory_space=pltpu.VMEM)] * count


def shifts(blocks, sign):
    arrived = [blocks[0]]
    for k in range(1, SLOTS):
        to = [(i, (i + sign * k) % SLOTS) for i in range(SLOTS)]
        arrived.append(lax.ppermute(blocks[k], "res", to))
    return arrived


def body(
    aligned_chain_features,
    pair_representation_state,
    gap_block_flags,
    pair_norm_gain,
    pair_head_weight,
    horizontal_scaling_factor,
    row_input_weight,
    horizontal_final_matrix,
    vertical_scaling_factor,
    column_input_weight,
    vertical_final_matrix,
    feedforward_scaling_factor,
    feedforward_widen_matrix,
    feedforward_shrink_matrix,
):
    groups = lax.axis_size("res")
    total_seqs, local_res, channels = aligned_chain_features.shape
    residues = pair_representation_state.shape[1]
    heads = pair_head_weight.shape[1]
    local_seqs = total_seqs // groups
    by_shifts = groups == SLOTS and local_res % SLAB == 0 and local_seqs % SLAB == 0
    seq_parts = 2 if by_shifts else 1
    res_parts = local_res // SLAB if by_shifts else 1
    part_seqs = local_seqs // seq_parts
    part_total = total_seqs // seq_parts
    part_res = local_res // res_parts
    here = lax.axis_index("res")

    def exchange(values):
        return lax.all_to_all(values, "res", split_axis=0, concat_axis=0, tiled=True)

    def kernel_call(kernel, name, micros, in_specs, out_shapes, scratch):
        return pl.pallas_call(
            kernel,
            out_shape=[jax.ShapeDtypeStruct(*shape) for shape in out_shapes],
            in_specs=in_specs,
            out_specs=in_vmem(len(out_shapes)),
            scratch_shapes=scratch,
            compiler_params=pltpu.CompilerParams(vmem_limit_bytes=VMEM_BYTES),
            cost_estimate=pl.CostEstimate(
                flops=int(micros * 1e9), bytes_accessed=1 << 20, transcendentals=0
            ),
            name=name,
        )

    def half_of(half):
        return aligned_chain_features[half * part_total : (half + 1) * part_total].reshape(
            groups, part_seqs, local_res, channels
        )

    if by_shifts:
        values = half_of(0)
        blocks = [
            lax.dynamic_index_in_dim(values, lax.rem(here + k, groups), 0, keepdims=False)
            for k in range(groups)
        ]
        arrived = [shifts(blocks, 1)]
    else:
        arrived = [[exchange(half_of(0))]]
    (bias_local,) = kernel_call(
        bias_kernel, "pair_bias", 5, in_vmem(3), [((heads, local_res, residues), BF16)], [],
    )(pair_norm_gain[None, :], pair_head_weight, pair_representation_state)
    if by_shifts:
        bias_local, *arrived[0] = lax.optimization_barrier((bias_local, *arrived[0]))
        bias_all = jnp.stack(shifts([bias_local] * groups, 1))
    else:
        bias_all = lax.all_gather(bias_local, "res", axis=0, tiled=False)
    for half in range(1, seq_parts):
        bias_all, values = lax.optimization_barrier((bias_all, half_of(half)))
        arrived.append([exchange(values)])

    column_block = (here * local_res) // BLOCK
    col_gap = lax.dynamic_slice_in_dim(gap_block_flags, column_block, 1, 1).reshape(1, total_seqs)
    place = here.astype(jnp.int32)[None]

    def row_attention(part, kinds, *after):
        gap = lax.dynamic_slice_in_dim(
            gap_block_flags, part * part_total + here * part_seqs, part_seqs, 0
        )
        by_row = (part_seqs, residues, channels)
        blocks = arrived[part]
        projected = kernel_call(
            functools.partial(project_kernel, heads, groups), "row_project", 3,
            in_vmem(2 + len(blocks)),
            [(by_row, BF16), (by_row, BF16), (by_row, BF16), (by_row, F32)], [],
        )(horizontal_scaling_factor[None, :], row_input_weight, *blocks)
        operands = (*projected, horizontal_final_matrix, bias_all, *blocks)
        count = local_res // len(kinds)
        outs = []
        for kind in kinds:
            outs += [((groups, part_seqs, count, channels), BF16)]
        return kernel_call(
            functools.partial(row_kernel, len(blocks), kinds, by_shifts), "row_attention", 10,
            [pl.BlockSpec(memory_space=pltpu.SMEM)] * 2
            + in_vmem(len(operands))
            + [pl.BlockSpec(memory_space=pl.ANY)] * len(after),
            outs,
            [
                pltpu.VMEM((heads, residues, residues), F32),
                pltpu.VMEM((part_seqs, residues, channels), BF16),
            ],
        )(gap, place, *operands, *after)

    if by_shifts:
        first = row_attention(0, (STACKED,))
        returned = exchange(first[0])
        kinds = (LISTED,) * (res_parts - 1) + (STACKED,)
        second = row_attention(1, kinds, first[0])
        finals = [shifts(list(part), -1) for part in second[:-1]]
        finals.append([exchange(second[-1])])
    else:
        (first,) = row_attention(0, (STACKED,))
        back = exchange(first).reshape(total_seqs, local_res, channels)
        kinds, finals = (STACKED,), [[jnp.swapaxes(back, 0, 1)]]
    done = []
    for c in range(res_parts):
        pieces, lows, own_gap = finals[c], ((kinds[c], 0),), col_gap
        if by_shifts:
            pieces, lows = [returned] + pieces, ((STACKED, c * part_res),) + lows
        if kinds[c] == LISTED:
            second = col_gap[:, part_total:].reshape(groups, part_seqs)
            second = jnp.roll(second, -here, axis=0).reshape(1, part_total)
            own_gap = jnp.concatenate([col_gap[:, :part_total], second], axis=1)
        before = done if c == res_parts - 1 else []
        if not by_shifts:
            shape = (part_res, total_seqs, channels)
        else:
            shape = (total_seqs, part_res * (1 + len(before)), channels)
        held = pltpu.VMEM((part_res, total_seqs, channels), BF16)
        done += kernel_call(
            functools.partial(column_kernel, heads, by_shifts, lows, len(before)),
            "column_transition", 10,
            [pl.BlockSpec(memory_space=pltpu.SMEM)] + in_vmem(7 + len(pieces) + len(before)),
            [(shape, BF16)],
            [
                held, held, held, held,
                pltpu.VMEM((part_res, total_seqs, channels), F32),
                held, held,
            ],
        )(
            place, own_gap.reshape(total_seqs, 1), vertical_scaling_factor[None, :], feedforward_scaling_factor[None, :],
            column_input_weight, vertical_final_matrix, feedforward_widen_matrix,
            feedforward_shrink_matrix, *pieces, *before,
        )
    return done[-1] if by_shifts else jnp.swapaxes(done[-1], 0, 1)


def solution(mesh):
    placed = (
        P("dp", "res", None),
        P(("dp", "res"), None, None),
        P("dp", None),
    ) + (P(),) * 11
    return jax.shard_map(
        body, mesh=mesh, in_specs=placed, out_specs=P("dp", "res", None), check_vma=False
    )
```

```python
import functools

import jax
import jax.numpy as jnp
from jax import lax
from jax.experimental import pallas as pl
from jax.experimental.pallas import tpu as pltpu
from jax.sharding import PartitionSpec as P

BLOCK = 128
EPSILON = 1e-05
MASKED_SCORE = -1000000000.0
LANES = 128
SLAB = 16
SLOTS = 8
STACKED, LISTED = 0, 1
F32 = jnp.float32
BF16 = jnp.bfloat16
VMEM_BYTES = 28 * 1024 * 1024


def layer_normalize(values_f, scale_gain):
    centred = values_f - jnp.mean(values_f, axis=-1, keepdims=True)
    spread = jnp.mean(centred * centred, axis=-1, keepdims=True)
    return centred * lax.rsqrt(spread + EPSILON) * scale_gain


def mm(lhs, rhs):
    return jnp.dot(lhs, rhs, preferred_element_type=F32)


def mm_nt(lhs, rhs):
    return lax.dot_general(lhs, rhs, (((1,), (1,)), ((), ())), preferred_element_type=F32)


def swap_matrix(outer, inner):
    size = outer * inner
    to = lax.broadcasted_iota(jnp.int32, (size, size), 0)
    come = lax.broadcasted_iota(jnp.int32, (size, size), 1)
    source = lax.rem(to, outer) * inner + lax.div(to, outer)
    return jnp.where(come == source, 1.0, 0.0).astype(BF16)


def bias_kernel(gain_ref, weight_ref, pair_ref, out_ref):
    local_res, residues, channels = pair_ref.shape
    heads = out_ref.shape[0]
    step = min(SLAB, local_res)
    few = min(4, step)
    width = heads * step
    head_at = lax.broadcasted_iota(jnp.int32, (heads, width), 0)
    spread = jnp.where(lax.broadcasted_iota(jnp.int32, (heads, width), 1) // step == head_at, 1.0, 0.0)
    wide = mm(weight_ref[...], spread.astype(BF16))
    lane = lax.broadcasted_iota(jnp.int32, wide.shape, 1)
    weights = [jnp.where(lane % step == i, wide, 0.0).astype(BF16) for i in range(step)]
    for p in range(0, local_res, step):
        projected = None
        for i in range(0, step, few):
            x = pair_ref[p + i : p + i + few].reshape(few * residues, channels)
            normed = layer_normalize(x.astype(F32), gain_ref[...]).astype(BF16)
            left = [normed[j * residues : (j + 1) * residues] for j in range(few)]
            part = mm(jnp.concatenate(left, axis=1), jnp.concatenate(weights[i : i + few], axis=0))
            projected = part if projected is None else projected + part
        out_ref[:, p : p + step] = projected.T.reshape(heads, step, residues).astype(BF16)


def softmax_lanes(scores):
    e = jnp.exp(scores - jnp.max(scores, axis=-1, keepdims=True))
    total = jnp.sum(e, axis=-1, keepdims=True)
    inverse = pl.reciprocal(total, approx=True)
    inverse = inverse * (2.0 - total * inverse)
    return (e * inverse).astype(BF16)


def gate_of(values):
    return 0.5 * jnp.tanh(0.5 * values) + 0.5


def pick_heads(parts, depth):
    lane = lax.broadcasted_iota(jnp.int32, parts[0].shape, 1)
    slot = lane // depth % len(parts)
    picked = parts[-1]
    for j in range(len(parts) - 2, -1, -1):
        picked = jnp.where(slot == j, parts[j], picked)
    return picked


def lane_mask(width, depth, slots, j):
    lane = lax.broadcasted_iota(jnp.int32, (1, width), 1)
    return jnp.where(lane // depth % slots == j, 1.0, 0.0).astype(BF16)


def rows_of(refs, slot, at):
    ref = refs[0].at[slot] if len(refs) == 1 else refs[slot]
    return ref[pl.ds(at, 1)].reshape(ref.shape[1:])


def project_kernel(heads, groups, gain_ref, win_ref, *refs):
    x_refs, (q_ref, k_ref, v_ref, gate_ref) = refs[:-4], refs[-4:]
    seqs, residues, channels = q_ref.shape
    scale = (channels // heads) ** (-0.5)
    batch = largest(seqs, 4)

    def dense(i, carry):
        x = [rows_of(x_refs, t, i * batch + j) for j in range(batch) for t in range(groups)]
        x = jnp.concatenate(x, axis=0).astype(F32)
        normed = layer_normalize(x, gain_ref[...]).astype(BF16)
        some = pl.ds(i * batch, batch)
        shape = (batch, residues, channels)
        q = (mm(normed, win_ref[:, :channels]) * scale).astype(BF16)
        q_ref[some] = q.reshape(shape)
        k_ref[some] = mm(normed, win_ref[:, channels : 2 * channels]).astype(BF16).reshape(shape)
        v_ref[some] = mm(normed, win_ref[:, 2 * channels : 3 * channels]).astype(BF16).reshape(shape)
        gate_ref[some] = gate_of(mm(normed, win_ref[:, 3 * channels :])).reshape(shape)
        return carry

    lax.fori_loop(0, seqs // batch, dense, 0)


def in_turn(tasks, scores_of, weights_of, mixed_of):
    results, scores = [], scores_of(tasks[0])
    for at, task in enumerate(tasks):
        ahead = scores_of(tasks[at + 1]) if at + 1 < len(tasks) else None
        results.append(mixed_of(task, weights_of(task, scores)))
        scores = ahead
    return results


def row_kernel(
    blocks, kinds, by_shifts, gap_ref, place_ref, q_ref, k_ref, v_ref, gate_ref, wout_ref, bias_ref, *refs
):
    x_refs, refs, (bias_scr, gated_scr) = refs[:blocks], refs[blocks:-2], refs[-2:]
    groups, heads, local_res, residues = bias_ref.shape
    out_refs = []
    for kind in kinds[::-1]:
        out_refs.insert(0, refs[-1:])
        refs = refs[:-1]
    seqs, _, channels = q_ref.shape
    depth = channels // heads
    per = LANES // depth
    batch = largest(seqs, 4)
    part_res = local_res // len(kinds)

    def home(slot):
        return slot if blocks == 1 else lax.rem(place_ref[0] - slot + groups, groups)

    def residue_at(place):
        return home(place // local_res) * local_res + place % local_res

    square = (residues, residues)
    residue = lax.broadcasted_iota(jnp.int32, square, 0)
    order = jnp.where(residue == residue_at(lax.broadcasted_iota(jnp.int32, square, 1)), 1.0, 0.0)
    order = order.astype(BF16)
    slots = list(range(groups))
    if by_shifts and blocks == 1:
        slots = [lax.rem(place_ref[0] - t + groups, groups) for t in range(groups)]
    for h in range(heads):
        rows = jnp.concatenate([bias_ref[slot, h] for slot in slots], axis=0)
        bias_scr[h] = mm(rows, order)
    masks = [lane_mask(LANES, depth, per, j) for j in range(per)]
    block_at = residue_at(lax.broadcasted_iota(jnp.int32, (1, residues), 1)) // BLOCK

    def attend(i, carry):
        tasks = [(u, g) for u in range(batch) for g in range(heads // per)]
        at = [i * batch + u for u in range(batch)]
        gaps = []
        for s in at:
            gap = jnp.zeros((1, residues), F32)
            for b in range(residues // BLOCK):
                closed = jnp.where(gap_ref[s, b] == 1, MASKED_SCORE, 0.0)
                gap = jnp.where(block_at == b, closed, gap)
            gaps.append(gap)
        gates = [gate_ref[s] for s in at]

        def lanes(ref, task):
            return ref[at[task[0]], :, task[1] * LANES : (task[1] + 1) * LANES]

        def scores_of(task):
            q = lanes(q_ref, task)
            return mm_nt(
                jnp.concatenate([q * mask for mask in masks], axis=0), lanes(k_ref, task)
            )

        def weights_of(task, scores):
            weights = []
            for j in range(per):
                own = scores[j * residues : (j + 1) * residues]
                own = own + bias_scr[task[1] * per + j] + gaps[task[0]]
                weights.append(softmax_lanes(own))
            return jnp.concatenate(weights, axis=0)

        def mixed_of(task, weights):
            mixed = mm(weights, lanes(v_ref, task))
            return pick_heads([mixed[j * residues : (j + 1) * residues] for j in range(per)], depth)

        attended = in_turn(tasks, scores_of, weights_of, mixed_of)
        halves = heads // per
        for u in range(batch):
            whole = jnp.concatenate(attended[u * halves : (u + 1) * halves], axis=1)
            gated_scr[at[u]] = (whole * gates[u]).astype(BF16)
        return carry

    lax.fori_loop(0, seqs // batch, attend, 0)

    def finish(i, carry):
        x = [rows_of(x_refs, t, i * batch + j) for j in range(batch) for t in range(groups)]
        gated = gated_scr[pl.ds(i * batch, batch)].reshape(batch * residues, channels)
        result = jnp.concatenate(x, axis=0).astype(F32) + mm(gated, wout_ref[...])
        result = result.astype(BF16).reshape(batch, groups, local_res, channels)
        for j in range(batch):
            s = i * batch + j
            for p, (kind, outs) in enumerate(zip(kinds, out_refs)):
                for t in range(groups):
                    rows = result[j, t, p * part_res : (p + 1) * part_res]
                    if kind == STACKED:
                        outs[0][home(t), s] = rows
                    elif blocks == 1:
                        outs[0][lax.rem(place_ref[0] - t + groups, groups), s] = rows
                    else:
                        outs[0][t, s] = rows
        return carry

    lax.fori_loop(0, seqs // batch, finish, 0)


def column_kernel(
    heads, turn, lows, earlier, place_ref, gap_ref, gain_ref, gain2_ref, win_ref, wout_ref,
    widen_ref, shrink_ref, *refs,
):
    pieces, places = [], []
    for kind, low in lows:
        if kind == STACKED:
            pieces += [(refs[0].at[g] if turn else refs[0], low) for g in range(SLOTS if turn else 1)]
            places += [len(places) + g for g in range(SLOTS)]
            refs = refs[1:]
        else:
            pieces += [(ref, low) for ref in refs[:SLOTS]]
            places += [len(places) + lax.rem(place_ref[0] + t, SLOTS) for t in range(SLOTS)]
            refs = refs[SLOTS:]
    refs = refs[1:] if earlier else refs
    (out_hbm, turned_scr, q_scr, k_scr, v_scr, gate_scr, gated_scr, done_scr, out_ref, sem) = refs
    local_res, seqs, channels = turned_scr.shape
    depth = channels // heads
    per = LANES // depth
    halves = heads // per
    scale = depth ** (-0.5)
    batch = largest(local_res, 8)
    pair = largest(local_res, 8)
    slabs = local_res // SLAB if turn else 0
    swap = swap_matrix(SLAB, SLAB)
    if not turn:
        turned_scr[...] = pieces[0][0][...]
    each = pieces[0][0].shape[0]
    fold = SLAB // each if turn else 1
    for c in range(slabs):
        parts = [
            piece[:, low + c * SLAB : low + (c + 1) * SLAB] for piece, low in pieces
        ]
        blocks = [
            jnp.concatenate(parts[i : i + fold], axis=0).reshape(SLAB * SLAB, channels)
            for i in range(0, len(parts), fold)
        ]
        turned = mm(swap, jnp.concatenate(blocks, axis=1)).astype(BF16)
        for g in range(seqs // SLAB):
            turned_scr[c * SLAB : (c + 1) * SLAB, g * SLAB : (g + 1) * SLAB] = turned[
                :, g * channels : (g + 1) * channels
            ].reshape(SLAB, SLAB, channels)

    def dense(i, carry):
        x = turned_scr[pl.ds(i * batch, batch)].reshape(batch * seqs, channels)
        normed = layer_normalize(x.astype(F32), gain_ref[...]).astype(BF16)
        q = (mm(normed, win_ref[:, :channels]) * scale).astype(BF16)
        k = mm(normed, win_ref[:, channels : 2 * channels]).astype(BF16)
        v = mm(normed, win_ref[:, 2 * channels : 3 * channels]).astype(BF16)
        gates = gate_of(mm(normed, win_ref[:, 3 * channels :]))
        shape = (batch, seqs, channels)
        q_scr[pl.ds(i * batch, batch)] = q.reshape(shape)
        k_scr[pl.ds(i * batch, batch)] = k.reshape(shape)
        v_scr[pl.ds(i * batch, batch)] = v.reshape(shape)
        gate_scr[pl.ds(i * batch, batch)] = gates.reshape(shape)
        return carry

    lax.fori_loop(0, local_res // batch, dense, 0)

    mask = jnp.broadcast_to(
        jnp.where(gap_ref[...] == 1, MASKED_SCORE, 0.0), (seqs, halves * seqs)
    )
    masks = [lane_mask(channels, depth, per, j) for j in range(per)]
    blank = jnp.zeros((seqs, LANES), BF16)

    def diagonal(values):
        rows = []
        for g in range(halves):
            own = values[:, g * LANES : (g + 1) * LANES]
            rows.append(jnp.concatenate([own if i == g else blank for i in range(halves)], axis=1))
        return jnp.concatenate(rows, axis=0)

    def attend(i, carry):
        at = [i * pair + u for u in range(pair)]
        gates = [gate_scr[r] for r in at]

        def scores_of(u):
            k = k_scr[at[u]]
            return mm_nt(jnp.concatenate([k * m for m in masks], axis=0), diagonal(q_scr[at[u]]))

        def weights_of(u, scores):
            weights = []
            for j in range(per):
                own = scores[j * seqs : (j + 1) * seqs] + mask
                e = jnp.exp(own - jnp.max(own, axis=0, keepdims=True))
                weights.append((e * (1.0 / jnp.sum(e, axis=0, keepdims=True))).astype(BF16))
            return weights

        def mixed_of(u, weights):
            v = v_scr[at[u]].T
            mixed = [None] * heads
            for j in range(per):
                left = [v[(g * per + j) * depth : (g * per + j + 1) * depth] for g in range(halves)]
                both = mm(jnp.concatenate(left, axis=0), weights[j])
                for g in range(halves):
                    mixed[g * per + j] = both[
                        g * depth : (g + 1) * depth, g * seqs : (g + 1) * seqs
                    ]
            return jnp.concatenate(mixed, axis=0).T

        attended = in_turn(list(range(pair)), scores_of, weights_of, mixed_of)
        for u in range(pair):
            gated_scr[at[u]] = (attended[u] * gates[u]).astype(BF16)
        return carry

    lax.fori_loop(0, local_res // pair, attend, 0)

    def finish(i, carry):
        x = turned_scr[pl.ds(i * batch, batch)].reshape(batch * seqs, channels)
        gated = gated_scr[pl.ds(i * batch, batch)].reshape(batch * seqs, channels)
        second = (x.astype(F32) + mm(gated, wout_ref[...])).astype(BF16)
        second_f = second.astype(F32)
        normed = layer_normalize(second_f, gain2_ref[...]).astype(BF16)
        hidden = jnp.maximum(mm(normed, widen_ref[...]), 0.0).astype(BF16)
        result = (second_f + mm(hidden, shrink_ref[...])).astype(BF16)
        done_scr[pl.ds(i * batch, batch)] = result.reshape(batch, seqs, channels)
        return carry

    lax.fori_loop(0, local_res // batch, finish, 0)
    if not turn:
        out_ref[...] = done_scr[...]
    for c in range(slabs):
        blocks = [
            done_scr[c * SLAB : (c + 1) * SLAB, g * SLAB : (g + 1) * SLAB].reshape(
                SLAB * SLAB, channels
            )
            for g in range(seqs // SLAB)
        ]
        turned = mm(swap, jnp.concatenate(blocks, axis=1)).astype(BF16)
        start = c * SLAB
        for g in range(seqs // SLAB):
            own = turned[:, g * channels : (g + 1) * channels].reshape(SLAB, SLAB, channels)
            for e in range(fold):
                place = places[g * fold + e]
                out_ref[pl.ds(place * each, each), start : start + SLAB] = own[
                    e * each : (e + 1) * each
                ]
    target = out_hbm.at[:, earlier : earlier + local_res] if turn else out_hbm
    copy = pltpu.make_async_copy(out_ref, target, sem)
    copy.start()
    copy.wait()


def largest(total, bound):
    return max(d for d in range(1, bound + 1) if total % d == 0)


def in_vmem(count):
    return [pl.BlockSpec(memory_space=pltpu.VMEM)] * count


def shifts(blocks, sign):
    arrived = [blocks[0]]
    for k in range(1, SLOTS):
        to = [(i, (i + sign * k) % SLOTS) for i in range(SLOTS)]
        arrived.append(lax.ppermute(blocks[k], "res", to))
    return arrived


def body(
    aligned_chain_features,
    pair_representation_state,
    gap_block_flags,
    pair_norm_gain,
    pair_head_weight,
    horizontal_scaling_factor,
    row_input_weight,
    horizontal_final_matrix,
    vertical_scaling_factor,
    column_input_weight,
    vertical_final_matrix,
    feedforward_scaling_factor,
    feedforward_widen_matrix,
    feedforward_shrink_matrix,
):
    groups = lax.axis_size("res")
    total_seqs, local_res, channels = aligned_chain_features.shape
    residues = pair_representation_state.shape[1]
    heads = pair_head_weight.shape[1]
    local_seqs = total_seqs // groups
    by_shifts = groups == SLOTS and local_res % SLAB == 0 and local_seqs % SLAB == 0
    seq_parts = 2 if by_shifts else 1
    res_parts = local_res // SLAB if by_shifts else 1
    part_seqs = local_seqs // seq_parts
    part_total = total_seqs // seq_parts
    part_res = local_res // res_parts
    here = lax.axis_index("res")

    def exchange(values):
        return lax.all_to_all(values, "res", split_axis=0, concat_axis=0, tiled=True)

    def kernel_call(
        kernel, name, micros, in_specs, out_shapes, scratch, space=pltpu.VMEM, aliases={}
    ):
        return pl.pallas_call(
            kernel,
            out_shape=[jax.ShapeDtypeStruct(*shape) for shape in out_shapes],
            in_specs=in_specs,
            out_specs=[pl.BlockSpec(memory_space=space)] * len(out_shapes),
            input_output_aliases=aliases,
            scratch_shapes=scratch,
            compiler_params=pltpu.CompilerParams(vmem_limit_bytes=VMEM_BYTES),
            cost_estimate=pl.CostEstimate(
                flops=int(micros * 1e9), bytes_accessed=1 << 20, transcendentals=0
            ),
            name=name,
        )

    def half_of(half):
        return aligned_chain_features[half * part_total : (half + 1) * part_total].reshape(
            groups, part_seqs, local_res, channels
        )

    if by_shifts:
        blocks = [
            lax.dynamic_slice_in_dim(
                aligned_chain_features, lax.rem(here + k, groups) * part_seqs, part_seqs, 0
            )
            for k in range(groups)
        ]
        arrived = [shifts(blocks, 1)]
    else:
        arrived = [[exchange(half_of(0))]]
    (bias_local,) = kernel_call(
        bias_kernel, "pair_bias", 5, in_vmem(3), [((heads, local_res, residues), BF16)], [],
    )(pair_norm_gain[None, :], pair_head_weight, pair_representation_state)
    if by_shifts:
        bias_local, arrived[0][1] = lax.optimization_barrier((bias_local, arrived[0][1]))
        bias_all = jnp.stack(shifts([bias_local] * groups, 1))
    else:
        bias_all = lax.all_gather(bias_local, "res", axis=0, tiled=False)
    for half in range(1, seq_parts):
        bias_all, values = lax.optimization_barrier((bias_all, half_of(half)))
        arrived.append([exchange(values)])

    column_block = (here * local_res) // BLOCK
    col_gap = lax.dynamic_slice_in_dim(gap_block_flags, column_block, 1, 1).reshape(1, total_seqs)
    place = here.astype(jnp.int32)[None]

    def row_attention(part, kinds, *after):
        gap = lax.dynamic_slice_in_dim(
            gap_block_flags, part * part_total + here * part_seqs, part_seqs, 0
        )
        by_row = (part_seqs, residues, channels)
        blocks = arrived[part]
        projected = kernel_call(
            functools.partial(project_kernel, heads, groups), "row_project", 3,
            in_vmem(2 + len(blocks)),
            [(by_row, BF16), (by_row, BF16), (by_row, BF16), (by_row, F32)], [],
        )(horizontal_scaling_factor[None, :], row_input_weight, *blocks)
        operands = (*projected, horizontal_final_matrix, bias_all, *blocks)
        count = local_res // len(kinds)
        outs = []
        for kind in kinds:
            outs += [((groups, part_seqs, count, channels), BF16)]
        return kernel_call(
            functools.partial(row_kernel, len(blocks), kinds, by_shifts), "row_attention", 10,
            [pl.BlockSpec(memory_space=pltpu.SMEM)] * 2
            + in_vmem(len(operands))
            + [pl.BlockSpec(memory_space=pl.ANY)] * len(after),
            outs,
            [
                pltpu.VMEM((heads, residues, residues), F32),
                pltpu.VMEM((part_seqs, residues, channels), BF16),
            ],
        )(gap, place, *operands, *after)

    if by_shifts:
        first = row_attention(0, (STACKED,))
        returned = exchange(first[0])
        kinds = (LISTED,) * (res_parts - 1) + (STACKED,)
        second = row_attention(1, kinds, first[0])
        finals = [shifts(list(part), -1) for part in second[:-1]]
        finals.append([exchange(second[-1])])
    else:
        (first,) = row_attention(0, (STACKED,))
        back = exchange(first).reshape(total_seqs, local_res, channels)
        kinds, finals = (STACKED,), [[jnp.swapaxes(back, 0, 1)]]
    done = []
    for c in range(res_parts):
        pieces, lows, own_gap = finals[c], ((kinds[c], 0),), col_gap
        if by_shifts:
            pieces, lows = [returned] + pieces, ((STACKED, c * part_res),) + lows
        if kinds[c] == LISTED:
            second = col_gap[:, part_total:].reshape(groups, part_seqs)
            second = jnp.roll(second, -here, axis=0).reshape(1, part_total)
            own_gap = jnp.concatenate([col_gap[:, :part_total], second], axis=1)
        shape = (total_seqs, local_res, channels)
        if not by_shifts:
            shape = (part_res, total_seqs, channels)
        part_shape = (total_seqs, part_res, channels) if by_shifts else shape
        before = done[-1:]
        at = 8 + len(pieces)
        held = pltpu.VMEM((part_res, total_seqs, channels), BF16)
        done += kernel_call(
            functools.partial(column_kernel, heads, by_shifts, lows, c * part_res),
            "column_transition", 10,
            [pl.BlockSpec(memory_space=pltpu.SMEM)]
            + in_vmem(7 + len(pieces))
            + [pl.BlockSpec(memory_space=pl.ANY)] * len(before),
            [(shape, BF16)],
            [
                held, held, held, held,
                pltpu.VMEM((part_res, total_seqs, channels), F32),
                held, held,
                pltpu.VMEM(part_shape, BF16),
                pltpu.SemaphoreType.DMA,
            ],
            pl.ANY,
            {at: 0} if before else {},
        )(
            place, own_gap.reshape(total_seqs, 1), vertical_scaling_factor[None, :], feedforward_scaling_factor[None, :],
            column_input_weight, vertical_final_matrix, feedforward_widen_matrix,
            feedforward_shrink_matrix, *pieces, *before,
        )
    return done[-1] if by_shifts else jnp.swapaxes(done[-1], 0, 1)


def solution(mesh):
    placed = (
        P("dp", "res", None),
        P(("dp", "res"), None, None),
        P("dp", None),
    ) + (P(),) * 11
    return jax.shard_map(
        body, mesh=mesh, in_specs=placed, out_specs=P("dp", "res", None), check_vma=False
    )
```

```python
import functools

import jax
import jax.numpy as jnp
from jax import lax
from jax.experimental import pallas as pl
from jax.experimental.pallas import tpu as pltpu
from jax.sharding import PartitionSpec as P

BLOCK = 128
EPSILON = 1e-05
MASKED_SCORE = -1000000000.0
LANES = 128
SLAB = 16
SLOTS = 8
STACKED, LISTED = 0, 1
F32 = jnp.float32
BF16 = jnp.bfloat16
VMEM_BYTES = 28 * 1024 * 1024


def layer_normalize(values_f, scale_gain):
    centred = values_f - jnp.mean(values_f, axis=-1, keepdims=True)
    spread = jnp.mean(centred * centred, axis=-1, keepdims=True)
    return centred * lax.rsqrt(spread + EPSILON) * scale_gain


def mm(lhs, rhs):
    return jnp.dot(lhs, rhs, preferred_element_type=F32)


def mm_nt(lhs, rhs):
    return lax.dot_general(lhs, rhs, (((1,), (1,)), ((), ())), preferred_element_type=F32)


def swap_matrix(outer, inner):
    size = outer * inner
    to = lax.broadcasted_iota(jnp.int32, (size, size), 0)
    come = lax.broadcasted_iota(jnp.int32, (size, size), 1)
    source = lax.rem(to, outer) * inner + lax.div(to, outer)
    return jnp.where(come == source, 1.0, 0.0).astype(BF16)


def bias_kernel(gain_ref, weight_ref, pair_ref, out_ref):
    local_res, residues, channels = pair_ref.shape
    heads = out_ref.shape[0]
    step = min(SLAB, local_res)
    few = min(4, step)
    width = heads * step
    head_at = lax.broadcasted_iota(jnp.int32, (heads, width), 0)
    spread = jnp.where(lax.broadcasted_iota(jnp.int32, (heads, width), 1) // step == head_at, 1.0, 0.0)
    wide = mm(weight_ref[...], spread.astype(BF16))
    lane = lax.broadcasted_iota(jnp.int32, wide.shape, 1)
    weights = [jnp.where(lane % step == i, wide, 0.0).astype(BF16) for i in range(step)]
    for p in range(0, local_res, step):
        projected = None
        for i in range(0, step, few):
            x = pair_ref[p + i : p + i + few].reshape(few * residues, channels)
            normed = layer_normalize(x.astype(F32), gain_ref[...]).astype(BF16)
            left = [normed[j * residues : (j + 1) * residues] for j in range(few)]
            part = mm(jnp.concatenate(left, axis=1), jnp.concatenate(weights[i : i + few], axis=0))
            projected = part if projected is None else projected + part
        out_ref[:, p : p + step] = projected.T.reshape(heads, step, residues).astype(BF16)


def softmax_lanes(scores):
    e = jnp.exp(scores - jnp.max(scores, axis=-1, keepdims=True))
    total = jnp.sum(e, axis=-1, keepdims=True)
    inverse = pl.reciprocal(total, approx=True)
    inverse = inverse * (2.0 - total * inverse)
    return (e * inverse).astype(BF16)


def gate_of(values):
    return 0.5 * jnp.tanh(0.5 * values) + 0.5


def pick_heads(parts, depth):
    lane = lax.broadcasted_iota(jnp.int32, parts[0].shape, 1)
    slot = lane // depth % len(parts)
    picked = parts[-1]
    for j in range(len(parts) - 2, -1, -1):
        picked = jnp.where(slot == j, parts[j], picked)
    return picked


def lane_mask(width, depth, slots, j):
    lane = lax.broadcasted_iota(jnp.int32, (1, width), 1)
    return jnp.where(lane // depth % slots == j, 1.0, 0.0).astype(BF16)


def rows_of(refs, slot, at):
    ref = refs[0].at[slot] if len(refs) == 1 else refs[slot]
    return ref[pl.ds(at, 1)].reshape(ref.shape[1:])


def project_kernel(heads, groups, gain_ref, win_ref, *refs):
    x_refs, (q_ref, k_ref, v_ref, gate_ref) = refs[:-4], refs[-4:]
    seqs, residues, channels = q_ref.shape
    scale = (channels // heads) ** (-0.5)
    batch = largest(seqs, 4)

    def dense(i, carry):
        x = [rows_of(x_refs, t, i * batch + j) for j in range(batch) for t in range(groups)]
        x = jnp.concatenate(x, axis=0).astype(F32)
        normed = layer_normalize(x, gain_ref[...]).astype(BF16)
        some = pl.ds(i * batch, batch)
        shape = (batch, residues, channels)
        q = (mm(normed, win_ref[:, :channels]) * scale).astype(BF16)
        q_ref[some] = q.reshape(shape)
        k_ref[some] = mm(normed, win_ref[:, channels : 2 * channels]).astype(BF16).reshape(shape)
        v_ref[some] = mm(normed, win_ref[:, 2 * channels : 3 * channels]).astype(BF16).reshape(shape)
        gate_ref[some] = gate_of(mm(normed, win_ref[:, 3 * channels :])).reshape(shape)
        return carry

    lax.fori_loop(0, seqs // batch, dense, 0)


def in_turn(tasks, scores_of, weights_of, mixed_of):
    results, scores = [], scores_of(tasks[0])
    for at, task in enumerate(tasks):
        ahead = scores_of(tasks[at + 1]) if at + 1 < len(tasks) else None
        results.append(mixed_of(task, weights_of(task, scores)))
        scores = ahead
    return results


def row_kernel(
    blocks, kinds, by_shifts, gap_ref, place_ref, q_ref, k_ref, v_ref, gate_ref, wout_ref, bias_ref, *refs
):
    x_refs, refs, (bias_scr, gated_scr) = refs[:blocks], refs[blocks:-2], refs[-2:]
    groups, heads, local_res, residues = bias_ref.shape
    out_refs = []
    for kind in kinds[::-1]:
        out_refs.insert(0, refs[-1:])
        refs = refs[:-1]
    seqs, _, channels = q_ref.shape
    depth = channels // heads
    per = LANES // depth
    batch = largest(seqs, 4)
    part_res = local_res // len(kinds)

    def home(slot):
        return slot if blocks == 1 else lax.rem(place_ref[0] - slot + groups, groups)

    def residue_at(place):
        return home(place // local_res) * local_res + place % local_res

    square = (residues, residues)
    residue = lax.broadcasted_iota(jnp.int32, square, 0)
    order = jnp.where(residue == residue_at(lax.broadcasted_iota(jnp.int32, square, 1)), 1.0, 0.0)
    order = order.astype(BF16)
    slots = list(range(groups))
    if by_shifts and blocks == 1:
        slots = [lax.rem(place_ref[0] - t + groups, groups) for t in range(groups)]
    for h in range(heads):
        rows = jnp.concatenate([bias_ref[slot, h] for slot in slots], axis=0)
        bias_scr[h] = mm(rows, order)
    masks = [lane_mask(LANES, depth, per, j) for j in range(per)]
    block_at = residue_at(lax.broadcasted_iota(jnp.int32, (1, residues), 1)) // BLOCK

    def attend(i, carry):
        tasks = [(u, g) for u in range(batch) for g in range(heads // per)]
        at = [i * batch + u for u in range(batch)]
        gaps = []
        for s in at:
            gap = jnp.zeros((1, residues), F32)
            for b in range(residues // BLOCK):
                closed = jnp.where(gap_ref[s, b] == 1, MASKED_SCORE, 0.0)
                gap = jnp.where(block_at == b, closed, gap)
            gaps.append(gap)
        gates = [gate_ref[s] for s in at]

        def lanes(ref, task):
            return ref[at[task[0]], :, task[1] * LANES : (task[1] + 1) * LANES]

        def scores_of(task):
            q = lanes(q_ref, task)
            return mm_nt(
                jnp.concatenate([q * mask for mask in masks], axis=0), lanes(k_ref, task)
            )

        def weights_of(task, scores):
            weights = []
            for j in range(per):
                own = scores[j * residues : (j + 1) * residues]
                own = own + bias_scr[task[1] * per + j] + gaps[task[0]]
                weights.append(softmax_lanes(own))
            return jnp.concatenate(weights, axis=0)

        def mixed_of(task, weights):
            mixed = mm(weights, lanes(v_ref, task))
            return pick_heads([mixed[j * residues : (j + 1) * residues] for j in range(per)], depth)

        attended = in_turn(tasks, scores_of, weights_of, mixed_of)
        halves = heads // per
        for u in range(batch):
            whole = jnp.concatenate(attended[u * halves : (u + 1) * halves], axis=1)
            gated_scr[at[u]] = (whole * gates[u]).astype(BF16)
        return carry

    lax.fori_loop(0, seqs // batch, attend, 0)

    def finish(i, carry):
        x = [rows_of(x_refs, t, i * batch + j) for j in range(batch) for t in range(groups)]
        gated = gated_scr[pl.ds(i * batch, batch)].reshape(batch * residues, channels)
        result = jnp.concatenate(x, axis=0).astype(F32) + mm(gated, wout_ref[...])
        result = result.astype(BF16).reshape(batch, groups, local_res, channels)
        for j in range(batch):
            s = i * batch + j
            for p, (kind, outs) in enumerate(zip(kinds, out_refs)):
                for t in range(groups):
                    rows = result[j, t, p * part_res : (p + 1) * part_res]
                    if kind == STACKED:
                        outs[0][home(t), s] = rows
                    elif blocks == 1:
                        outs[0][lax.rem(place_ref[0] - t + groups, groups), s] = rows
                    else:
                        outs[0][t, s] = rows
        return carry

    lax.fori_loop(0, seqs // batch, finish, 0)


def column_kernel(
    heads, turn, lows, earlier, place_ref, gap_ref, gain_ref, gain2_ref, win_ref, wout_ref,
    widen_ref, shrink_ref, *refs,
):
    pieces, places = [], []
    for kind, low in lows:
        if kind == STACKED:
            pieces += [(refs[0].at[g] if turn else refs[0], low) for g in range(SLOTS if turn else 1)]
            places += [len(places) + g for g in range(SLOTS)]
            refs = refs[1:]
        else:
            pieces += [(ref, low) for ref in refs[:SLOTS]]
            places += [len(places) + lax.rem(place_ref[0] + t, SLOTS) for t in range(SLOTS)]
            refs = refs[SLOTS:]
    refs = refs[1:] if earlier else refs
    (out_hbm, turned_scr, q_scr, k_scr, v_scr, gate_scr, gated_scr, done_scr, out_ref, sem) = refs
    local_res, seqs, channels = turned_scr.shape
    depth = channels // heads
    per = LANES // depth
    halves = heads // per
    scale = depth ** (-0.5)
    batch = largest(local_res, 8)
    pair = largest(local_res, 4)
    slabs = local_res // SLAB if turn else 0
    swap = swap_matrix(SLAB, SLAB)
    if not turn:
        turned_scr[...] = pieces[0][0][...]
    each = pieces[0][0].shape[0]
    fold = SLAB // each if turn else 1
    for c in range(slabs):
        parts = [
            piece[:, low + c * SLAB : low + (c + 1) * SLAB] for piece, low in pieces
        ]
        blocks = [
            jnp.concatenate(parts[i : i + fold], axis=0).reshape(SLAB * SLAB, channels)
            for i in range(0, len(parts), fold)
        ]
        turned = mm(swap, jnp.concatenate(blocks, axis=1)).astype(BF16)
        for g in range(seqs // SLAB):
            turned_scr[c * SLAB : (c + 1) * SLAB, g * SLAB : (g + 1) * SLAB] = turned[
                :, g * channels : (g + 1) * channels
            ].reshape(SLAB, SLAB, channels)

    def dense(i, carry):
        x = turned_scr[pl.ds(i * batch, batch)].reshape(batch * seqs, channels)
        normed = layer_normalize(x.astype(F32), gain_ref[...]).astype(BF16)
        q = (mm(normed, win_ref[:, :channels]) * scale).astype(BF16)
        k = mm(normed, win_ref[:, channels : 2 * channels]).astype(BF16)
        v = mm(normed, win_ref[:, 2 * channels : 3 * channels]).astype(BF16)
        gates = gate_of(mm(normed, win_ref[:, 3 * channels :]))
        shape = (batch, seqs, channels)
        q_scr[pl.ds(i * batch, batch)] = q.reshape(shape)
        k_scr[pl.ds(i * batch, batch)] = k.reshape(shape)
        v_scr[pl.ds(i * batch, batch)] = v.reshape(shape)
        gate_scr[pl.ds(i * batch, batch)] = gates.reshape(shape)
        return carry

    lax.fori_loop(0, local_res // batch, dense, 0)

    mask = jnp.broadcast_to(
        jnp.where(gap_ref[...] == 1, MASKED_SCORE, 0.0), (seqs, halves * seqs)
    )
    masks = [lane_mask(channels, depth, per, j) for j in range(per)]
    blank = jnp.zeros((seqs, LANES), BF16)

    def diagonal(values):
        rows = []
        for g in range(halves):
            own = values[:, g * LANES : (g + 1) * LANES]
            rows.append(jnp.concatenate([own if i == g else blank for i in range(halves)], axis=1))
        return jnp.concatenate(rows, axis=0)

    def attend(i, carry):
        at = [i * pair + u for u in range(pair)]
        gates = [gate_scr[r] for r in at]

        def scores_of(u):
            k = k_scr[at[u]]
            return mm_nt(jnp.concatenate([k * m for m in masks], axis=0), diagonal(q_scr[at[u]]))

        def weights_of(u, scores):
            weights = []
            for j in range(per):
                own = scores[j * seqs : (j + 1) * seqs] + mask
                e = jnp.exp(own - jnp.max(own, axis=0, keepdims=True))
                weights.append((e * (1.0 / jnp.sum(e, axis=0, keepdims=True))).astype(BF16))
            return weights

        def mixed_of(u, weights):
            v = v_scr[at[u]].T
            mixed = [None] * heads
            for j in range(per):
                left = [v[(g * per + j) * depth : (g * per + j + 1) * depth] for g in range(halves)]
                both = mm(jnp.concatenate(left, axis=0), weights[j])
                for g in range(halves):
                    mixed[g * per + j] = both[
                        g * depth : (g + 1) * depth, g * seqs : (g + 1) * seqs
                    ]
            return jnp.concatenate(mixed, axis=0).T

        attended = in_turn(list(range(pair)), scores_of, weights_of, mixed_of)
        for u in range(pair):
            gated_scr[at[u]] = (attended[u] * gates[u]).astype(BF16)
        return carry

    lax.fori_loop(0, local_res // pair, attend, 0)

    def finish(i, carry):
        x = turned_scr[pl.ds(i * batch, batch)].reshape(batch * seqs, channels)
        gated = gated_scr[pl.ds(i * batch, batch)].reshape(batch * seqs, channels)
        second = (x.astype(F32) + mm(gated, wout_ref[...])).astype(BF16)
        second_f = second.astype(F32)
        normed = layer_normalize(second_f, gain2_ref[...]).astype(BF16)
        hidden = jnp.maximum(mm(normed, widen_ref[...]), 0.0).astype(BF16)
        result = (second_f + mm(hidden, shrink_ref[...])).astype(BF16)
        done_scr[pl.ds(i * batch, batch)] = result.reshape(batch, seqs, channels)
        return carry

    lax.fori_loop(0, local_res // batch, finish, 0)
    if not turn:
        out_ref[...] = done_scr[...]
    for c in range(slabs):
        blocks = [
            done_scr[c * SLAB : (c + 1) * SLAB, g * SLAB : (g + 1) * SLAB].reshape(
                SLAB * SLAB, channels
            )
            for g in range(seqs // SLAB)
        ]
        turned = mm(swap, jnp.concatenate(blocks, axis=1)).astype(BF16)
        start = c * SLAB
        for g in range(seqs // SLAB):
            own = turned[:, g * channels : (g + 1) * channels].reshape(SLAB, SLAB, channels)
            for e in range(fold):
                place = places[g * fold + e]
                out_ref[pl.ds(place * each, each), start : start + SLAB] = own[
                    e * each : (e + 1) * each
                ]
    target = out_hbm.at[:, earlier : earlier + local_res] if turn else out_hbm
    copy = pltpu.make_async_copy(out_ref, target, sem)
    copy.start()
    copy.wait()


def largest(total, bound):
    return max(d for d in range(1, bound + 1) if total % d == 0)


def in_vmem(count):
    return [pl.BlockSpec(memory_space=pltpu.VMEM)] * count


def shifts(blocks, sign):
    arrived = [blocks[0]]
    for k in range(1, SLOTS):
        to = [(i, (i + sign * k) % SLOTS) for i in range(SLOTS)]
        arrived.append(lax.ppermute(blocks[k], "res", to))
    return arrived


def body(
    aligned_chain_features,
    pair_representation_state,
    gap_block_flags,
    pair_norm_gain,
    pair_head_weight,
    horizontal_scaling_factor,
    row_input_weight,
    horizontal_final_matrix,
    vertical_scaling_factor,
    column_input_weight,
    vertical_final_matrix,
    feedforward_scaling_factor,
    feedforward_widen_matrix,
    feedforward_shrink_matrix,
):
    groups = lax.axis_size("res")
    total_seqs, local_res, channels = aligned_chain_features.shape
    residues = pair_representation_state.shape[1]
    heads = pair_head_weight.shape[1]
    local_seqs = total_seqs // groups
    by_shifts = groups == SLOTS and local_res % SLAB == 0 and local_seqs % SLAB == 0
    seq_parts = 2 if by_shifts else 1
    res_parts = local_res // SLAB if by_shifts else 1
    part_seqs = local_seqs // seq_parts
    part_total = total_seqs // seq_parts
    part_res = local_res // res_parts
    here = lax.axis_index("res")

    def exchange(values):
        return lax.all_to_all(values, "res", split_axis=0, concat_axis=0, tiled=True)

    def kernel_call(
        kernel, name, micros, in_specs, out_shapes, scratch, space=pltpu.VMEM, aliases={}
    ):
        return pl.pallas_call(
            kernel,
            out_shape=[jax.ShapeDtypeStruct(*shape) for shape in out_shapes],
            in_specs=in_specs,
            out_specs=[pl.BlockSpec(memory_space=space)] * len(out_shapes),
            input_output_aliases=aliases,
            scratch_shapes=scratch,
            compiler_params=pltpu.CompilerParams(vmem_limit_bytes=VMEM_BYTES),
            cost_estimate=pl.CostEstimate(
                flops=int(micros * 1e9), bytes_accessed=1 << 20, transcendentals=0
            ),
            name=name,
        )

    def half_of(half):
        return aligned_chain_features[half * part_total : (half + 1) * part_total].reshape(
            groups, part_seqs, local_res, channels
        )

    if by_shifts:
        blocks = [
            lax.dynamic_slice_in_dim(
                aligned_chain_features, lax.rem(here + k, groups) * part_seqs, part_seqs, 0
            )
            for k in range(groups)
        ]
        arrived = [shifts(blocks, 1)]
    else:
        arrived = [[exchange(half_of(0))]]
    (bias_local,) = kernel_call(
        bias_kernel, "pair_bias", 5, in_vmem(3), [((heads, local_res, residues), BF16)], [],
    )(pair_norm_gain[None, :], pair_head_weight, pair_representation_state)
    if by_shifts:
        bias_local, arrived[0][1] = lax.optimization_barrier((bias_local, arrived[0][1]))
        bias_all = jnp.stack(shifts([bias_local] * groups, 1))
    else:
        bias_all = lax.all_gather(bias_local, "res", axis=0, tiled=False)
    for half in range(1, seq_parts):
        bias_all, values, *arrived[0] = lax.optimization_barrier(
            (bias_all, half_of(half), *arrived[0])
        )
        arrived.append([exchange(values)])

    column_block = (here * local_res) // BLOCK
    col_gap = lax.dynamic_slice_in_dim(gap_block_flags, column_block, 1, 1).reshape(1, total_seqs)
    place = here.astype(jnp.int32)[None]

    def row_attention(part, kinds, *after):
        gap = lax.dynamic_slice_in_dim(
            gap_block_flags, part * part_total + here * part_seqs, part_seqs, 0
        )
        by_row = (part_seqs, residues, channels)
        blocks = arrived[part]
        projected = kernel_call(
            functools.partial(project_kernel, heads, groups), "row_project", 3,
            in_vmem(2 + len(blocks)),
            [(by_row, BF16), (by_row, BF16), (by_row, BF16), (by_row, F32)], [],
        )(horizontal_scaling_factor[None, :], row_input_weight, *blocks)
        operands = (*projected, horizontal_final_matrix, bias_all, *blocks)
        count = local_res // len(kinds)
        outs = []
        for kind in kinds:
            outs += [((groups, part_seqs, count, channels), BF16)]
        return kernel_call(
            functools.partial(row_kernel, len(blocks), kinds, by_shifts), "row_attention", 10,
            [pl.BlockSpec(memory_space=pltpu.SMEM)] * 2
            + in_vmem(len(operands))
            + [pl.BlockSpec(memory_space=pl.ANY)] * len(after),
            outs,
            [
                pltpu.VMEM((heads, residues, residues), F32),
                pltpu.VMEM((part_seqs, residues, channels), BF16),
            ],
        )(gap, place, *operands, *after)

    if by_shifts:
        first = row_attention(0, (STACKED,))
        returned = exchange(first[0])
        kinds = (LISTED,) * (res_parts - 1) + (STACKED,)
        second = row_attention(1, kinds, first[0])
        finals = [shifts(list(part), -1) for part in second[:-1]]
        finals.append([exchange(second[-1])])
    else:
        (first,) = row_attention(0, (STACKED,))
        back = exchange(first).reshape(total_seqs, local_res, channels)
        kinds, finals = (STACKED,), [[jnp.swapaxes(back, 0, 1)]]
    done = []
    for c in range(res_parts):
        pieces, lows, own_gap = finals[c], ((kinds[c], 0),), col_gap
        if by_shifts:
            pieces, lows = [returned] + pieces, ((STACKED, c * part_res),) + lows
        if kinds[c] == LISTED:
            second = col_gap[:, part_total:].reshape(groups, part_seqs)
            second = jnp.roll(second, -here, axis=0).reshape(1, part_total)
            own_gap = jnp.concatenate([col_gap[:, :part_total], second], axis=1)
        shape = (total_seqs, local_res, channels)
        if not by_shifts:
            shape = (part_res, total_seqs, channels)
        part_shape = (total_seqs, part_res, channels) if by_shifts else shape
        before = done[-1:]
        at = 8 + len(pieces)
        held = pltpu.VMEM((part_res, total_seqs, channels), BF16)
        done += kernel_call(
            functools.partial(column_kernel, heads, by_shifts, lows, c * part_res),
            "column_transition", 10,
            [pl.BlockSpec(memory_space=pltpu.SMEM)]
            + in_vmem(7 + len(pieces))
            + [pl.BlockSpec(memory_space=pl.ANY)] * len(before),
            [(shape, BF16)],
            [
                held, held, held, held,
                pltpu.VMEM((part_res, total_seqs, channels), F32),
                held, held,
                pltpu.VMEM(part_shape, BF16),
                pltpu.SemaphoreType.DMA,
            ],
            pl.ANY,
            {at: 0} if before else {},
        )(
            place, own_gap.reshape(total_seqs, 1), vertical_scaling_factor[None, :], feedforward_scaling_factor[None, :],
            column_input_weight, vertical_final_matrix, feedforward_widen_matrix,
            feedforward_shrink_matrix, *pieces, *before,
        )
    return done[-1] if by_shifts else jnp.swapaxes(done[-1], 0, 1)


def solution(mesh):
    placed = (
        P("dp", "res", None),
        P(("dp", "res"), None, None),
        P("dp", None),
    ) + (P(),) * 11
    return jax.shard_map(
        body, mesh=mesh, in_specs=placed, out_specs=P("dp", "res", None), check_vma=False
    )
```

```python
import functools

import jax
import jax.numpy as jnp
from jax import lax
from jax.experimental import pallas as pl
from jax.experimental.pallas import tpu as pltpu
from jax.sharding import PartitionSpec as P

BLOCK = 128
EPSILON = 1e-05
MASKED_SCORE = -1000000000.0
LANES = 128
SLAB = 16
SLOTS = 8
STACKED, LISTED = 0, 1
F32 = jnp.float32
BF16 = jnp.bfloat16
VMEM_BYTES = 28 * 1024 * 1024


def layer_normalize(values_f, scale_gain):
    centred = values_f - jnp.mean(values_f, axis=-1, keepdims=True)
    spread = jnp.mean(centred * centred, axis=-1, keepdims=True)
    return centred * lax.rsqrt(spread + EPSILON) * scale_gain


def mm(lhs, rhs):
    return jnp.dot(lhs, rhs, preferred_element_type=F32)


def mm_nt(lhs, rhs):
    return lax.dot_general(lhs, rhs, (((1,), (1,)), ((), ())), preferred_element_type=F32)


def swap_matrix(outer, inner):
    size = outer * inner
    to = lax.broadcasted_iota(jnp.int32, (size, size), 0)
    come = lax.broadcasted_iota(jnp.int32, (size, size), 1)
    source = lax.rem(to, outer) * inner + lax.div(to, outer)
    return jnp.where(come == source, 1.0, 0.0).astype(BF16)


def bias_kernel(gain_ref, weight_ref, pair_ref, out_ref):
    local_res, residues, channels = pair_ref.shape
    heads = out_ref.shape[0]
    step = min(SLAB, local_res)
    few = min(4, step)
    width = heads * step
    head_at = lax.broadcasted_iota(jnp.int32, (heads, width), 0)
    spread = jnp.where(lax.broadcasted_iota(jnp.int32, (heads, width), 1) // step == head_at, 1.0, 0.0)
    wide = mm(weight_ref[...], spread.astype(BF16))
    lane = lax.broadcasted_iota(jnp.int32, wide.shape, 1)
    weights = [jnp.where(lane % step == i, wide, 0.0).astype(BF16) for i in range(step)]
    for p in range(0, local_res, step):
        projected = None
        for i in range(0, step, few):
            x = pair_ref[p + i : p + i + few].reshape(few * residues, channels)
            normed = layer_normalize(x.astype(F32), gain_ref[...]).astype(BF16)
            left = [normed[j * residues : (j + 1) * residues] for j in range(few)]
            part = mm(jnp.concatenate(left, axis=1), jnp.concatenate(weights[i : i + few], axis=0))
            projected = part if projected is None else projected + part
        out_ref[:, p : p + step] = projected.T.reshape(heads, step, residues).astype(BF16)


def softmax_lanes(scores):
    e = jnp.exp(scores - jnp.max(scores, axis=-1, keepdims=True))
    total = jnp.sum(e, axis=-1, keepdims=True)
    inverse = pl.reciprocal(total, approx=True)
    inverse = inverse * (2.0 - total * inverse)
    return (e * inverse).astype(BF16)


def gate_of(values):
    return 0.5 * jnp.tanh(0.5 * values) + 0.5


def pick_heads(parts, depth):
    lane = lax.broadcasted_iota(jnp.int32, parts[0].shape, 1)
    slot = lane // depth % len(parts)
    picked = parts[-1]
    for j in range(len(parts) - 2, -1, -1):
        picked = jnp.where(slot == j, parts[j], picked)
    return picked


def lane_mask(width, depth, slots, j):
    lane = lax.broadcasted_iota(jnp.int32, (1, width), 1)
    return jnp.where(lane // depth % slots == j, 1.0, 0.0).astype(BF16)


def rows_of(refs, slot, at):
    ref = refs[0].at[slot] if len(refs) == 1 else refs[slot]
    return ref[pl.ds(at, 1)].reshape(ref.shape[1:])


def project_kernel(heads, groups, gain_ref, win_ref, *refs):
    x_refs, (q_ref, k_ref, v_ref, gate_ref) = refs[:-4], refs[-4:]
    seqs, residues, channels = q_ref.shape
    scale = (channels // heads) ** (-0.5)
    batch = largest(seqs, 4)

    def dense(i, carry):
        x = [rows_of(x_refs, t, i * batch + j) for j in range(batch) for t in range(groups)]
        x = jnp.concatenate(x, axis=0).astype(F32)
        normed = layer_normalize(x, gain_ref[...]).astype(BF16)
        some = pl.ds(i * batch, batch)
        shape = (batch, residues, channels)
        q = (mm(normed, win_ref[:, :channels]) * scale).astype(BF16)
        q_ref[some] = q.reshape(shape)
        k_ref[some] = mm(normed, win_ref[:, channels : 2 * channels]).astype(BF16).reshape(shape)
        v_ref[some] = mm(normed, win_ref[:, 2 * channels : 3 * channels]).astype(BF16).reshape(shape)
        gate_ref[some] = gate_of(mm(normed, win_ref[:, 3 * channels :])).reshape(shape)
        return carry

    lax.fori_loop(0, seqs // batch, dense, 0)


def in_turn(tasks, scores_of, weights_of, mixed_of):
    results, scores = [], scores_of(tasks[0])
    for at, task in enumerate(tasks):
        ahead = scores_of(tasks[at + 1]) if at + 1 < len(tasks) else None
        results.append(mixed_of(task, weights_of(task, scores)))
        scores = ahead
    return results


def row_kernel(
    blocks, kinds, by_shifts, gap_ref, place_ref, q_ref, k_ref, v_ref, gate_ref, wout_ref, bias_ref, *refs
):
    x_refs, refs, (bias_scr, gated_scr) = refs[:blocks], refs[blocks:-2], refs[-2:]
    groups, heads, local_res, residues = bias_ref.shape
    out_refs = []
    for kind in kinds[::-1]:
        out_refs.insert(0, refs[-1:])
        refs = refs[:-1]
    seqs, _, channels = q_ref.shape
    depth = channels // heads
    per = LANES // depth
    batch = largest(seqs, 4)
    part_res = local_res // len(kinds)

    def home(slot):
        return slot if blocks == 1 else lax.rem(place_ref[0] - slot + groups, groups)

    def residue_at(place):
        return home(place // local_res) * local_res + place % local_res

    square = (residues, residues)
    residue = lax.broadcasted_iota(jnp.int32, square, 0)
    order = jnp.where(residue == residue_at(lax.broadcasted_iota(jnp.int32, square, 1)), 1.0, 0.0)
    order = order.astype(BF16)
    slots = list(range(groups))
    if by_shifts and blocks == 1:
        slots = [lax.rem(place_ref[0] - t + groups, groups) for t in range(groups)]
    for h in range(heads):
        rows = jnp.concatenate([bias_ref[slot, h] for slot in slots], axis=0)
        bias_scr[h] = mm(rows, order)
    masks = [lane_mask(LANES, depth, per, j) for j in range(per)]
    block_at = residue_at(lax.broadcasted_iota(jnp.int32, (1, residues), 1)) // BLOCK

    def attend(i, carry):
        tasks = [(u, g) for u in range(batch) for g in range(heads // per)]
        at = [i * batch + u for u in range(batch)]
        gaps = []
        for s in at:
            gap = jnp.zeros((1, residues), F32)
            for b in range(residues // BLOCK):
                closed = jnp.where(gap_ref[s, b] == 1, MASKED_SCORE, 0.0)
                gap = jnp.where(block_at == b, closed, gap)
            gaps.append(gap)
        gates = [gate_ref[s] for s in at]

        def lanes(ref, task):
            return ref[at[task[0]], :, task[1] * LANES : (task[1] + 1) * LANES]

        def scores_of(task):
            q = lanes(q_ref, task)
            return mm_nt(
                jnp.concatenate([q * mask for mask in masks], axis=0), lanes(k_ref, task)
            )

        def weights_of(task, scores):
            weights = []
            for j in range(per):
                own = scores[j * residues : (j + 1) * residues]
                own = own + bias_scr[task[1] * per + j] + gaps[task[0]]
                weights.append(softmax_lanes(own))
            return jnp.concatenate(weights, axis=0)

        def mixed_of(task, weights):
            mixed = mm(weights, lanes(v_ref, task))
            return pick_heads([mixed[j * residues : (j + 1) * residues] for j in range(per)], depth)

        attended = in_turn(tasks, scores_of, weights_of, mixed_of)
        halves = heads // per
        for u in range(batch):
            whole = jnp.concatenate(attended[u * halves : (u + 1) * halves], axis=1)
            gated_scr[at[u]] = (whole * gates[u]).astype(BF16)
        return carry

    lax.fori_loop(0, seqs // batch, attend, 0)

    def finish(i, carry):
        x = [rows_of(x_refs, t, i * batch + j) for j in range(batch) for t in range(groups)]
        gated = gated_scr[pl.ds(i * batch, batch)].reshape(batch * residues, channels)
        result = jnp.concatenate(x, axis=0).astype(F32) + mm(gated, wout_ref[...])
        result = result.astype(BF16).reshape(batch, groups, local_res, channels)
        for j in range(batch):
            s = i * batch + j
            for p, (kind, outs) in enumerate(zip(kinds, out_refs)):
                for t in range(groups):
                    rows = result[j, t, p * part_res : (p + 1) * part_res]
                    if kind == STACKED:
                        outs[0][home(t), s] = rows
                    elif blocks == 1:
                        outs[0][lax.rem(place_ref[0] - t + groups, groups), s] = rows
                    else:
                        outs[0][t, s] = rows
        return carry

    lax.fori_loop(0, seqs // batch, finish, 0)


def column_kernel(
    heads, turn, lows, earlier, place_ref, gap_ref, gain_ref, gain2_ref, win_ref, wout_ref,
    widen_ref, shrink_ref, *refs,
):
    pieces, places = [], []
    for kind, low in lows:
        if kind == STACKED:
            pieces += [(refs[0].at[g] if turn else refs[0], low) for g in range(SLOTS if turn else 1)]
            places += [len(places) + g for g in range(SLOTS)]
            refs = refs[1:]
        else:
            pieces += [(ref, low) for ref in refs[:SLOTS]]
            places += [len(places) + lax.rem(place_ref[0] + t, SLOTS) for t in range(SLOTS)]
            refs = refs[SLOTS:]
    refs = refs[1:] if earlier else refs
    (out_hbm, turned_scr, q_scr, k_scr, v_scr, gate_scr, gated_scr, done_scr, out_ref, sem) = refs
    local_res, seqs, channels = turned_scr.shape
    depth = channels // heads
    per = LANES // depth
    halves = heads // per
    scale = depth ** (-0.5)
    batch = largest(local_res, 8)
    pair = largest(local_res, 4)
    slabs = local_res // SLAB if turn else 0
    swap = swap_matrix(SLAB, SLAB)
    if not turn:
        turned_scr[...] = pieces[0][0][...]
    each = pieces[0][0].shape[0]
    fold = SLAB // each if turn else 1
    for c in range(slabs):
        parts = [
            piece[:, low + c * SLAB : low + (c + 1) * SLAB] for piece, low in pieces
        ]
        blocks = [
            jnp.concatenate(parts[i : i + fold], axis=0).reshape(SLAB * SLAB, channels)
            for i in range(0, len(parts), fold)
        ]
        turned = mm(swap, jnp.concatenate(blocks, axis=1)).astype(BF16)
        for g in range(seqs // SLAB):
            turned_scr[c * SLAB : (c + 1) * SLAB, g * SLAB : (g + 1) * SLAB] = turned[
                :, g * channels : (g + 1) * channels
            ].reshape(SLAB, SLAB, channels)

    def dense(i, carry):
        x = turned_scr[pl.ds(i * batch, batch)].reshape(batch * seqs, channels)
        normed = layer_normalize(x.astype(F32), gain_ref[...]).astype(BF16)
        q = (mm(normed, win_ref[:, :channels]) * scale).astype(BF16)
        k = mm(normed, win_ref[:, channels : 2 * channels]).astype(BF16)
        v = mm(normed, win_ref[:, 2 * channels : 3 * channels]).astype(BF16)
        gates = gate_of(mm(normed, win_ref[:, 3 * channels :]))
        shape = (batch, seqs, channels)
        q_scr[pl.ds(i * batch, batch)] = q.reshape(shape)
        k_scr[pl.ds(i * batch, batch)] = k.reshape(shape)
        v_scr[pl.ds(i * batch, batch)] = v.reshape(shape)
        gate_scr[pl.ds(i * batch, batch)] = gates.reshape(shape)
        return carry

    lax.fori_loop(0, local_res // batch, dense, 0)

    mask = jnp.broadcast_to(
        jnp.where(gap_ref[...] == 1, MASKED_SCORE, 0.0), (seqs, halves * seqs)
    )
    masks = [lane_mask(channels, depth, per, j) for j in range(per)]
    blank = jnp.zeros((seqs, LANES), BF16)

    def diagonal(values):
        rows = []
        for g in range(halves):
            own = values[:, g * LANES : (g + 1) * LANES]
            rows.append(jnp.concatenate([own if i == g else blank for i in range(halves)], axis=1))
        return jnp.concatenate(rows, axis=0)

    def attend(i, carry):
        at = [i * pair + u for u in range(pair)]
        gates = [gate_scr[r] for r in at]

        def scores_of(u):
            k = k_scr[at[u]]
            return mm_nt(jnp.concatenate([k * m for m in masks], axis=0), diagonal(q_scr[at[u]]))

        def weights_of(u, scores):
            weights = []
            for j in range(per):
                own = scores[j * seqs : (j + 1) * seqs] + mask
                e = jnp.exp(own - jnp.max(own, axis=0, keepdims=True))
                weights.append((e * (1.0 / jnp.sum(e, axis=0, keepdims=True))).astype(BF16))
            return weights

        def mixed_of(u, weights):
            v = v_scr[at[u]].T
            mixed = [None] * heads
            for j in range(per):
                left = [v[(g * per + j) * depth : (g * per + j + 1) * depth] for g in range(halves)]
                both = mm(jnp.concatenate(left, axis=0), weights[j])
                for g in range(halves):
                    mixed[g * per + j] = both[
                        g * depth : (g + 1) * depth, g * seqs : (g + 1) * seqs
                    ]
            return jnp.concatenate(mixed, axis=0).T

        attended = in_turn(list(range(pair)), scores_of, weights_of, mixed_of)
        for u in range(pair):
            gated_scr[at[u]] = (attended[u] * gates[u]).astype(BF16)
        return carry

    lax.fori_loop(0, local_res // pair, attend, 0)

    def finish(i, carry):
        x = turned_scr[pl.ds(i * batch, batch)].reshape(batch * seqs, channels)
        gated = gated_scr[pl.ds(i * batch, batch)].reshape(batch * seqs, channels)
        second = (x.astype(F32) + mm(gated, wout_ref[...])).astype(BF16)
        second_f = second.astype(F32)
        normed = layer_normalize(second_f, gain2_ref[...]).astype(BF16)
        hidden = jnp.maximum(mm(normed, widen_ref[...]), 0.0).astype(BF16)
        result = (second_f + mm(hidden, shrink_ref[...])).astype(BF16)
        done_scr[pl.ds(i * batch, batch)] = result.reshape(batch, seqs, channels)
        return carry

    lax.fori_loop(0, local_res // batch, finish, 0)
    if not turn:
        out_ref[...] = done_scr[...]
    for c in range(slabs):
        blocks = [
            done_scr[c * SLAB : (c + 1) * SLAB, g * SLAB : (g + 1) * SLAB].reshape(
                SLAB * SLAB, channels
            )
            for g in range(seqs // SLAB)
        ]
        turned = mm(swap, jnp.concatenate(blocks, axis=1)).astype(BF16)
        start = c * SLAB
        for g in range(seqs // SLAB):
            own = turned[:, g * channels : (g + 1) * channels].reshape(SLAB, SLAB, channels)
            for e in range(fold):
                place = places[g * fold + e]
                out_ref[pl.ds(place * each, each), start : start + SLAB] = own[
                    e * each : (e + 1) * each
                ]
    target = out_hbm.at[:, earlier : earlier + local_res] if turn else out_hbm
    copy = pltpu.make_async_copy(out_ref, target, sem)
    copy.start()
    copy.wait()


def largest(total, bound):
    return max(d for d in range(1, bound + 1) if total % d == 0)


def in_vmem(count):
    return [pl.BlockSpec(memory_space=pltpu.VMEM)] * count


def shifts(blocks, sign):
    arrived = [blocks[0]]
    for k in range(1, SLOTS):
        to = [(i, (i + sign * k) % SLOTS) for i in range(SLOTS)]
        arrived.append(lax.ppermute(blocks[k], "res", to))
    return arrived


def body(
    aligned_chain_features,
    pair_representation_state,
    gap_block_flags,
    pair_norm_gain,
    pair_head_weight,
    horizontal_scaling_factor,
    row_input_weight,
    horizontal_final_matrix,
    vertical_scaling_factor,
    column_input_weight,
    vertical_final_matrix,
    feedforward_scaling_factor,
    feedforward_widen_matrix,
    feedforward_shrink_matrix,
):
    groups = lax.axis_size("res")
    total_seqs, local_res, channels = aligned_chain_features.shape
    residues = pair_representation_state.shape[1]
    heads = pair_head_weight.shape[1]
    local_seqs = total_seqs // groups
    by_shifts = groups == SLOTS and local_res % SLAB == 0 and local_seqs % SLAB == 0
    seq_parts = 2 if by_shifts else 1
    res_parts = local_res // SLAB if by_shifts else 1
    part_seqs = local_seqs // seq_parts
    part_total = total_seqs // seq_parts
    part_res = local_res // res_parts
    here = lax.axis_index("res")

    def exchange(values):
        return lax.all_to_all(values, "res", split_axis=0, concat_axis=0, tiled=True)

    def kernel_call(
        kernel, name, micros, in_specs, out_shapes, scratch, space=pltpu.VMEM, aliases={}
    ):
        return pl.pallas_call(
            kernel,
            out_shape=[jax.ShapeDtypeStruct(*shape) for shape in out_shapes],
            in_specs=in_specs,
            out_specs=[pl.BlockSpec(memory_space=space)] * len(out_shapes),
            input_output_aliases=aliases,
            scratch_shapes=scratch,
            compiler_params=pltpu.CompilerParams(vmem_limit_bytes=VMEM_BYTES),
            cost_estimate=pl.CostEstimate(
                flops=int(micros * 1e9), bytes_accessed=1 << 20, transcendentals=0
            ),
            name=name,
        )

    def half_of(half):
        return aligned_chain_features[half * part_total : (half + 1) * part_total].reshape(
            groups, part_seqs, local_res, channels
        )

    if by_shifts:

        def cut(features, k):
            start = lax.rem(here + k, groups) * part_seqs
            return lax.dynamic_slice_in_dim(features, start, part_seqs, 0)

        foremost, features = lax.optimization_barrier(
            (cut(aligned_chain_features, 1), aligned_chain_features)
        )
        blocks = [cut(features, k) for k in range(groups)]
        blocks[1] = foremost
        arrived = [shifts(blocks, 1)]
    else:
        arrived = [[exchange(half_of(0))]]
    (bias_local,) = kernel_call(
        bias_kernel, "pair_bias", 5, in_vmem(3), [((heads, local_res, residues), BF16)], [],
    )(pair_norm_gain[None, :], pair_head_weight, pair_representation_state)
    if by_shifts:
        bias_local, *arrived[0] = lax.optimization_barrier((bias_local, *arrived[0]))
        bias_all = jnp.stack(shifts([bias_local] * groups, 1))
    else:
        bias_all = lax.all_gather(bias_local, "res", axis=0, tiled=False)
    for half in range(1, seq_parts):
        bias_all, values = lax.optimization_barrier((bias_all, half_of(half)))
        arrived.append([exchange(values)])

    column_block = (here * local_res) // BLOCK
    col_gap = lax.dynamic_slice_in_dim(gap_block_flags, column_block, 1, 1).reshape(1, total_seqs)
    place = here.astype(jnp.int32)[None]

    def row_attention(part, kinds, *after):
        gap = lax.dynamic_slice_in_dim(
            gap_block_flags, part * part_total + here * part_seqs, part_seqs, 0
        )
        by_row = (part_seqs, residues, channels)
        blocks = arrived[part]
        projected = kernel_call(
            functools.partial(project_kernel, heads, groups), "row_project", 3,
            in_vmem(2 + len(blocks)),
            [(by_row, BF16), (by_row, BF16), (by_row, BF16), (by_row, F32)], [],
        )(horizontal_scaling_factor[None, :], row_input_weight, *blocks)
        operands = (*projected, horizontal_final_matrix, bias_all, *blocks)
        count = local_res // len(kinds)
        outs = []
        for kind in kinds:
            outs += [((groups, part_seqs, count, channels), BF16)]
        return kernel_call(
            functools.partial(row_kernel, len(blocks), kinds, by_shifts), "row_attention", 10,
            [pl.BlockSpec(memory_space=pltpu.SMEM)] * 2
            + in_vmem(len(operands))
            + [pl.BlockSpec(memory_space=pl.ANY)] * len(after),
            outs,
            [
                pltpu.VMEM((heads, residues, residues), F32),
                pltpu.VMEM((part_seqs, residues, channels), BF16),
            ],
        )(gap, place, *operands, *after)

    if by_shifts:
        first = row_attention(0, (STACKED,))
        returned = exchange(first[0])
        kinds = (LISTED,) * (res_parts - 1) + (STACKED,)
        second = row_attention(1, kinds, first[0])
        finals = [shifts(list(part), -1) for part in second[:-1]]
        finals.append([exchange(second[-1])])
    else:
        (first,) = row_attention(0, (STACKED,))
        back = exchange(first).reshape(total_seqs, local_res, channels)
        kinds, finals = (STACKED,), [[jnp.swapaxes(back, 0, 1)]]
    done = []
    for c in range(res_parts):
        pieces, lows, own_gap = finals[c], ((kinds[c], 0),), col_gap
        if by_shifts:
            pieces, lows = [returned] + pieces, ((STACKED, c * part_res),) + lows
        if kinds[c] == LISTED:
            second = col_gap[:, part_total:].reshape(groups, part_seqs)
            second = jnp.roll(second, -here, axis=0).reshape(1, part_total)
            own_gap = jnp.concatenate([col_gap[:, :part_total], second], axis=1)
        shape = (total_seqs, local_res, channels)
        if not by_shifts:
            shape = (part_res, total_seqs, channels)
        part_shape = (total_seqs, part_res, channels) if by_shifts else shape
        before = done[-1:]
        at = 8 + len(pieces)
        held = pltpu.VMEM((part_res, total_seqs, channels), BF16)
        done += kernel_call(
            functools.partial(column_kernel, heads, by_shifts, lows, c * part_res),
            "column_transition", 10,
            [pl.BlockSpec(memory_space=pltpu.SMEM)]
            + in_vmem(7 + len(pieces))
            + [pl.BlockSpec(memory_space=pl.ANY)] * len(before),
            [(shape, BF16)],
            [
                held, held, held, held,
                pltpu.VMEM((part_res, total_seqs, channels), F32),
                held, held,
                pltpu.VMEM(part_shape, BF16),
                pltpu.SemaphoreType.DMA,
            ],
            pl.ANY,
            {at: 0} if before else {},
        )(
            place, own_gap.reshape(total_seqs, 1), vertical_scaling_factor[None, :], feedforward_scaling_factor[None, :],
            column_input_weight, vertical_final_matrix, feedforward_widen_matrix,
            feedforward_shrink_matrix, *pieces, *before,
        )
    return done[-1] if by_shifts else jnp.swapaxes(done[-1], 0, 1)


def solution(mesh):
    placed = (
        P("dp", "res", None),
        P(("dp", "res"), None, None),
        P("dp", None),
    ) + (P(),) * 11
    return jax.shard_map(
        body, mesh=mesh, in_specs=placed, out_specs=P("dp", "res", None), check_vma=False
    )
```

```python
import functools

import jax
import jax.numpy as jnp
from jax import lax
from jax.experimental import pallas as pl
from jax.experimental.pallas import tpu as pltpu
from jax.sharding import PartitionSpec as P

BLOCK = 128
EPSILON = 1e-05
MASKED_SCORE = -1000000000.0
LANES = 128
SLAB = 16
SLOTS = 8
STACKED, LISTED = 0, 1
F32 = jnp.float32
BF16 = jnp.bfloat16
VMEM_BYTES = 28 * 1024 * 1024


def layer_normalize(values_f, scale_gain):
    centred = values_f - jnp.mean(values_f, axis=-1, keepdims=True)
    spread = jnp.mean(centred * centred, axis=-1, keepdims=True)
    return centred * lax.rsqrt(spread + EPSILON) * scale_gain


def mm(lhs, rhs):
    return jnp.dot(lhs, rhs, preferred_element_type=F32)


def mm_nt(lhs, rhs):
    return lax.dot_general(lhs, rhs, (((1,), (1,)), ((), ())), preferred_element_type=F32)


def swap_matrix(outer, inner):
    size = outer * inner
    to = lax.broadcasted_iota(jnp.int32, (size, size), 0)
    come = lax.broadcasted_iota(jnp.int32, (size, size), 1)
    source = lax.rem(to, outer) * inner + lax.div(to, outer)
    return jnp.where(come == source, 1.0, 0.0).astype(BF16)


def bias_kernel(gain_ref, weight_ref, pair_ref, out_ref):
    local_res, residues, channels = pair_ref.shape
    heads = out_ref.shape[0]
    step = min(SLAB, local_res)
    few = min(4, step)
    width = heads * step
    head_at = lax.broadcasted_iota(jnp.int32, (heads, width), 0)
    spread = jnp.where(lax.broadcasted_iota(jnp.int32, (heads, width), 1) // step == head_at, 1.0, 0.0)
    wide = mm(weight_ref[...], spread.astype(BF16))
    lane = lax.broadcasted_iota(jnp.int32, wide.shape, 1)
    weights = [jnp.where(lane % step == i, wide, 0.0).astype(BF16) for i in range(step)]
    for p in range(0, local_res, step):
        projected = None
        for i in range(0, step, few):
            x = pair_ref[p + i : p + i + few].reshape(few * residues, channels)
            normed = layer_normalize(x.astype(F32), gain_ref[...]).astype(BF16)
            left = [normed[j * residues : (j + 1) * residues] for j in range(few)]
            part = mm(jnp.concatenate(left, axis=1), jnp.concatenate(weights[i : i + few], axis=0))
            projected = part if projected is None else projected + part
        out_ref[:, p : p + step] = projected.T.reshape(heads, step, residues).astype(BF16)


def softmax_lanes(scores):
    e = jnp.exp(scores - jnp.max(scores, axis=-1, keepdims=True))
    total = jnp.sum(e, axis=-1, keepdims=True)
    inverse = pl.reciprocal(total, approx=True)
    inverse = inverse * (2.0 - total * inverse)
    return (e * inverse).astype(BF16)


def gate_of(values):
    return 0.5 * jnp.tanh(0.5 * values) + 0.5


def pick_heads(parts, depth):
    lane = lax.broadcasted_iota(jnp.int32, parts[0].shape, 1)
    slot = lane // depth % len(parts)
    picked = parts[-1]
    for j in range(len(parts) - 2, -1, -1):
        picked = jnp.where(slot == j, parts[j], picked)
    return picked


def lane_mask(width, depth, slots, j):
    lane = lax.broadcasted_iota(jnp.int32, (1, width), 1)
    return jnp.where(lane // depth % slots == j, 1.0, 0.0).astype(BF16)


def rows_of(refs, slot, at):
    ref = refs[0].at[slot] if len(refs) == 1 else refs[slot]
    return ref[pl.ds(at, 1)].reshape(ref.shape[1:])


def project_kernel(heads, groups, gain_ref, win_ref, *refs):
    x_refs, (q_ref, k_ref, v_ref, gate_ref) = refs[:-4], refs[-4:]
    seqs, residues, channels = q_ref.shape
    scale = (channels // heads) ** (-0.5)
    batch = largest(seqs, 4)

    def dense(i, carry):
        x = [rows_of(x_refs, t, i * batch + j) for j in range(batch) for t in range(groups)]
        x = jnp.concatenate(x, axis=0).astype(F32)
        normed = layer_normalize(x, gain_ref[...]).astype(BF16)
        some = pl.ds(i * batch, batch)
        shape = (batch, residues, channels)
        q = (mm(normed, win_ref[:, :channels]) * scale).astype(BF16)
        q_ref[some] = q.reshape(shape)
        k_ref[some] = mm(normed, win_ref[:, channels : 2 * channels]).astype(BF16).reshape(shape)
        v_ref[some] = mm(normed, win_ref[:, 2 * channels : 3 * channels]).astype(BF16).reshape(shape)
        gate_ref[some] = gate_of(mm(normed, win_ref[:, 3 * channels :])).reshape(shape)
        return carry

    lax.fori_loop(0, seqs // batch, dense, 0)


def in_turn(tasks, scores_of, weights_of, mixed_of):
    results, scores = [], scores_of(tasks[0])
    for at, task in enumerate(tasks):
        ahead = scores_of(tasks[at + 1]) if at + 1 < len(tasks) else None
        results.append(mixed_of(task, weights_of(task, scores)))
        scores = ahead
    return results


def row_kernel(
    blocks, kinds, by_shifts, gap_ref, place_ref, q_ref, k_ref, v_ref, gate_ref, wout_ref, bias_ref, *refs
):
    x_refs, refs, (bias_scr, gated_scr) = refs[:blocks], refs[blocks:-2], refs[-2:]
    groups, heads, local_res, residues = bias_ref.shape
    out_refs = []
    for kind in kinds[::-1]:
        out_refs.insert(0, refs[-1:])
        refs = refs[:-1]
    seqs, _, channels = q_ref.shape
    depth = channels // heads
    per = LANES // depth
    batch = largest(seqs, 4)
    part_res = local_res // len(kinds)

    def home(slot):
        return slot if blocks == 1 else lax.rem(place_ref[0] - slot + groups, groups)

    def residue_at(place):
        return home(place // local_res) * local_res + place % local_res

    square = (residues, residues)
    residue = lax.broadcasted_iota(jnp.int32, square, 0)
    order = jnp.where(residue == residue_at(lax.broadcasted_iota(jnp.int32, square, 1)), 1.0, 0.0)
    order = order.astype(BF16)
    slots = list(range(groups))
    if by_shifts and blocks == 1:
        slots = [lax.rem(place_ref[0] - t + groups, groups) for t in range(groups)]
    for h in range(heads):
        rows = jnp.concatenate([bias_ref[slot, h] for slot in slots], axis=0)
        bias_scr[h] = mm(rows, order)
    masks = [lane_mask(LANES, depth, per, j) for j in range(per)]
    block_at = residue_at(lax.broadcasted_iota(jnp.int32, (1, residues), 1)) // BLOCK

    def attend(i, carry):
        tasks = [(u, g) for u in range(batch) for g in range(heads // per)]
        at = [i * batch + u for u in range(batch)]
        gaps = []
        for s in at:
            gap = jnp.zeros((1, residues), F32)
            for b in range(residues // BLOCK):
                closed = jnp.where(gap_ref[s, b] == 1, MASKED_SCORE, 0.0)
                gap = jnp.where(block_at == b, closed, gap)
            gaps.append(gap)
        gates = [gate_ref[s] for s in at]

        def lanes(ref, task):
            return ref[at[task[0]], :, task[1] * LANES : (task[1] + 1) * LANES]

        def scores_of(task):
            q = lanes(q_ref, task)
            return mm_nt(
                jnp.concatenate([q * mask for mask in masks], axis=0), lanes(k_ref, task)
            )

        def weights_of(task, scores):
            weights = []
            for j in range(per):
                own = scores[j * residues : (j + 1) * residues]
                own = own + bias_scr[task[1] * per + j] + gaps[task[0]]
                weights.append(softmax_lanes(own))
            return jnp.concatenate(weights, axis=0)

        def mixed_of(task, weights):
            mixed = mm(weights, lanes(v_ref, task))
            return pick_heads([mixed[j * residues : (j + 1) * residues] for j in range(per)], depth)

        attended = in_turn(tasks, scores_of, weights_of, mixed_of)
        halves = heads // per
        for u in range(batch):
            whole = jnp.concatenate(attended[u * halves : (u + 1) * halves], axis=1)
            gated_scr[at[u]] = (whole * gates[u]).astype(BF16)
        return carry

    lax.fori_loop(0, seqs // batch, attend, 0)

    def finish(i, carry):
        x = [rows_of(x_refs, t, i * batch + j) for j in range(batch) for t in range(groups)]
        gated = gated_scr[pl.ds(i * batch, batch)].reshape(batch * residues, channels)
        result = jnp.concatenate(x, axis=0).astype(F32) + mm(gated, wout_ref[...])
        result = result.astype(BF16).reshape(batch, groups, local_res, channels)
        for j in range(batch):
            s = i * batch + j
            for p, (kind, outs) in enumerate(zip(kinds, out_refs)):
                for t in range(groups):
                    rows = result[j, t, p * part_res : (p + 1) * part_res]
                    if kind == STACKED:
                        outs[0][home(t), s] = rows
                    elif blocks == 1:
                        outs[0][lax.rem(place_ref[0] - t + groups, groups), s] = rows
                    else:
                        outs[0][t, s] = rows
        return carry

    lax.fori_loop(0, seqs // batch, finish, 0)


def column_kernel(
    heads, turn, lows, earlier, place_ref, gap_ref, gain_ref, gain2_ref, win_ref, wout_ref,
    widen_ref, shrink_ref, *refs,
):
    pieces, places = [], []
    for kind, low in lows:
        if kind == STACKED:
            pieces += [(refs[0].at[g] if turn else refs[0], low) for g in range(SLOTS if turn else 1)]
            places += [len(places) + g for g in range(SLOTS)]
            refs = refs[1:]
        else:
            pieces += [(ref, low) for ref in refs[:SLOTS]]
            places += [len(places) + lax.rem(place_ref[0] + t, SLOTS) for t in range(SLOTS)]
            refs = refs[SLOTS:]
    refs = refs[1:] if earlier else refs
    (out_hbm, turned_scr, q_scr, k_scr, v_scr, gate_scr, gated_scr, done_scr, out_ref, sem) = refs
    local_res, seqs, channels = turned_scr.shape
    depth = channels // heads
    per = LANES // depth
    halves = heads // per
    scale = depth ** (-0.5)
    batch = largest(local_res, 8)
    slabs = local_res // SLAB if turn else 0
    swap = swap_matrix(SLAB, SLAB)
    if not turn:
        turned_scr[...] = pieces[0][0][...]
    each = pieces[0][0].shape[0]
    fold = SLAB // each if turn else 1
    for c in range(slabs):
        parts = [
            piece[:, low + c * SLAB : low + (c + 1) * SLAB] for piece, low in pieces
        ]
        blocks = [
            jnp.concatenate(parts[i : i + fold], axis=0).reshape(SLAB * SLAB, channels)
            for i in range(0, len(parts), fold)
        ]
        turned = mm(swap, jnp.concatenate(blocks, axis=1)).astype(BF16)
        for g in range(seqs // SLAB):
            turned_scr[c * SLAB : (c + 1) * SLAB, g * SLAB : (g + 1) * SLAB] = turned[
                :, g * channels : (g + 1) * channels
            ].reshape(SLAB, SLAB, channels)

    shape = (batch, seqs, channels)

    def dense(i):
        some, held = slice(i * batch, (i + 1) * batch), []

        def slot(j):
            return mm(held[0], win_ref[:, j * channels : (j + 1) * channels])

        def norm():
            x = turned_scr[some].reshape(batch * seqs, channels).astype(F32)
            held.append(layer_normalize(x, gain_ref[...]).astype(BF16))

        def query():
            q_scr[some] = (slot(0) * scale).astype(BF16).reshape(shape)

        def key():
            k_scr[some] = slot(1).astype(BF16).reshape(shape)

        def value():
            v_scr[some] = slot(2).astype(BF16).reshape(shape)

        def gate():
            gate_scr[some] = gate_of(slot(3)).reshape(shape)

        return [norm, query, key, value, gate]

    mask = jnp.broadcast_to(
        jnp.where(gap_ref[...] == 1, MASKED_SCORE, 0.0), (seqs, halves * seqs)
    )
    masks = [lane_mask(channels, depth, per, j) for j in range(per)]
    blank = jnp.zeros((seqs, LANES), BF16)

    def diagonal(values):
        rows = []
        for g in range(halves):
            own = values[:, g * LANES : (g + 1) * LANES]
            rows.append(jnp.concatenate([own if i == g else blank for i in range(halves)], axis=1))
        return jnp.concatenate(rows, axis=0)

    def scores_of(r):
        k = k_scr[r]
        return mm_nt(jnp.concatenate([k * m for m in masks], axis=0), diagonal(q_scr[r]))

    def weights_of(r, scores):
        weights = []
        for j in range(per):
            own = scores[j * seqs : (j + 1) * seqs] + mask
            e = jnp.exp(own - jnp.max(own, axis=0, keepdims=True))
            weights.append((e * (1.0 / jnp.sum(e, axis=0, keepdims=True))).astype(BF16))
        return weights

    def mixed_of(r, weights):
        v = v_scr[r].T
        mixed = [None] * heads
        for j in range(per):
            left = [v[(g * per + j) * depth : (g * per + j + 1) * depth] for g in range(halves)]
            both = mm(jnp.concatenate(left, axis=0), weights[j])
            for g in range(halves):
                mixed[g * per + j] = both[g * depth : (g + 1) * depth, g * seqs : (g + 1) * seqs]
        gated_scr[r] = (jnp.concatenate(mixed, axis=0).T * gate_scr[r]).astype(BF16)

    def finish(i):
        some, held = slice(i * batch, (i + 1) * batch), {}

        def second():
            x = turned_scr[some].reshape(batch * seqs, channels)
            gated = gated_scr[some].reshape(batch * seqs, channels)
            rounded = (x.astype(F32) + mm(gated, wout_ref[...])).astype(BF16).astype(F32)
            held["second"] = rounded
            held["normed"] = layer_normalize(rounded, gain2_ref[...]).astype(BF16)

        def widen(j):
            columns = slice(j * channels, (j + 1) * channels)
            part = jnp.maximum(mm(held["normed"], widen_ref[:, columns]), 0.0).astype(BF16)
            held.setdefault("hidden", []).append(part)

        def shrink():
            hidden = jnp.concatenate(held["hidden"], axis=1)
            result = (held["second"] + mm(hidden, shrink_ref[...])).astype(BF16)
            done_scr[some] = result.reshape(shape)

        steps = [functools.partial(widen, j) for j in range(widen_ref.shape[1] // channels)]
        return [second, *steps, shrink]

    batches = local_res // batch
    for step in dense(0):
        step()
    for i in range(batches):
        beside = (dense(i + 1) if i + 1 < batches else []) + (finish(i - 1) if i else [])
        tasks = list(range(i * batch, (i + 1) * batch))
        scores = scores_of(tasks[0])
        for n, r in enumerate(tasks):
            ahead = scores_of(tasks[n + 1]) if n + 1 < len(tasks) else None
            weights = weights_of(r, scores)
            for step in beside[:1]:
                step()
            beside = beside[1:]
            mixed_of(r, weights)
            scores = ahead
        for step in beside:
            step()
    for step in finish(batches - 1):
        step()
    if not turn:
        out_ref[...] = done_scr[...]
    for c in range(slabs):
        blocks = [
            done_scr[c * SLAB : (c + 1) * SLAB, g * SLAB : (g + 1) * SLAB].reshape(
                SLAB * SLAB, channels
            )
            for g in range(seqs // SLAB)
        ]
        turned = mm(swap, jnp.concatenate(blocks, axis=1)).astype(BF16)
        start = c * SLAB
        for g in range(seqs // SLAB):
            own = turned[:, g * channels : (g + 1) * channels].reshape(SLAB, SLAB, channels)
            for e in range(fold):
                place = places[g * fold + e]
                out_ref[pl.ds(place * each, each), start : start + SLAB] = own[
                    e * each : (e + 1) * each
                ]
    target = out_hbm.at[:, earlier : earlier + local_res] if turn else out_hbm
    copy = pltpu.make_async_copy(out_ref, target, sem)
    copy.start()
    copy.wait()


def largest(total, bound):
    return max(d for d in range(1, bound + 1) if total % d == 0)


def in_vmem(count):
    return [pl.BlockSpec(memory_space=pltpu.VMEM)] * count


def shifts(blocks, sign):
    arrived = [blocks[0]]
    for k in range(1, SLOTS):
        to = [(i, (i + sign * k) % SLOTS) for i in range(SLOTS)]
        arrived.append(lax.ppermute(blocks[k], "res", to))
    return arrived


def body(
    aligned_chain_features,
    pair_representation_state,
    gap_block_flags,
    pair_norm_gain,
    pair_head_weight,
    horizontal_scaling_factor,
    row_input_weight,
    horizontal_final_matrix,
    vertical_scaling_factor,
    column_input_weight,
    vertical_final_matrix,
    feedforward_scaling_factor,
    feedforward_widen_matrix,
    feedforward_shrink_matrix,
):
    groups = lax.axis_size("res")
    total_seqs, local_res, channels = aligned_chain_features.shape
    residues = pair_representation_state.shape[1]
    heads = pair_head_weight.shape[1]
    local_seqs = total_seqs // groups
    by_shifts = groups == SLOTS and local_res % SLAB == 0 and local_seqs % SLAB == 0
    seq_parts = 2 if by_shifts else 1
    res_parts = local_res // SLAB if by_shifts else 1
    part_seqs = local_seqs // seq_parts
    part_total = total_seqs // seq_parts
    part_res = local_res // res_parts
    here = lax.axis_index("res")

    def exchange(values):
        return lax.all_to_all(values, "res", split_axis=0, concat_axis=0, tiled=True)

    def kernel_call(
        kernel, name, micros, in_specs, out_shapes, scratch, space=pltpu.VMEM, aliases={}
    ):
        return pl.pallas_call(
            kernel,
            out_shape=[jax.ShapeDtypeStruct(*shape) for shape in out_shapes],
            in_specs=in_specs,
            out_specs=[pl.BlockSpec(memory_space=space)] * len(out_shapes),
            input_output_aliases=aliases,
            scratch_shapes=scratch,
            compiler_params=pltpu.CompilerParams(vmem_limit_bytes=VMEM_BYTES),
            cost_estimate=pl.CostEstimate(
                flops=int(micros * 1e9), bytes_accessed=1 << 20, transcendentals=0
            ),
            name=name,
        )

    def half_of(half):
        return aligned_chain_features[half * part_total : (half + 1) * part_total].reshape(
            groups, part_seqs, local_res, channels
        )

    if by_shifts:

        def cut(features, k):
            start = lax.rem(here + k, groups) * part_seqs
            return lax.dynamic_slice_in_dim(features, start, part_seqs, 0)

        foremost, features = lax.optimization_barrier(
            (cut(aligned_chain_features, 1), aligned_chain_features)
        )
        blocks = [cut(features, k) for k in range(groups)]
        blocks[1] = foremost
        arrived = [shifts(blocks, 1)]
    else:
        arrived = [[exchange(half_of(0))]]
    (bias_local,) = kernel_call(
        bias_kernel, "pair_bias", 5, in_vmem(3), [((heads, local_res, residues), BF16)], [],
    )(pair_norm_gain[None, :], pair_head_weight, pair_representation_state)
    if by_shifts:
        bias_local, *arrived[0] = lax.optimization_barrier((bias_local, *arrived[0]))
        bias_all = jnp.stack(shifts([bias_local] * groups, 1))
    else:
        bias_all = lax.all_gather(bias_local, "res", axis=0, tiled=False)
    for half in range(1, seq_parts):
        bias_all, values = lax.optimization_barrier((bias_all, half_of(half)))
        arrived.append([exchange(values)])

    column_block = (here * local_res) // BLOCK
    col_gap = lax.dynamic_slice_in_dim(gap_block_flags, column_block, 1, 1).reshape(1, total_seqs)
    place = here.astype(jnp.int32)[None]

    def row_attention(part, kinds, *after):
        gap = lax.dynamic_slice_in_dim(
            gap_block_flags, part * part_total + here * part_seqs, part_seqs, 0
        )
        by_row = (part_seqs, residues, channels)
        blocks = arrived[part]
        projected = kernel_call(
            functools.partial(project_kernel, heads, groups), "row_project", 3,
            in_vmem(2 + len(blocks)),
            [(by_row, BF16), (by_row, BF16), (by_row, BF16), (by_row, F32)], [],
        )(horizontal_scaling_factor[None, :], row_input_weight, *blocks)
        operands = (*projected, horizontal_final_matrix, bias_all, *blocks)
        count = local_res // len(kinds)
        outs = []
        for kind in kinds:
            outs += [((groups, part_seqs, count, channels), BF16)]
        return kernel_call(
            functools.partial(row_kernel, len(blocks), kinds, by_shifts), "row_attention", 10,
            [pl.BlockSpec(memory_space=pltpu.SMEM)] * 2
            + in_vmem(len(operands))
            + [pl.BlockSpec(memory_space=pl.ANY)] * len(after),
            outs,
            [
                pltpu.VMEM((heads, residues, residues), F32),
                pltpu.VMEM((part_seqs, residues, channels), BF16),
            ],
        )(gap, place, *operands, *after)

    if by_shifts:
        first = row_attention(0, (STACKED,))
        returned = exchange(first[0])
        kinds = (LISTED,) * (res_parts - 1) + (STACKED,)
        second = row_attention(1, kinds, first[0])
        finals = [shifts(list(part), -1) for part in second[:-1]]
        finals.append([exchange(second[-1])])
    else:
        (first,) = row_attention(0, (STACKED,))
        back = exchange(first).reshape(total_seqs, local_res, channels)
        kinds, finals = (STACKED,), [[jnp.swapaxes(back, 0, 1)]]
    done = []
    for c in range(res_parts):
        pieces, lows, own_gap = finals[c], ((kinds[c], 0),), col_gap
        if by_shifts:
            pieces, lows = [returned] + pieces, ((STACKED, c * part_res),) + lows
        if kinds[c] == LISTED:
            second = col_gap[:, part_total:].reshape(groups, part_seqs)
            second = jnp.roll(second, -here, axis=0).reshape(1, part_total)
            own_gap = jnp.concatenate([col_gap[:, :part_total], second], axis=1)
        shape = (total_seqs, local_res, channels)
        if not by_shifts:
            shape = (part_res, total_seqs, channels)
        part_shape = (total_seqs, part_res, channels) if by_shifts else shape
        before = done[-1:]
        at = 8 + len(pieces)
        held = pltpu.VMEM((part_res, total_seqs, channels), BF16)
        done += kernel_call(
            functools.partial(column_kernel, heads, by_shifts, lows, c * part_res),
            "column_transition", 10,
            [pl.BlockSpec(memory_space=pltpu.SMEM)]
            + in_vmem(7 + len(pieces))
            + [pl.BlockSpec(memory_space=pl.ANY)] * len(before),
            [(shape, BF16)],
            [
                held, held, held, held,
                pltpu.VMEM((part_res, total_seqs, channels), F32),
                held, held,
                pltpu.VMEM(part_shape, BF16),
                pltpu.SemaphoreType.DMA,
            ],
            pl.ANY,
            {at: 0} if before else {},
        )(
            place, own_gap.reshape(total_seqs, 1), vertical_scaling_factor[None, :], feedforward_scaling_factor[None, :],
            column_input_weight, vertical_final_matrix, feedforward_widen_matrix,
            feedforward_shrink_matrix, *pieces, *before,
        )
    return done[-1] if by_shifts else jnp.swapaxes(done[-1], 0, 1)


def solution(mesh):
    placed = (
        P("dp", "res", None),
        P(("dp", "res"), None, None),
        P("dp", None),
    ) + (P(),) * 11
    return jax.shard_map(
        body, mesh=mesh, in_specs=placed, out_specs=P("dp", "res", None), check_vma=False
    )
```

```python
import functools

import jax
import jax.numpy as jnp
from jax import lax
from jax.experimental import pallas as pl
from jax.experimental.pallas import tpu as pltpu
from jax.sharding import PartitionSpec as P

BLOCK = 128
EPSILON = 1e-05
MASKED_SCORE = -1000000000.0
LANES = 128
SLAB = 16
SLOTS = 8
STACKED, LISTED = 0, 1
F32 = jnp.float32
BF16 = jnp.bfloat16
VMEM_BYTES = 28 * 1024 * 1024


def layer_normalize(values_f, scale_gain):
    centred = values_f - jnp.mean(values_f, axis=-1, keepdims=True)
    spread = jnp.mean(centred * centred, axis=-1, keepdims=True)
    return centred * lax.rsqrt(spread + EPSILON) * scale_gain


def mm(lhs, rhs):
    return jnp.dot(lhs, rhs, preferred_element_type=F32)


def mm_nt(lhs, rhs):
    return lax.dot_general(lhs, rhs, (((1,), (1,)), ((), ())), preferred_element_type=F32)


def swap_matrix(outer, inner):
    size = outer * inner
    to = lax.broadcasted_iota(jnp.int32, (size, size), 0)
    come = lax.broadcasted_iota(jnp.int32, (size, size), 1)
    source = lax.rem(to, outer) * inner + lax.div(to, outer)
    return jnp.where(come == source, 1.0, 0.0).astype(BF16)


def bias_kernel(gain_ref, weight_ref, pair_ref, out_ref):
    local_res, residues, channels = pair_ref.shape
    heads = out_ref.shape[0]
    step = min(SLAB, local_res)
    few = min(4, step)
    width = heads * step
    head_at = lax.broadcasted_iota(jnp.int32, (heads, width), 0)
    spread = jnp.where(lax.broadcasted_iota(jnp.int32, (heads, width), 1) // step == head_at, 1.0, 0.0)
    wide = mm(weight_ref[...], spread.astype(BF16))
    lane = lax.broadcasted_iota(jnp.int32, wide.shape, 1)
    weights = [jnp.where(lane % step == i, wide, 0.0).astype(BF16) for i in range(step)]
    for p in range(0, local_res, step):
        projected = None
        for i in range(0, step, few):
            x = pair_ref[p + i : p + i + few].reshape(few * residues, channels)
            normed = layer_normalize(x.astype(F32), gain_ref[...]).astype(BF16)
            left = [normed[j * residues : (j + 1) * residues] for j in range(few)]
            part = mm(jnp.concatenate(left, axis=1), jnp.concatenate(weights[i : i + few], axis=0))
            projected = part if projected is None else projected + part
        out_ref[:, p : p + step] = projected.T.reshape(heads, step, residues).astype(BF16)


def softmax_lanes(scores):
    e = jnp.exp(scores - jnp.max(scores, axis=-1, keepdims=True))
    total = jnp.sum(e, axis=-1, keepdims=True)
    inverse = pl.reciprocal(total, approx=True)
    inverse = inverse * (2.0 - total * inverse)
    return (e * inverse).astype(BF16)


def gate_of(values):
    return 0.5 * jnp.tanh(0.5 * values) + 0.5


def pick_heads(parts, depth):
    lane = lax.broadcasted_iota(jnp.int32, parts[0].shape, 1)
    slot = lane // depth % len(parts)
    picked = parts[-1]
    for j in range(len(parts) - 2, -1, -1):
        picked = jnp.where(slot == j, parts[j], picked)
    return picked


def lane_mask(width, depth, slots, j):
    lane = lax.broadcasted_iota(jnp.int32, (1, width), 1)
    return jnp.where(lane // depth % slots == j, 1.0, 0.0).astype(BF16)


def rows_of(refs, slot, at):
    ref = refs[0].at[slot] if len(refs) == 1 else refs[slot]
    return ref[pl.ds(at, 1)].reshape(ref.shape[1:])


def project_kernel(heads, groups, gain_ref, win_ref, *refs):
    x_refs, (q_ref, k_ref, v_ref, gate_ref) = refs[:-4], refs[-4:]
    seqs, residues, channels = q_ref.shape
    scale = (channels // heads) ** (-0.5)
    batch = largest(seqs, 4)

    def dense(i, carry):
        x = [rows_of(x_refs, t, i * batch + j) for j in range(batch) for t in range(groups)]
        x = jnp.concatenate(x, axis=0).astype(F32)
        normed = layer_normalize(x, gain_ref[...]).astype(BF16)
        some = pl.ds(i * batch, batch)
        shape = (batch, residues, channels)
        q = (mm(normed, win_ref[:, :channels]) * scale).astype(BF16)
        q_ref[some] = q.reshape(shape)
        k_ref[some] = mm(normed, win_ref[:, channels : 2 * channels]).astype(BF16).reshape(shape)
        v_ref[some] = mm(normed, win_ref[:, 2 * channels : 3 * channels]).astype(BF16).reshape(shape)
        gate_ref[some] = gate_of(mm(normed, win_ref[:, 3 * channels :])).reshape(shape)
        return carry

    lax.fori_loop(0, seqs // batch, dense, 0)


def in_turn(tasks, scores_of, weights_of, mixed_of):
    results, scores = [], scores_of(tasks[0])
    for at, task in enumerate(tasks):
        ahead = scores_of(tasks[at + 1]) if at + 1 < len(tasks) else None
        results.append(mixed_of(task, weights_of(task, scores)))
        scores = ahead
    return results


def row_kernel(
    blocks, kinds, by_shifts, gap_ref, place_ref, q_ref, k_ref, v_ref, gate_ref, wout_ref, bias_ref, *refs
):
    x_refs, refs, (bias_scr, gated_scr) = refs[:blocks], refs[blocks:-2], refs[-2:]
    groups, heads, local_res, residues = bias_ref.shape
    out_refs = []
    for kind in kinds[::-1]:
        out_refs.insert(0, refs[-1:])
        refs = refs[:-1]
    seqs, _, channels = q_ref.shape
    depth = channels // heads
    per = LANES // depth
    batch = largest(seqs, 4)
    part_res = local_res // len(kinds)

    def home(slot):
        return slot if blocks == 1 else lax.rem(place_ref[0] - slot + groups, groups)

    def residue_at(place):
        return home(place // local_res) * local_res + place % local_res

    square = (residues, residues)
    residue = lax.broadcasted_iota(jnp.int32, square, 0)
    order = jnp.where(residue == residue_at(lax.broadcasted_iota(jnp.int32, square, 1)), 1.0, 0.0)
    order = order.astype(BF16)
    slots = list(range(groups))
    if by_shifts and blocks == 1:
        slots = [lax.rem(place_ref[0] - t + groups, groups) for t in range(groups)]
    for h in range(heads):
        rows = jnp.concatenate([bias_ref[slot, h] for slot in slots], axis=0)
        bias_scr[h] = mm(rows, order)
    masks = [lane_mask(LANES, depth, per, j) for j in range(per)]
    block_at = residue_at(lax.broadcasted_iota(jnp.int32, (1, residues), 1)) // BLOCK

    def attend(i, carry):
        tasks = [(u, g) for u in range(batch) for g in range(heads // per)]
        at = [i * batch + u for u in range(batch)]
        gaps = []
        for s in at:
            gap = jnp.zeros((1, residues), F32)
            for b in range(residues // BLOCK):
                closed = jnp.where(gap_ref[s, b] == 1, MASKED_SCORE, 0.0)
                gap = jnp.where(block_at == b, closed, gap)
            gaps.append(gap)
        gates = [gate_ref[s] for s in at]

        def lanes(ref, task):
            return ref[at[task[0]], :, task[1] * LANES : (task[1] + 1) * LANES]

        def scores_of(task):
            q = lanes(q_ref, task)
            return mm_nt(
                jnp.concatenate([q * mask for mask in masks], axis=0), lanes(k_ref, task)
            )

        def weights_of(task, scores):
            weights = []
            for j in range(per):
                own = scores[j * residues : (j + 1) * residues]
                own = own + bias_scr[task[1] * per + j] + gaps[task[0]]
                weights.append(softmax_lanes(own))
            return jnp.concatenate(weights, axis=0)

        def mixed_of(task, weights):
            mixed = mm(weights, lanes(v_ref, task))
            return pick_heads([mixed[j * residues : (j + 1) * residues] for j in range(per)], depth)

        attended = in_turn(tasks, scores_of, weights_of, mixed_of)
        halves = heads // per
        for u in range(batch):
            whole = jnp.concatenate(attended[u * halves : (u + 1) * halves], axis=1)
            gated_scr[at[u]] = (whole * gates[u]).astype(BF16)
        return carry

    lax.fori_loop(0, seqs // batch, attend, 0)

    def finish(i, carry):
        x = [rows_of(x_refs, t, i * batch + j) for j in range(batch) for t in range(groups)]
        gated = gated_scr[pl.ds(i * batch, batch)].reshape(batch * residues, channels)
        result = jnp.concatenate(x, axis=0).astype(F32) + mm(gated, wout_ref[...])
        result = result.astype(BF16).reshape(batch, groups, local_res, channels)
        for j in range(batch):
            s = i * batch + j
            for p, (kind, outs) in enumerate(zip(kinds, out_refs)):
                for t in range(groups):
                    rows = result[j, t, p * part_res : (p + 1) * part_res]
                    if kind == STACKED:
                        outs[0][home(t), s] = rows
                    elif blocks == 1:
                        outs[0][lax.rem(place_ref[0] - t + groups, groups), s] = rows
                    else:
                        outs[0][t, s] = rows
        return carry

    lax.fori_loop(0, seqs // batch, finish, 0)


def column_kernel(
    heads, turn, lows, earlier, place_ref, gap_ref, gain_ref, gain2_ref, win_ref, wout_ref,
    widen_ref, shrink_hbm, *refs,
):
    pieces, places = [], []
    for kind, low in lows:
        if kind == STACKED:
            pieces += [(refs[0].at[g] if turn else refs[0], low) for g in range(SLOTS if turn else 1)]
            places += list(range(SLOTS))
            refs = refs[1:]
        else:
            pieces += [(ref, low) for ref in refs[:SLOTS]]
            places += [lax.rem(place_ref[0] + t, SLOTS) for t in range(SLOTS)]
            refs = refs[SLOTS:]
    refs = refs[1:] if earlier else refs
    (out_hbm, turned_scr, q_scr, k_scr, v_scr, gate_scr, gated_scr, done_scr) = refs[:8]
    shrink_ref, sems, out_refs = refs[8], refs[9], refs[10:]
    fetch = pltpu.make_async_copy(shrink_hbm, shrink_ref, sems.at[0])
    fetch.start()
    local_res, seqs, channels = turned_scr.shape
    depth = channels // heads
    per = LANES // depth
    halves = heads // per
    scale = depth ** (-0.5)
    batch = largest(local_res, 8)
    slabs = local_res // SLAB if turn else 0
    swap = swap_matrix(SLAB, SLAB)
    if not turn:
        turned_scr[...] = pieces[0][0][...]
    each = pieces[0][0].shape[0]
    fold = SLAB // each if turn else 1
    for c in range(slabs):
        parts = [
            piece[:, low + c * SLAB : low + (c + 1) * SLAB] for piece, low in pieces
        ]
        blocks = [
            jnp.concatenate(parts[i : i + fold], axis=0).reshape(SLAB * SLAB, channels)
            for i in range(0, len(parts), fold)
        ]
        turned = mm(swap, jnp.concatenate(blocks, axis=1)).astype(BF16)
        for g in range(seqs // SLAB):
            turned_scr[c * SLAB : (c + 1) * SLAB, g * SLAB : (g + 1) * SLAB] = turned[
                :, g * channels : (g + 1) * channels
            ].reshape(SLAB, SLAB, channels)

    shape = (batch, seqs, channels)

    def dense(i):
        some, held = slice(i * batch, (i + 1) * batch), []

        def slot(j):
            return mm(held[0], win_ref[:, j * channels : (j + 1) * channels])

        def norm():
            x = turned_scr[some].reshape(batch * seqs, channels).astype(F32)
            held.append(layer_normalize(x, gain_ref[...]).astype(BF16))

        def query():
            q_scr[some] = (slot(0) * scale).astype(BF16).reshape(shape)

        def key():
            k_scr[some] = slot(1).astype(BF16).reshape(shape)

        def value():
            v_scr[some] = slot(2).astype(BF16).reshape(shape)

        def gate():
            gate_scr[some] = gate_of(slot(3)).reshape(shape)

        return [norm, query, key, value, gate]

    mask = jnp.broadcast_to(
        jnp.where(gap_ref[...] == 1, MASKED_SCORE, 0.0), (seqs, halves * seqs)
    )
    masks = [lane_mask(channels, depth, per, j) for j in range(per)]
    blank = jnp.zeros((seqs, LANES), BF16)

    def diagonal(values):
        rows = []
        for g in range(halves):
            own = values[:, g * LANES : (g + 1) * LANES]
            rows.append(jnp.concatenate([own if i == g else blank for i in range(halves)], axis=1))
        return jnp.concatenate(rows, axis=0)

    def scores_of(r):
        k = k_scr[r]
        return mm_nt(jnp.concatenate([k * m for m in masks], axis=0), diagonal(q_scr[r]))

    def weights_of(r, scores):
        weights = []
        for j in range(per):
            own = scores[j * seqs : (j + 1) * seqs] + mask
            e = jnp.exp(own - jnp.max(own, axis=0, keepdims=True))
            weights.append((e * (1.0 / jnp.sum(e, axis=0, keepdims=True))).astype(BF16))
        return weights

    def mixed_of(r, weights):
        v = v_scr[r].T
        mixed = [None] * heads
        for j in range(per):
            left = [v[(g * per + j) * depth : (g * per + j + 1) * depth] for g in range(halves)]
            both = mm(jnp.concatenate(left, axis=0), weights[j])
            for g in range(halves):
                mixed[g * per + j] = both[g * depth : (g + 1) * depth, g * seqs : (g + 1) * seqs]
        gated_scr[r] = (jnp.concatenate(mixed, axis=0).T * gate_scr[r]).astype(BF16)

    def finish(i):
        some, held = slice(i * batch, (i + 1) * batch), {}

        def second():
            x = turned_scr[some].reshape(batch * seqs, channels)
            gated = gated_scr[some].reshape(batch * seqs, channels)
            rounded = (x.astype(F32) + mm(gated, wout_ref[...])).astype(BF16).astype(F32)
            held["second"] = rounded
            held["normed"] = layer_normalize(rounded, gain2_ref[...]).astype(BF16)

        def widen(j):
            columns = slice(j * channels, (j + 1) * channels)
            part = jnp.maximum(mm(held["normed"], widen_ref[:, columns]), 0.0).astype(BF16)
            held.setdefault("hidden", []).append(part)

        def shrink():
            hidden = jnp.concatenate(held["hidden"], axis=1)
            result = (held["second"] + mm(hidden, shrink_ref[...])).astype(BF16)
            done_scr[some] = result.reshape(shape)

        steps = [functools.partial(widen, j) for j in range(widen_ref.shape[1] // channels)]
        return [second, *steps, shrink]

    batches = local_res // batch
    for step in dense(0):
        step()
    fetch.wait()
    for i in range(batches):
        beside = (dense(i + 1) if i + 1 < batches else []) + (finish(i - 1) if i else [])
        tasks = list(range(i * batch, (i + 1) * batch))
        scores = scores_of(tasks[0])
        for n, r in enumerate(tasks):
            ahead = scores_of(tasks[n + 1]) if n + 1 < len(tasks) else None
            weights = weights_of(r, scores)
            for step in beside[:1]:
                step()
            beside = beside[1:]
            mixed_of(r, weights)
            scores = ahead
        for step in beside:
            step()
    for step in finish(batches - 1):
        step()
    if not turn:
        out_refs[0][...] = done_scr[...]
    target = out_hbm.at[:, earlier : earlier + local_res] if turn else out_hbm
    share = seqs // len(lows)
    copies = []
    for p in range(len(lows)):
        if turn:
            blocks = [
                done_scr[:, at : at + SLAB].reshape(SLAB * SLAB, channels)
                for at in range(p * share, (p + 1) * share, SLAB)
            ]
            turned = mm(swap, jnp.concatenate(blocks, axis=1)).astype(BF16)
            for g in range(share // SLAB):
                own = turned[:, g * channels : (g + 1) * channels].reshape(SLAB, SLAB, channels)
                for e in range(fold):
                    place = places[(p * share // SLAB + g) * fold + e]
                    out_refs[p][pl.ds(place * each, each)] = own[e * each : (e + 1) * each]
        rows = pl.ds(p * share, share) if turn else slice(None)
        copies.append(
            pltpu.make_async_copy(out_refs[p], target.at[rows], sems.at[1 + p])
        )
        copies[-1].start()
    for copy in copies:
        copy.wait()


def largest(total, bound):
    return max(d for d in range(1, bound + 1) if total % d == 0)


def in_vmem(count):
    return [pl.BlockSpec(memory_space=pltpu.VMEM)] * count


def shifts(blocks, sign):
    arrived = [blocks[0]]
    for k in range(1, SLOTS):
        to = [(i, (i + sign * k) % SLOTS) for i in range(SLOTS)]
        arrived.append(lax.ppermute(blocks[k], "res", to))
    return arrived


def body(
    aligned_chain_features,
    pair_representation_state,
    gap_block_flags,
    pair_norm_gain,
    pair_head_weight,
    horizontal_scaling_factor,
    row_input_weight,
    horizontal_final_matrix,
    vertical_scaling_factor,
    column_input_weight,
    vertical_final_matrix,
    feedforward_scaling_factor,
    feedforward_widen_matrix,
    feedforward_shrink_matrix,
):
    groups = lax.axis_size("res")
    total_seqs, local_res, channels = aligned_chain_features.shape
    residues = pair_representation_state.shape[1]
    heads = pair_head_weight.shape[1]
    local_seqs = total_seqs // groups
    by_shifts = groups == SLOTS and local_res % SLAB == 0 and local_seqs % SLAB == 0
    seq_parts = 2 if by_shifts else 1
    res_parts = local_res // SLAB if by_shifts else 1
    part_seqs = local_seqs // seq_parts
    part_total = total_seqs // seq_parts
    part_res = local_res // res_parts
    here = lax.axis_index("res")

    def exchange(values):
        return lax.all_to_all(values, "res", split_axis=0, concat_axis=0, tiled=True)

    def kernel_call(
        kernel, name, micros, in_specs, out_shapes, scratch, space=pltpu.VMEM, aliases={}
    ):
        return pl.pallas_call(
            kernel,
            out_shape=[jax.ShapeDtypeStruct(*shape) for shape in out_shapes],
            in_specs=in_specs,
            out_specs=[pl.BlockSpec(memory_space=space)] * len(out_shapes),
            input_output_aliases=aliases,
            scratch_shapes=scratch,
            compiler_params=pltpu.CompilerParams(vmem_limit_bytes=VMEM_BYTES),
            cost_estimate=pl.CostEstimate(
                flops=int(micros * 1e9), bytes_accessed=1 << 20, transcendentals=0
            ),
            name=name,
        )

    def half_of(half):
        return aligned_chain_features[half * part_total : (half + 1) * part_total].reshape(
            groups, part_seqs, local_res, channels
        )

    if by_shifts:

        def cut(features, k):
            start = lax.rem(here + k, groups) * part_seqs
            return lax.dynamic_slice_in_dim(features, start, part_seqs, 0)

        foremost, features = lax.optimization_barrier(
            (cut(aligned_chain_features, 1), aligned_chain_features)
        )
        blocks = [cut(features, k) for k in range(groups)]
        blocks[1] = foremost
        arrived = [shifts(blocks, 1)]
    else:
        arrived = [[exchange(half_of(0))]]
    (bias_local,) = kernel_call(
        bias_kernel, "pair_bias", 5, in_vmem(3), [((heads, local_res, residues), BF16)], [],
    )(pair_norm_gain[None, :], pair_head_weight, pair_representation_state)
    if by_shifts:
        bias_local, *arrived[0] = lax.optimization_barrier((bias_local, *arrived[0]))
        bias_all = jnp.stack(shifts([bias_local] * groups, 1))
    else:
        bias_all = lax.all_gather(bias_local, "res", axis=0, tiled=False)
    for half in range(1, seq_parts):
        bias_all, values = lax.optimization_barrier((bias_all, half_of(half)))
        arrived.append([exchange(values)])

    column_block = (here * local_res) // BLOCK
    col_gap = lax.dynamic_slice_in_dim(gap_block_flags, column_block, 1, 1).reshape(1, total_seqs)
    place = here.astype(jnp.int32)[None]

    def row_attention(part, kinds, *after):
        gap = lax.dynamic_slice_in_dim(
            gap_block_flags, part * part_total + here * part_seqs, part_seqs, 0
        )
        by_row = (part_seqs, residues, channels)
        blocks = arrived[part]
        projected = kernel_call(
            functools.partial(project_kernel, heads, groups), "row_project", 3,
            in_vmem(2 + len(blocks)),
            [(by_row, BF16), (by_row, BF16), (by_row, BF16), (by_row, F32)], [],
        )(horizontal_scaling_factor[None, :], row_input_weight, *blocks)
        operands = (*projected, horizontal_final_matrix, bias_all, *blocks)
        count = local_res // len(kinds)
        outs = []
        for kind in kinds:
            outs += [((groups, part_seqs, count, channels), BF16)]
        return kernel_call(
            functools.partial(row_kernel, len(blocks), kinds, by_shifts), "row_attention", 10,
            [pl.BlockSpec(memory_space=pltpu.SMEM)] * 2
            + in_vmem(len(operands))
            + [pl.BlockSpec(memory_space=pl.ANY)] * len(after),
            outs,
            [
                pltpu.VMEM((heads, residues, residues), F32),
                pltpu.VMEM((part_seqs, residues, channels), BF16),
            ],
        )(gap, place, *operands, *after)

    if by_shifts:
        first = row_attention(0, (STACKED,))
        returned = exchange(first[0])
        kinds = (LISTED,) * (res_parts - 1) + (STACKED,)
        second = row_attention(1, kinds, first[0])
        finals = [shifts(list(part), -1) for part in second[:-1]]
        finals.append([exchange(second[-1])])
    else:
        (first,) = row_attention(0, (STACKED,))
        back = exchange(first).reshape(total_seqs, local_res, channels)
        kinds, finals = (STACKED,), [[jnp.swapaxes(back, 0, 1)]]
    done = []
    for c in range(res_parts):
        pieces, lows, own_gap = finals[c], ((kinds[c], 0),), col_gap
        if by_shifts:
            pieces, lows = [returned] + pieces, ((STACKED, c * part_res),) + lows
        if kinds[c] == LISTED:
            second = col_gap[:, part_total:].reshape(groups, part_seqs)
            second = jnp.roll(second, -here, axis=0).reshape(1, part_total)
            own_gap = jnp.concatenate([col_gap[:, :part_total], second], axis=1)
        shape = (total_seqs, local_res, channels)
        if not by_shifts:
            shape = (part_res, total_seqs, channels)
        part_shape = (total_seqs, part_res, channels) if by_shifts else shape
        before = done[-1:]
        at = 8 + len(pieces)
        held = pltpu.VMEM((part_res, total_seqs, channels), BF16)
        done += kernel_call(
            functools.partial(column_kernel, heads, by_shifts, lows, c * part_res),
            "column_transition", 10,
            [pl.BlockSpec(memory_space=pltpu.SMEM)]
            + in_vmem(6)
            + [pl.BlockSpec(memory_space=pltpu.HBM)]
            + in_vmem(len(pieces))
            + [pl.BlockSpec(memory_space=pl.ANY)] * len(before),
            [(shape, BF16)],
            [
                held, held, held, held,
                pltpu.VMEM((part_res, total_seqs, channels), F32),
                held, held,
                pltpu.VMEM(feedforward_shrink_matrix.shape, BF16),
                pltpu.SemaphoreType.DMA((1 + len(lows),)),
            ]
            + [pltpu.VMEM((part_shape[0] // len(lows), *part_shape[1:]), BF16)] * len(lows),
            pl.ANY,
            {at: 0} if before else {},
        )(
            place, own_gap.reshape(total_seqs, 1), vertical_scaling_factor[None, :], feedforward_scaling_factor[None, :],
            column_input_weight, vertical_final_matrix, feedforward_widen_matrix,
            feedforward_shrink_matrix, *pieces, *before,
        )
    return done[-1] if by_shifts else jnp.swapaxes(done[-1], 0, 1)


def solution(mesh):
    placed = (
        P("dp", "res", None),
        P(("dp", "res"), None, None),
        P("dp", None),
    ) + (P(),) * 11
    return jax.shard_map(
        body, mesh=mesh, in_specs=placed, out_specs=P("dp", "res", None), check_vma=False
    )
```

```python
import functools

import jax
import jax.numpy as jnp
from jax import lax
from jax.experimental import pallas as pl
from jax.experimental.pallas import tpu as pltpu
from jax.sharding import PartitionSpec as P

BLOCK = 128
EPSILON = 1e-05
MASKED_SCORE = -1000000000.0
LANES = 128
SLAB = 16
SLOTS = 8
STACKED, LISTED = 0, 1
F32 = jnp.float32
BF16 = jnp.bfloat16
VMEM_BYTES = 16 * 1024 * 1024


def layer_normalize(values_f, scale_gain):
    centred = values_f - jnp.mean(values_f, axis=-1, keepdims=True)
    spread = jnp.mean(centred * centred, axis=-1, keepdims=True)
    return centred * lax.rsqrt(spread + EPSILON) * scale_gain


def mm(lhs, rhs):
    return jnp.dot(lhs, rhs, preferred_element_type=F32)


def mm_nt(lhs, rhs):
    return lax.dot_general(lhs, rhs, (((1,), (1,)), ((), ())), preferred_element_type=F32)


def swap_matrix(outer, inner):
    size = outer * inner
    to = lax.broadcasted_iota(jnp.int32, (size, size), 0)
    come = lax.broadcasted_iota(jnp.int32, (size, size), 1)
    source = lax.rem(to, outer) * inner + lax.div(to, outer)
    return jnp.where(come == source, 1.0, 0.0).astype(BF16)


def bias_kernel(gain_ref, weight_ref, pair_ref, out_ref):
    local_res, residues, channels = pair_ref.shape
    heads = out_ref.shape[0]
    step = min(SLAB, local_res)
    few = min(4, step)
    width = heads * step
    head_at = lax.broadcasted_iota(jnp.int32, (heads, width), 0)
    spread = jnp.where(lax.broadcasted_iota(jnp.int32, (heads, width), 1) // step == head_at, 1.0, 0.0)
    wide = mm(weight_ref[...], spread.astype(BF16))
    lane = lax.broadcasted_iota(jnp.int32, wide.shape, 1)
    weights = [jnp.where(lane % step == i, wide, 0.0).astype(BF16) for i in range(step)]
    for p in range(0, local_res, step):
        projected = None
        for i in range(0, step, few):
            x = pair_ref[p + i : p + i + few].reshape(few * residues, channels)
            normed = layer_normalize(x.astype(F32), gain_ref[...]).astype(BF16)
            left = [normed[j * residues : (j + 1) * residues] for j in range(few)]
            part = mm(jnp.concatenate(left, axis=1), jnp.concatenate(weights[i : i + few], axis=0))
            projected = part if projected is None else projected + part
        out_ref[:, p : p + step] = projected.T.reshape(heads, step, residues).astype(BF16)


def softmax_lanes(scores):
    e = jnp.exp(scores - jnp.max(scores, axis=-1, keepdims=True))
    total = jnp.sum(e, axis=-1, keepdims=True)
    inverse = pl.reciprocal(total, approx=True)
    inverse = inverse * (2.0 - total * inverse)
    return (e * inverse).astype(BF16)


def gate_of(values):
    return 0.5 * jnp.tanh(0.5 * values) + 0.5


def pick_heads(parts, depth):
    lane = lax.broadcasted_iota(jnp.int32, parts[0].shape, 1)
    slot = lane // depth % len(parts)
    picked = parts[-1]
    for j in range(len(parts) - 2, -1, -1):
        picked = jnp.where(slot == j, parts[j], picked)
    return picked


def lane_mask(width, depth, slots, j):
    lane = lax.broadcasted_iota(jnp.int32, (1, width), 1)
    return jnp.where(lane // depth % slots == j, 1.0, 0.0).astype(BF16)


def rows_of(refs, slot, at):
    ref = refs[0].at[slot] if len(refs) == 1 else refs[slot]
    return ref[pl.ds(at, 1)].reshape(ref.shape[1:])


def project_kernel(heads, groups, gain_ref, win_ref, *refs):
    x_refs, (q_ref, k_ref, v_ref, gate_ref) = refs[:-4], refs[-4:]
    seqs, residues, channels = q_ref.shape
    scale = (channels // heads) ** (-0.5)
    batch = largest(seqs, 4)

    def dense(i, carry):
        x = [rows_of(x_refs, t, i * batch + j) for j in range(batch) for t in range(groups)]
        x = jnp.concatenate(x, axis=0).astype(F32)
        normed = layer_normalize(x, gain_ref[...]).astype(BF16)
        some = pl.ds(i * batch, batch)
        shape = (batch, residues, channels)
        q = (mm(normed, win_ref[:, :channels]) * scale).astype(BF16)
        q_ref[some] = q.reshape(shape)
        k_ref[some] = mm(normed, win_ref[:, channels : 2 * channels]).astype(BF16).reshape(shape)
        v_ref[some] = mm(normed, win_ref[:, 2 * channels : 3 * channels]).astype(BF16).reshape(shape)
        gate_ref[some] = gate_of(mm(normed, win_ref[:, 3 * channels :])).reshape(shape)
        return carry

    lax.fori_loop(0, seqs // batch, dense, 0)


def in_turn(tasks, scores_of, weights_of, mixed_of):
    results, scores = [], scores_of(tasks[0])
    for at, task in enumerate(tasks):
        ahead = scores_of(tasks[at + 1]) if at + 1 < len(tasks) else None
        results.append(mixed_of(task, weights_of(task, scores)))
        scores = ahead
    return results


def row_kernel(
    blocks, kinds, by_shifts, gap_ref, place_ref, q_ref, k_ref, v_ref, gate_ref, wout_ref, bias_ref, *refs
):
    x_refs, refs, (bias_scr, gated_scr) = refs[:blocks], refs[blocks:-2], refs[-2:]
    groups, heads, local_res, residues = bias_ref.shape
    out_refs = []
    for kind in kinds[::-1]:
        out_refs.insert(0, refs[-1:])
        refs = refs[:-1]
    seqs, _, channels = q_ref.shape
    depth = channels // heads
    per = LANES // depth
    batch = largest(seqs, 4)
    part_res = local_res // len(kinds)

    def home(slot):
        return slot if blocks == 1 else lax.rem(place_ref[0] - slot + groups, groups)

    def residue_at(place):
        return home(place // local_res) * local_res + place % local_res

    square = (residues, residues)
    residue = lax.broadcasted_iota(jnp.int32, square, 0)
    order = jnp.where(residue == residue_at(lax.broadcasted_iota(jnp.int32, square, 1)), 1.0, 0.0)
    order = order.astype(BF16)
    slots = list(range(groups))
    if by_shifts and blocks == 1:
        slots = [lax.rem(place_ref[0] - t + groups, groups) for t in range(groups)]
    for h in range(heads):
        rows = jnp.concatenate([bias_ref[slot, h] for slot in slots], axis=0)
        bias_scr[h] = mm(rows, order)
    masks = [lane_mask(LANES, depth, per, j) for j in range(per)]
    block_at = residue_at(lax.broadcasted_iota(jnp.int32, (1, residues), 1)) // BLOCK

    def attend(i, carry):
        tasks = [(u, g) for u in range(batch) for g in range(heads // per)]
        at = [i * batch + u for u in range(batch)]
        gaps = []
        for s in at:
            gap = jnp.zeros((1, residues), F32)
            for b in range(residues // BLOCK):
                closed = jnp.where(gap_ref[s, b] == 1, MASKED_SCORE, 0.0)
                gap = jnp.where(block_at == b, closed, gap)
            gaps.append(gap)
        gates = [gate_ref[s] for s in at]

        def lanes(ref, task):
            return ref[at[task[0]], :, task[1] * LANES : (task[1] + 1) * LANES]

        def scores_of(task):
            q = lanes(q_ref, task)
            return mm_nt(
                jnp.concatenate([q * mask for mask in masks], axis=0), lanes(k_ref, task)
            )

        def weights_of(task, scores):
            weights = []
            for j in range(per):
                own = scores[j * residues : (j + 1) * residues]
                own = own + bias_scr[task[1] * per + j] + gaps[task[0]]
                weights.append(softmax_lanes(own))
            return jnp.concatenate(weights, axis=0)

        def mixed_of(task, weights):
            mixed = mm(weights, lanes(v_ref, task))
            return pick_heads([mixed[j * residues : (j + 1) * residues] for j in range(per)], depth)

        attended = in_turn(tasks, scores_of, weights_of, mixed_of)
        halves = heads // per
        for u in range(batch):
            whole = jnp.concatenate(attended[u * halves : (u + 1) * halves], axis=1)
            gated_scr[at[u]] = (whole * gates[u]).astype(BF16)
        return carry

    lax.fori_loop(0, seqs // batch, attend, 0)

    def finish(i, carry):
        x = [rows_of(x_refs, t, i * batch + j) for j in range(batch) for t in range(groups)]
        gated = gated_scr[pl.ds(i * batch, batch)].reshape(batch * residues, channels)
        result = jnp.concatenate(x, axis=0).astype(F32) + mm(gated, wout_ref[...])
        result = result.astype(BF16).reshape(batch, groups, local_res, channels)
        for j in range(batch):
            s = i * batch + j
            for p, (kind, outs) in enumerate(zip(kinds, out_refs)):
                for t in range(groups):
                    rows = result[j, t, p * part_res : (p + 1) * part_res]
                    if kind == STACKED:
                        outs[0][home(t), s] = rows
                    elif blocks == 1:
                        outs[0][lax.rem(place_ref[0] - t + groups, groups), s] = rows
                    else:
                        outs[0][t, s] = rows
        return carry

    lax.fori_loop(0, seqs // batch, finish, 0)


def column_kernel(
    heads, turn, lows, earlier, place_ref, gap_ref, gain_ref, gain2_ref, win_ref, wout_ref,
    widen_ref, shrink_ref, *refs,
):
    pieces, places = [], []
    for kind, low in lows:
        if kind == STACKED:
            pieces += [(refs[0].at[g] if turn else refs[0], low) for g in range(SLOTS if turn else 1)]
            places += [len(places) + g for g in range(SLOTS)]
            refs = refs[1:]
        else:
            pieces += [(ref, low) for ref in refs[:SLOTS]]
            places += [len(places) + lax.rem(place_ref[0] + t, SLOTS) for t in range(SLOTS)]
            refs = refs[SLOTS:]
    refs = refs[1:] if earlier else refs
    (out_hbm, turned_scr, q_scr, k_scr, v_scr, gate_scr, gated_scr, done_scr, out_ref, sem) = refs
    local_res, seqs, channels = turned_scr.shape
    depth = channels // heads
    per = LANES // depth
    halves = heads // per
    scale = depth ** (-0.5)
    batch = largest(local_res, 8)
    slabs = local_res // SLAB if turn else 0
    swap = swap_matrix(SLAB, SLAB)
    if not turn:
        turned_scr[...] = pieces[0][0][...]
    each = pieces[0][0].shape[0]
    fold = SLAB // each if turn else 1
    for c in range(slabs):
        parts = [
            piece[:, low + c * SLAB : low + (c + 1) * SLAB] for piece, low in pieces
        ]
        blocks = [
            jnp.concatenate(parts[i : i + fold], axis=0).reshape(SLAB * SLAB, channels)
            for i in range(0, len(parts), fold)
        ]
        turned = mm(swap, jnp.concatenate(blocks, axis=1)).astype(BF16)
        for g in range(seqs // SLAB):
            turned_scr[c * SLAB : (c + 1) * SLAB, g * SLAB : (g + 1) * SLAB] = turned[
                :, g * channels : (g + 1) * channels
            ].reshape(SLAB, SLAB, channels)

    shape = (batch, seqs, channels)

    def dense(i):
        some, held = slice(i * batch, (i + 1) * batch), []

        def slot(j):
            return mm(held[0], win_ref[:, j * channels : (j + 1) * channels])

        def norm():
            x = turned_scr[some].reshape(batch * seqs, channels).astype(F32)
            held.append(layer_normalize(x, gain_ref[...]).astype(BF16))

        def query():
            q_scr[some] = (slot(0) * scale).astype(BF16).reshape(shape)

        def key():
            k_scr[some] = slot(1).astype(BF16).reshape(shape)

        def value():
            v_scr[some] = slot(2).astype(BF16).reshape(shape)

        def gate():
            gate_scr[some] = gate_of(slot(3)).reshape(shape)

        return [norm, query, key, value, gate]

    mask = jnp.broadcast_to(
        jnp.where(gap_ref[...] == 1, MASKED_SCORE, 0.0), (seqs, halves * seqs)
    )
    masks = [lane_mask(channels, depth, per, j) for j in range(per)]
    blank = jnp.zeros((seqs, LANES), BF16)

    def diagonal(values):
        rows = []
        for g in range(halves):
            own = values[:, g * LANES : (g + 1) * LANES]
            rows.append(jnp.concatenate([own if i == g else blank for i in range(halves)], axis=1))
        return jnp.concatenate(rows, axis=0)

    def scores_of(r):
        k = k_scr[r]
        return mm_nt(jnp.concatenate([k * m for m in masks], axis=0), diagonal(q_scr[r]))

    def weights_of(r, scores):
        weights = []
        for j in range(per):
            own = scores[j * seqs : (j + 1) * seqs] + mask
            e = jnp.exp(own - jnp.max(own, axis=0, keepdims=True))
            weights.append((e * (1.0 / jnp.sum(e, axis=0, keepdims=True))).astype(BF16))
        return weights

    def mixed_of(r, weights):
        v = v_scr[r].T
        mixed = [None] * heads
        for j in range(per):
            left = [v[(g * per + j) * depth : (g * per + j + 1) * depth] for g in range(halves)]
            both = mm(jnp.concatenate(left, axis=0), weights[j])
            for g in range(halves):
                mixed[g * per + j] = both[g * depth : (g + 1) * depth, g * seqs : (g + 1) * seqs]
        gated_scr[r] = (jnp.concatenate(mixed, axis=0).T * gate_scr[r]).astype(BF16)

    def finish(i):
        some, held = slice(i * batch, (i + 1) * batch), {}

        def second():
            x = turned_scr[some].reshape(batch * seqs, channels)
            gated = gated_scr[some].reshape(batch * seqs, channels)
            rounded = (x.astype(F32) + mm(gated, wout_ref[...])).astype(BF16).astype(F32)
            held["second"] = rounded
            held["normed"] = layer_normalize(rounded, gain2_ref[...]).astype(BF16)

        def widen(j):
            columns = slice(j * channels, (j + 1) * channels)
            part = jnp.maximum(mm(held["normed"], widen_ref[:, columns]), 0.0).astype(BF16)
            held.setdefault("hidden", []).append(part)

        def shrink():
            hidden = jnp.concatenate(held["hidden"], axis=1)
            result = (held["second"] + mm(hidden, shrink_ref[...])).astype(BF16)
            done_scr[some] = result.reshape(shape)

        steps = [functools.partial(widen, j) for j in range(widen_ref.shape[1] // channels)]
        return [second, *steps, shrink]

    batches = local_res // batch
    for step in dense(0):
        step()
    for i in range(batches):
        beside = (dense(i + 1) if i + 1 < batches else []) + (finish(i - 1) if i else [])
        tasks = list(range(i * batch, (i + 1) * batch))
        scores = scores_of(tasks[0])
        for n, r in enumerate(tasks):
            ahead = scores_of(tasks[n + 1]) if n + 1 < len(tasks) else None
            weights = weights_of(r, scores)
            for step in beside[:1]:
                step()
            beside = beside[1:]
            mixed_of(r, weights)
            scores = ahead
        for step in beside:
            step()
    for step in finish(batches - 1):
        step()
    if not turn:
        out_ref[...] = done_scr[...]
    for c in range(slabs):
        blocks = [
            done_scr[c * SLAB : (c + 1) * SLAB, g * SLAB : (g + 1) * SLAB].reshape(
                SLAB * SLAB, channels
            )
            for g in range(seqs // SLAB)
        ]
        turned = mm(swap, jnp.concatenate(blocks, axis=1)).astype(BF16)
        start = c * SLAB
        for g in range(seqs // SLAB):
            own = turned[:, g * channels : (g + 1) * channels].reshape(SLAB, SLAB, channels)
            for e in range(fold):
                place = places[g * fold + e]
                out_ref[pl.ds(place * each, each), start : start + SLAB] = own[
                    e * each : (e + 1) * each
                ]
    target = out_hbm.at[:, earlier : earlier + local_res] if turn else out_hbm
    copy = pltpu.make_async_copy(out_ref, target, sem)
    copy.start()
    copy.wait()


def largest(total, bound):
    return max(d for d in range(1, bound + 1) if total % d == 0)


def in_vmem(count):
    return [pl.BlockSpec(memory_space=pltpu.VMEM)] * count


def shifts(blocks, sign):
    arrived = [blocks[0]]
    for k in range(1, SLOTS):
        to = [(i, (i + sign * k) % SLOTS) for i in range(SLOTS)]
        arrived.append(lax.ppermute(blocks[k], "res", to))
    return arrived


def body(
    aligned_chain_features,
    pair_representation_state,
    gap_block_flags,
    pair_norm_gain,
    pair_head_weight,
    horizontal_scaling_factor,
    row_input_weight,
    horizontal_final_matrix,
    vertical_scaling_factor,
    column_input_weight,
    vertical_final_matrix,
    feedforward_scaling_factor,
    feedforward_widen_matrix,
    feedforward_shrink_matrix,
):
    groups = lax.axis_size("res")
    total_seqs, local_res, channels = aligned_chain_features.shape
    residues = pair_representation_state.shape[1]
    heads = pair_head_weight.shape[1]
    local_seqs = total_seqs // groups
    by_shifts = groups == SLOTS and local_res % SLAB == 0 and local_seqs % SLAB == 0
    seq_parts = 2 if by_shifts else 1
    res_parts = local_res // SLAB if by_shifts else 1
    part_seqs = local_seqs // seq_parts
    part_total = total_seqs // seq_parts
    part_res = local_res // res_parts
    here = lax.axis_index("res")

    def exchange(values):
        return lax.all_to_all(values, "res", split_axis=0, concat_axis=0, tiled=True)

    def kernel_call(
        kernel, name, micros, in_specs, out_shapes, scratch, space=pltpu.VMEM, aliases={}
    ):
        return pl.pallas_call(
            kernel,
            out_shape=[jax.ShapeDtypeStruct(*shape) for shape in out_shapes],
            in_specs=in_specs,
            out_specs=[pl.BlockSpec(memory_space=space)] * len(out_shapes),
            input_output_aliases=aliases,
            scratch_shapes=scratch,
            compiler_params=pltpu.CompilerParams(vmem_limit_bytes=VMEM_BYTES),
            cost_estimate=pl.CostEstimate(
                flops=int(micros * 1e9), bytes_accessed=1 << 20, transcendentals=0
            ),
            name=name,
        )

    def half_of(half):
        return aligned_chain_features[half * part_total : (half + 1) * part_total].reshape(
            groups, part_seqs, local_res, channels
        )

    if by_shifts:

        def cut(features, k):
            start = lax.rem(here + k, groups) * part_seqs
            return lax.dynamic_slice_in_dim(features, start, part_seqs, 0)

        foremost, features = lax.optimization_barrier(
            (cut(aligned_chain_features, 1), aligned_chain_features)
        )
        blocks = [cut(features, k) for k in range(groups)]
        blocks[1] = foremost
        arrived = [shifts(blocks, 1)]
    else:
        arrived = [[exchange(half_of(0))]]
    (bias_local,) = kernel_call(
        bias_kernel, "pair_bias", 5, in_vmem(3), [((heads, local_res, residues), BF16)], [],
    )(pair_norm_gain[None, :], pair_head_weight, pair_representation_state)
    if by_shifts:
        bias_local, *arrived[0] = lax.optimization_barrier((bias_local, *arrived[0]))
        bias_all = jnp.stack(shifts([bias_local] * groups, 1))
    else:
        bias_all = lax.all_gather(bias_local, "res", axis=0, tiled=False)
    for half in range(1, seq_parts):
        bias_all, values = lax.optimization_barrier((bias_all, half_of(half)))
        arrived.append([exchange(values)])

    column_block = (here * local_res) // BLOCK
    col_gap = lax.dynamic_slice_in_dim(gap_block_flags, column_block, 1, 1).reshape(1, total_seqs)
    place = here.astype(jnp.int32)[None]

    def row_attention(part, kinds, *after):
        gap = lax.dynamic_slice_in_dim(
            gap_block_flags, part * part_total + here * part_seqs, part_seqs, 0
        )
        by_row = (part_seqs, residues, channels)
        blocks = arrived[part]
        projected = kernel_call(
            functools.partial(project_kernel, heads, groups), "row_project", 3,
            in_vmem(2 + len(blocks)),
            [(by_row, BF16), (by_row, BF16), (by_row, BF16), (by_row, F32)], [],
        )(horizontal_scaling_factor[None, :], row_input_weight, *blocks)
        operands = (*projected, horizontal_final_matrix, bias_all, *blocks)
        count = local_res // len(kinds)
        outs = []
        for kind in kinds:
            outs += [((groups, part_seqs, count, channels), BF16)]
        return kernel_call(
            functools.partial(row_kernel, len(blocks), kinds, by_shifts), "row_attention", 10,
            [pl.BlockSpec(memory_space=pltpu.SMEM)] * 2
            + in_vmem(len(operands))
            + [pl.BlockSpec(memory_space=pl.ANY)] * len(after),
            outs,
            [
                pltpu.VMEM((heads, residues, residues), F32),
                pltpu.VMEM((part_seqs, residues, channels), BF16),
            ],
        )(gap, place, *operands, *after)

    if by_shifts:
        first = row_attention(0, (STACKED,))
        returned = exchange(first[0])
        kinds = (LISTED,) * (res_parts - 1) + (STACKED,)
        second = row_attention(1, kinds, first[0])
        finals = [shifts(list(part), -1) for part in second[:-1]]
        finals.append([exchange(second[-1])])
    else:
        (first,) = row_attention(0, (STACKED,))
        back = exchange(first).reshape(total_seqs, local_res, channels)
        kinds, finals = (STACKED,), [[jnp.swapaxes(back, 0, 1)]]
    done = []
    for c in range(res_parts):
        pieces, lows, own_gap = finals[c], ((kinds[c], 0),), col_gap
        if by_shifts:
            pieces, lows = [returned] + pieces, ((STACKED, c * part_res),) + lows
        if kinds[c] == LISTED:
            second = col_gap[:, part_total:].reshape(groups, part_seqs)
            second = jnp.roll(second, -here, axis=0).reshape(1, part_total)
            own_gap = jnp.concatenate([col_gap[:, :part_total], second], axis=1)
        shape = (total_seqs, local_res, channels)
        if not by_shifts:
            shape = (part_res, total_seqs, channels)
        part_shape = (total_seqs, part_res, channels) if by_shifts else shape
        before = done[-1:]
        at = 8 + len(pieces)
        held = pltpu.VMEM((part_res, total_seqs, channels), BF16)
        done += kernel_call(
            functools.partial(column_kernel, heads, by_shifts, lows, c * part_res),
            "column_transition", 10,
            [pl.BlockSpec(memory_space=pltpu.SMEM)]
            + in_vmem(7 + len(pieces))
            + [pl.BlockSpec(memory_space=pl.ANY)] * len(before),
            [(shape, BF16)],
            [
                held, held, held, held,
                pltpu.VMEM((part_res, total_seqs, channels), F32),
                held, held,
                pltpu.VMEM(part_shape, BF16),
                pltpu.SemaphoreType.DMA,
            ],
            pl.ANY,
            {at: 0} if before else {},
        )(
            place, own_gap.reshape(total_seqs, 1), vertical_scaling_factor[None, :], feedforward_scaling_factor[None, :],
            column_input_weight, vertical_final_matrix, feedforward_widen_matrix,
            feedforward_shrink_matrix, *pieces, *before,
        )
    return done[-1] if by_shifts else jnp.swapaxes(done[-1], 0, 1)


def solution(mesh):
    placed = (
        P("dp", "res", None),
        P(("dp", "res"), None, None),
        P("dp", None),
    ) + (P(),) * 11
    return jax.shard_map(
        body, mesh=mesh, in_specs=placed, out_specs=P("dp", "res", None), check_vma=False
    )
```
